32 devices in a mesh: row: 2 (over core), seq: 16 (over z, y, x).
Axes of the slice: x: 2, y: 2, z: 4, core: 2. Of those that a mesh axis runs over, the one named last changes fastest.
Arguments:
- block_in: bfloat16 [4, 4096, 768], P('row', 'seq'), may hold values from -6 to 6
- lengths: int32 [4, 8], P('row'), may hold values from 1 to 3841, as said below
- mixer_gain: float32 [768], replicated, may hold values from 0.5 to 1.5
- mixer_bias: float32 [768], replicated, may hold values from -1.75 to 1.75
- in_weight: bfloat16 [768, 2304], replicated, may hold values from -0.21875 to 0.21875
- short_taps: float32 [3, 2304], replicated, may hold values from -4 to 4
- filter_in: float32 [33, 64], replicated, may hold values from -2 to 2
- filter_in_bias: float32 [64], replicated, may hold values from -3.140625 to 3.140625
- filter_mid: float32 [64, 64], replicated, may hold values from -1.5 to 1.5
- filter_mid_bias: float32 [64], replicated, may hold values from -3.140625 to 3.140625
- filter_freq: float32 [64], replicated, may hold values from 0.5 to 2
- filter_out: float32 [64, 768], replicated, may hold values from -0.03125 to 0.03125
- filter_skip: float32 [768], replicated, may hold values from -6 to 6
- decay_rate: float32 [768], replicated, may hold values from 1.2207031e-05 to 0.1
- out_weight: bfloat16 [768, 768], replicated, may hold values from -0.4375 to 0.4375
- feed_gain: float32 [768], replicated, may hold values from 0.5 to 1.5
- feed_bias: float32 [768], replicated, may hold values from -1.75 to 1.75
- up_weight: bfloat16 [768, 3072], replicated, may hold values from -0.21875 to 0.21875
- down_weight: bfloat16 [3072, 768], replicated, may hold values from -0.15625 to 0.15625
- cotangent: bfloat16 [4, 4096, 768], P('row', 'seq'), may hold values from -6 to 6
Outputs:
- block_out: bfloat16 [4, 4096, 768], P('row', 'seq')
- grad_input: float32 [4, 4096, 768], P('row', 'seq')
- grad_mixer_gain: float32 [768], replicated
- grad_mixer_bias: float32 [768], replicated
- grad_in_weight: float32 [768, 2304], P('seq')
- grad_short_taps: float32 [3, 2304], replicated
- grad_filter_in: float32 [33, 64], replicated
- grad_filter_in_bias: float32 [64], replicated
- grad_filter_mid: float32 [64, 64], replicated
- grad_filter_mid_bias: float32 [64], replicated
- grad_filter_freq: float32 [64], replicated
- grad_filter_out: float32 [64, 768], replicated
- grad_filter_skip: float32 [768], replicated
- grad_out_weight: float32 [768, 768], P('seq')
- grad_feed_gain: float32 [768], replicated
- grad_feed_bias: float32 [768], replicated
- grad_up_weight: float32 [768, 3072], P('seq')
- grad_down_weight: float32 [3072, 768], P('seq')
The draws below stay inside these ranges and needn't reach their ends.
Inputs may be any that keep to these rules, and one draw needn't show every extreme that they name: `lengths`: lengths are positive; in each row they sum to less than 4096, and the positions after their sum are padding.
All inputs are finite; a program needn't handle non-finite values.
Results may differ from the reference program's by a relative error of at most 0.015.
Values may be sent and summed in bfloat16 or wider, within the bound.
A program may use at most 256 MiB of HBM per device.

```python
import math
import jax
import jax.numpy as jnp
from jax import lax

D = 768
FF = 3072
FILT_HID = 64
POS_FEAT = 33
DOCS = 8
TOK_DEV = 256
SEQ_LEN = 4096
ROWS = 4


def cuts_of(cut_key, total):
    order = jax.random.permutation(cut_key, TOK_DEV)
    valid = (order >= 1) & (order < total)
    ranking = jnp.argsort(jnp.where(valid, 0, 1), stable=True)
    chosen = jnp.sort(order[ranking[:DOCS - 2]])
    bounds = jnp.concatenate([jnp.zeros((1,), jnp.int32), chosen.astype(jnp.int32), jnp.reshape(total, (1,)).astype(jnp.int32)])
    return jnp.diff(bounds)


def draw_lengths(key, part):
    key = jax.random.fold_in(key, 7)
    pick_key, pad_key, cut_key = jax.random.split(key, 3)
    padding = jax.random.randint(pad_key, (ROWS,), 1, TOK_DEV // 2 + 1)
    small_total = TOK_DEV - 1 - padding
    smalls = jax.vmap(cuts_of)(jax.random.split(cut_key, ROWS), small_total)
    slot = jax.random.randint(pick_key, (ROWS,), 0, DOCS)
    columns = jnp.arange(DOCS, dtype=jnp.int32)
    source = jnp.clip(jnp.where(columns[None, :] < slot[:, None], columns[None, :], columns[None, :] - 1), 0, DOCS - 2)
    picked = jnp.take_along_axis(smalls, source, axis=1)
    long_doc = SEQ_LEN - TOK_DEV + 1
    return jnp.where(columns[None, :] == slot[:, None], long_doc, picked).astype(jnp.int32)


def level_of(rng, dims, cuts, smallest, largest):
    def one(axis_at, shards_of):
        draws = jax.random.uniform(jax.random.fold_in(jax.random.fold_in(rng, 6), axis_at), (shards_of,), jnp.float32, smallest / len(cuts), largest / len(cuts))
        return jnp.repeat(jnp.exp(draws), dims[axis_at] // shards_of).reshape((-1,) + (1,) * (len(dims) - axis_at - 1))

    level = one(*cuts[0])
    for cut in cuts[1:]:
        level = level * one(*cut)
    return level


def normal_values(own_key, dims, scale, most, pieces=(), kind=jnp.bfloat16):
    values = jax.random.normal(own_key, dims, jnp.float32) * scale
    if len(pieces) > 0:
        values = level_of(own_key, dims, pieces, -0.22, 0.18) * values
    return jnp.clip(values, min=-most, max=most).astype(kind)


def setup_inputs(seed: int = 0) -> dict:
    keys = jax.random.split(jax.random.key(seed), 21)
    block_in = normal_values(keys[0], (ROWS, SEQ_LEN, D), 1.0, 6.0, ((0, 2), (1, 16)))
    lengths = draw_lengths(jax.random.fold_in(keys[20], 71), 0)
    mixer_gain = jnp.clip(1.0 + 0.1 * jax.random.normal(keys[2], (D,), jnp.float32), 0.5, 1.5)
    mixer_bias = normal_values(keys[3], (D,), 0.3, 1.75, (), jnp.float32)
    in_weight = normal_values(keys[4], (D, 3 * D), D ** -0.5, 0.21875)
    short_taps = normal_values(keys[5], (3, 3 * D), 0.7, 4.0, (), jnp.float32)
    filter_in = normal_values(keys[6], (POS_FEAT, FILT_HID), (POS_FEAT // 4) ** -0.5, 2.0, (), jnp.float32)
    filter_in_bias = jnp.clip(jax.random.uniform(keys[7], (FILT_HID,), jnp.float32, -3.140625, 3.140625), -3.140625, 3.140625)
    filter_mid = normal_values(keys[8], (FILT_HID, FILT_HID), (FILT_HID // 4) ** -0.5, 1.5, (), jnp.float32)
    filter_mid_bias = jnp.clip(jax.random.uniform(keys[9], (FILT_HID,), jnp.float32, -3.140625, 3.140625), -3.140625, 3.140625)
    filter_freq = jnp.clip(jnp.exp(jax.random.uniform(keys[10], (FILT_HID,), jnp.float32, math.log(0.5), math.log(2.0))), 0.5, 2.0)
    filter_out = normal_values(keys[11], (FILT_HID, D), (FILT_HID * SEQ_LEN // 8) ** -0.5, 0.03125, (), jnp.float32)
    filter_skip = normal_values(keys[12], (D,), 1.0, 6.0, (), jnp.float32)
    decay_rate = jnp.clip(jnp.exp(jax.random.uniform(keys[13], (D,), jnp.float32, math.log(1.220703143189894e-05), math.log(0.1))), 1.220703143189894e-05, 0.1)
    out_weight = normal_values(keys[14], (D, D), (D // 4) ** -0.5, 0.4375)
    feed_gain = jnp.clip(1.0 + 0.1 * jax.random.normal(keys[15], (D,), jnp.float32), 0.5, 1.5)
    feed_bias = normal_values(keys[16], (D,), 0.3, 1.75, (), jnp.float32)
    up_weight = normal_values(keys[17], (D, FF), D ** -0.5, 0.21875)
    down_weight = normal_values(keys[18], (FF, D), (FF // 2) ** -0.5, 0.15625)
    cotangent = normal_values(keys[19], (ROWS, SEQ_LEN, D), 1.0, 6.0, ((0, 2), (1, 16)))
    return dict(block_in=block_in, lengths=lengths, mixer_gain=mixer_gain, mixer_bias=mixer_bias, in_weight=in_weight, short_taps=short_taps, filter_in=filter_in, filter_in_bias=filter_in_bias, filter_mid=filter_mid, filter_mid_bias=filter_mid_bias, filter_freq=filter_freq, filter_out=filter_out, filter_skip=filter_skip, decay_rate=decay_rate, out_weight=out_weight, feed_gain=feed_gain, feed_bias=feed_bias, up_weight=up_weight, down_weight=down_weight, cotangent=cotangent)


HIGHEST = lax.Precision.HIGHEST

@jax.custom_vjp
def low(v):
    return lax.optimization_barrier(v.astype(jnp.bfloat16)).astype(jnp.float32)

@jax.custom_vjp
def low_back(v):
    return v

def low_keep(v):
    return (low(v), None)

def low_pass(kept, grad):
    return (grad,)

def back_keep(v):
    return (v, None)

def back_low(kept, grad):
    return (low(grad),)
low.defvjp(low_keep, low_pass)
low_back.defvjp(back_keep, back_low)

def layer_norm(values, gain, offset):
    center = values - lax.optimization_barrier(jnp.mean(values, axis=-1, keepdims=True))
    spread = lax.optimization_barrier(jnp.mean(center * center, axis=-1, keepdims=True))
    return center * lax.rsqrt(spread + 1e-05) * gain + offset

def features(length, feat_count):
    band_count = (feat_count - 1) // 2
    positions = jnp.arange(length).astype(jnp.int32)
    band_freq = jnp.arange(1, band_count + 1).astype(jnp.int32)
    turn_index = positions[:, None] * band_freq[None, :] % length
    angles = 2.0 * math.pi / length * turn_index.astype(jnp.float32)
    ramp_feat = positions.astype(jnp.float32)[:, None] / length
    return jnp.concatenate([ramp_feat, jnp.cos(angles), -jnp.sin(angles)], axis=1)

def make_filter(filter_in, filter_in_bias, filter_mid, filter_mid_bias, filter_freq, filter_out, decay_rate, length):
    feats = features(length, filter_in.shape[0])
    hidden = jnp.sin(filter_freq * (jnp.dot(feats, filter_in, precision=HIGHEST) + filter_in_bias))
    hidden = jnp.sin(filter_freq * (jnp.dot(hidden, filter_mid, precision=HIGHEST) + filter_mid_bias))
    raw_filter = jnp.dot(hidden, filter_out, precision=HIGHEST)
    positions = jnp.arange(length).astype(jnp.float32)
    return raw_filter * jnp.exp(-positions[:, None] * decay_rate[None, :])

def hyena_row(block, row_ends, decay_rate, mixer_gain, mixer_bias, in_weight, short_taps, filter_in, filter_in_bias, filter_mid, filter_mid_bias, filter_freq, filter_out, filter_skip, out_weight, feed_gain, feed_bias, up_weight, down_weight):
    length = block.shape[0]
    model_width = block.shape[1]
    positions = jnp.arange(length).astype(jnp.int32)
    live_mask = (positions < row_ends[-1]).astype(jnp.float32)[:, None]
    doc_index = lax.optimization_barrier(jnp.sum((positions[:, None] >= row_ends[None, :]).astype(jnp.int32), axis=1))
    normed = low(layer_norm(block, mixer_gain, mixer_bias))
    projected = low(low_back(jnp.dot(normed, in_weight, precision=HIGHEST)))
    short_mix = short_taps[0] * projected
    for tap_lag in (1, 2):
        moved = jnp.pad(projected, ((tap_lag, 0), (0, 0)))[:length]
        moved_doc = jnp.pad(doc_index, (tap_lag, 0), constant_values=-1)[:length]
        short_mix = short_mix + short_taps[tap_lag] * moved * (moved_doc == doc_index).astype(jnp.float32)[:, None]
    gate_out = short_mix[:, :model_width]
    gate_in = short_mix[:, model_width:2 * model_width]
    stream_v = short_mix[:, 2 * model_width:]
    carried = low(low_back(gate_in * stream_v * live_mask))
    filt = make_filter(filter_in, filter_in_bias, filter_mid, filter_mid_bias, filter_freq, filter_out, decay_rate, length)
    spectrum = jnp.fft.rfft(carried, n=2 * length, axis=0) * jnp.fft.rfft(filt, n=2 * length, axis=0)
    conv = jnp.fft.irfft(spectrum, n=2 * length, axis=0)[:length] + filter_skip * carried
    conv = low(low_back(conv))
    product = low(gate_out * conv * live_mask)
    mixed = block + low_back(jnp.dot(product, out_weight, precision=HIGHEST))
    normed_two = low(layer_norm(mixed, feed_gain, feed_bias))
    pre_act = low_back(jnp.dot(normed_two, up_weight, precision=HIGHEST))
    activ = low(jax.nn.gelu(pre_act))
    return mixed + low_back(jnp.dot(activ, down_weight, precision=HIGHEST))

def reference(block_in, lengths, mixer_gain, mixer_bias, in_weight, short_taps, filter_in, filter_in_bias, filter_mid, filter_mid_bias, filter_freq, filter_out, filter_skip, decay_rate, out_weight, feed_gain, feed_bias, up_weight, down_weight, cotangent):
    params = (mixer_gain, mixer_bias, in_weight.astype(jnp.float32), short_taps, filter_in, filter_in_bias, filter_mid, filter_mid_bias, filter_freq, filter_out, filter_skip, out_weight.astype(jnp.float32), feed_gain, feed_bias, up_weight.astype(jnp.float32), down_weight.astype(jnp.float32))
    doc_ends = jnp.cumsum(lengths, axis=1).astype(jnp.int32)

    def one_row(totals, item):
        block, row_ends, cot_row = item

        def forward(block_row, *weights):
            return hyena_row(block_row, row_ends, decay_rate, *weights)
        result, pull = jax.vjp(forward, block, *params)
        grads = pull(cot_row)
        summed = tuple((a + b for a, b in zip(totals, grads[1:])))
        return (summed, (result.astype(jnp.bfloat16), grads[0]))
    start_totals = tuple((jnp.zeros_like(p) for p in params))
    totals, (outputs, grad_rows) = lax.scan(one_row, start_totals, (block_in.astype(jnp.float32), doc_ends, cotangent.astype(jnp.float32)))
    return (outputs, grad_rows, totals[0], totals[1], totals[2], totals[3], totals[4], totals[5], totals[6], totals[7], totals[8], totals[9], totals[10], totals[11], totals[12], totals[13], totals[14], totals[15])
```

```python
import functools
import math

import jax
import jax.numpy as jnp
from jax import lax
from jax.experimental import pallas as pl
from jax.experimental.pallas import tpu as pltpu
from jax.sharding import PartitionSpec as P

HIGHEST = lax.Precision.HIGHEST


def shifted(array, axis, by):
    peers = lax.axis_size(axis)
    pairs = [(i, i + by) for i in range(peers) if 0 <= i + by < peers]
    return lax.ppermute(array, axis, pairs)


def layer_norm(values, gain, offset):
    center = values - jnp.mean(values, axis=-1, keepdims=True)
    spread = jnp.mean(center * center, axis=-1, keepdims=True)
    return center * lax.rsqrt(spread + 1e-05) * gain + offset


def features(length, feat_count):
    band_count = (feat_count - 1) // 2
    positions = jnp.arange(length, dtype=jnp.int32)
    band_freq = jnp.arange(1, band_count + 1, dtype=jnp.int32)
    turn_index = positions[:, None] * band_freq[None, :] % length
    angles = 2.0 * math.pi / length * turn_index.astype(jnp.float32)
    ramp_feat = positions.astype(jnp.float32)[:, None] / length
    return jnp.concatenate([ramp_feat, jnp.cos(angles), -jnp.sin(angles)], axis=1)


def filter_rows(
    filter_in,
    filter_in_bias,
    filter_mid,
    filter_mid_bias,
    filter_freq,
    out_part,
    decay_part,
    length,
):
    feats = features(length, filter_in.shape[0])
    hidden = jnp.sin(filter_freq * (jnp.dot(feats, filter_in, precision=HIGHEST) + filter_in_bias))
    hidden = jnp.sin(
        filter_freq * (jnp.dot(hidden, filter_mid, precision=HIGHEST) + filter_mid_bias)
    )
    raw_filter = jnp.einsum("lh,hc->cl", hidden, out_part, precision=HIGHEST)
    positions = jnp.arange(length, dtype=jnp.float32)
    return raw_filter * jnp.exp(-decay_part[:, None] * positions[None, :])


def angle_table(angle_index, period):
    turned = 2.0 * math.pi / period * angle_index.astype(jnp.float32)
    return (jnp.cos(turned), jnp.sin(turned))


def dft_tables(length):
    half_rows = math.isqrt(length // 2)
    while length % half_rows:
        half_rows = half_rows - 1
    full_rows = 2 * half_rows
    col_count = length // half_rows
    total = full_rows * col_count
    row_index = jnp.arange(full_rows, dtype=jnp.int32)
    col_index = jnp.arange(col_count, dtype=jnp.int32)
    first_table = angle_table(
        row_index[:, None] * row_index[None, :half_rows] % full_rows, full_rows
    )
    second = angle_table(col_index[:, None] * col_index[None, :] % col_count, col_count)
    twiddle = angle_table(row_index[:, None] * col_index[None, :] % total, total)
    return (half_rows, col_count, first_table, second, twiddle)


def forward_dft(signal, tables):
    half_rows, col_count, first_table, second, twiddle = tables
    leading = signal.shape[:-1]
    grid_view = signal.reshape(leading + (half_rows, col_count))
    real_part = jnp.einsum("kn,...nm->...km", first_table[0], grid_view, precision=HIGHEST)
    imag_part = -jnp.einsum("kn,...nm->...km", first_table[1], grid_view, precision=HIGHEST)
    turn_real = real_part * twiddle[0] + imag_part * twiddle[1]
    turn_imag = imag_part * twiddle[0] - real_part * twiddle[1]
    out_real = jnp.einsum("...kn,nj->...kj", turn_real, second[0], precision=HIGHEST) + jnp.einsum(
        "...kn,nj->...kj", turn_imag, second[1], precision=HIGHEST
    )
    out_imag = jnp.einsum("...kn,nj->...kj", turn_imag, second[0], precision=HIGHEST) - jnp.einsum(
        "...kn,nj->...kj", turn_real, second[1], precision=HIGHEST
    )
    return (out_real, out_imag)


def inverse_dft(spec_real, spec_imag, tables):
    half_rows, col_count, first_table, second, twiddle = tables
    leading = spec_real.shape[:-2]
    real_part = jnp.einsum("...kj,jn->...kn", spec_real, second[0], precision=HIGHEST) - jnp.einsum(
        "...kj,jn->...kn", spec_imag, second[1], precision=HIGHEST
    )
    imag_part = jnp.einsum("...kj,jn->...kn", spec_imag, second[0], precision=HIGHEST) + jnp.einsum(
        "...kj,jn->...kn", spec_real, second[1], precision=HIGHEST
    )
    turn_real = real_part * twiddle[0] - imag_part * twiddle[1]
    turn_imag = imag_part * twiddle[0] + real_part * twiddle[1]
    grid_view = jnp.einsum(
        "kn,...km->...nm", first_table[0], turn_real, precision=HIGHEST
    ) - jnp.einsum("kn,...km->...nm", first_table[1], turn_imag, precision=HIGHEST)
    grid_view = grid_view * (1.0 / (2 * half_rows * col_count))
    return grid_view.reshape(leading + (half_rows * col_count,))


MESH = pl.DeviceIdType.MESH
VMEM_LIMIT = 56 * 1024 * 1024


def seq_weights(core, groups):
    weights = []
    w = 1
    while w < groups:
        weights.append(w)
        w *= 2
    first = weights[0] + core * (weights[1] - weights[0])
    second = weights[1] - core * (weights[1] - weights[0])
    return [first, second] + weights[2:]


def reduce_kernel(
    rows,
    groups,
    gin,
    gout,
    gup,
    gdown,
    small,
    last,
    in_o,
    out_o,
    up_o,
    down_o,
    small_o,
    last_o,
    own,
    core_buf,
    step_buf,
    wide_buf,
    fin_own,
    fin_buf,
    small_row,
    small_sum,
    small_part,
    small_done,
    last_row,
    last_sum,
    core_ss,
    core_rs,
    step_ss,
    step_rs,
    wide_ss,
    wide_rs,
    fin_sem,
    srow_ss,
    srow_rs,
    spart_ss,
    spart_rs,
    sdone_ss,
    sdone_rs,
    lrow_ss,
    lrow_rs,
    last_ss,
    last_rs,
):
    me = lax.axis_index("seq")
    row = lax.axis_index("row")
    core = lax.rem(row, 2)
    sib = row + 1 - 2 * core
    unit_rows, half = own.shape[2], own.shape[3]
    chunk = small_part.shape[1]
    barrier = pltpu.get_barrier_semaphore()
    for d in range(1, rows):
        pl.semaphore_signal(
            barrier, inc=1, device_id={"row": lax.rem(row + d, rows)}, device_id_type=MESH
        )
    for d in range(1, groups):
        pl.semaphore_signal(
            barrier, inc=1, device_id={"seq": lax.rem(me + d, groups)}, device_id_type=MESH
        )
    pl.semaphore_wait(barrier, rows + groups - 2)

    weights = seq_weights(core, groups)
    bits = [lax.rem(me // w, 2) for w in weights]
    steps = len(weights)
    sib_weights = seq_weights(1 - core, groups)
    sib_bits = [lax.rem(me // w, 2) for w in sib_weights]

    def shard_of(k, i, mine, weights=weights, bits=bits):
        at = 0
        for j in range(k):
            at = at + bits[j] * weights[j]
        at = at + (bits[k] if mine else 1 - bits[k]) * weights[k]
        for j in range(k + 1, steps):
            t = (i >> (steps - 1 - j)) & 1
            at = at + (bits[j] if t else 1 - bits[j]) * weights[j]
        return at

    order = [(False, i) for i in range(groups // 2)] + [(True, i) for i in range(groups // 2)]
    sib_order = [shard_of(0, i, mine, sib_weights, sib_bits) for mine, i in order]
    order = [shard_of(0, i, mine) for mine, i in order]
    parts = [(gin, 3, unit_rows, 0), (gout, 1, unit_rows, 3), (gup, 4, unit_rows, 4)]

    def core_copies(n, s):
        out = []
        for p, (ref, cols, _, _) in enumerate(parts):
            out.append(
                (ref.at[pl.ds(s * unit_rows, unit_rows), pl.ds((1 - core) * cols * half, cols * half)], p)
            )
        out.append((gdown.at[pl.ds(s * 4 * unit_rows, 4 * unit_rows), pl.ds((1 - core) * half, half)], 3))
        dst = [
            core_buf[0].at[n],
            core_buf[1].at[n],
            core_buf[2].at[n],
            core_buf[3].at[n],
        ]
        return [
            pltpu.make_async_remote_copy(
                src_ref=src,
                dst_ref=dst[p],
                send_sem=core_ss.at[n, p],
                recv_sem=core_rs.at[n, p],
                device_id={"row": sib},
                device_id_type=MESH,
            )
            for src, p in out
        ]

    srow = [
        pltpu.make_async_remote_copy(
            src_ref=small,
            dst_ref=small_row.at[d - 1],
            send_sem=srow_ss.at[d - 1],
            recv_sem=srow_rs.at[d - 1],
            device_id={"row": lax.rem(row + d, rows)},
            device_id_type=MESH,
        )
        for d in range(1, rows)
    ]
    lrow = [
        pltpu.make_async_remote_copy(
            src_ref=last,
            dst_ref=last_row.at[d - 1],
            send_sem=lrow_ss.at[d - 1],
            recv_sem=lrow_rs.at[d - 1],
            device_id={"row": lax.rem(row + d, rows)},
            device_id_type=MESH,
        )
        for d in range(1, rows)
    ]
    for c in srow + lrow:
        c.start()
    core_list = [core_copies(n, s) for n, s in enumerate(sib_order)]
    for cs in core_list:
        for c in cs:
            c.start()

    for c in srow + lrow:
        c.wait()
    total = small[...]
    tail = last[...]
    for d in range(rows - 1):
        total = total + small_row[d]
        tail = tail + last_row[d]
    small_sum[...] = total
    last_sum[...] = tail
    last_o[me] = tail
    spart = []
    lcp = []
    for d in range(1, groups):
        to = lax.rem(me + d, groups)
        spart.append(
            pltpu.make_async_remote_copy(
                src_ref=small_sum.at[pl.ds(to * chunk, chunk)],
                dst_ref=small_part.at[d - 1],
                send_sem=spart_ss.at[d - 1],
                recv_sem=spart_rs.at[d - 1],
                device_id={"seq": to},
                device_id_type=MESH,
            )
        )
        lcp.append(
            pltpu.make_async_remote_copy(
                src_ref=last_sum,
                dst_ref=last_o.at[me],
                send_sem=last_ss.at[d - 1],
                recv_sem=last_rs.at[d - 1],
                device_id={"seq": to},
                device_id_type=MESH,
            )
        )
    for c in spart + lcp:
        c.start()

    def step_copy(k, i):
        return pltpu.make_async_remote_copy(
            src_ref=own.at[shard_of(k, i, False)],
            dst_ref=step_buf[k].at[i],
            send_sem=step_ss[k].at[i],
            recv_sem=step_rs[k].at[i],
            device_id={"seq": me + weights[k] * (1 - 2 * bits[k])},
            device_id_type=MESH,
        )

    def add_core(n, s):
        for ref, cols, _, first in parts:
            buf = core_buf[{0: 0, 3: 1, 4: 2}[first]]
            for c in range(cols):
                mine = ref[
                    pl.ds(s * unit_rows, unit_rows), pl.ds(core * cols * half + c * half, half)
                ]
                own[s, first + c] = mine + buf[n, :, c * half : (c + 1) * half]
        for c in range(4):
            mine = gdown[
                pl.ds(s * 4 * unit_rows + c * unit_rows, unit_rows), pl.ds(core * half, half)
            ]
            own[s, 8 + c] = mine + core_buf[3][n, c * unit_rows : (c + 1) * unit_rows]

    copies = [[step_copy(k, i) for i in range(groups >> (k + 1))] for k in range(steps)]
    for n, s in enumerate(order):
        for c in core_list[n]:
            c.wait_recv()
        add_core(n, s)
        if n < groups // 2:
            copies[0][n].start()

    for c in spart:
        c.wait()
    total = small_sum[pl.ds(me * chunk, chunk)]
    for d in range(groups - 1):
        total = total + small_part[d]
    small_done[...] = total
    small_o[pl.ds(me * chunk, chunk)] = total
    sdone = [
        pltpu.make_async_remote_copy(
            src_ref=small_done,
            dst_ref=small_o.at[pl.ds(me * chunk, chunk)],
            send_sem=sdone_ss.at[d - 1],
            recv_sem=sdone_rs.at[d - 1],
            device_id={"seq": lax.rem(me + d, groups)},
            device_id_type=MESH,
        )
        for d in range(1, groups)
    ]
    for c in sdone:
        c.start()

    for k in range(steps):
        count = groups >> (k + 1)
        for i in range(count):
            copies[k][i].wait_recv()
            s = shard_of(k, i, True)
            own[s] = own[s] + step_buf[k][i]
            if k + 1 < steps and i < count // 2:
                copies[k + 1][i].start()

    w = 2
    n = 0
    while w < rows:
        bit = lax.rem(row // w, 2)
        c = pltpu.make_async_remote_copy(
            src_ref=own.at[me],
            dst_ref=wide_buf.at[n],
            send_sem=wide_ss.at[n],
            recv_sem=wide_rs.at[n],
            device_id={"row": row + w * (1 - 2 * bit)},
            device_id_type=MESH,
        )
        c.start()
        c.wait()
        own[me] = own[me] + wide_buf[n]
        w *= 2
        n += 1

    fin_own[...] = own[me]
    fin = pltpu.make_async_remote_copy(
        src_ref=fin_own,
        dst_ref=fin_buf,
        send_sem=fin_sem.at[0],
        recv_sem=fin_sem.at[1],
        device_id={"row": sib},
        device_id_type=MESH,
    )
    fin.start()

    def put(where, buf):
        for ref, cols, _, first in parts:
            out = {0: in_o, 3: out_o, 4: up_o}[first]
            for c in range(cols):
                out[:, pl.ds(where * cols * half + c * half, half)] = buf[first + c].astype(
                    jnp.float32
                )
        for c in range(4):
            down_o[c * unit_rows : (c + 1) * unit_rows, pl.ds(where * half, half)] = buf[
                8 + c
            ].astype(jnp.float32)

    put(core, fin_own)
    for cs in core_list:
        for c in cs:
            c.wait_send()
    for cs in copies:
        for c in cs:
            c.wait_send()
    for c in sdone + lcp:
        c.wait()
    fin.wait()
    put(1 - core, fin_buf)


def reduce_all(gin, gout, gup, gdown, small, last):
    rows, groups = lax.axis_size("row"), lax.axis_size("seq")
    width = gin.shape[0]
    unit = width // groups
    half = width // 2
    wide = max(1, rows.bit_length() - 2)
    low, f32 = jnp.bfloat16, jnp.float32
    steps = groups.bit_length() - 1
    chunk = small.shape[0] // groups
    dma = pltpu.SemaphoreType.DMA
    vm = pl.BlockSpec(memory_space=pltpu.VMEM)
    return pl.pallas_call(
        functools.partial(reduce_kernel, rows, groups),
        out_shape=(
            jax.ShapeDtypeStruct((unit, 3 * width), f32),
            jax.ShapeDtypeStruct((unit, width), f32),
            jax.ShapeDtypeStruct((unit, 4 * width), f32),
            jax.ShapeDtypeStruct((4 * unit, width), f32),
            jax.ShapeDtypeStruct(small.shape, f32),
            jax.ShapeDtypeStruct((groups,) + last.shape, f32),
        ),
        in_specs=[vm] * 6,
        out_specs=(vm,) * 6,
        scratch_shapes=[
            pltpu.VMEM((groups, 12, unit, half), low),
            [
                pltpu.VMEM((groups, unit, 3 * half), low),
                pltpu.VMEM((groups, unit, half), low),
                pltpu.VMEM((groups, unit, 4 * half), low),
                pltpu.VMEM((groups, 4 * unit, half), low),
            ],
            [pltpu.VMEM((groups >> (k + 1), 12, unit, half), low) for k in range(steps)],
            pltpu.VMEM((wide, 12, unit, half), low),
            pltpu.VMEM((12, unit, half), low),
            pltpu.VMEM((12, unit, half), low),
            pltpu.VMEM((rows - 1,) + small.shape, f32),
            pltpu.VMEM(small.shape, f32),
            pltpu.VMEM((groups - 1, chunk, small.shape[1]), f32),
            pltpu.VMEM((chunk, small.shape[1]), f32),
            pltpu.VMEM((rows - 1,) + last.shape, f32),
            pltpu.VMEM(last.shape, f32),
            dma((groups, 4)),
            dma((groups, 4)),
            [dma((groups >> (k + 1),)) for k in range(steps)],
            [dma((groups >> (k + 1),)) for k in range(steps)],
            dma((wide,)),
            dma((wide,)),
            dma((2,)),
            dma((rows - 1,)),
            dma((rows - 1,)),
            dma((groups - 1,)),
            dma((groups - 1,)),
            dma((groups - 1,)),
            dma((groups - 1,)),
            dma((rows - 1,)),
            dma((rows - 1,)),
            dma((groups - 1,)),
            dma((groups - 1,)),
        ],
        compiler_params=pltpu.CompilerParams(
            collective_id=0, has_side_effects=True, vmem_limit_bytes=VMEM_LIMIT
        ),
        name="reduce_all",
    )(gin, gout, gup, gdown, small, last)


def shards(
    block_in,
    lengths,
    mixer_gain,
    mixer_bias,
    in_weight,
    short_taps,
    filter_in,
    filter_in_bias,
    filter_mid,
    filter_mid_bias,
    filter_freq,
    filter_out,
    filter_skip,
    decay_rate,
    out_weight,
    feed_gain,
    feed_bias,
    up_weight,
    down_weight,
    cotangent,
):
    row_count, tok_count, model_width = block_in.shape
    groups = lax.axis_size("seq")
    length = tok_count * groups
    narrow = model_width // groups
    seq_place = lax.axis_index("seq")
    chan_start = seq_place * narrow
    positions = seq_place * tok_count + jnp.arange(tok_count, dtype=jnp.int32)
    doc_ends = jnp.cumsum(lengths, axis=1)
    live_mask = (positions[None, :] < doc_ends[:, -1:]).astype(jnp.float32)

    def doc_of(where):
        return jnp.sum((where[None, :, None] >= doc_ends[:, None, :]).astype(jnp.int32), axis=2)

    own_doc = doc_of(positions)
    tap_masks = []
    for tap_lag in range(3):
        same_doc = (positions[None, :] >= tap_lag) & (doc_of(positions - tap_lag) == own_doc)
        tap_masks.append(same_doc.astype(jnp.float32))
    block_float = block_in.astype(jnp.float32)
    normed, norm_pull = jax.vjp(layer_norm, block_float, mixer_gain, mixer_bias)
    normed_low = normed.astype(jnp.bfloat16)
    projected = jnp.einsum(
        "rtd,dc->rct", normed_low, in_weight, preferred_element_type=jnp.float32
    ).astype(jnp.bfloat16)
    left_rim = shifted(projected[:, :, tok_count - 2 :], "seq", 1)
    extended = jnp.concatenate([left_rim, projected], axis=2).astype(jnp.float32)
    short_mix = jnp.zeros(projected.shape, jnp.float32)
    for tap_lag in range(3):
        window = extended[:, :, 2 - tap_lag : 2 - tap_lag + tok_count]
        short_mix = (
            short_mix + short_taps[tap_lag][None, :, None] * window * tap_masks[tap_lag][:, None, :]
        )
    gate_out = short_mix[:, :model_width]
    gate_in = short_mix[:, model_width : 2 * model_width]
    stream_v = short_mix[:, 2 * model_width :]
    carried = (gate_in * stream_v * live_mask[:, None, :]).astype(jnp.bfloat16)
    spread_in = lax.all_to_all(carried, "seq", split_axis=1, concat_axis=2, tiled=True)
    out_part = lax.dynamic_slice_in_dim(filter_out, chan_start, narrow, 1)
    decay_part = lax.dynamic_slice_in_dim(decay_rate, chan_start, narrow, 0)
    skip_part = lax.dynamic_slice_in_dim(filter_skip, chan_start, narrow, 0)

    def build_filter(first_w, first_b, mid_w, mid_b, freq_w, last_w):
        return filter_rows(first_w, first_b, mid_w, mid_b, freq_w, last_w, decay_part, length)

    filt, filter_pull = jax.vjp(
        build_filter, filter_in, filter_in_bias, filter_mid, filter_mid_bias, filter_freq, out_part
    )
    tables = dft_tables(length)
    signal = spread_in.astype(jnp.float32)
    sig_real, sig_imag = forward_dft(signal, tables)
    fil_real, fil_imag = forward_dft(filt, tables)
    conv = inverse_dft(
        sig_real * fil_real - sig_imag * fil_imag, sig_real * fil_imag + sig_imag * fil_real, tables
    )
    conv = conv + skip_part[None, :, None] * signal
    back_home = lax.all_to_all(
        conv.astype(jnp.bfloat16), "seq", split_axis=2, concat_axis=1, tiled=True
    )
    conv_float = back_home.astype(jnp.float32)
    product_low = (gate_out * conv_float * live_mask[:, None, :]).astype(jnp.bfloat16)
    mixed = block_float + jnp.einsum(
        "rct,cd->rtd", product_low, out_weight, preferred_element_type=jnp.float32
    )
    normed_two, feed_pull = jax.vjp(layer_norm, mixed, feed_gain, feed_bias)
    normed_two_low = normed_two.astype(jnp.bfloat16)
    pre_act = jnp.einsum(
        "rtd,df->rtf", normed_two_low, up_weight, preferred_element_type=jnp.float32
    )
    activ, gelu_pull = jax.vjp(jax.nn.gelu, pre_act)
    activ_low = activ.astype(jnp.bfloat16)
    block_out = (
        mixed
        + jnp.einsum("rtf,fd->rtd", activ_low, down_weight, preferred_element_type=jnp.float32)
    ).astype(jnp.bfloat16)
    grad_float = cotangent.astype(jnp.float32)
    grad_down = jnp.einsum("rtf,rtd->fd", activ_low, cotangent, preferred_element_type=jnp.float32)
    grad_activ = jnp.einsum(
        "rtd,fd->rtf", cotangent, down_weight, preferred_element_type=jnp.float32
    )
    grad_pre = gelu_pull(grad_activ)[0].astype(jnp.bfloat16)
    grad_up = jnp.einsum(
        "rtd,rtf->df", normed_two_low, grad_pre, preferred_element_type=jnp.float32
    )
    grad_normed_two = jnp.einsum(
        "rtf,df->rtd", grad_pre, up_weight, preferred_element_type=jnp.float32
    )
    grad_mixed_part, grad_feed_gain, grad_feed_bias = feed_pull(grad_normed_two)
    grad_mixed = grad_float + grad_mixed_part
    grad_mixed_low = grad_mixed.astype(jnp.bfloat16)
    grad_outw = jnp.einsum(
        "rct,rtd->cd", product_low, grad_mixed_low, preferred_element_type=jnp.float32
    )
    grad_product = (
        jnp.einsum("rtd,cd->rct", grad_mixed_low, out_weight, preferred_element_type=jnp.float32)
        * live_mask[:, None, :]
    )
    grad_gate_out = grad_product * conv_float
    grad_conv = (grad_product * gate_out).astype(jnp.bfloat16)
    grad_spread = lax.all_to_all(grad_conv, "seq", split_axis=1, concat_axis=2, tiled=True).astype(
        jnp.float32
    )
    back_real, back_imag = forward_dft(grad_spread, tables)
    grad_signal = inverse_dft(
        fil_real * back_real + fil_imag * back_imag,
        fil_real * back_imag - fil_imag * back_real,
        tables,
    )
    grad_signal = grad_signal + skip_part[None, :, None] * grad_spread
    grad_filt = inverse_dft(
        jnp.sum(sig_real * back_real + sig_imag * back_imag, axis=0),
        jnp.sum(sig_real * back_imag - sig_imag * back_real, axis=0),
        tables,
    )
    grad_skip_part = jnp.sum(grad_spread * signal, axis=(0, 2))
    grad_first_w, grad_first_b, grad_mid_w, grad_mid_b, grad_freq_w, grad_last_part = filter_pull(
        grad_filt
    )
    grad_carried = lax.all_to_all(
        grad_signal.astype(jnp.bfloat16), "seq", split_axis=2, concat_axis=1, tiled=True
    )
    grad_carried = grad_carried.astype(jnp.float32) * live_mask[:, None, :]
    grad_short = jnp.concatenate(
        [grad_gate_out, grad_carried * stream_v, grad_carried * gate_in], axis=1
    )
    grad_extended = jnp.zeros(extended.shape, jnp.float32)
    tap_grads = []
    for tap_lag in range(3):
        masked = grad_short * tap_masks[tap_lag][:, None, :]
        window = extended[:, :, 2 - tap_lag : 2 - tap_lag + tok_count]
        tap_grads.append(jnp.sum(masked * window, axis=(0, 2)))
        grad_extended = grad_extended + jnp.pad(
            short_taps[tap_lag][None, :, None] * masked, ((0, 0), (0, 0), (2 - tap_lag, tap_lag))
        )
    grad_taps = jnp.stack(tap_grads)
    rim_back = shifted(grad_extended[:, :, :2].astype(jnp.bfloat16), "seq", -1).astype(jnp.float32)
    grad_proj = grad_extended[:, :, 2:] + jnp.pad(rim_back, ((0, 0), (0, 0), (tok_count - 2, 0)))
    grad_proj_low = grad_proj.astype(jnp.bfloat16)
    grad_inw = jnp.einsum(
        "rtd,rct->dc", normed_low, grad_proj_low, preferred_element_type=jnp.float32
    )
    grad_normed = jnp.einsum(
        "rct,dc->rtd", grad_proj_low, in_weight, preferred_element_type=jnp.float32
    )
    grad_input_part, grad_mixer_gain, grad_mixer_bias = norm_pull(grad_normed)
    grad_input = grad_mixed + grad_input_part
    grad_skip = lax.dynamic_update_slice_in_dim(
        jnp.zeros(filter_skip.shape, jnp.float32), grad_skip_part, chan_start, 0
    )
    pieces = (
        grad_mixer_gain,
        grad_mixer_bias,
        grad_taps,
        grad_first_w,
        grad_first_b,
        grad_mid_w,
        grad_mid_b,
        grad_freq_w,
        grad_skip,
        grad_feed_gain,
        grad_feed_bias,
    )
    flat = jnp.concatenate([p.reshape(-1) for p in pieces])
    chunk = -(-flat.shape[0] // (groups * 8 * 128)) * 8
    flat = jnp.pad(flat, (0, groups * chunk * 128 - flat.shape[0])).reshape(groups * chunk, 128)
    low = jnp.bfloat16
    s_in, s_out, s_up, s_down, flat, last_all = reduce_all(
        grad_inw.astype(low),
        grad_outw.astype(low),
        grad_up.astype(low),
        grad_down.astype(low),
        flat,
        grad_last_part,
    )
    shares = (s_in, s_out, s_up, s_down)
    flat = flat.reshape(-1)
    summed = []
    at = 0
    for p in pieces:
        summed.append(flat[at : at + p.size].reshape(p.shape))
        at += p.size
    grad_last = last_all.transpose(1, 0, 2).reshape(filter_out.shape)
    summed = summed[:8] + [grad_last] + summed[8:]
    return (
        block_out,
        grad_input,
        summed[0],
        summed[1],
        shares[0],
        summed[2],
        summed[3],
        summed[4],
        summed[5],
        summed[6],
        summed[7],
        summed[8],
        summed[9],
        shares[1],
        summed[10],
        summed[11],
        shares[2],
        shares[3],
    )


def solution(mesh):
    placed = (
        P("row", "seq", None),
        P("row", None),
        P(),
        P(),
        P(),
        P(),
        P(),
        P(),
        P(),
        P(),
        P(),
        P(),
        P(),
        P(),
        P(),
        P(),
        P(),
        P(),
        P(),
        P("row", "seq", None),
    )
    return jax.shard_map(
        shards,
        mesh=mesh,
        in_specs=placed,
        out_specs=(
            P("row", "seq", None),
            P("row", "seq", None),
            P(),
            P(),
            P("seq", None),
            P(),
            P(),
            P(),
            P(),
            P(),
            P(),
            P(),
            P(),
            P("seq", None),
            P(),
            P(),
            P("seq", None),
            P("seq", None),
        ),
        check_vma=False,
    )
```

```python
import functools
import math

import jax
import jax.numpy as jnp
import numpy as np
from jax import lax
from jax.experimental import pallas as pl
from jax.experimental.pallas import tpu as pltpu
from jax.sharding import PartitionSpec as P

HIGHEST = lax.Precision.HIGHEST


def shifted(array, axis, by):
    peers = lax.axis_size(axis)
    pairs = [(i, i + by) for i in range(peers) if 0 <= i + by < peers]
    return lax.ppermute(array, axis, pairs)


def layer_norm(values, gain, offset):
    center = values - jnp.mean(values, axis=-1, keepdims=True)
    spread = jnp.mean(center * center, axis=-1, keepdims=True)
    return center * lax.rsqrt(spread + 1e-05) * gain + offset


def features(length, feat_count):
    band_count = (feat_count - 1) // 2
    positions = jnp.arange(length, dtype=jnp.int32)
    band_freq = jnp.arange(1, band_count + 1, dtype=jnp.int32)
    turn_index = positions[:, None] * band_freq[None, :] % length
    angles = 2.0 * math.pi / length * turn_index.astype(jnp.float32)
    ramp_feat = positions.astype(jnp.float32)[:, None] / length
    return jnp.concatenate([ramp_feat, jnp.cos(angles), -jnp.sin(angles)], axis=1)


def filter_rows(
    filter_in,
    filter_in_bias,
    filter_mid,
    filter_mid_bias,
    filter_freq,
    out_part,
    decay_part,
    length,
):
    feats = features(length, filter_in.shape[0])
    hidden = jnp.sin(filter_freq * (jnp.dot(feats, filter_in, precision=HIGHEST) + filter_in_bias))
    hidden = jnp.sin(
        filter_freq * (jnp.dot(hidden, filter_mid, precision=HIGHEST) + filter_mid_bias)
    )
    raw_filter = jnp.einsum("lh,hc->cl", hidden, out_part, precision=HIGHEST)
    positions = jnp.arange(length, dtype=jnp.float32)
    return raw_filter * jnp.exp(-decay_part[:, None] * positions[None, :])


MESH = pl.DeviceIdType.MESH
VMEM_LIMIT = 56 * 1024 * 1024


def seq_weights(core, groups):
    weights = []
    w = 1
    while w < groups:
        weights.append(w)
        w *= 2
    first = weights[0] + core * (weights[1] - weights[0])
    second = weights[1] - core * (weights[1] - weights[0])
    return [first, second] + weights[2:]


def reduce_kernel(
    rows,
    groups,
    gin,
    gout,
    gup,
    gdown,
    small,
    last,
    in_o,
    out_o,
    up_o,
    down_o,
    small_o,
    last_o,
    own,
    core_buf,
    step_buf,
    wide_buf,
    fin_own,
    fin_buf,
    small_row,
    small_sum,
    small_part,
    small_done,
    last_row,
    last_sum,
    core_ss,
    core_rs,
    step_ss,
    step_rs,
    wide_ss,
    wide_rs,
    fin_sem,
    srow_ss,
    srow_rs,
    spart_ss,
    spart_rs,
    sdone_ss,
    sdone_rs,
    lrow_ss,
    lrow_rs,
    last_ss,
    last_rs,
):
    me = lax.axis_index("seq")
    row = lax.axis_index("row")
    core = lax.rem(row, 2)
    sib = row + 1 - 2 * core
    unit_rows, half = own.shape[2], own.shape[3]
    chunk = small_part.shape[1]
    barrier = pltpu.get_barrier_semaphore()
    for d in range(1, rows):
        pl.semaphore_signal(
            barrier, inc=1, device_id={"row": lax.rem(row + d, rows)}, device_id_type=MESH
        )
    for d in range(1, groups):
        pl.semaphore_signal(
            barrier, inc=1, device_id={"seq": lax.rem(me + d, groups)}, device_id_type=MESH
        )
    pl.semaphore_wait(barrier, rows + groups - 2)

    weights = seq_weights(core, groups)
    bits = [lax.rem(me // w, 2) for w in weights]
    steps = len(weights)
    sib_weights = seq_weights(1 - core, groups)
    sib_bits = [lax.rem(me // w, 2) for w in sib_weights]

    def shard_of(k, i, mine, weights=weights, bits=bits):
        at = 0
        for j in range(k):
            at = at + bits[j] * weights[j]
        at = at + (bits[k] if mine else 1 - bits[k]) * weights[k]
        for j in range(k + 1, steps):
            t = (i >> (steps - 1 - j)) & 1
            at = at + (bits[j] if t else 1 - bits[j]) * weights[j]
        return at

    order = [(False, i) for i in range(groups // 2)] + [(True, i) for i in range(groups // 2)]
    sib_order = [shard_of(0, i, mine, sib_weights, sib_bits) for mine, i in order]
    order = [shard_of(0, i, mine) for mine, i in order]
    parts = [(gin, 3, unit_rows, 0), (gout, 1, unit_rows, 3), (gup, 4, unit_rows, 4)]

    def core_copies(n, s):
        out = []
        for p, (ref, cols, _, _) in enumerate(parts):
            out.append(
                (ref.at[pl.ds(s * unit_rows, unit_rows), pl.ds((1 - core) * cols * half, cols * half)], p)
            )
        out.append((gdown.at[pl.ds(s * 4 * unit_rows, 4 * unit_rows), pl.ds((1 - core) * half, half)], 3))
        dst = [
            core_buf[0].at[n],
            core_buf[1].at[n],
            core_buf[2].at[n],
            core_buf[3].at[n],
        ]
        return [
            pltpu.make_async_remote_copy(
                src_ref=src,
                dst_ref=dst[p],
                send_sem=core_ss.at[n, p],
                recv_sem=core_rs.at[n, p],
                device_id={"row": sib},
                device_id_type=MESH,
            )
            for src, p in out
        ]

    srow = [
        pltpu.make_async_remote_copy(
            src_ref=small,
            dst_ref=small_row.at[d - 1],
            send_sem=srow_ss.at[d - 1],
            recv_sem=srow_rs.at[d - 1],
            device_id={"row": lax.rem(row + d, rows)},
            device_id_type=MESH,
        )
        for d in range(1, rows)
    ]
    lrow = [
        pltpu.make_async_remote_copy(
            src_ref=last,
            dst_ref=last_row.at[d - 1],
            send_sem=lrow_ss.at[d - 1],
            recv_sem=lrow_rs.at[d - 1],
            device_id={"row": lax.rem(row + d, rows)},
            device_id_type=MESH,
        )
        for d in range(1, rows)
    ]
    for c in srow + lrow:
        c.start()
    core_list = [core_copies(n, s) for n, s in enumerate(sib_order)]
    for cs in core_list:
        for c in cs:
            c.start()

    for c in srow + lrow:
        c.wait()
    total = small[...]
    tail = last[...]
    for d in range(rows - 1):
        total = total + small_row[d]
        tail = tail + last_row[d]
    small_sum[...] = total
    last_sum[...] = tail
    last_o[me] = tail
    spart = []
    lcp = []
    for d in range(1, groups):
        to = lax.rem(me + d, groups)
        spart.append(
            pltpu.make_async_remote_copy(
                src_ref=small_sum.at[pl.ds(to * chunk, chunk)],
                dst_ref=small_part.at[d - 1],
                send_sem=spart_ss.at[d - 1],
                recv_sem=spart_rs.at[d - 1],
                device_id={"seq": to},
                device_id_type=MESH,
            )
        )
        lcp.append(
            pltpu.make_async_remote_copy(
                src_ref=last_sum,
                dst_ref=last_o.at[me],
                send_sem=last_ss.at[d - 1],
                recv_sem=last_rs.at[d - 1],
                device_id={"seq": to},
                device_id_type=MESH,
            )
        )
    for c in spart + lcp:
        c.start()

    def step_copy(k, i):
        return pltpu.make_async_remote_copy(
            src_ref=own.at[shard_of(k, i, False)],
            dst_ref=step_buf[k].at[i],
            send_sem=step_ss[k].at[i],
            recv_sem=step_rs[k].at[i],
            device_id={"seq": me + weights[k] * (1 - 2 * bits[k])},
            device_id_type=MESH,
        )

    def add_core(n, s):
        for ref, cols, _, first in parts:
            buf = core_buf[{0: 0, 3: 1, 4: 2}[first]]
            for c in range(cols):
                mine = ref[
                    pl.ds(s * unit_rows, unit_rows), pl.ds(core * cols * half + c * half, half)
                ]
                own[s, first + c] = mine + buf[n, :, c * half : (c + 1) * half]
        for c in range(4):
            mine = gdown[
                pl.ds(s * 4 * unit_rows + c * unit_rows, unit_rows), pl.ds(core * half, half)
            ]
            own[s, 8 + c] = mine + core_buf[3][n, c * unit_rows : (c + 1) * unit_rows]

    copies = [[step_copy(k, i) for i in range(groups >> (k + 1))] for k in range(steps)]
    for n, s in enumerate(order):
        for c in core_list[n]:
            c.wait_recv()
        add_core(n, s)
        if n < groups // 2:
            copies[0][n].start()

    for c in spart:
        c.wait()
    total = small_sum[pl.ds(me * chunk, chunk)]
    for d in range(groups - 1):
        total = total + small_part[d]
    small_done[...] = total
    small_o[pl.ds(me * chunk, chunk)] = total
    sdone = [
        pltpu.make_async_remote_copy(
            src_ref=small_done,
            dst_ref=small_o.at[pl.ds(me * chunk, chunk)],
            send_sem=sdone_ss.at[d - 1],
            recv_sem=sdone_rs.at[d - 1],
            device_id={"seq": lax.rem(me + d, groups)},
            device_id_type=MESH,
        )
        for d in range(1, groups)
    ]
    for c in sdone:
        c.start()

    for k in range(steps):
        count = groups >> (k + 1)
        for i in range(count):
            copies[k][i].wait_recv()
            s = shard_of(k, i, True)
            own[s] = own[s] + step_buf[k][i]
            if k + 1 < steps and i < count // 2:
                copies[k + 1][i].start()

    w = 2
    n = 0
    while w < rows:
        bit = lax.rem(row // w, 2)
        c = pltpu.make_async_remote_copy(
            src_ref=own.at[me],
            dst_ref=wide_buf.at[n],
            send_sem=wide_ss.at[n],
            recv_sem=wide_rs.at[n],
            device_id={"row": row + w * (1 - 2 * bit)},
            device_id_type=MESH,
        )
        c.start()
        c.wait()
        own[me] = own[me] + wide_buf[n]
        w *= 2
        n += 1

    fin_own[...] = own[me]
    fin = pltpu.make_async_remote_copy(
        src_ref=fin_own,
        dst_ref=fin_buf,
        send_sem=fin_sem.at[0],
        recv_sem=fin_sem.at[1],
        device_id={"row": sib},
        device_id_type=MESH,
    )
    fin.start()

    def put(where, buf):
        for ref, cols, _, first in parts:
            out = {0: in_o, 3: out_o, 4: up_o}[first]
            for c in range(cols):
                out[:, pl.ds(where * cols * half + c * half, half)] = buf[first + c].astype(
                    jnp.float32
                )
        for c in range(4):
            down_o[c * unit_rows : (c + 1) * unit_rows, pl.ds(where * half, half)] = buf[
                8 + c
            ].astype(jnp.float32)

    put(core, fin_own)
    for cs in core_list:
        for c in cs:
            c.wait_send()
    for cs in copies:
        for c in cs:
            c.wait_send()
    for c in sdone + lcp:
        c.wait()
    fin.wait()
    put(1 - core, fin_buf)


def reduce_all(gin, gout, gup, gdown, small, last):
    rows, groups = lax.axis_size("row"), lax.axis_size("seq")
    width = gin.shape[0]
    unit = width // groups
    half = width // 2
    wide = max(1, rows.bit_length() - 2)
    low, f32 = jnp.bfloat16, jnp.float32
    steps = groups.bit_length() - 1
    chunk = small.shape[0] // groups
    dma = pltpu.SemaphoreType.DMA
    vm = pl.BlockSpec(memory_space=pltpu.VMEM)
    return pl.pallas_call(
        functools.partial(reduce_kernel, rows, groups),
        out_shape=(
            jax.ShapeDtypeStruct((unit, 3 * width), f32),
            jax.ShapeDtypeStruct((unit, width), f32),
            jax.ShapeDtypeStruct((unit, 4 * width), f32),
            jax.ShapeDtypeStruct((4 * unit, width), f32),
            jax.ShapeDtypeStruct(small.shape, f32),
            jax.ShapeDtypeStruct((groups,) + last.shape, f32),
        ),
        in_specs=[vm] * 6,
        out_specs=(vm,) * 6,
        scratch_shapes=[
            pltpu.VMEM((groups, 12, unit, half), low),
            [
                pltpu.VMEM((groups, unit, 3 * half), low),
                pltpu.VMEM((groups, unit, half), low),
                pltpu.VMEM((groups, unit, 4 * half), low),
                pltpu.VMEM((groups, 4 * unit, half), low),
            ],
            [pltpu.VMEM((groups >> (k + 1), 12, unit, half), low) for k in range(steps)],
            pltpu.VMEM((wide, 12, unit, half), low),
            pltpu.VMEM((12, unit, half), low),
            pltpu.VMEM((12, unit, half), low),
            pltpu.VMEM((rows - 1,) + small.shape, f32),
            pltpu.VMEM(small.shape, f32),
            pltpu.VMEM((groups - 1, chunk, small.shape[1]), f32),
            pltpu.VMEM((chunk, small.shape[1]), f32),
            pltpu.VMEM((rows - 1,) + last.shape, f32),
            pltpu.VMEM(last.shape, f32),
            dma((groups, 4)),
            dma((groups, 4)),
            [dma((groups >> (k + 1),)) for k in range(steps)],
            [dma((groups >> (k + 1),)) for k in range(steps)],
            dma((wide,)),
            dma((wide,)),
            dma((2,)),
            dma((rows - 1,)),
            dma((rows - 1,)),
            dma((groups - 1,)),
            dma((groups - 1,)),
            dma((groups - 1,)),
            dma((groups - 1,)),
            dma((rows - 1,)),
            dma((rows - 1,)),
            dma((groups - 1,)),
            dma((groups - 1,)),
        ],
        compiler_params=pltpu.CompilerParams(
            collective_id=0, has_side_effects=True, vmem_limit_bytes=VMEM_LIMIT
        ),
        name="reduce_all",
    )(gin, gout, gup, gdown, small, last)


LANES = 128


def spectrum_tables(length):
    period = 2 * length
    first = period // LANES
    k1 = np.arange(first // 2 + 1, dtype=np.int64)[:, None, None]
    n2 = np.arange(LANES, dtype=np.int64)[None, :, None]
    k2 = np.arange(LANES, dtype=np.int64)[None, None, :]
    angle = 2.0 * np.pi / period * (n2 * (k1 + first * k2) % period)
    cos, sin = np.cos(angle), np.sin(angle)
    full = np.concatenate(
        [np.concatenate([cos, -sin], axis=2), np.concatenate([sin, cos], axis=2)], axis=1
    ).astype(np.float32)
    high = full.astype(jnp.bfloat16)
    rest = (full - high.astype(np.float32)).astype(jnp.bfloat16)
    return high, rest


def half_dft(x):
    count = 2 * len(x)
    if count == 2:
        return [(x[0], None), (x[0], None)]
    even, odd = half_dft(x[0::2]), half_dft(x[1::2])
    out = [None] * (count // 2 + 1)
    for k in range(count // 4 + 1):
        er, ei = even[k]
        orr, oi = odd[k]
        if k == 0:
            out[0] = (er + orr, None)
            out[count // 2] = (er - orr, None)
        elif 4 * k == count:
            out[k] = (er, -orr)
        else:
            c, s = math.cos(2 * math.pi * k / count), math.sin(2 * math.pi * k / count)
            tr = orr * c + oi * s
            ti = oi * c - orr * s
            out[k] = (er + tr, ei + ti)
            out[count // 2 - k] = (er - tr, ti - ei)
    return out


def half_inverse(spec):
    count = 2 * (len(spec) - 1)
    if count == 2:
        return [spec[0][0] + spec[1][0]]
    even, odd = [], []
    for k in range(count // 4 + 1):
        ar, ai = spec[k]
        br, bi = spec[count // 2 - k]
        if k == 0:
            even.append((ar + br, None))
            odd.append((ar - br, None))
        elif 4 * k == count:
            even.append((ar + ar, None))
            odd.append((-(ai + ai), None))
        else:
            c, s = math.cos(2 * math.pi * k / count), math.sin(2 * math.pi * k / count)
            dr, di = ar - br, ai + bi
            even.append((ar + br, ai - bi))
            odd.append((dr * c - di * s, dr * s + di * c))
    out = [None] * (count // 2)
    out[0::2] = half_inverse(even)
    out[1::2] = half_inverse(odd)
    return out


def split_dot(a, high, rest, back):
    a_high = a.astype(jnp.bfloat16)
    a_rest = (a - a_high.astype(jnp.float32)).astype(jnp.bfloat16)
    dims = (((1,), (1 if back else 0,)), ((), ()))

    def dot(p, q):
        return lax.dot_general(p, q, dims, preferred_element_type=jnp.float32)

    return dot(a_high, high) + (dot(a_rest, high) + dot(a_high, rest))


def tile_loop(tiles, body):
    def step(i, carry):
        body(pl.multiple_of(i * 8, 8))
        return carry

    lax.fori_loop(0, tiles, step, 0)


def first_stage(load, spec, tiles):
    zero = jnp.zeros((8, LANES), jnp.float32)

    def body(at):
        for k, (re, im) in enumerate(half_dft(load(at))):
            spec[k, pl.ds(at, 8), :LANES] = re
            spec[k, pl.ds(at, 8), LANES:] = zero if im is None else im

    tile_loop(tiles, body)


def last_stage(spec, store, tiles, scale):
    def body(at):
        freqs = spec.shape[0]
        values = []
        for k in range(freqs):
            re = spec[k, pl.ds(at, 8), :LANES]
            im = None if k in (0, freqs - 1) else spec[k, pl.ds(at, 8), LANES:]
            values.append((re, im))
        for n, v in enumerate(half_inverse(values)):
            store(n, at, v * scale)

    tile_loop(tiles, body)


def greet(groups, me):
    barrier = pltpu.get_barrier_semaphore()
    for d in range(1, groups):
        pl.semaphore_signal(
            barrier, inc=1, device_id={"seq": lax.rem(me + d, groups)}, device_id_type=MESH
        )
    pl.semaphore_wait(barrier, groups - 1)


def to_channels(groups, me, narrow, src, recv, ss, rs, ls):
    local = pltpu.make_async_copy(
        src.at[:, pl.ds(pl.multiple_of(me * narrow, 8), narrow), :], recv.at[me], ls
    )
    out = [local]
    for d in range(1, groups):
        to = lax.rem(me + d, groups)
        out.append(
            pltpu.make_async_remote_copy(
                src_ref=src.at[:, pl.ds(pl.multiple_of(to * narrow, 8), narrow), :],
                dst_ref=recv.at[me],
                send_sem=ss.at[d - 1],
                recv_sem=rs.at[d - 1],
                device_id={"seq": to},
                device_id_type=MESH,
            )
        )
    return out


def to_positions(groups, me, narrow, send, dst, ss, rs, ls):
    mine = dst.at[:, pl.ds(pl.multiple_of(me * narrow, 8), narrow), :]
    out = [pltpu.make_async_copy(send.at[me], mine, ls)]
    for d in range(1, groups):
        to = lax.rem(me + d, groups)
        out.append(
            pltpu.make_async_remote_copy(
                src_ref=send.at[to],
                dst_ref=mine,
                send_sem=ss.at[d - 1],
                recv_sem=rs.at[d - 1],
                device_id={"seq": to},
                device_id_type=MESH,
            )
        )
    return out


def spread(recv, wide, narrow):
    per = recv.shape[3] // LANES

    def step(s, carry):
        for r in range(recv.shape[1]):
            for h in range(per):
                wide[s * per + h, r * narrow : (r + 1) * narrow, :] = recv[
                    s, r, :, h * LANES : (h + 1) * LANES
                ].astype(jnp.float32)
        return carry

    lax.fori_loop(0, recv.shape[0], step, 0)


def gather_back(wide, send, narrow):
    per = send.shape[3] // LANES

    def step(s, carry):
        for r in range(send.shape[1]):
            for h in range(per):
                send[s, r, :, h * LANES : (h + 1) * LANES] = wide[
                    s * per + h, r * narrow : (r + 1) * narrow, :
                ].astype(jnp.bfloat16)
        return carry

    lax.fori_loop(0, send.shape[0], step, 0)


def freq_loop(freqs, unroll, body):
    def step(i, carry):
        for j in range(unroll):
            body(i * unroll + j)
        return carry

    lax.fori_loop(0, freqs // unroll, step, 0)


UNROLL = {33: 3, 65: 5}


def conv_kernel(
    groups,
    w_ref,
    filt_ref,
    high_ref,
    rest_ref,
    z_ref,
    w_spec,
    h_spec,
    high,
    rest,
    recv,
    wide,
    back,
    send,
    in_ss,
    in_rs,
    out_ss,
    out_rs,
    local,
):
    me = lax.axis_index("seq")
    narrow = filt_ref.shape[0]
    count, freqs = wide.shape[0], high.shape[0]
    rows = w_ref.shape[0]
    unroll = UNROLL.get(freqs, 1)
    tables = [
        pltpu.make_async_copy(high_ref, high, local.at[0]),
        pltpu.make_async_copy(rest_ref, rest, local.at[1]),
    ]
    for c in tables:
        c.start()
    greet(groups, me)
    inward = to_channels(groups, me, narrow, w_ref, recv, in_ss, in_rs, local.at[2])
    for c in inward:
        c.start()

    def load_filter(at):
        return [
            filt_ref[pl.ds(at, 8), n * LANES : (n + 1) * LANES] for n in range(count)
        ]

    first_stage(load_filter, h_spec, narrow // 8)
    for c in tables:
        c.wait()

    def filter_freq_step(k):
        h_spec[k] = split_dot(h_spec[k], high[k], rest[k], False)

    freq_loop(freqs, unroll, filter_freq_step)
    for c in inward:
        c.wait()
    spread(recv, wide, narrow)
    first_stage(
        lambda at: [wide[n, pl.ds(at, 8), :] for n in range(count)], w_spec, rows * narrow // 8
    )

    def forward_step(k):
        w_spec[k] = split_dot(w_spec[k], high[k], rest[k], False)

    def inverse_step(k):
        h = h_spec[k]
        hr, hi = h[:, :LANES], h[:, LANES:]
        parts = []
        for r in range(rows):
            w = w_spec[k, r * narrow : (r + 1) * narrow]
            wr, wi = w[:, :LANES], w[:, LANES:]
            parts.append(jnp.concatenate([wr * hr - wi * hi, wr * hi + wi * hr], axis=1))
        back[k] = split_dot(jnp.concatenate(parts, axis=0), high[k], rest[k], True)

    freq_loop(freqs, unroll, forward_step)
    freq_loop(freqs, unroll, inverse_step)

    def store(n, at, v):
        wide[n, pl.ds(at, 8), :] = v

    last_stage(back, store, rows * narrow // 8, 1.0 / (2 * count * LANES))
    gather_back(wide, send, narrow)
    outward = to_positions(groups, me, narrow, send, z_ref, out_ss, out_rs, local.at[3])
    for c in outward:
        c.start()
    for c in outward:
        c.wait()


def conv_back_kernel(
    groups,
    g_ref,
    w_spec,
    h_spec,
    high_ref,
    rest_ref,
    gw_ref,
    gh_ref,
    high,
    rest,
    recv,
    wide,
    g_spec,
    back,
    send,
    in_ss,
    in_rs,
    out_ss,
    out_rs,
    local,
):
    me = lax.axis_index("seq")
    narrow = gh_ref.shape[0]
    count, freqs = wide.shape[0], high.shape[0]
    rows = g_ref.shape[0]
    unroll = UNROLL.get(freqs, 1)
    tables = [
        pltpu.make_async_copy(high_ref, high, local.at[0]),
        pltpu.make_async_copy(rest_ref, rest, local.at[1]),
    ]
    for c in tables:
        c.start()
    greet(groups, me)
    inward = to_channels(groups, me, narrow, g_ref, recv, in_ss, in_rs, local.at[2])
    for c in inward:
        c.start()
    for c in tables:
        c.wait()
    for c in inward:
        c.wait()
    spread(recv, wide, narrow)
    first_stage(
        lambda at: [wide[n, pl.ds(at, 8), :] for n in range(count)], g_spec, rows * narrow // 8
    )

    def forward_step(k):
        g_spec[k] = split_dot(g_spec[k], high[k], rest[k], False)

    def inverse_step(k):
        h = h_spec[k]
        hr, hi = h[:, :LANES], h[:, LANES:]
        parts = []
        hsum = None
        for r in range(rows):
            w = w_spec[k, r * narrow : (r + 1) * narrow]
            wr, wi = w[:, :LANES], w[:, LANES:]
            g = g_spec[k, r * narrow : (r + 1) * narrow]
            gr, gi = g[:, :LANES], g[:, LANES:]
            parts.append(jnp.concatenate([hr * gr + hi * gi, hr * gi - hi * gr], axis=1))
            pair = (wr * gr + wi * gi, wr * gi - wi * gr)
            hsum = pair if hsum is None else (hsum[0] + pair[0], hsum[1] + pair[1])
        parts.append(jnp.concatenate(hsum, axis=1))
        back[k] = split_dot(jnp.concatenate(parts, axis=0), high[k], rest[k], True)

    freq_loop(freqs, unroll, forward_step)
    freq_loop(freqs, unroll, inverse_step)

    def store(n, at, v):
        wide[n, pl.ds(at, 8), :] = v

    last_stage(back, store, (rows + 1) * narrow // 8, 1.0 / (2 * count * LANES))
    gather_back(wide, send, narrow)
    outward = to_positions(groups, me, narrow, send, gw_ref, out_ss, out_rs, local.at[3])
    for c in outward:
        c.start()
    for n in range(count):
        gh_ref[:, n * LANES : (n + 1) * LANES] = wide[n, rows * narrow :, :]
    for c in outward:
        c.wait()


def conv_scratch(groups, rows, narrow, tok, freqs, count, extra, backward):
    low, f32 = jnp.bfloat16, jnp.float32
    dma = pltpu.SemaphoreType.DMA
    wide_rows = (rows + extra) * narrow
    out = [
        pltpu.VMEM((freqs, 2 * LANES, 2 * LANES), low),
        pltpu.VMEM((freqs, 2 * LANES, 2 * LANES), low),
        pltpu.VMEM((groups, rows, narrow, tok), low),
        pltpu.VMEM((count, wide_rows, LANES), f32),
    ]
    if backward:
        out.append(pltpu.VMEM((freqs, rows * narrow, 2 * LANES), f32))
    return out + [
        pltpu.VMEM((freqs, wide_rows, 2 * LANES), f32),
        pltpu.VMEM((groups, rows, narrow, tok), low),
        dma((groups - 1,)),
        dma((groups - 1,)),
        dma((groups - 1,)),
        dma((groups - 1,)),
        dma((4,)),
    ]


def conv_params(cid):
    return pltpu.CompilerParams(
        collective_id=cid, has_side_effects=True, vmem_limit_bytes=VMEM_LIMIT
    )


def conv_forward(carried, filt, tables):
    rows, _, tok = carried.shape
    narrow, length = filt.shape
    groups = lax.axis_size("seq")
    count = length // LANES
    freqs = count + 1
    vm = pl.BlockSpec(memory_space=pltpu.VMEM)
    hbm = pl.BlockSpec(memory_space=pl.ANY)
    return pl.pallas_call(
        functools.partial(conv_kernel, groups),
        out_shape=(
            jax.ShapeDtypeStruct(carried.shape, jnp.bfloat16),
            jax.ShapeDtypeStruct((freqs, rows * narrow, 2 * LANES), jnp.float32),
            jax.ShapeDtypeStruct((freqs, narrow, 2 * LANES), jnp.float32),
        ),
        in_specs=[vm, vm, hbm, hbm],
        out_specs=(vm,) * 3,
        scratch_shapes=conv_scratch(groups, rows, narrow, tok, freqs, count, 0, False),
        compiler_params=conv_params(1),
        name="conv_forward",
    )(carried, filt, *tables)


def conv_backward(grad, w_spec, h_spec, tables):
    rows, _, tok = grad.shape
    freqs, narrow, _ = h_spec.shape
    groups = lax.axis_size("seq")
    count = freqs - 1
    vm = pl.BlockSpec(memory_space=pltpu.VMEM)
    hbm = pl.BlockSpec(memory_space=pl.ANY)
    return pl.pallas_call(
        functools.partial(conv_back_kernel, groups),
        out_shape=(
            jax.ShapeDtypeStruct(grad.shape, jnp.bfloat16),
            jax.ShapeDtypeStruct((narrow, count * LANES), jnp.float32),
        ),
        in_specs=[vm, vm, vm, hbm, hbm],
        out_specs=(vm,) * 2,
        scratch_shapes=conv_scratch(groups, rows, narrow, tok, freqs, count, 1, True),
        compiler_params=conv_params(2),
        name="conv_backward",
    )(grad, w_spec, h_spec, *tables)


def shards(
    block_in,
    lengths,
    mixer_gain,
    mixer_bias,
    in_weight,
    short_taps,
    filter_in,
    filter_in_bias,
    filter_mid,
    filter_mid_bias,
    filter_freq,
    filter_out,
    filter_skip,
    decay_rate,
    out_weight,
    feed_gain,
    feed_bias,
    up_weight,
    down_weight,
    cotangent,
):
    row_count, tok_count, model_width = block_in.shape
    groups = lax.axis_size("seq")
    length = tok_count * groups
    narrow = model_width // groups
    seq_place = lax.axis_index("seq")
    chan_start = seq_place * narrow
    positions = seq_place * tok_count + jnp.arange(tok_count, dtype=jnp.int32)
    doc_ends = jnp.cumsum(lengths, axis=1)
    live_mask = (positions[None, :] < doc_ends[:, -1:]).astype(jnp.float32)

    def doc_of(where):
        return jnp.sum((where[None, :, None] >= doc_ends[:, None, :]).astype(jnp.int32), axis=2)

    own_doc = doc_of(positions)
    tap_masks = []
    for tap_lag in range(3):
        same_doc = (positions[None, :] >= tap_lag) & (doc_of(positions - tap_lag) == own_doc)
        tap_masks.append(same_doc.astype(jnp.float32))
    block_float = block_in.astype(jnp.float32)
    normed, norm_pull = jax.vjp(layer_norm, block_float, mixer_gain, mixer_bias)
    normed_low = normed.astype(jnp.bfloat16)
    projected = jnp.einsum(
        "rtd,dc->rct", normed_low, in_weight, preferred_element_type=jnp.float32
    ).astype(jnp.bfloat16)
    left_rim = shifted(projected[:, :, tok_count - 2 :], "seq", 1)
    extended = jnp.concatenate([left_rim, projected], axis=2).astype(jnp.float32)
    short_mix = jnp.zeros(projected.shape, jnp.float32)
    for tap_lag in range(3):
        window = extended[:, :, 2 - tap_lag : 2 - tap_lag + tok_count]
        short_mix = (
            short_mix + short_taps[tap_lag][None, :, None] * window * tap_masks[tap_lag][:, None, :]
        )
    gate_out = short_mix[:, :model_width]
    gate_in = short_mix[:, model_width : 2 * model_width]
    stream_v = short_mix[:, 2 * model_width :]
    carried = (gate_in * stream_v * live_mask[:, None, :]).astype(jnp.bfloat16)
    out_part = lax.dynamic_slice_in_dim(filter_out, chan_start, narrow, 1)
    decay_part = lax.dynamic_slice_in_dim(decay_rate, chan_start, narrow, 0)
    skip_part = lax.dynamic_slice_in_dim(filter_skip, chan_start, narrow, 0)

    def build_filter(first_w, first_b, mid_w, mid_b, freq_w, last_w):
        return filter_rows(first_w, first_b, mid_w, mid_b, freq_w, last_w, decay_part, length)

    filt, filter_pull = jax.vjp(
        build_filter, filter_in, filter_in_bias, filter_mid, filter_mid_bias, filter_freq, out_part
    )
    tables = tuple(jnp.asarray(t) for t in spectrum_tables(length))
    at_zero = jnp.arange(length) == 0
    with_skip = filt + jnp.where(at_zero[None, :], skip_part[:, None], 0.0)
    back_home, w_spec, h_spec = conv_forward(carried, with_skip, tables)
    conv_float = back_home.astype(jnp.float32)
    product_low = (gate_out * conv_float * live_mask[:, None, :]).astype(jnp.bfloat16)
    mixed = block_float + jnp.einsum(
        "rct,cd->rtd", product_low, out_weight, preferred_element_type=jnp.float32
    )
    normed_two, feed_pull = jax.vjp(layer_norm, mixed, feed_gain, feed_bias)
    normed_two_low = normed_two.astype(jnp.bfloat16)
    pre_act = jnp.einsum(
        "rtd,df->rtf", normed_two_low, up_weight, preferred_element_type=jnp.float32
    )
    activ, gelu_pull = jax.vjp(jax.nn.gelu, pre_act)
    activ_low = activ.astype(jnp.bfloat16)
    block_out = (
        mixed
        + jnp.einsum("rtf,fd->rtd", activ_low, down_weight, preferred_element_type=jnp.float32)
    ).astype(jnp.bfloat16)
    grad_float = cotangent.astype(jnp.float32)
    grad_down = jnp.einsum("rtf,rtd->fd", activ_low, cotangent, preferred_element_type=jnp.float32)
    grad_activ = jnp.einsum(
        "rtd,fd->rtf", cotangent, down_weight, preferred_element_type=jnp.float32
    )
    grad_pre = gelu_pull(grad_activ)[0].astype(jnp.bfloat16)
    grad_up = jnp.einsum(
        "rtd,rtf->df", normed_two_low, grad_pre, preferred_element_type=jnp.float32
    )
    grad_normed_two = jnp.einsum(
        "rtf,df->rtd", grad_pre, up_weight, preferred_element_type=jnp.float32
    )
    grad_mixed_part, grad_feed_gain, grad_feed_bias = feed_pull(grad_normed_two)
    grad_mixed = grad_float + grad_mixed_part
    grad_mixed_low = grad_mixed.astype(jnp.bfloat16)
    grad_outw = jnp.einsum(
        "rct,rtd->cd", product_low, grad_mixed_low, preferred_element_type=jnp.float32
    )
    grad_product = (
        jnp.einsum("rtd,cd->rct", grad_mixed_low, out_weight, preferred_element_type=jnp.float32)
        * live_mask[:, None, :]
    )
    grad_gate_out = grad_product * conv_float
    grad_conv = (grad_product * gate_out).astype(jnp.bfloat16)
    grad_carried, grad_filt = conv_backward(grad_conv, w_spec, h_spec, tables)
    grad_skip_part = grad_filt[:, 0]
    grad_first_w, grad_first_b, grad_mid_w, grad_mid_b, grad_freq_w, grad_last_part = filter_pull(
        grad_filt
    )
    grad_carried = grad_carried.astype(jnp.float32) * live_mask[:, None, :]
    grad_short = jnp.concatenate(
        [grad_gate_out, grad_carried * stream_v, grad_carried * gate_in], axis=1
    )
    grad_extended = jnp.zeros(extended.shape, jnp.float32)
    tap_grads = []
    for tap_lag in range(3):
        masked = grad_short * tap_masks[tap_lag][:, None, :]
        window = extended[:, :, 2 - tap_lag : 2 - tap_lag + tok_count]
        tap_grads.append(jnp.sum(masked * window, axis=(0, 2)))
        grad_extended = grad_extended + jnp.pad(
            short_taps[tap_lag][None, :, None] * masked, ((0, 0), (0, 0), (2 - tap_lag, tap_lag))
        )
    grad_taps = jnp.stack(tap_grads)
    rim_back = shifted(grad_extended[:, :, :2].astype(jnp.bfloat16), "seq", -1).astype(jnp.float32)
    grad_proj = grad_extended[:, :, 2:] + jnp.pad(rim_back, ((0, 0), (0, 0), (tok_count - 2, 0)))
    grad_proj_low = grad_proj.astype(jnp.bfloat16)
    grad_inw = jnp.einsum(
        "rtd,rct->dc", normed_low, grad_proj_low, preferred_element_type=jnp.float32
    )
    grad_normed = jnp.einsum(
        "rct,dc->rtd", grad_proj_low, in_weight, preferred_element_type=jnp.float32
    )
    grad_input_part, grad_mixer_gain, grad_mixer_bias = norm_pull(grad_normed)
    grad_input = grad_mixed + grad_input_part
    grad_skip = lax.dynamic_update_slice_in_dim(
        jnp.zeros(filter_skip.shape, jnp.float32), grad_skip_part, chan_start, 0
    )
    pieces = (
        grad_mixer_gain,
        grad_mixer_bias,
        grad_taps,
        grad_first_w,
        grad_first_b,
        grad_mid_w,
        grad_mid_b,
        grad_freq_w,
        grad_skip,
        grad_feed_gain,
        grad_feed_bias,
    )
    flat = jnp.concatenate([p.reshape(-1) for p in pieces])
    chunk = -(-flat.shape[0] // (groups * 8 * 128)) * 8
    flat = jnp.pad(flat, (0, groups * chunk * 128 - flat.shape[0])).reshape(groups * chunk, 128)
    low = jnp.bfloat16
    s_in, s_out, s_up, s_down, flat, last_all = reduce_all(
        grad_inw.astype(low),
        grad_outw.astype(low),
        grad_up.astype(low),
        grad_down.astype(low),
        flat,
        grad_last_part,
    )
    shares = (s_in, s_out, s_up, s_down)
    flat = flat.reshape(-1)
    summed = []
    at = 0
    for p in pieces:
        summed.append(flat[at : at + p.size].reshape(p.shape))
        at += p.size
    grad_last = last_all.transpose(1, 0, 2).reshape(filter_out.shape)
    summed = summed[:8] + [grad_last] + summed[8:]
    return (
        block_out,
        grad_input,
        summed[0],
        summed[1],
        shares[0],
        summed[2],
        summed[3],
        summed[4],
        summed[5],
        summed[6],
        summed[7],
        summed[8],
        summed[9],
        shares[1],
        summed[10],
        summed[11],
        shares[2],
        shares[3],
    )


def solution(mesh):
    placed = (
        P("row", "seq", None),
        P("row", None),
        P(),
        P(),
        P(),
        P(),
        P(),
        P(),
        P(),
        P(),
        P(),
        P(),
        P(),
        P(),
        P(),
        P(),
        P(),
        P(),
        P(),
        P("row", "seq", None),
    )
    return jax.shard_map(
        shards,
        mesh=mesh,
        in_specs=placed,
        out_specs=(
            P("row", "seq", None),
            P("row", "seq", None),
            P(),
            P(),
            P("seq", None),
            P(),
            P(),
            P(),
            P(),
            P(),
            P(),
            P(),
            P(),
            P("seq", None),
            P(),
            P(),
            P("seq", None),
            P("seq", None),
        ),
        check_vma=False,
    )
```

```python
import functools
import math

import jax
import jax.numpy as jnp
import numpy as np
from jax import lax
from jax.experimental import pallas as pl
from jax.experimental.pallas import tpu as pltpu
from jax.sharding import PartitionSpec as P

HIGHEST = lax.Precision.HIGHEST


def shifted(array, axis, by):
    peers = lax.axis_size(axis)
    pairs = [(i, i + by) for i in range(peers) if 0 <= i + by < peers]
    return lax.ppermute(array, axis, pairs)


def layer_norm(values, gain, offset):
    center = values - jnp.mean(values, axis=-1, keepdims=True)
    spread = jnp.mean(center * center, axis=-1, keepdims=True)
    return center * lax.rsqrt(spread + 1e-05) * gain + offset


MESH = pl.DeviceIdType.MESH
VMEM_LIMIT = 56 * 1024 * 1024
LANES = 128


def seq_weights(core, groups):
    weights = []
    w = 1
    while w < groups:
        weights.append(w)
        w *= 2
    first = weights[0] + core * (weights[1] - weights[0])
    second = weights[1] - core * (weights[1] - weights[0])
    return [first, second] + weights[2:]


class Halving:
    def __init__(self, groups, me, core, parts, own, first=0):
        self.groups, self.me, self.core, self.parts, self.own, self.first = (
            groups,
            me,
            core,
            parts,
            own,
            first,
        )
        self.weights = seq_weights(core, groups)
        self.bits = [lax.rem(me // w, 2) for w in self.weights]
        self.steps = len(self.weights)
        self.half = own.shape[3]
        self.unit = own.shape[2]

    def shard_of(self, n, core):
        weights = seq_weights(core, self.groups)
        at = 0
        for j in range(self.steps):
            bit = lax.rem(self.me // weights[j], 2)
            keep = (n >> (self.steps - 1 - j)) & 1
            at = at + (bit if keep else 1 - bit) * weights[j]
        return at

    def core_setup(self, bufs, ss, rs, sib):
        self.bufs = bufs
        self.core_copies = []
        for n in range(self.groups):
            s = self.shard_of(n, 1 - self.core)
            row = []
            for p, (ref, high, cols, _) in enumerate(self.parts):
                src = ref.at[
                    pl.ds(pl.multiple_of(s * high * self.unit, 8), high * self.unit),
                    pl.ds(
                        pl.multiple_of((1 - self.core) * cols * self.half, LANES), cols * self.half
                    ),
                ]
                row.append(
                    pltpu.make_async_remote_copy(
                        src_ref=src,
                        dst_ref=bufs[p].at[n],
                        send_sem=ss.at[n, p],
                        recv_sem=rs.at[n, p],
                        device_id={"row": sib},
                        device_id_type=MESH,
                    )
                )
            self.core_copies.append(row)

    def core_start(self):
        for row in self.core_copies:
            for c in row:
                c.start()

    def core_finish(self, n):
        for c in self.core_copies[n]:
            c.wait_recv()
        s = self.shard_of(n, self.core)
        for p, (ref, high, cols, first) in enumerate(self.parts):
            for h in range(high):
                for c in range(cols):
                    mine = ref[
                        pl.ds(pl.multiple_of((s * high + h) * self.unit, 8), self.unit),
                        pl.ds(
                            pl.multiple_of((self.core * cols + c) * self.half, LANES), self.half
                        ),
                    ]
                    self.own[n, first + h * cols + c] = (
                        mine
                        + self.bufs[p][
                            n,
                            h * self.unit : (h + 1) * self.unit,
                            c * self.half : (c + 1) * self.half,
                        ]
                    )

    def step_setup(self, bufs, ss, rs, steps):
        self.step_bufs = dict(zip(steps, bufs))
        self.copies = {}
        for at, k in enumerate(steps):
            for i in range(self.groups >> (k + 1)):
                self.copies[k, i] = pltpu.make_async_remote_copy(
                    src_ref=self.own.at[self.slot(k) + i],
                    dst_ref=bufs[at].at[i],
                    send_sem=ss[at].at[i],
                    recv_sem=rs[at].at[i],
                    device_id={"seq": self.me + self.weights[k] * (1 - 2 * self.bits[k])},
                    device_id_type=MESH,
                )

    def slot(self, k):
        return self.groups - (self.groups >> k) - self.first

    def start(self, k, i):
        self.copies[k, i].start()

    def finish(self, k, i):
        self.copies[k, i].wait_recv()
        at = self.slot(k + 1) + i
        self.own[at] = self.own[at] + self.step_bufs[k][i]

    def count(self, k):
        return self.groups >> (k + 1)

    def wait_sends(self):
        for c in self.copies.values():
            c.wait_send()

    def wait_core_sends(self):
        for row in self.core_copies:
            for c in row:
                c.wait_send()


EARLY = 9
EARLY_STEPS = (0, 1)


def early_parts(gout, gup, gdown):
    return [(gout, 1, 1, 0), (gup, 1, 4, 1), (gdown, 4, 1, 5)]


def greet_all(rows, groups, me, row):
    barrier = pltpu.get_barrier_semaphore()
    for d in range(1, rows):
        pl.semaphore_signal(
            barrier, inc=1, device_id={"row": lax.rem(row + d, rows)}, device_id_type=MESH
        )
    for d in range(1, groups):
        pl.semaphore_signal(
            barrier, inc=1, device_id={"seq": lax.rem(me + d, groups)}, device_id_type=MESH
        )
    pl.semaphore_wait(barrier, rows + groups - 2)


def row_masks(lengths, row, start, tok):
    where = lax.broadcasted_iota(jnp.int32, (8, tok), 1) + start
    ends = []
    total = 0
    for k in range(lengths.shape[1]):
        total = total + lengths[row, k]
        ends.append(total)

    def doc(at):
        out = jnp.zeros(at.shape, jnp.int32)
        for e in ends:
            out = out + (at >= e).astype(jnp.int32)
        return out

    own = doc(where)
    masks = []
    for lag in (1, 2):
        same = (where >= lag) & (doc(where - lag) == own)
        masks.append(same.astype(jnp.float32)[:1])
    return masks + [(where < total).astype(jnp.float32)[:1]]


def window_of(values, lane, edge):
    early, late = edge[:, 0:1], edge[:, 1:2]
    one = jnp.where(lane == 0, late, pltpu.roll(values, 1, 1))
    two = jnp.where(lane == 0, early, jnp.where(lane == 1, late, pltpu.roll(values, 2, 1)))
    return one, two


def spread_taps(taps, padded, wide):
    padded[...] = jnp.zeros_like(padded)
    padded[: taps.shape[0], :] = taps[...]
    for j in range(taps.shape[0]):
        pick = (lax.broadcasted_iota(jnp.int32, (8, LANES), 0) == j).astype(jnp.float32)
        wide[j] = exact_dot(padded[...], pick, 0, 0)


def norm_parts(values):
    center = values - jnp.mean(values, axis=-1, keepdims=True)
    scale = lax.rsqrt(jnp.mean(center * center, axis=-1, keepdims=True) + 1e-05)
    return center * scale, scale


STRIP = 32


def finish_kernel(
    rows,
    groups,
    gw_ref,
    ggo_ref,
    u_ref,
    edge_ref,
    lengths,
    taps,
    weight,
    block,
    gm_ref,
    gain,
    offset,
    feed_gain,
    feed_bias,
    early,
    mid_s,
    first_s,
    last,
    gi_ref,
    fin_o,
    small_o,
    last_o,
    padded,
    wide_taps,
    tap_sum,
    gu,
    gu_low,
    rim,
    rim_out,
    rim_in,
    normed,
    gin,
    small,
    own,
    own_early,
    core_buf,
    step_buf,
    early_buf,
    wide_buf,
    small_row,
    small_sum,
    small_part,
    small_done,
    last_row,
    last_sum,
    rim_sem,
    core_ss,
    core_rs,
    step_ss,
    step_rs,
    early_ss,
    early_rs,
    wide_ss,
    wide_rs,
    fin_ss,
    fin_rs,
    srow_ss,
    srow_rs,
    spart_ss,
    spart_rs,
    sdone_ss,
    sdone_rs,
    lrow_ss,
    lrow_rs,
    last_ss,
    last_rs,
):
    me = lax.axis_index("seq")
    row = lax.axis_index("row")
    core = lax.rem(row, 2)
    sib = row + 1 - 2 * core
    chunk = small_part.shape[1]
    held, width, tok = gw_ref.shape
    low, f32 = jnp.bfloat16, jnp.float32
    greet_all(rows, groups, me, row)

    late = Halving(groups, me, core, [(gin, 1, 3, 0)], own)
    late.core_setup(core_buf, core_ss, core_rs, sib)
    late.step_setup(step_buf, step_ss, step_rs, range(late.steps))
    later = range(EARLY_STEPS[-1] + 1, late.steps)
    rest = Halving(groups, me, core, (), own_early, first=groups - early.shape[0])
    rest.step_setup(early_buf, early_ss, early_rs, later)

    def advance(h, k):
        for i in range(h.count(k)):
            h.finish(k, i)
            if k + 1 < h.steps and i < h.count(k + 1):
                h.start(k + 1, i)

    own_early[...] = early[...]
    for i in range(rest.count(later[0])):
        rest.start(later[0], i)
    lrow = [
        pltpu.make_async_remote_copy(
            src_ref=last,
            dst_ref=last_row.at[d - 1],
            send_sem=lrow_ss.at[d - 1],
            recv_sem=lrow_rs.at[d - 1],
            device_id={"row": lax.rem(row + d, rows)},
            device_id_type=MESH,
        )
        for d in range(1, rows)
    ]
    for c in lrow:
        c.start()

    spread_taps(taps, padded, wide_taps)
    tap_sum[...] = jnp.zeros_like(tap_sum)
    lane = lax.broadcasted_iota(jnp.int32, (STRIP, tok), 1)
    for r in range(held):
        same1, same2, live = row_masks(lengths, r, me * tok, tok)

        def strip(i, carry, r=r, same1=same1, same2=same2, live=live):
            at = [pl.multiple_of(i * STRIP + g * width, STRIP) for g in range(3)]
            tap = [
                [
                    jnp.concatenate([wide_taps[j, pl.ds(a, STRIP), :]] * (tok // LANES), axis=1)
                    for j in range(3)
                ]
                for a in at
            ]
            u = [u_ref[r, pl.ds(a, STRIP), :].astype(f32) for a in at]
            shifts = [
                window_of(v, lane, edge_ref[r, pl.ds(a, STRIP), :].astype(f32))
                for v, a in zip(u, at)
            ]
            gate_in, stream = [
                tap[g][0] * u[g] + tap[g][1] * shifts[g][0] * same1 + tap[g][2] * shifts[g][1] * same2
                for g in (1, 2)
            ]
            gw = gw_ref[r, pl.ds(at[0], STRIP), :].astype(f32) * live
            grads = [ggo_ref[r, pl.ds(at[0], STRIP), :], gw * stream, gw * gate_in]
            for g in range(3):
                m1, m2 = grads[g] * same1, grads[g] * same2
                for j, p in enumerate((grads[g] * u[g], m1 * shifts[g][0], m2 * shifts[g][1])):
                    total = p[:, :LANES]
                    for h in range(1, tok // LANES):
                        total = total + p[:, h * LANES : (h + 1) * LANES]
                    tap_sum[j, pl.ds(at[g], STRIP), :] += total
                b1 = pltpu.roll(tap[g][1] * m1, tok - 1, 1)
                b2 = pltpu.roll(tap[g][2] * m2, tok - 2, 1)
                gu[r, pl.ds(at[g], STRIP), :] = (
                    tap[g][0] * grads[g]
                    + jnp.where(lane < tok - 1, b1, 0.0)
                    + jnp.where(lane < tok - 2, b2, 0.0)
                )
                over = jnp.where(lane < tok - 1, 0.0, b1) + jnp.where(lane < tok - 2, 0.0, b2)
                rim[r, pl.ds(at[g], STRIP), :] = over[:, tok - LANES :].astype(low)
            return carry

        lax.fori_loop(0, width // STRIP, strip, 0)

    def edge_pick(r):
        line = lax.broadcasted_iota(jnp.int32, (8, LANES), 0)
        spot = lax.broadcasted_iota(jnp.int32, (8, LANES), 1)
        return ((spot == line - 2 * r + LANES - 2) & (line >= 2 * r) & (line < 2 * r + 2)).astype(low)

    packed = None
    for r in range(held):
        piece = lax.dot_general(
            edge_pick(r), rim[r], (((1,), (1,)), ((), ())), preferred_element_type=f32
        )
        packed = piece if packed is None else packed + piece
    rim_out[...] = packed
    rim_copy = pltpu.make_async_remote_copy(
        src_ref=rim_out,
        dst_ref=rim_in,
        send_sem=rim_sem.at[0],
        recv_sem=rim_sem.at[1],
        device_id={"seq": lax.rem(me + groups - 1, groups)},
        device_id_type=MESH,
    )
    rim_copy.start()

    at = mid_s.shape[0] + first_s.shape[0]
    small[:at, :] = jnp.concatenate([mid_s[...], first_s[...]], axis=0)
    small[at:, :] = jnp.zeros((small.shape[0] - at, LANES), f32)
    per = width // LANES

    def put_small(first, line):
        for i in range(line.shape[1] // LANES):
            small[first + i : first + i + 1, :] = line[:, i * LANES : (i + 1) * LANES]

    ones = jnp.ones((8, LANES), f32)
    for j in range(3):
        put_small(at + 2 * per + 3 * per * j, exact_dot(ones, tap_sum[j], 1, 1)[:1])
    put_small(at + 11 * per, feed_gain[...][None, :])
    put_small(at + 12 * per, feed_bias[...][None, :])
    gain_row, offset_row = gain[...][None, :], offset[...][None, :]
    for r in range(held):
        hat, _ = norm_parts(block[r].astype(f32))
        normed[r * tok : (r + 1) * tok, :] = (hat * gain_row + offset_row).astype(low)
    advance(rest, later[0])

    rim_copy.wait()
    came = rim_in[...].astype(low)
    for r in range(held):
        add = lax.dot_general(
            came, edge_pick(r), (((0,), (0,)), ((), ())), preferred_element_type=f32
        )
        split = tok - LANES
        gu_low[:, r * tok : r * tok + split] = gu[r, :, :split].astype(low)
        gu_low[:, r * tok + split : (r + 1) * tok] = (gu[r, :, split:] + add).astype(low)

    piece = 256

    def weight_grad(i, carry):
        cols = pl.ds(pl.multiple_of(i * piece, piece), piece)
        gin[:, cols] = lax.dot_general(
            normed[...], gu_low[cols, :], (((0,), (1,)), ((), ())), preferred_element_type=f32
        ).astype(low)
        return carry

    lax.fori_loop(0, 3 * width // piece, weight_grad, 0)
    late.core_start()

    gains = [jnp.zeros((1, width), f32), jnp.zeros((1, width), f32)]
    for r in range(held):
        turned = lax.dot_general(
            weight[...],
            gu_low[:, r * tok : (r + 1) * tok],
            (((1,), (0,)), ((), ())),
            preferred_element_type=f32,
        )
        grad = turned.T
        hat, scale = norm_parts(block[r].astype(f32))
        gains[0] = gains[0] + jnp.sum(grad * hat, axis=0, keepdims=True)
        gains[1] = gains[1] + jnp.sum(grad, axis=0, keepdims=True)
        pulled = grad * gain_row
        pulled = pulled - jnp.mean(pulled, axis=-1, keepdims=True)
        pulled = pulled - hat * jnp.mean(pulled * hat, axis=-1, keepdims=True)
        gi_ref[r] = gm_ref[r] + scale * pulled
        if r == 0:
            for n in range(groups):
                late.core_finish(n)
                if n < late.count(0):
                    late.start(0, n)
    put_small(at, gains[0])
    put_small(at + per, gains[1])

    srow = [
        pltpu.make_async_remote_copy(
            src_ref=small,
            dst_ref=small_row.at[d - 1],
            send_sem=srow_ss.at[d - 1],
            recv_sem=srow_rs.at[d - 1],
            device_id={"row": lax.rem(row + d, rows)},
            device_id_type=MESH,
        )
        for d in range(1, rows)
    ]
    for c in srow:
        c.start()
    for c in srow + lrow:
        c.wait()
    total = small[...]
    tail = last[...]
    for d in range(rows - 1):
        total = total + small_row[d]
        tail = tail + last_row[d]
    small_sum[...] = total
    last_sum[...] = tail
    last_o[me] = tail
    spart = []
    lcp = []
    for d in range(1, groups):
        to = lax.rem(me + d, groups)
        spart.append(
            pltpu.make_async_remote_copy(
                src_ref=small_sum.at[pl.ds(to * chunk, chunk)],
                dst_ref=small_part.at[d - 1],
                send_sem=spart_ss.at[d - 1],
                recv_sem=spart_rs.at[d - 1],
                device_id={"seq": to},
                device_id_type=MESH,
            )
        )
        lcp.append(
            pltpu.make_async_remote_copy(
                src_ref=last_sum,
                dst_ref=last_o.at[me],
                send_sem=last_ss.at[d - 1],
                recv_sem=last_rs.at[d - 1],
                device_id={"seq": to},
                device_id_type=MESH,
            )
        )
    for c in spart + lcp:
        c.start()
    advance(late, 0)
    for k in later[1:]:
        advance(rest, k)
    for c in spart:
        c.wait()
    total = small_sum[pl.ds(me * chunk, chunk)]
    for d in range(groups - 1):
        total = total + small_part[d]
    small_done[...] = total
    small_o[pl.ds(me * chunk, chunk)] = total
    sdone = [
        pltpu.make_async_remote_copy(
            src_ref=small_done,
            dst_ref=small_o.at[pl.ds(me * chunk, chunk)],
            send_sem=sdone_ss.at[d - 1],
            recv_sem=sdone_rs.at[d - 1],
            device_id={"seq": lax.rem(me + d, groups)},
            device_id_type=MESH,
        )
        for d in range(1, groups)
    ]
    for c in sdone:
        c.start()
    for k in range(1, late.steps):
        advance(late, k)

    halves = [(rest, early.shape[0] - 1, 0, EARLY), (late, groups - 1, EARLY, 3)]
    w = 2
    n = 0
    while w < rows:
        bit = lax.rem(row // w, 2)
        for p, (h, slot, _, _) in enumerate(halves):
            c = pltpu.make_async_remote_copy(
                src_ref=h.own.at[slot],
                dst_ref=wide_buf[p].at[n],
                send_sem=wide_ss.at[n, p],
                recv_sem=wide_rs.at[n, p],
                device_id={"row": row + w * (1 - 2 * bit)},
                device_id_type=MESH,
            )
            c.start()
            c.wait()
            h.own[slot] = h.own[slot] + wide_buf[p][n]
        w *= 2
        n += 1

    fin = []
    for p, (h, slot, first, units) in enumerate(halves):
        fin_o[core, first : first + units] = h.own[slot]
        c = pltpu.make_async_remote_copy(
            src_ref=h.own.at[slot],
            dst_ref=fin_o.at[core, pl.ds(first, units)],
            send_sem=fin_ss.at[p],
            recv_sem=fin_rs.at[p],
            device_id={"row": sib},
            device_id_type=MESH,
        )
        c.start()
        fin.append(c)
    late.wait_core_sends()
    late.wait_sends()
    rest.wait_sends()
    for c in sdone + lcp:
        c.wait()
    for c in fin:
        c.wait()


def finish(gw, ggo, u, edge, lengths, taps, weight, block, gm, vectors, early, sums):
    rows, groups = lax.axis_size("row"), lax.axis_size("seq")
    held, width, tok = gw.shape
    unit = width // groups
    half = width // 2
    wide = max(1, rows.bit_length() - 2)
    low, f32 = jnp.bfloat16, jnp.float32
    steps = groups.bit_length() - 1
    later = range(EARLY_STEPS[-1] + 1, steps)
    used = sums[0].shape[0] + sums[1].shape[0] + 13 * (width // LANES)
    lines = used + -used % (8 * groups)
    chunk = lines // groups
    last = sums[2]
    dma = pltpu.SemaphoreType.DMA
    vm = pl.BlockSpec(memory_space=pltpu.VMEM)
    sm = pl.BlockSpec(memory_space=pltpu.SMEM)
    return pl.pallas_call(
        functools.partial(finish_kernel, rows, groups),
        out_shape=(
            jax.ShapeDtypeStruct(gm.shape, f32),
            jax.ShapeDtypeStruct((2, EARLY + 3, unit, half), low),
            jax.ShapeDtypeStruct((lines, LANES), f32),
            jax.ShapeDtypeStruct((groups,) + last.shape, f32),
        ),
        in_specs=[vm] * 4 + [sm] + [vm] * 12,
        out_specs=(vm,) * 4,
        scratch_shapes=[
            pltpu.VMEM((8, 3 * width), f32),
            pltpu.VMEM((3, 3 * width, LANES), f32),
            pltpu.VMEM((3, 3 * width, LANES), f32),
            pltpu.VMEM((held, 3 * width, tok), f32),
            pltpu.VMEM((3 * width, held * tok), low),
            pltpu.VMEM((held, 3 * width, LANES), low),
            pltpu.VMEM((8, 3 * width), f32),
            pltpu.VMEM((8, 3 * width), f32),
            pltpu.VMEM((held * tok, width), low),
            pltpu.VMEM((width, 3 * width), low),
            pltpu.VMEM((lines, LANES), f32),
            pltpu.VMEM((groups, 3, unit, half), low),
            pltpu.VMEM(early.shape, low),
            [pltpu.VMEM((groups, unit, 3 * half), low)],
            [pltpu.VMEM((groups >> (k + 1), 3, unit, half), low) for k in range(steps)],
            [pltpu.VMEM((groups >> (k + 1), EARLY, unit, half), low) for k in later],
            [
                pltpu.VMEM((wide, EARLY, unit, half), low),
                pltpu.VMEM((wide, 3, unit, half), low),
            ],
            pltpu.VMEM((rows - 1, lines, LANES), f32),
            pltpu.VMEM((lines, LANES), f32),
            pltpu.VMEM((groups - 1, chunk, LANES), f32),
            pltpu.VMEM((chunk, LANES), f32),
            pltpu.VMEM((rows - 1,) + last.shape, f32),
            pltpu.VMEM(last.shape, f32),
            dma((2,)),
            dma((groups, 1)),
            dma((groups, 1)),
            [dma((groups >> (k + 1),)) for k in range(steps)],
            [dma((groups >> (k + 1),)) for k in range(steps)],
            [dma((groups >> (k + 1),)) for k in later],
            [dma((groups >> (k + 1),)) for k in later],
            dma((wide, 2)),
            dma((wide, 2)),
            dma((2,)),
            dma((2,)),
            dma((rows - 1,)),
            dma((rows - 1,)),
            dma((groups - 1,)),
            dma((groups - 1,)),
            dma((groups - 1,)),
            dma((groups - 1,)),
            dma((rows - 1,)),
            dma((rows - 1,)),
            dma((groups - 1,)),
            dma((groups - 1,)),
        ],
        compiler_params=pltpu.CompilerParams(
            collective_id=0, has_side_effects=True, vmem_limit_bytes=VMEM_LIMIT
        ),
        name="finish",
    )(gw, ggo, u, edge, lengths, taps, weight, block, gm, *vectors, early, *sums)


def unpack_kernel(
    feat,
    fin,
    small,
    last,
    gain_o,
    bias_o,
    in_o,
    taps_o,
    first_o,
    first_b_o,
    mid_o,
    mid_b_o,
    freq_o,
    last_o,
    skip_o,
    out_o,
    feed_gain_o,
    feed_bias_o,
    up_o,
    down_o,
):
    f32 = jnp.float32
    unit, half = fin.shape[2], fin.shape[3]
    hidden = mid_o.shape[0]
    width = gain_o.shape[0]
    per = width // LANES
    outs = [(out_o, 1, 1, 0), (up_o, 1, 4, 1), (down_o, 4, 1, 5), (in_o, 1, 3, EARLY)]
    for core in range(2):
        for out, high, cols, first in outs:
            for h in range(high):
                for c in range(cols):
                    at = (core * cols + c) * half
                    out[h * unit : (h + 1) * unit, at : at + half] = fin[
                        core, first + h * cols + c
                    ].astype(f32)

    def line(first, count):
        pieces = [small[first + i : first + i + 1, :] for i in range(count)]
        return jnp.concatenate(pieces, axis=1)

    at = hidden + -(-(feat + 1) // 8) * 8
    gain_o[...] = line(at, per)[0]
    bias_o[...] = line(at + per, per)[0]
    for j in range(3):
        taps_o[j : j + 1, :] = line(at + 2 * per + 3 * per * j, 3 * per)
    feed_gain_o[...] = line(at + 11 * per, per)[0]
    feed_bias_o[...] = line(at + 12 * per, per)[0]
    first_o[...] = small[hidden : hidden + feat, :hidden]
    first_b_o[...] = small[hidden + feat : hidden + feat + 1, :hidden][0]
    mid_o[...] = small[:hidden, :hidden]
    shape = (hidden, hidden)
    same = lax.broadcasted_iota(jnp.int32, shape, 0) == lax.broadcasted_iota(jnp.int32, shape, 1)
    for out, col in ((mid_b_o, hidden), (freq_o, hidden + 1)):
        out[...] = jnp.sum(
            jnp.where(same, small[:hidden, col : col + 1], 0.0), axis=0, keepdims=True
        )[0]
    turned = last[...].T
    last_o[...] = turned[:hidden]
    skip_o[...] = turned[hidden : hidden + 1][0]


def unpack(fin, small, last, feat, hidden, width):
    f32 = jnp.float32
    unit = fin.shape[2]
    vm = pl.BlockSpec(memory_space=pltpu.VMEM)
    shapes = [
        (width,),
        (width,),
        (unit, 3 * width),
        (3, 3 * width),
        (feat, hidden),
        (hidden,),
        (hidden, hidden),
        (hidden,),
        (hidden,),
        (hidden, width),
        (width,),
        (unit, width),
        (width,),
        (width,),
        (unit, 4 * width),
        (4 * unit, width),
    ]
    return pl.pallas_call(
        functools.partial(unpack_kernel, feat),
        out_shape=tuple(jax.ShapeDtypeStruct(x, f32) for x in shapes),
        in_specs=[vm] * 3,
        out_specs=(vm,) * len(shapes),
        compiler_params=pltpu.CompilerParams(vmem_limit_bytes=VMEM_LIMIT),
        name="unpack",
    )(fin, small, last.reshape(width, LANES))


def spectrum_tables(length):
    period = 2 * length
    first = period // LANES
    k1 = np.arange(first // 2 + 1, dtype=np.int64)[:, None, None]
    n2 = np.arange(LANES, dtype=np.int64)[None, :, None]
    k2 = np.arange(LANES, dtype=np.int64)[None, None, :]
    angle = 2.0 * np.pi / period * (n2 * (k1 + first * k2) % period)
    full = np.concatenate([np.cos(angle), np.sin(angle)], axis=2).astype(np.float32)
    high = full.astype(jnp.bfloat16)
    rest = (full - high.astype(np.float32)).astype(jnp.bfloat16)
    return high, rest


def feature_rows(length, feat_count):
    bands = (feat_count - 1) // 2
    at = np.arange(length, dtype=np.int64)[None, :]
    angle = 2.0 * np.pi / length * (at * np.arange(1, bands + 1)[:, None] % length)
    rows = [at / length, np.cos(angle), -np.sin(angle), np.ones((1, length))]
    rows = np.concatenate(rows, axis=0)
    pad = -rows.shape[0] % 8
    return np.pad(rows, ((0, pad), (0, 0))).astype(np.float32)


def sin_cos(x):
    n = jnp.round(x * (2.0 / math.pi))
    r = x - n * 1.5703125
    r = r - n * 4.837512969970703125e-4
    r = r - n * 7.549789948768648e-8
    z = r * r
    s = r + r * z * (-1.6666654611e-1 + z * (8.3321608736e-3 - z * 1.9515295891e-4))
    c = (
        1.0
        - 0.5 * z
        + z * z * (4.166664568298827e-2 + z * (-1.388731625493765e-3 + z * 2.443315711809948e-5))
    )
    q = n.astype(jnp.int32) & 3
    odd = (q & 1) == 1
    sine = jnp.where(odd, c, s)
    cosine = jnp.where(odd, s, c)
    sine = jnp.where(q >= 2, -sine, sine)
    cosine = jnp.where((q == 1) | (q == 2), -cosine, cosine)
    return sine, cosine


def exact_dot(p, q, left, right):
    return lax.dot_general(
        p, q, (((left,), (right,)), ((), ())), preferred_element_type=jnp.float32, precision=HIGHEST
    )


def column_of(row):
    size = row.shape[1]
    shape = (size, size)
    same = lax.broadcasted_iota(jnp.int32, shape, 0) == lax.broadcasted_iota(jnp.int32, shape, 1)
    return jnp.sum(jnp.where(same, row, 0.0), axis=1, keepdims=True)


class FilterNet:
    def __init__(self, me, narrow, params, aug):
        first, first_b, mid, mid_b, freq, last, skip, decay, self.feats = params
        feat = first.shape[0]
        aug[...] = jnp.zeros_like(aug)
        aug[:feat, :] = first[...]
        aug[feat : feat + 1, :] = first_b[...][None, :]
        self.aug = aug
        self.mid = mid
        self.mid_b = column_of(mid_b[...][None, :])
        self.freq = column_of(freq[...][None, :])
        width = skip.shape[0]
        shape = (narrow, width)
        pick = (
            lax.broadcasted_iota(jnp.int32, shape, 1)
            == lax.broadcasted_iota(jnp.int32, shape, 0) + me * narrow
        )
        self.skip = jnp.sum(jnp.where(pick, skip[...][None, :], 0.0), axis=1, keepdims=True)
        self.decay = jnp.sum(jnp.where(pick, decay[...][None, :], 0.0), axis=1, keepdims=True)
        self.last = exact_dot(pick.astype(jnp.float32), last[...], 1, 1)
        self.narrow = narrow

    def layers(self, at, size):
        feats = self.feats[:, pl.ds(at, size)]
        pre1 = exact_dot(self.aug[...], feats, 0, 0)
        a1, c1 = sin_cos(self.freq * pre1)
        pre2 = exact_dot(self.mid[...], a1, 0, 0) + self.mid_b
        a2, c2 = sin_cos(self.freq * pre2)
        return feats, pre1, a1, c1, pre2, a2, c2

    def fade(self, at, size):
        where = lax.broadcasted_iota(jnp.int32, (self.narrow, size), 1) + at
        return jnp.exp(-self.decay * where.astype(jnp.float32)), where

    def build(self, at, size):
        a2 = self.layers(at, size)[5]
        fade, where = self.fade(at, size)
        return exact_dot(self.last, a2, 1, 0) * fade + jnp.where(where == 0, self.skip, 0.0)

    def pull(self, at, size, grad, first_o, mid_o, last_o):
        feats, pre1, a1, c1, pre2, a2, c2 = self.layers(at, size)
        fade, where = self.fade(at, size)
        hidden = a1.shape[0]
        raw = grad * fade
        last_o[:, :hidden] += exact_dot(raw, a2, 1, 1)
        last_o[:, hidden : hidden + 1] += jnp.sum(
            jnp.where(where == 0, grad, 0.0), axis=1, keepdims=True
        )
        turned2 = exact_dot(self.last, raw, 0, 0) * c2
        freq = jnp.sum(turned2 * pre2, axis=1, keepdims=True)
        down2 = turned2 * self.freq
        mid_o[:, :hidden] += exact_dot(a1, down2, 1, 1)
        mid_o[:, hidden : hidden + 1] += jnp.sum(down2, axis=1, keepdims=True)
        turned1 = exact_dot(self.mid[...], down2, 1, 0) * c1
        freq = freq + jnp.sum(turned1 * pre1, axis=1, keepdims=True)
        mid_o[:, hidden + 1 : hidden + 2] += freq
        down1 = turned1 * self.freq
        first_o[:, :hidden] += exact_dot(feats, down1, 1, 1)


CHUNK = 4


def half_dft(x):
    count = 2 * len(x)
    if count == 2:
        return [(x[0], None), (x[0], None)]
    even, odd = half_dft(x[0::2]), half_dft(x[1::2])
    out = [None] * (count // 2 + 1)
    for k in range(count // 4 + 1):
        er, ei = even[k]
        orr, oi = odd[k]
        if k == 0:
            out[0] = (er + orr, None)
            out[count // 2] = (er - orr, None)
        elif 4 * k == count:
            out[k] = (er, -orr)
        else:
            c, s = math.cos(2 * math.pi * k / count), math.sin(2 * math.pi * k / count)
            tr = orr * c + oi * s
            ti = oi * c - orr * s
            out[k] = (er + tr, ei + ti)
            out[count // 2 - k] = (er - tr, ti - ei)
    return out


def half_inverse(spec):
    count = 2 * (len(spec) - 1)
    if count == 2:
        return [spec[0][0] + spec[1][0]]
    even, odd = [], []
    for k in range(count // 4 + 1):
        ar, ai = spec[k]
        br, bi = spec[count // 2 - k]
        if k == 0:
            even.append((ar + br, None))
            odd.append((ar - br, None))
        elif 4 * k == count:
            even.append((ar + ar, None))
            odd.append((-(ai + ai), None))
        else:
            c, s = math.cos(2 * math.pi * k / count), math.sin(2 * math.pi * k / count)
            dr, di = ar - br, ai + bi
            even.append((ar + br, ai - bi))
            odd.append((dr * c - di * s, dr * s + di * c))
    out = [None] * (count // 2)
    out[0::2] = half_inverse(even)
    out[1::2] = half_inverse(odd)
    return out


def turn_of(table):
    cos, sin = table[:, :LANES], table[:, LANES:]
    return jnp.concatenate(
        [jnp.concatenate([cos, -sin], axis=1), jnp.concatenate([sin, cos], axis=1)], axis=0
    )


def split_dot(a, high, rest, back):
    a_high = a.astype(jnp.bfloat16)
    a_rest = (a - a_high.astype(jnp.float32)).astype(jnp.bfloat16)
    dims = (((1,), (1 if back else 0,)), ((), ()))
    high, rest = turn_of(high), turn_of(rest)

    def dot(p, q):
        return lax.dot_general(p, q, dims, preferred_element_type=jnp.float32)

    return dot(a_high, high) + (dot(a_rest, high) + dot(a_high, rest))


def tile_loop(tiles, body):
    def step(i, carry):
        body(pl.multiple_of(i * 8, 8))
        return carry

    lax.fori_loop(0, tiles, step, 0)


def first_stage(load, spec, tiles):
    zero = jnp.zeros((8, LANES), jnp.float32)

    def body(at):
        for k, (re, im) in enumerate(half_dft(load(at))):
            spec[k, pl.ds(at, 8), :LANES] = re
            spec[k, pl.ds(at, 8), LANES:] = zero if im is None else im

    tile_loop(tiles, body)


def last_stage(spec, store, tiles, scale):
    def body(at):
        freqs = spec.shape[0]
        values = []
        for k in range(freqs):
            re = spec[k, pl.ds(at, 8), :LANES]
            im = None if k in (0, freqs - 1) else spec[k, pl.ds(at, 8), LANES:]
            values.append((re, im))
        for n, v in enumerate(half_inverse(values)):
            store(n, at, v * scale)

    tile_loop(tiles, body)


def greet(groups, me):
    barrier = pltpu.get_barrier_semaphore()
    for d in range(1, groups):
        pl.semaphore_signal(
            barrier, inc=1, device_id={"seq": lax.rem(me + d, groups)}, device_id_type=MESH
        )
    pl.semaphore_wait(barrier, groups - 1)


def to_channels(groups, me, narrow, src, recv, ss, rs, ls):
    local = pltpu.make_async_copy(
        src.at[:, pl.ds(pl.multiple_of(me * narrow, 8), narrow), :], recv.at[me], ls
    )
    out = [local]
    for d in range(1, groups):
        to = lax.rem(me + d, groups)
        out.append(
            pltpu.make_async_remote_copy(
                src_ref=src.at[:, pl.ds(pl.multiple_of(to * narrow, 8), narrow), :],
                dst_ref=recv.at[me],
                send_sem=ss.at[d - 1],
                recv_sem=rs.at[d - 1],
                device_id={"seq": to},
                device_id_type=MESH,
            )
        )
    return out


def to_positions(groups, me, narrow, send, dst, ss, rs, ls):
    mine = dst.at[:, pl.ds(pl.multiple_of(me * narrow, 8), narrow), :]
    out = [pltpu.make_async_copy(send.at[me], mine, ls)]
    for d in range(1, groups):
        to = lax.rem(me + d, groups)
        out.append(
            pltpu.make_async_remote_copy(
                src_ref=send.at[to],
                dst_ref=mine,
                send_sem=ss.at[d - 1],
                recv_sem=rs.at[d - 1],
                device_id={"seq": to},
                device_id_type=MESH,
            )
        )
    return out


def spread(recv, wide, narrow):
    per = recv.shape[3] // LANES

    def step(s, carry):
        for r in range(recv.shape[1]):
            for h in range(per):
                wide[s * per + h, r * narrow : (r + 1) * narrow, :] = recv[
                    s, r, :, h * LANES : (h + 1) * LANES
                ].astype(jnp.float32)
        return carry

    lax.fori_loop(0, recv.shape[0], step, 0)


def gather_back(wide, send, narrow):
    per = send.shape[3] // LANES

    def step(s, carry):
        for r in range(send.shape[1]):
            for h in range(per):
                send[s, r, :, h * LANES : (h + 1) * LANES] = wide[
                    s * per + h, r * narrow : (r + 1) * narrow, :
                ].astype(jnp.bfloat16)
        return carry

    lax.fori_loop(0, send.shape[0], step, 0)


def freq_loop(freqs, unroll, body):
    def step(i, carry):
        for j in range(unroll):
            body(i * unroll + j)
        return carry

    lax.fori_loop(0, freqs // unroll, step, 0)


UNROLL = {33: 3, 65: 5}


def conv_kernel(
    groups,
    w_ref,
    first,
    first_b,
    mid,
    mid_b,
    freq,
    last,
    skip,
    decay,
    feats,
    high_ref,
    rest_ref,
    z_ref,
    w_spec,
    h_spec,
    high,
    rest,
    recv,
    wide,
    back,
    send,
    in_ss,
    in_rs,
    out_ss,
    out_rs,
    local,
    aug,
    filt,
):
    me = lax.axis_index("seq")
    narrow = h_spec.shape[1]
    count, freqs = wide.shape[0], high.shape[0]
    rows = w_ref.shape[0]
    unroll = UNROLL.get(freqs, 1)
    tables = [
        pltpu.make_async_copy(high_ref, high, local.at[0]),
        pltpu.make_async_copy(rest_ref, rest, local.at[1]),
    ]
    for c in tables:
        c.start()
    greet(groups, me)
    inward = to_channels(groups, me, narrow, w_ref, recv, in_ss, in_rs, local.at[2])
    for c in inward:
        c.start()

    net = FilterNet(me, narrow, (first, first_b, mid, mid_b, freq, last, skip, decay, feats), aug)

    def build(i, carry):
        size = CHUNK * LANES
        values = net.build(pl.multiple_of(i * size, LANES), size)
        for j in range(CHUNK):
            filt[i * CHUNK + j] = values[:, j * LANES : (j + 1) * LANES]
        return carry

    lax.fori_loop(0, count // CHUNK, build, 0)
    first_stage(
        lambda at: [filt[n, pl.ds(at, 8), :] for n in range(count)], h_spec, narrow // 8
    )
    for c in tables:
        c.wait()

    def filter_freq_step(k):
        h_spec[k] = split_dot(h_spec[k], high[k], rest[k], False)

    freq_loop(freqs, unroll, filter_freq_step)
    for c in inward:
        c.wait()
    spread(recv, wide, narrow)
    first_stage(
        lambda at: [wide[n, pl.ds(at, 8), :] for n in range(count)], w_spec, rows * narrow // 8
    )

    def forward_step(k):
        w_spec[k] = split_dot(w_spec[k], high[k], rest[k], False)

    def inverse_step(k):
        h = h_spec[k]
        hr, hi = h[:, :LANES], h[:, LANES:]
        parts = []
        for r in range(rows):
            w = w_spec[k, r * narrow : (r + 1) * narrow]
            wr, wi = w[:, :LANES], w[:, LANES:]
            parts.append(jnp.concatenate([wr * hr - wi * hi, wr * hi + wi * hr], axis=1))
        back[k] = split_dot(jnp.concatenate(parts, axis=0), high[k], rest[k], True)

    freq_loop(freqs, unroll, forward_step)
    freq_loop(freqs, unroll, inverse_step)

    def store(n, at, v):
        wide[n, pl.ds(at, 8), :] = v

    last_stage(back, store, rows * narrow // 8, 1.0 / (2 * count * LANES))
    gather_back(wide, send, narrow)
    outward = to_positions(groups, me, narrow, send, z_ref, out_ss, out_rs, local.at[3])
    for c in outward:
        c.start()
    for c in outward:
        c.wait()


def conv_back_kernel(
    rows_all,
    groups,
    g_ref,
    w_spec,
    h_spec,
    high_ref,
    rest_ref,
    gout,
    gup,
    gdown,
    first,
    first_b,
    mid,
    mid_b,
    freq,
    last,
    skip,
    decay,
    feats,
    gw_ref,
    early_o,
    first_o,
    mid_o,
    last_o,
    high,
    rest,
    recv,
    wide,
    back,
    send,
    in_ss,
    in_rs,
    out_ss,
    out_rs,
    local,
    own,
    core_buf,
    step_buf,
    core_ss,
    core_rs,
    step_ss,
    step_rs,
    aug,
):
    me = lax.axis_index("seq")
    row = lax.axis_index("row")
    core = lax.rem(row, 2)
    narrow = h_spec.shape[1]
    count, freqs = wide.shape[0], high.shape[0]
    rows = g_ref.shape[0]
    unroll = UNROLL.get(freqs, 1)
    tables = [
        pltpu.make_async_copy(high_ref, high, local.at[0]),
        pltpu.make_async_copy(rest_ref, rest, local.at[1]),
    ]
    for c in tables:
        c.start()
    greet_all(rows_all, groups, me, row)
    inward = to_channels(groups, me, narrow, g_ref, recv, in_ss, in_rs, local.at[2])
    for c in inward:
        c.start()
    early = Halving(groups, me, core, early_parts(gout, gup, gdown), own)
    early.core_setup(core_buf, core_ss, core_rs, row + 1 - 2 * core)
    early.step_setup(step_buf, step_ss, step_rs, EARLY_STEPS)
    early.core_start()
    for n in range(groups):
        early.core_finish(n)
        if n < early.count(0):
            early.start(0, n)
    for c in tables:
        c.wait()
    for c in inward:
        c.wait()
    spread(recv, wide, narrow)
    first_stage(
        lambda at: [wide[n, pl.ds(at, 8), :] for n in range(count)], back, rows * narrow // 8
    )

    def forward_step(k):
        back[k, : rows * narrow] = split_dot(back[k, : rows * narrow], high[k], rest[k], False)

    def inverse_step(k):
        h = h_spec[k]
        hr, hi = h[:, :LANES], h[:, LANES:]
        parts = []
        hsum = None
        for r in range(rows):
            w = w_spec[k, r * narrow : (r + 1) * narrow]
            wr, wi = w[:, :LANES], w[:, LANES:]
            g = back[k, r * narrow : (r + 1) * narrow]
            gr, gi = g[:, :LANES], g[:, LANES:]
            parts.append(jnp.concatenate([hr * gr + hi * gi, hr * gi - hi * gr], axis=1))
            pair = (wr * gr + wi * gi, wr * gi - wi * gr)
            hsum = pair if hsum is None else (hsum[0] + pair[0], hsum[1] + pair[1])
        parts.append(jnp.concatenate(hsum, axis=1))
        back[k] = split_dot(jnp.concatenate(parts, axis=0), high[k], rest[k], True)

    freq_loop(freqs, unroll, forward_step)
    for i in range(early.count(1)):
        early.finish(0, i)
        early.start(1, i)
    freq_loop(freqs, unroll, inverse_step)

    def store(n, at, v):
        wide[n, pl.ds(at, 8), :] = v

    last_stage(back, store, (rows + 1) * narrow // 8, 1.0 / (2 * count * LANES))
    gather_back(wide, send, narrow)
    outward = to_positions(groups, me, narrow, send, gw_ref, out_ss, out_rs, local.at[3])
    for c in outward:
        c.start()
    net = FilterNet(me, narrow, (first, first_b, mid, mid_b, freq, last, skip, decay, feats), aug)
    for out in (first_o, mid_o, last_o):
        out[...] = jnp.zeros_like(out)

    def pull(i, carry):
        size = CHUNK * LANES
        grad = [wide[i * CHUNK + j, rows * narrow :, :] for j in range(CHUNK)]
        net.pull(
            pl.multiple_of(i * size, LANES),
            size,
            jnp.concatenate(grad, axis=1),
            first_o,
            mid_o,
            last_o,
        )
        return carry

    lax.fori_loop(0, count // CHUNK, pull, 0)
    for i in range(early.count(1), early.count(0)):
        early.finish(0, i)
    for i in range(early.count(1)):
        early.finish(1, i)
        early_o[i] = own[early.slot(2) + i]
    early.wait_core_sends()
    early.wait_sends()
    for c in outward:
        c.wait()


def conv_scratch(groups, rows, narrow, tok, freqs, count, extra):
    low, f32 = jnp.bfloat16, jnp.float32
    dma = pltpu.SemaphoreType.DMA
    wide_rows = (rows + extra) * narrow
    out = [
        pltpu.VMEM((freqs, LANES, 2 * LANES), low),
        pltpu.VMEM((freqs, LANES, 2 * LANES), low),
        pltpu.VMEM((groups, rows, narrow, tok), low),
        pltpu.VMEM((count, wide_rows, LANES), f32),
    ]
    return out + [
        pltpu.VMEM((freqs, wide_rows, 2 * LANES), f32),
        pltpu.VMEM((groups, rows, narrow, tok), low),
        dma((groups - 1,)),
        dma((groups - 1,)),
        dma((groups - 1,)),
        dma((groups - 1,)),
        dma((4,)),
    ]


def conv_params(cid):
    return pltpu.CompilerParams(
        collective_id=cid, has_side_effects=True, vmem_limit_bytes=VMEM_LIMIT
    )


def conv_forward(carried, params, tables):
    rows, width, tok = carried.shape
    groups = lax.axis_size("seq")
    narrow, length = width // groups, tok * groups
    count = length // LANES
    freqs = count + 1
    vm = pl.BlockSpec(memory_space=pltpu.VMEM)
    hbm = pl.BlockSpec(memory_space=pl.ANY)
    return pl.pallas_call(
        functools.partial(conv_kernel, groups),
        out_shape=(
            jax.ShapeDtypeStruct(carried.shape, jnp.bfloat16),
            jax.ShapeDtypeStruct((freqs, rows * narrow, 2 * LANES), jnp.float32),
            jax.ShapeDtypeStruct((freqs, narrow, 2 * LANES), jnp.float32),
        ),
        in_specs=[vm] * 10 + [hbm, hbm],
        out_specs=(vm,) * 3,
        scratch_shapes=conv_scratch(groups, rows, narrow, tok, freqs, count, 0)
        + [
            pltpu.VMEM((params[-1].shape[0], params[0].shape[1]), jnp.float32),
            pltpu.VMEM((count, narrow, LANES), jnp.float32),
        ],
        compiler_params=conv_params(1),
        name="conv_forward",
    )(carried, *params, *tables)


def conv_backward(grad, w_spec, h_spec, tables, gout, gup, gdown, params):
    rows, _, tok = grad.shape
    freqs, narrow, _ = h_spec.shape
    groups = lax.axis_size("seq")
    count = freqs - 1
    half = gout.shape[0] // 2
    vm = pl.BlockSpec(memory_space=pltpu.VMEM)
    hbm = pl.BlockSpec(memory_space=pl.ANY)
    low, f32 = jnp.bfloat16, jnp.float32
    dma = pltpu.SemaphoreType.DMA
    kept = groups >> len(EARLY_STEPS)
    feat_rows, hidden = params[-1].shape[0], params[0].shape[1]
    return pl.pallas_call(
        functools.partial(conv_back_kernel, lax.axis_size("row"), groups),
        out_shape=(
            jax.ShapeDtypeStruct(grad.shape, low),
            jax.ShapeDtypeStruct((kept, EARLY, narrow, half), low),
            jax.ShapeDtypeStruct((feat_rows, LANES), f32),
            jax.ShapeDtypeStruct((hidden, LANES), f32),
            jax.ShapeDtypeStruct((narrow, LANES), f32),
        ),
        in_specs=[vm, vm, vm, hbm, hbm] + [vm] * 12,
        out_specs=(vm,) * 5,
        scratch_shapes=conv_scratch(groups, rows, narrow, tok, freqs, count, 1)
        + [
            pltpu.VMEM((groups, EARLY, narrow, half), low),
            [
                pltpu.VMEM((groups, narrow, half), low),
                pltpu.VMEM((groups, narrow, 4 * half), low),
                pltpu.VMEM((groups, 4 * narrow, half), low),
            ],
            [pltpu.VMEM((groups >> (k + 1), EARLY, narrow, half), low) for k in EARLY_STEPS],
            dma((groups, 3)),
            dma((groups, 3)),
            [dma((groups >> (k + 1),)) for k in EARLY_STEPS],
            [dma((groups >> (k + 1),)) for k in EARLY_STEPS],
            pltpu.VMEM((feat_rows, hidden), f32),
        ],
        compiler_params=conv_params(2),
        name="conv_backward",
    )(grad, w_spec, h_spec, *tables, gout, gup, gdown, *params)


def shards(
    block_in,
    lengths,
    mixer_gain,
    mixer_bias,
    in_weight,
    short_taps,
    filter_in,
    filter_in_bias,
    filter_mid,
    filter_mid_bias,
    filter_freq,
    filter_out,
    filter_skip,
    decay_rate,
    out_weight,
    feed_gain,
    feed_bias,
    up_weight,
    down_weight,
    cotangent,
):
    row_count, tok_count, model_width = block_in.shape
    groups = lax.axis_size("seq")
    length = tok_count * groups
    seq_place = lax.axis_index("seq")
    positions = seq_place * tok_count + jnp.arange(tok_count, dtype=jnp.int32)
    doc_ends = jnp.cumsum(lengths, axis=1)
    live_mask = (positions[None, :] < doc_ends[:, -1:]).astype(jnp.float32)

    def doc_of(where):
        return jnp.sum((where[None, :, None] >= doc_ends[:, None, :]).astype(jnp.int32), axis=2)

    own_doc = doc_of(positions)
    tap_masks = []
    for tap_lag in range(3):
        same_doc = (positions[None, :] >= tap_lag) & (doc_of(positions - tap_lag) == own_doc)
        tap_masks.append(same_doc.astype(jnp.float32))
    block_float = block_in.astype(jnp.float32)
    normed_low = layer_norm(block_float, mixer_gain, mixer_bias).astype(jnp.bfloat16)
    projected = jnp.einsum(
        "rtd,dc->rct", normed_low, in_weight, preferred_element_type=jnp.float32
    ).astype(jnp.bfloat16)
    left_rim = shifted(projected[:, :, tok_count - 2 :], "seq", 1)
    extended = jnp.concatenate([left_rim, projected], axis=2).astype(jnp.float32)
    short_mix = jnp.zeros(projected.shape, jnp.float32)
    for tap_lag in range(3):
        window = extended[:, :, 2 - tap_lag : 2 - tap_lag + tok_count]
        short_mix = (
            short_mix + short_taps[tap_lag][None, :, None] * window * tap_masks[tap_lag][:, None, :]
        )
    gate_out = short_mix[:, :model_width]
    gate_in = short_mix[:, model_width : 2 * model_width]
    stream_v = short_mix[:, 2 * model_width :]
    carried = (gate_in * stream_v * live_mask[:, None, :]).astype(jnp.bfloat16)
    tables = tuple(jnp.asarray(t) for t in spectrum_tables(length))
    params = (
        filter_in,
        filter_in_bias,
        filter_mid,
        filter_mid_bias,
        filter_freq,
        filter_out,
        filter_skip,
        decay_rate,
        jnp.asarray(feature_rows(length, filter_in.shape[0])),
    )
    back_home, w_spec, h_spec = conv_forward(carried, params, tables)
    conv_float = back_home.astype(jnp.float32)
    product_low = (gate_out * conv_float * live_mask[:, None, :]).astype(jnp.bfloat16)
    mixed = block_float + jnp.einsum(
        "rct,cd->rtd", product_low, out_weight, preferred_element_type=jnp.float32
    )
    normed_two, feed_pull = jax.vjp(layer_norm, mixed, feed_gain, feed_bias)
    normed_two_low = normed_two.astype(jnp.bfloat16)
    pre_act = jnp.einsum(
        "rtd,df->rtf", normed_two_low, up_weight, preferred_element_type=jnp.float32
    )
    activ, gelu_pull = jax.vjp(jax.nn.gelu, pre_act)
    activ_low = activ.astype(jnp.bfloat16)
    block_out = (
        mixed
        + jnp.einsum("rtf,fd->rtd", activ_low, down_weight, preferred_element_type=jnp.float32)
    ).astype(jnp.bfloat16)
    grad_float = cotangent.astype(jnp.float32)
    grad_down = jnp.einsum("rtf,rtd->fd", activ_low, cotangent, preferred_element_type=jnp.float32)
    grad_activ = jnp.einsum(
        "rtd,fd->rtf", cotangent, down_weight, preferred_element_type=jnp.float32
    )
    grad_pre = gelu_pull(grad_activ)[0].astype(jnp.bfloat16)
    grad_up = jnp.einsum(
        "rtd,rtf->df", normed_two_low, grad_pre, preferred_element_type=jnp.float32
    )
    grad_normed_two = jnp.einsum(
        "rtf,df->rtd", grad_pre, up_weight, preferred_element_type=jnp.float32
    )
    grad_mixed_part, grad_feed_gain, grad_feed_bias = feed_pull(grad_normed_two)
    grad_mixed = grad_float + grad_mixed_part
    grad_mixed_low = grad_mixed.astype(jnp.bfloat16)
    grad_outw = jnp.einsum(
        "rct,rtd->cd", product_low, grad_mixed_low, preferred_element_type=jnp.float32
    )
    grad_product = (
        jnp.einsum("rtd,cd->rct", grad_mixed_low, out_weight, preferred_element_type=jnp.float32)
        * live_mask[:, None, :]
    )
    grad_gate_out = grad_product * conv_float
    grad_conv = (grad_product * gate_out).astype(jnp.bfloat16)
    low = jnp.bfloat16
    grad_carried, early, first_sum, mid_sum, last_sum = conv_backward(
        grad_conv,
        w_spec,
        h_spec,
        tables,
        grad_outw.astype(low),
        grad_up.astype(low),
        grad_down.astype(low),
        params,
    )
    grad_input, fin, small, last_all = finish(
        grad_carried,
        grad_gate_out,
        projected,
        left_rim,
        lengths,
        short_taps,
        in_weight,
        block_in,
        grad_mixed,
        (mixer_gain, mixer_bias, grad_feed_gain, grad_feed_bias),
        early,
        (mid_sum, first_sum, last_sum),
    )
    done = unpack(fin, small, last_all, filter_in.shape[0], filter_mid.shape[0], model_width)
    return (block_out, grad_input, *done)


def solution(mesh):
    placed = (
        P("row", "seq", None),
        P("row", None),
        P(),
        P(),
        P(),
        P(),
        P(),
        P(),
        P(),
        P(),
        P(),
        P(),
        P(),
        P(),
        P(),
        P(),
        P(),
        P(),
        P(),
        P("row", "seq", None),
    )
    return jax.shard_map(
        shards,
        mesh=mesh,
        in_specs=placed,
        out_specs=(
            P("row", "seq", None),
            P("row", "seq", None),
            P(),
            P(),
            P("seq", None),
            P(),
            P(),
            P(),
            P(),
            P(),
            P(),
            P(),
            P(),
            P("seq", None),
            P(),
            P(),
            P("seq", None),
            P("seq", None),
        ),
        check_vma=False,
    )
```

```python
import functools
import math

import jax
import jax.numpy as jnp
import numpy as np
from jax import lax
from jax.experimental import pallas as pl
from jax.experimental.pallas import tpu as pltpu
from jax.sharding import PartitionSpec as P

HIGHEST = lax.Precision.HIGHEST


def layer_norm(values, gain, offset):
    center = values - jnp.mean(values, axis=-1, keepdims=True)
    spread = jnp.mean(center * center, axis=-1, keepdims=True)
    return center * lax.rsqrt(spread + 1e-05) * gain + offset


MESH = pl.DeviceIdType.MESH
VMEM_LIMIT = 56 * 1024 * 1024
LANES = 128


def seq_weights(order, groups):
    weights = []
    w = 1
    while w < groups:
        weights.append(w)
        w *= 2
    first = weights[0] + order * (weights[1] - weights[0])
    second = weights[1] - order * (weights[1] - weights[0])
    return [first, second] + weights[2:]


class Halving:
    def __init__(self, groups, me, core, order, parts, own, first=0, base=0):
        self.groups, self.me, self.core, self.parts, self.own, self.first = (
            groups,
            me,
            core,
            parts,
            own,
            first,
        )
        self.order, self.other = (core, 1 - core) if order is None else (order, order)
        self.weights = seq_weights(self.order, groups)
        self.bits = [lax.rem(me // w, 2) for w in self.weights]
        self.steps = len(self.weights)
        self.half = own.shape[3]
        self.base = base * 2 * self.half
        self.unit = own.shape[2]

    def shard_of(self, n, order):
        weights = seq_weights(order, self.groups)
        at = 0
        for j in range(self.steps):
            bit = lax.rem(self.me // weights[j], 2)
            keep = (n >> (self.steps - 1 - j)) & 1
            at = at + (bit if keep else 1 - bit) * weights[j]
        return at

    def core_setup(self, bufs, ss, rs, sib):
        self.bufs = bufs
        self.core_copies = []
        for n in range(self.groups):
            s = self.shard_of(n, self.other)
            row = []
            for p, (ref, high, cols, _) in enumerate(self.parts):
                src = ref.at[
                    pl.ds(pl.multiple_of(s * high * self.unit, 8), high * self.unit),
                    pl.ds(
                        pl.multiple_of(self.base + (1 - self.core) * cols * self.half, LANES),
                        cols * self.half,
                    ),
                ]
                row.append(
                    pltpu.make_async_remote_copy(
                        src_ref=src,
                        dst_ref=bufs[p].at[n],
                        send_sem=ss.at[n, p],
                        recv_sem=rs.at[n, p],
                        device_id={"row": sib},
                        device_id_type=MESH,
                    )
                )
            self.core_copies.append(row)

    def core_start(self):
        for row in self.core_copies:
            for c in row:
                c.start()

    def core_finish(self, n):
        for c in self.core_copies[n]:
            c.wait_recv()
        s = self.shard_of(n, self.order)
        for p, (ref, high, cols, first) in enumerate(self.parts):
            for h in range(high):
                for c in range(cols):
                    mine = ref[
                        pl.ds(pl.multiple_of((s * high + h) * self.unit, 8), self.unit),
                        pl.ds(
                            pl.multiple_of(
                                self.base + (self.core * cols + c) * self.half, LANES
                            ),
                            self.half,
                        ),
                    ]
                    self.own[n, first + h * cols + c] = (
                        mine
                        + self.bufs[p][
                            n,
                            h * self.unit : (h + 1) * self.unit,
                            c * self.half : (c + 1) * self.half,
                        ]
                    )

    def step_setup(self, bufs, ss, rs, steps):
        self.step_bufs = dict(zip(steps, bufs))
        self.copies = {}
        for at, k in enumerate(steps):
            for i in range(self.groups >> (k + 1)):
                self.copies[k, i] = pltpu.make_async_remote_copy(
                    src_ref=self.own.at[self.slot(k) + i],
                    dst_ref=bufs[at].at[i],
                    send_sem=ss[at].at[i],
                    recv_sem=rs[at].at[i],
                    device_id={"seq": self.me + self.weights[k] * (1 - 2 * self.bits[k])},
                    device_id_type=MESH,
                )

    def slot(self, k):
        return self.groups - (self.groups >> k) - self.first

    def start(self, k, i):
        self.copies[k, i].start()

    def finish(self, k, i):
        self.copies[k, i].wait_recv()
        at = self.slot(k + 1) + i
        self.own[at] = self.own[at] + self.step_bufs[k][i]

    def count(self, k):
        return self.groups >> (k + 1)

    def wait_sends(self):
        for c in self.copies.values():
            c.wait_send()

    def wait_core_sends(self):
        for row in self.core_copies:
            for c in row:
                c.wait_send()


EARLY = (4, 4, 1)
LATE = (1, 1, 1)
ORDERS = (0, 1, None)
EARLY_STEPS = (0,)


class Crew:
    def __init__(self, members):
        self.members = members
        self.groups, self.steps = members[0].groups, members[0].steps

    def core_setup(self, bufs, ss, rs, sib):
        for p, h in enumerate(self.members):
            h.core_setup([bufs[p]], ss[p], rs[p], sib)

    def step_setup(self, bufs, ss, rs, steps):
        for p, h in enumerate(self.members):
            h.step_setup(bufs[p], ss[p], rs[p], steps)

    def core_start(self):
        for n in range(self.groups):
            for h in self.members:
                for c in h.core_copies[n]:
                    c.start()

    def count(self, k):
        return self.groups >> (k + 1)

    def core_finish(self, n):
        for h in self.members:
            h.core_finish(n)
            if n < self.count(0):
                h.start(0, n)

    def start(self, k, i):
        for h in self.members:
            h.start(k, i)

    def finish(self, k, i, onward):
        for h in self.members:
            h.finish(k, i)
            if onward and k + 1 < self.steps and i < self.count(k + 1):
                h.start(k + 1, i)

    def advance(self, k):
        for i in range(self.count(k)):
            self.finish(k, i, True)

    def wait_sends(self):
        for h in self.members:
            h.wait_sends()

    def wait_core_sends(self):
        for h in self.members:
            h.wait_core_sends()


def early_crew(groups, me, core, gout, gup, gdown, owns):
    parts = [[(gup, 1, 4, 0)], [(gdown, 4, 1, 0)], [(gout, 1, 1, 0)]]
    return Crew([Halving(groups, me, core, o, p, w) for o, p, w in zip(ORDERS, parts, owns)])


def greet_all(rows, groups, me, row):
    barrier = pltpu.get_barrier_semaphore()
    for d in range(1, rows):
        pl.semaphore_signal(
            barrier, inc=1, device_id={"row": lax.rem(row + d, rows)}, device_id_type=MESH
        )
    for d in range(1, groups):
        pl.semaphore_signal(
            barrier, inc=1, device_id={"seq": lax.rem(me + d, groups)}, device_id_type=MESH
        )
    pl.semaphore_wait(barrier, rows + groups - 2)


def row_masks(lengths, row, start, tok):
    where = lax.broadcasted_iota(jnp.int32, (8, tok), 1) + start
    ends = []
    total = 0
    for k in range(lengths.shape[1]):
        total = total + lengths[row, k]
        ends.append(total)

    def doc(at):
        out = jnp.zeros(at.shape, jnp.int32)
        for e in ends:
            out = out + (at >= e).astype(jnp.int32)
        return out

    own = doc(where)
    masks = []
    for lag in (1, 2):
        same = (where >= lag) & (doc(where - lag) == own)
        masks.append(same.astype(jnp.float32)[:1])
    return masks + [(where < total).astype(jnp.float32)[:1]]


def edge_pick(r):
    line = lax.broadcasted_iota(jnp.int32, (8, LANES), 0)
    spot = lax.broadcasted_iota(jnp.int32, (8, LANES), 1)
    pick = (spot == line - 2 * r + LANES - 2) & (line >= 2 * r) & (line < 2 * r + 2)
    return pick.astype(jnp.bfloat16)


def pack_edges(tiles):
    out = None
    for r, tile in enumerate(tiles):
        piece = lax.dot_general(
            edge_pick(r), tile, (((1,), (1,)), ((), ())), preferred_element_type=jnp.float32
        )
        out = piece if out is None else out + piece
    return out


def unpack_edge(lines, r):
    return lax.dot_general(
        lines.astype(jnp.bfloat16),
        edge_pick(r),
        (((0,), (0,)), ((), ())),
        preferred_element_type=jnp.float32,
    )


def window_of(values, lane, edge):
    early, late = edge[:, LANES - 2 : LANES - 1], edge[:, LANES - 1 :]
    one = jnp.where(lane == 0, late, pltpu.roll(values, 1, 1))
    two = jnp.where(lane == 0, early, jnp.where(lane == 1, late, pltpu.roll(values, 2, 1)))
    return one, two


def spread_taps(taps, padded, wide):
    padded[...] = jnp.zeros_like(padded)
    padded[: taps.shape[0], :] = taps[...]
    turned = padded[...].T
    for j in range(taps.shape[0]):
        wide[j] = jnp.broadcast_to(turned[:, j : j + 1], wide.shape[1:])


def norm_parts(values):
    center = values - jnp.mean(values, axis=-1, keepdims=True)
    scale = lax.rsqrt(jnp.mean(center * center, axis=-1, keepdims=True) + 1e-05)
    return center * scale, scale


STRIP = 128


def finish_kernel(
    rows,
    groups,
    gw_ref,
    ggo_ref,
    u_ref,
    edge_ref,
    lengths,
    taps,
    weight,
    block,
    gm_ref,
    gain,
    offset,
    feed_gain,
    feed_bias,
    early,
    mid_s,
    first_s,
    last,
    gi_ref,
    fin_o,
    small_o,
    last_o,
    padded,
    wide_taps,
    edges,
    tap_sum,
    gu,
    gu_low,
    rim,
    rim_out,
    rim_in,
    normed,
    gin,
    small,
    own,
    own_early,
    core_buf,
    step_buf,
    early_buf,
    wide_buf,
    small_row,
    small_sum,
    small_part,
    small_done,
    last_row,
    last_sum,
    rim_sem,
    core_ss,
    core_rs,
    step_ss,
    step_rs,
    early_ss,
    early_rs,
    wide_ss,
    wide_rs,
    fin_ss,
    fin_rs,
    srow_ss,
    srow_rs,
    spart_ss,
    spart_rs,
    sdone_ss,
    sdone_rs,
    lrow_ss,
    lrow_rs,
    last_ss,
    last_rs,
):
    me = lax.axis_index("seq")
    row = lax.axis_index("row")
    core = lax.rem(row, 2)
    sib = row + 1 - 2 * core
    chunk = small_part.shape[1]
    held, width, tok = gw_ref.shape
    low, f32 = jnp.bfloat16, jnp.float32
    greet_all(rows, groups, me, row)

    late = Crew(
        [
            Halving(groups, me, core, o, [(gin, 1, 1, 0)], own[p], base=p)
            for p, o in enumerate(ORDERS)
        ]
    )
    late.core_setup(core_buf, core_ss, core_rs, sib)
    late.step_setup(step_buf, step_ss, step_rs, range(late.steps))
    later = range(EARLY_STEPS[-1] + 1, late.steps)
    rest = Crew(
        [
            Halving(groups, me, core, o, (), w, first=groups - e.shape[0])
            for o, w, e in zip(ORDERS, own_early, early)
        ]
    )
    rest.step_setup(early_buf, early_ss, early_rs, later)
    for w, e in zip(own_early, early):
        w[...] = e[...]
    for i in range(rest.count(later[0])):
        rest.start(later[0], i)
    lrow = [
        pltpu.make_async_remote_copy(
            src_ref=last,
            dst_ref=last_row.at[d - 1],
            send_sem=lrow_ss.at[d - 1],
            recv_sem=lrow_rs.at[d - 1],
            device_id={"row": lax.rem(row + d, rows)},
            device_id_type=MESH,
        )
        for d in range(1, rows)
    ]
    for c in lrow:
        c.start()

    spread_taps(taps, padded, wide_taps)
    tap_sum[...] = jnp.zeros_like(tap_sum)
    lane = lax.broadcasted_iota(jnp.int32, (STRIP, tok), 1)
    for r in range(held):
        same1, same2, live = row_masks(lengths, r, me * tok, tok)
        edges[...] = unpack_edge(edge_ref[...], r)

        def strip(i, carry, r=r, same1=same1, same2=same2, live=live):
            at = [pl.multiple_of(i * STRIP + g * width, STRIP) for g in range(3)]
            tap = [
                [
                    jnp.concatenate([wide_taps[j, pl.ds(a, STRIP), :]] * (tok // LANES), axis=1)
                    for j in range(3)
                ]
                for a in at
            ]
            u = [u_ref[r, pl.ds(a, STRIP), :].astype(f32) for a in at]
            shifts = [
                window_of(v, lane, edges[pl.ds(a, STRIP), :])
                for v, a in zip(u, at)
            ]
            gate_in, stream = [
                tap[g][0] * u[g] + tap[g][1] * shifts[g][0] * same1 + tap[g][2] * shifts[g][1] * same2
                for g in (1, 2)
            ]
            gw = gw_ref[r, pl.ds(at[0], STRIP), :].astype(f32) * live
            grads = [ggo_ref[r, pl.ds(at[0], STRIP), :] * live, gw * stream, gw * gate_in]
            for g in range(3):
                m1, m2 = grads[g] * same1, grads[g] * same2
                for j, p in enumerate((grads[g] * u[g], m1 * shifts[g][0], m2 * shifts[g][1])):
                    total = p[:, :LANES]
                    for h in range(1, tok // LANES):
                        total = total + p[:, h * LANES : (h + 1) * LANES]
                    tap_sum[j, pl.ds(at[g], STRIP), :] += total
                b1 = pltpu.roll(tap[g][1] * m1, tok - 1, 1)
                b2 = pltpu.roll(tap[g][2] * m2, tok - 2, 1)
                gu[r, pl.ds(at[g], STRIP), :] = (
                    tap[g][0] * grads[g]
                    + jnp.where(lane < tok - 1, b1, 0.0)
                    + jnp.where(lane < tok - 2, b2, 0.0)
                )
                over = jnp.where(lane < tok - 1, 0.0, b1) + jnp.where(lane < tok - 2, 0.0, b2)
                rim[r, pl.ds(at[g], STRIP), :] = over[:, tok - LANES :].astype(low)
            return carry

        lax.fori_loop(0, width // STRIP, strip, 0)

    rim_out[...] = pack_edges([rim[r] for r in range(held)])
    rim_copy = pltpu.make_async_remote_copy(
        src_ref=rim_out,
        dst_ref=rim_in,
        send_sem=rim_sem.at[0],
        recv_sem=rim_sem.at[1],
        device_id={"seq": lax.rem(me + groups - 1, groups)},
        device_id_type=MESH,
    )
    rim_copy.start()

    at = mid_s.shape[0] + first_s.shape[0]
    small[:at, :] = jnp.concatenate([mid_s[...], first_s[...]], axis=0)
    small[at:, :] = jnp.zeros((small.shape[0] - at, LANES), f32)
    per = width // LANES

    def put_small(first, line):
        for i in range(line.shape[1] // LANES):
            small[first + i : first + i + 1, :] = line[:, i * LANES : (i + 1) * LANES]

    ones = jnp.ones((8, LANES), low)

    def lane_sums(values):
        high = values.astype(low)
        rest = (values - high.astype(f32)).astype(low)
        dims = (((1,), (1,)), ((), ()))
        return lax.dot_general(ones, high, dims, preferred_element_type=f32) + lax.dot_general(
            ones, rest, dims, preferred_element_type=f32
        )

    for j in range(3):
        put_small(at + 2 * per + 3 * per * j, lane_sums(tap_sum[j])[:1])
    put_small(at + 11 * per, feed_gain[...][None, :])
    put_small(at + 12 * per, feed_bias[...][None, :])
    gain_row, offset_row = gain[...][None, :], offset[...][None, :]
    for r in range(held):
        hat, _ = norm_parts(block[r].astype(f32))
        normed[:, r * tok : (r + 1) * tok] = (hat * gain_row + offset_row).T.astype(low)
    rest.advance(later[0])

    rim_copy.wait()
    for r in range(held):
        add = unpack_edge(rim_in[...], r)
        split = tok - LANES
        gu_low[:, r * tok : r * tok + split] = gu[r, :, :split].astype(low)
        gu_low[:, r * tok + split : (r + 1) * tok] = (gu[r, :, split:] + add).astype(low)

    piece = 256

    def weight_grad(i, carry):
        cols = pl.ds(pl.multiple_of(i * piece, piece), piece)
        gin[:, cols] = lax.dot_general(
            normed[...], gu_low[cols, :], (((1,), (1,)), ((), ())), preferred_element_type=f32
        ).astype(low)
        return carry

    lax.fori_loop(0, 3 * width // piece, weight_grad, 0)
    late.core_start()
    rest.advance(later[1])

    gains = [jnp.zeros((1, width), f32), jnp.zeros((1, width), f32)]
    for r in range(held):
        turned = lax.dot_general(
            weight[...],
            gu_low[:, r * tok : (r + 1) * tok],
            (((1,), (0,)), ((), ())),
            preferred_element_type=f32,
        )
        grad = turned.T
        hat, scale = norm_parts(block[r].astype(f32))
        gains[0] = gains[0] + jnp.sum(grad * hat, axis=0, keepdims=True)
        gains[1] = gains[1] + jnp.sum(grad, axis=0, keepdims=True)
        pulled = grad * gain_row
        pulled = pulled - jnp.mean(pulled, axis=-1, keepdims=True)
        pulled = pulled - hat * jnp.mean(pulled * hat, axis=-1, keepdims=True)
        gi_ref[r] = gm_ref[r] + scale * pulled
        if r == 0:
            for n in range(groups):
                late.core_finish(n)
    put_small(at, gains[0])
    put_small(at + per, gains[1])

    srow = [
        pltpu.make_async_remote_copy(
            src_ref=small,
            dst_ref=small_row.at[d - 1],
            send_sem=srow_ss.at[d - 1],
            recv_sem=srow_rs.at[d - 1],
            device_id={"row": lax.rem(row + d, rows)},
            device_id_type=MESH,
        )
        for d in range(1, rows)
    ]
    for c in srow:
        c.start()
    for c in srow + lrow:
        c.wait()
    total = small[...]
    tail = last[...]
    for d in range(rows - 1):
        total = total + small_row[d]
        tail = tail + last_row[d]
    small_sum[...] = total
    last_sum[...] = tail
    last_o[me] = tail
    spart = []
    lcp = []
    for d in range(1, groups):
        to = lax.rem(me + d, groups)
        spart.append(
            pltpu.make_async_remote_copy(
                src_ref=small_sum.at[pl.ds(to * chunk, chunk)],
                dst_ref=small_part.at[d - 1],
                send_sem=spart_ss.at[d - 1],
                recv_sem=spart_rs.at[d - 1],
                device_id={"seq": to},
                device_id_type=MESH,
            )
        )
        lcp.append(
            pltpu.make_async_remote_copy(
                src_ref=last_sum,
                dst_ref=last_o.at[me],
                send_sem=last_ss.at[d - 1],
                recv_sem=last_rs.at[d - 1],
                device_id={"seq": to},
                device_id_type=MESH,
            )
        )
    for c in spart + lcp:
        c.start()
    late.advance(0)
    for k in later[2:]:
        rest.advance(k)
    for c in spart:
        c.wait()
    total = small_sum[pl.ds(me * chunk, chunk)]
    for d in range(groups - 1):
        total = total + small_part[d]
    small_done[...] = total
    small_o[pl.ds(me * chunk, chunk)] = total
    sdone = [
        pltpu.make_async_remote_copy(
            src_ref=small_done,
            dst_ref=small_o.at[pl.ds(me * chunk, chunk)],
            send_sem=sdone_ss.at[d - 1],
            recv_sem=sdone_rs.at[d - 1],
            device_id={"seq": lax.rem(me + d, groups)},
            device_id_type=MESH,
        )
        for d in range(1, groups)
    ]
    for c in sdone:
        c.start()
    for k in range(1, late.steps):
        late.advance(k)

    halves = []
    place = 0
    for h, e, units in zip(rest.members, early, EARLY):
        halves.append((h, e.shape[0] - 1, place, units))
        place += units
    for h, units in zip(late.members, LATE):
        halves.append((h, groups - 1, place, units))
        place += units
    w = 2
    n = 0
    while w < rows:
        bit = lax.rem(row // w, 2)
        for p, (h, slot, _, _) in enumerate(halves):
            c = pltpu.make_async_remote_copy(
                src_ref=h.own.at[slot],
                dst_ref=wide_buf[p].at[n],
                send_sem=wide_ss.at[n, p],
                recv_sem=wide_rs.at[n, p],
                device_id={"row": row + w * (1 - 2 * bit)},
                device_id_type=MESH,
            )
            c.start()
            c.wait()
            h.own[slot] = h.own[slot] + wide_buf[p][n]
        w *= 2
        n += 1

    fin = []
    for p, (h, slot, first, units) in enumerate(halves):
        fin_o[core, first : first + units] = h.own[slot]
        c = pltpu.make_async_remote_copy(
            src_ref=h.own.at[slot],
            dst_ref=fin_o.at[core, pl.ds(first, units)],
            send_sem=fin_ss.at[p],
            recv_sem=fin_rs.at[p],
            device_id={"row": sib},
            device_id_type=MESH,
        )
        c.start()
        fin.append(c)
    late.wait_core_sends()
    late.wait_sends()
    rest.wait_sends()
    for c in sdone + lcp:
        c.wait()
    for c in fin:
        c.wait()


def finish(gw, ggo, u, edge, lengths, taps, weight, block, gm, vectors, early, sums):
    rows, groups = lax.axis_size("row"), lax.axis_size("seq")
    held, width, tok = gw.shape
    unit = width // groups
    half = width // 2
    wide = max(1, rows.bit_length() - 2)
    low, f32 = jnp.bfloat16, jnp.float32
    steps = groups.bit_length() - 1
    later = range(EARLY_STEPS[-1] + 1, steps)
    used = sums[0].shape[0] + sums[1].shape[0] + 13 * (width // LANES)
    lines = used + -used % (8 * groups)
    chunk = lines // groups
    last = sums[2]
    dma = pltpu.SemaphoreType.DMA
    vm = pl.BlockSpec(memory_space=pltpu.VMEM)
    sm = pl.BlockSpec(memory_space=pltpu.SMEM)
    return pl.pallas_call(
        functools.partial(finish_kernel, rows, groups),
        out_shape=(
            jax.ShapeDtypeStruct(gm.shape, f32),
            jax.ShapeDtypeStruct((2, sum(EARLY) + sum(LATE), unit, half), low),
            jax.ShapeDtypeStruct((lines, LANES), f32),
            jax.ShapeDtypeStruct((groups,) + last.shape, f32),
        ),
        in_specs=[vm] * 4 + [sm] + [vm] * 8 + [[vm] * 3] + [vm] * 3,
        out_specs=(vm,) * 4,
        scratch_shapes=[
            pltpu.VMEM((8, 3 * width), f32),
            pltpu.VMEM((3, 3 * width, LANES), f32),
            pltpu.VMEM((3 * width, LANES), f32),
            pltpu.VMEM((3, 3 * width, LANES), f32),
            pltpu.VMEM((held, 3 * width, tok), f32),
            pltpu.VMEM((3 * width, held * tok), low),
            pltpu.VMEM((held, 3 * width, LANES), low),
            pltpu.VMEM((8, 3 * width), f32),
            pltpu.VMEM((8, 3 * width), f32),
            pltpu.VMEM((width, held * tok), low),
            pltpu.VMEM((width, 3 * width), low),
            pltpu.VMEM((lines, LANES), f32),
            [pltpu.VMEM((groups, n, unit, half), low) for n in LATE],
            [pltpu.VMEM(e.shape, low) for e in early],
            [pltpu.VMEM((groups, unit, n * half), low) for n in LATE],
            [
                [pltpu.VMEM((groups >> (k + 1), n, unit, half), low) for k in range(steps)]
                for n in LATE
            ],
            [[pltpu.VMEM((groups >> (k + 1), n, unit, half), low) for k in later] for n in EARLY],
            [pltpu.VMEM((wide, n, unit, half), low) for n in EARLY + LATE],
            pltpu.VMEM((rows - 1, lines, LANES), f32),
            pltpu.VMEM((lines, LANES), f32),
            pltpu.VMEM((groups - 1, chunk, LANES), f32),
            pltpu.VMEM((chunk, LANES), f32),
            pltpu.VMEM((rows - 1,) + last.shape, f32),
            pltpu.VMEM(last.shape, f32),
            dma((2,)),
            [dma((groups, 1)) for _ in LATE],
            [dma((groups, 1)) for _ in LATE],
            [[dma((groups >> (k + 1),)) for k in range(steps)] for _ in LATE],
            [[dma((groups >> (k + 1),)) for k in range(steps)] for _ in LATE],
            [[dma((groups >> (k + 1),)) for k in later] for _ in EARLY],
            [[dma((groups >> (k + 1),)) for k in later] for _ in EARLY],
            dma((wide, 6)),
            dma((wide, 6)),
            dma((6,)),
            dma((6,)),
            dma((rows - 1,)),
            dma((rows - 1,)),
            dma((groups - 1,)),
            dma((groups - 1,)),
            dma((groups - 1,)),
            dma((groups - 1,)),
            dma((rows - 1,)),
            dma((rows - 1,)),
            dma((groups - 1,)),
            dma((groups - 1,)),
        ],
        compiler_params=pltpu.CompilerParams(
            collective_id=0, has_side_effects=True, vmem_limit_bytes=VMEM_LIMIT
        ),
        name="finish",
    )(gw, ggo, u, edge, lengths, taps, weight, block, gm, *vectors, early, *sums)


def unpack_kernel(
    feat,
    fin,
    small,
    last,
    gain_o,
    bias_o,
    in_o,
    taps_o,
    first_o,
    first_b_o,
    mid_o,
    mid_b_o,
    freq_o,
    last_o,
    skip_o,
    out_o,
    feed_gain_o,
    feed_bias_o,
    up_o,
    down_o,
):
    f32 = jnp.float32
    unit, half = fin.shape[2], fin.shape[3]
    hidden = mid_o.shape[0]
    width = gain_o.shape[0]
    per = width // LANES
    outs = [(up_o, 1, 4, 0, 0), (down_o, 4, 1, 4, 0), (out_o, 1, 1, 8, 0)]
    outs = outs + [(in_o, 1, 1, 9 + p, 2 * p) for p in range(3)]
    for core in range(2):
        for out, high, cols, first, base in outs:
            for h in range(high):
                for c in range(cols):
                    at = (base + core * cols + c) * half
                    out[h * unit : (h + 1) * unit, at : at + half] = fin[
                        core, first + h * cols + c
                    ].astype(f32)

    def line(first, count):
        pieces = [small[first + i : first + i + 1, :] for i in range(count)]
        return jnp.concatenate(pieces, axis=1)

    at = hidden + -(-(feat + 1) // 8) * 8
    gain_o[...] = line(at, per)[0]
    bias_o[...] = line(at + per, per)[0]
    for j in range(3):
        taps_o[j : j + 1, :] = line(at + 2 * per + 3 * per * j, 3 * per)
    feed_gain_o[...] = line(at + 11 * per, per)[0]
    feed_bias_o[...] = line(at + 12 * per, per)[0]
    first_o[...] = small[hidden : hidden + feat, :hidden]
    first_b_o[...] = small[hidden + feat : hidden + feat + 1, :hidden][0]
    mid_o[...] = small[:hidden, :hidden]
    shape = (hidden, hidden)
    same = lax.broadcasted_iota(jnp.int32, shape, 0) == lax.broadcasted_iota(jnp.int32, shape, 1)
    for out, col in ((mid_b_o, hidden), (freq_o, hidden + 1)):
        out[...] = jnp.sum(
            jnp.where(same, small[:hidden, col : col + 1], 0.0), axis=0, keepdims=True
        )[0]
    turned = last[...].T
    last_o[...] = turned[:hidden]
    skip_o[...] = turned[hidden : hidden + 1][0]


def unpack(fin, small, last, feat, hidden, width):
    f32 = jnp.float32
    unit = fin.shape[2]
    vm = pl.BlockSpec(memory_space=pltpu.VMEM)
    shapes = [
        (width,),
        (width,),
        (unit, 3 * width),
        (3, 3 * width),
        (feat, hidden),
        (hidden,),
        (hidden, hidden),
        (hidden,),
        (hidden,),
        (hidden, width),
        (width,),
        (unit, width),
        (width,),
        (width,),
        (unit, 4 * width),
        (4 * unit, width),
    ]
    return pl.pallas_call(
        functools.partial(unpack_kernel, feat),
        out_shape=tuple(jax.ShapeDtypeStruct(x, f32) for x in shapes),
        in_specs=[vm] * 3,
        out_specs=(vm,) * len(shapes),
        compiler_params=pltpu.CompilerParams(vmem_limit_bytes=VMEM_LIMIT),
        name="unpack",
    )(fin, small, last.reshape(width, LANES))


def spectrum_tables(length):
    period = 2 * length
    first = period // LANES
    k1 = np.arange(first // 2 + 1, dtype=np.int64)[:, None, None]
    n2 = np.arange(LANES, dtype=np.int64)[None, :, None]
    k2 = np.arange(LANES, dtype=np.int64)[None, None, :]
    angle = 2.0 * np.pi / period * (n2 * (k1 + first * k2) % period)
    full = np.concatenate([np.cos(angle), np.sin(angle)], axis=2).astype(np.float32)
    high = full.astype(jnp.bfloat16)
    rest = (full - high.astype(np.float32)).astype(jnp.bfloat16)
    return high, rest


def feature_rows(length, feat_count):
    bands = (feat_count - 1) // 2
    at = np.arange(length, dtype=np.int64)[None, :]
    angle = 2.0 * np.pi / length * (at * np.arange(1, bands + 1)[:, None] % length)
    rows = [at / length, np.cos(angle), -np.sin(angle), np.ones((1, length))]
    rows = np.concatenate(rows, axis=0)
    pad = -rows.shape[0] % 8
    return np.pad(rows, ((0, pad), (0, 0))).astype(np.float32)


def sin_cos(x):
    n = jnp.round(x * (2.0 / math.pi))
    r = x - n * 1.5703125
    r = r - n * 4.837512969970703125e-4
    r = r - n * 7.549789948768648e-8
    z = r * r
    s = r + r * z * (-1.6666654611e-1 + z * (8.3321608736e-3 - z * 1.9515295891e-4))
    c = (
        1.0
        - 0.5 * z
        + z * z * (4.166664568298827e-2 + z * (-1.388731625493765e-3 + z * 2.443315711809948e-5))
    )
    q = n.astype(jnp.int32) & 3
    odd = (q & 1) == 1
    sine = jnp.where(odd, c, s)
    cosine = jnp.where(odd, s, c)
    sine = jnp.where(q >= 2, -sine, sine)
    cosine = jnp.where((q == 1) | (q == 2), -cosine, cosine)
    return sine, cosine


def exact_dot(p, q, left, right):
    low = jnp.bfloat16

    def dot(x, y):
        return lax.dot_general(
            x, y, (((left,), (right,)), ((), ())), preferred_element_type=jnp.float32
        )

    ph, qh = p.astype(low), q.astype(low)
    pl_, ql = (p - ph.astype(jnp.float32)).astype(low), (q - qh.astype(jnp.float32)).astype(low)
    return dot(ph, qh) + (dot(pl_, qh) + dot(ph, ql))


def column_of(row):
    size = row.shape[1]
    shape = (size, size)
    same = lax.broadcasted_iota(jnp.int32, shape, 0) == lax.broadcasted_iota(jnp.int32, shape, 1)
    return jnp.sum(jnp.where(same, row, 0.0), axis=1, keepdims=True)


class FilterNet:
    def __init__(self, me, narrow, params, aug):
        first, first_b, mid, mid_b, freq, last, skip, decay, self.feats = params
        feat = first.shape[0]
        aug[...] = jnp.zeros_like(aug)
        aug[:feat, :] = first[...]
        aug[feat : feat + 1, :] = first_b[...][None, :]
        self.aug = aug
        self.mid = mid
        self.mid_b = column_of(mid_b[...][None, :])
        self.freq = column_of(freq[...][None, :])
        width = skip.shape[0]
        shape = (narrow, width)
        pick = (
            lax.broadcasted_iota(jnp.int32, shape, 1)
            == lax.broadcasted_iota(jnp.int32, shape, 0) + me * narrow
        )
        self.skip = jnp.sum(jnp.where(pick, skip[...][None, :], 0.0), axis=1, keepdims=True)
        self.decay = jnp.sum(jnp.where(pick, decay[...][None, :], 0.0), axis=1, keepdims=True)
        self.last = exact_dot(pick.astype(jnp.float32), last[...], 1, 1)
        self.narrow = narrow

    def layers(self, at, size):
        feats = self.feats[:, pl.ds(at, size)]
        pre1 = exact_dot(self.aug[...], feats, 0, 0)
        a1, c1 = sin_cos(self.freq * pre1)
        pre2 = exact_dot(self.mid[...], a1, 0, 0) + self.mid_b
        a2, c2 = sin_cos(self.freq * pre2)
        return feats, pre1, a1, c1, pre2, a2, c2

    def fade(self, at, size):
        where = lax.broadcasted_iota(jnp.int32, (self.narrow, size), 1) + at
        return jnp.exp(-self.decay * where.astype(jnp.float32)), where

    def build(self, at, size):
        a2 = self.layers(at, size)[5]
        fade, where = self.fade(at, size)
        return exact_dot(self.last, a2, 1, 0) * fade + jnp.where(where == 0, self.skip, 0.0)

    def pull(self, at, size, grad, first_o, mid_o, last_o):
        feats, pre1, a1, c1, pre2, a2, c2 = self.layers(at, size)
        fade, where = self.fade(at, size)
        hidden = a1.shape[0]
        raw = grad * fade
        last_o[:, :hidden] += exact_dot(raw, a2, 1, 1)
        last_o[:, hidden : hidden + 1] += jnp.sum(
            jnp.where(where == 0, grad, 0.0), axis=1, keepdims=True
        )
        turned2 = exact_dot(self.last, raw, 0, 0) * c2
        freq = jnp.sum(turned2 * pre2, axis=1, keepdims=True)
        down2 = turned2 * self.freq
        mid_o[:, :hidden] += exact_dot(a1, down2, 1, 1)
        mid_o[:, hidden : hidden + 1] += jnp.sum(down2, axis=1, keepdims=True)
        turned1 = exact_dot(self.mid[...], down2, 1, 0) * c1
        freq = freq + jnp.sum(turned1 * pre1, axis=1, keepdims=True)
        mid_o[:, hidden + 1 : hidden + 2] += freq
        down1 = turned1 * self.freq
        first_o[:, :hidden] += exact_dot(feats, down1, 1, 1)


CHUNK = 4


def half_dft(x):
    count = 2 * len(x)
    if count == 2:
        return [(x[0], None), (x[0], None)]
    even, odd = half_dft(x[0::2]), half_dft(x[1::2])
    out = [None] * (count // 2 + 1)
    for k in range(count // 4 + 1):
        er, ei = even[k]
        orr, oi = odd[k]
        if k == 0:
            out[0] = (er + orr, None)
            out[count // 2] = (er - orr, None)
        elif 4 * k == count:
            out[k] = (er, -orr)
        else:
            c, s = math.cos(2 * math.pi * k / count), math.sin(2 * math.pi * k / count)
            tr = orr * c + oi * s
            ti = oi * c - orr * s
            out[k] = (er + tr, ei + ti)
            out[count // 2 - k] = (er - tr, ti - ei)
    return out


def half_inverse(spec):
    count = 2 * (len(spec) - 1)
    if count == 2:
        return [spec[0][0] + spec[1][0]]
    even, odd = [], []
    for k in range(count // 4 + 1):
        ar, ai = spec[k]
        br, bi = spec[count // 2 - k]
        if k == 0:
            even.append((ar + br, None))
            odd.append((ar - br, None))
        elif 4 * k == count:
            even.append((ar + ar, None))
            odd.append((-(ai + ai), None))
        else:
            c, s = math.cos(2 * math.pi * k / count), math.sin(2 * math.pi * k / count)
            dr, di = ar - br, ai + bi
            even.append((ar + br, ai - bi))
            odd.append((dr * c - di * s, dr * s + di * c))
    out = [None] * (count // 2)
    out[0::2] = half_inverse(even)
    out[1::2] = half_inverse(odd)
    return out


def turn_of(table):
    cos, sin = table[:, :LANES], table[:, LANES:]
    return jnp.concatenate(
        [jnp.concatenate([cos, -sin], axis=1), jnp.concatenate([sin, cos], axis=1)], axis=0
    )


def split_dot(a, high, rest, back):
    a_high = a.astype(jnp.bfloat16)
    a_rest = (a - a_high.astype(jnp.float32)).astype(jnp.bfloat16)
    dims = (((1,), (1 if back else 0,)), ((), ()))
    high, rest = turn_of(high), turn_of(rest)

    def dot(p, q):
        return lax.dot_general(p, q, dims, preferred_element_type=jnp.float32)

    rows = a.shape[0]
    both = dot(jnp.concatenate([a_high, a_rest], axis=0), high)
    return both[:rows] + (both[rows:] + dot(a_high, rest))


def tile_loop(tiles, body):
    def step(i, carry):
        body(pl.multiple_of(i * 8, 8))
        return carry

    lax.fori_loop(0, tiles, step, 0, unroll=3 if tiles % 3 == 0 else 1)


def first_stage(load, spec, tiles):
    zero = jnp.zeros((8, LANES), jnp.float32)

    def body(at):
        for k, (re, im) in enumerate(half_dft(load(at))):
            spec[k, pl.ds(at, 8), :LANES] = re
            spec[k, pl.ds(at, 8), LANES:] = zero if im is None else im

    tile_loop(tiles, body)


def last_stage(spec, store, tiles, scale):
    def body(at):
        freqs = spec.shape[0]
        values = []
        for k in range(freqs):
            re = spec[k, pl.ds(at, 8), :LANES]
            im = None if k in (0, freqs - 1) else spec[k, pl.ds(at, 8), LANES:]
            values.append((re, im))
        for n, v in enumerate(half_inverse(values)):
            store(n, at, v * scale)

    tile_loop(tiles, body)


def greet(groups, me):
    barrier = pltpu.get_barrier_semaphore()
    for d in range(1, groups):
        pl.semaphore_signal(
            barrier, inc=1, device_id={"seq": lax.rem(me + d, groups)}, device_id_type=MESH
        )


def met(groups):
    pl.semaphore_wait(pltpu.get_barrier_semaphore(), groups - 1)


def to_channels(groups, me, narrow, src, recv, ss, rs, ls):
    local = pltpu.make_async_copy(
        src.at[:, pl.ds(pl.multiple_of(me * narrow, 8), narrow), :], recv.at[me], ls
    )
    out = [local]
    for d in range(1, groups):
        to = lax.rem(me + d, groups)
        out.append(
            pltpu.make_async_remote_copy(
                src_ref=src.at[:, pl.ds(pl.multiple_of(to * narrow, 8), narrow), :],
                dst_ref=recv.at[me],
                send_sem=ss.at[d - 1],
                recv_sem=rs.at[d - 1],
                device_id={"seq": to},
                device_id_type=MESH,
            )
        )
    return out


def to_positions(groups, me, narrow, send, dst, ss, rs, ls):
    mine = dst.at[:, pl.ds(pl.multiple_of(me * narrow, 8), narrow), :]
    out = [pltpu.make_async_copy(send.at[me], mine, ls)]
    for d in range(1, groups):
        to = lax.rem(me + d, groups)
        out.append(
            pltpu.make_async_remote_copy(
                src_ref=send.at[to],
                dst_ref=mine,
                send_sem=ss.at[d - 1],
                recv_sem=rs.at[d - 1],
                device_id={"seq": to},
                device_id_type=MESH,
            )
        )
    return out


def spread(recv, wide, narrow):
    per = recv.shape[3] // LANES

    def step(s, carry):
        for r in range(recv.shape[1]):
            for h in range(per):
                wide[s * per + h, r * narrow : (r + 1) * narrow, :] = recv[
                    s, r, :, h * LANES : (h + 1) * LANES
                ].astype(jnp.float32)
        return carry

    lax.fori_loop(0, recv.shape[0], step, 0, unroll=4)


def gather_back(wide, send, narrow):
    per = send.shape[3] // LANES

    def step(s, carry):
        for r in range(send.shape[1]):
            for h in range(per):
                send[s, r, :, h * LANES : (h + 1) * LANES] = wide[
                    s * per + h, r * narrow : (r + 1) * narrow, :
                ].astype(jnp.bfloat16)
        return carry

    lax.fori_loop(0, send.shape[0], step, 0, unroll=4)


def freq_loop(freqs, unroll, body):
    def step(i, carry):
        for j in range(unroll):
            body(i * unroll + j)
        return carry

    lax.fori_loop(0, freqs // unroll, step, 0)


UNROLL = {33: 11, 65: 13}


def conv_kernel(
    groups,
    block,
    lengths,
    gain,
    offset,
    weight,
    taps,
    first,
    first_b,
    mid,
    mid_b,
    freq,
    last,
    skip,
    decay,
    feats,
    high_ref,
    rest_ref,
    z_ref,
    w_spec,
    h_spec,
    u_ref,
    gate_ref,
    edge_o,
    high,
    rest,
    recv,
    wide,
    back,
    send,
    in_ss,
    in_rs,
    out_ss,
    out_rs,
    local,
    aug,
    filt,
    normed,
    w_ref,
    padded,
    wide_taps,
    edges,
    rim_out,
    rim_in,
    rim_sem,
):
    me = lax.axis_index("seq")
    narrow = h_spec.shape[1]
    count, freqs = wide.shape[0], high.shape[0]
    rows, width, tok = w_ref.shape
    low, f32 = jnp.bfloat16, jnp.float32
    unroll = UNROLL.get(freqs, 1)
    tables = [
        pltpu.make_async_copy(high_ref, high, local.at[0]),
        pltpu.make_async_copy(rest_ref, rest, local.at[1]),
    ]
    for c in tables:
        c.start()
    greet(groups, me)

    gain_row, offset_row = gain[...][None, :], offset[...][None, :]
    for r in range(rows):
        hat, _ = norm_parts(block[r].astype(f32))
        normed[:, r * tok : (r + 1) * tok] = (hat * gain_row + offset_row).T.astype(low)
    piece = 256

    def project(i, carry):
        cols = pl.ds(pl.multiple_of(i * piece, piece), piece)
        part = lax.dot_general(
            weight[:, cols], normed[...], (((0,), (0,)), ((), ())), preferred_element_type=f32
        ).astype(low)
        for r in range(rows):
            u_ref[r, cols, :] = part[:, r * tok : (r + 1) * tok]
        return carry

    lax.fori_loop(0, 3 * width // piece, project, 0)
    rim_out[...] = pack_edges([u_ref[r, :, tok - LANES :] for r in range(rows)])
    met(groups)
    rim_copy = pltpu.make_async_remote_copy(
        src_ref=rim_out,
        dst_ref=rim_in,
        send_sem=rim_sem.at[0],
        recv_sem=rim_sem.at[1],
        device_id={"seq": lax.rem(me + 1, groups)},
        device_id_type=MESH,
    )
    rim_copy.start()
    spread_taps(taps, padded, wide_taps)
    lane = lax.broadcasted_iota(jnp.int32, (STRIP, tok), 1)
    masks = [row_masks(lengths, r, me * tok, tok) for r in range(rows)]
    rim_copy.wait()
    edge_o[...] = rim_in[...]
    for r in range(rows):
        same1, same2, live = masks[r]
        edges[...] = unpack_edge(rim_in[...], r)

        def strip(i, carry, r=r, same1=same1, same2=same2, live=live):
            mixes = []
            for g in range(3):
                at = pl.ds(pl.multiple_of(i * STRIP + g * width, STRIP), STRIP)
                tap = [
                    jnp.concatenate([wide_taps[j, at, :]] * (tok // LANES), axis=1)
                    for j in range(3)
                ]
                u = u_ref[r, at, :].astype(f32)
                one, two = window_of(u, lane, edges[at, :])
                mixes.append(tap[0] * u + tap[1] * one * same1 + tap[2] * two * same2)
            at = pl.ds(pl.multiple_of(i * STRIP, STRIP), STRIP)
            gate_ref[r, at, :] = mixes[0] * live
            w_ref[r, at, :] = (mixes[1] * mixes[2] * live).astype(low)
            return carry

        lax.fori_loop(0, width // STRIP, strip, 0)
    inward = to_channels(groups, me, narrow, w_ref, recv, in_ss, in_rs, local.at[2])
    for c in inward:
        c.start()

    net = FilterNet(me, narrow, (first, first_b, mid, mid_b, freq, last, skip, decay, feats), aug)

    def build(i, carry):
        size = CHUNK * LANES
        values = net.build(pl.multiple_of(i * size, LANES), size)
        for j in range(CHUNK):
            filt[i * CHUNK + j] = values[:, j * LANES : (j + 1) * LANES]
        return carry

    lax.fori_loop(0, count // CHUNK, build, 0)
    first_stage(
        lambda at: [filt[n, pl.ds(at, 8), :] for n in range(count)], h_spec, narrow // 8
    )
    for c in tables:
        c.wait()

    def filter_freq_step(k):
        h_spec[k] = split_dot(h_spec[k], high[k], rest[k], False)

    freq_loop(freqs, unroll, filter_freq_step)
    for c in inward:
        c.wait()
    spread(recv, wide, narrow)
    first_stage(
        lambda at: [wide[n, pl.ds(at, 8), :] for n in range(count)], w_spec, rows * narrow // 8
    )

    def forward_step(k):
        w_spec[k] = split_dot(w_spec[k], high[k], rest[k], False)

    def inverse_step(k):
        h = h_spec[k]
        hr, hi = h[:, :LANES], h[:, LANES:]
        parts = []
        for r in range(rows):
            w = w_spec[k, r * narrow : (r + 1) * narrow]
            wr, wi = w[:, :LANES], w[:, LANES:]
            parts.append(jnp.concatenate([wr * hr - wi * hi, wr * hi + wi * hr], axis=1))
        back[k] = split_dot(jnp.concatenate(parts, axis=0), high[k], rest[k], True)

    freq_loop(freqs, unroll, forward_step)
    freq_loop(freqs, unroll, inverse_step)

    def store(n, at, v):
        wide[n, pl.ds(at, 8), :] = v

    last_stage(back, store, rows * narrow // 8, 1.0 / (2 * count * LANES))
    gather_back(wide, send, narrow)
    outward = to_positions(groups, me, narrow, send, z_ref, out_ss, out_rs, local.at[3])
    for c in outward:
        c.start()
    for c in outward:
        c.wait()


def conv_back_kernel(
    rows_all,
    groups,
    g_ref,
    w_spec,
    h_spec,
    high_ref,
    rest_ref,
    gout,
    gup,
    gdown,
    first,
    first_b,
    mid,
    mid_b,
    freq,
    last,
    skip,
    decay,
    feats,
    gw_ref,
    early_o,
    first_o,
    mid_o,
    last_o,
    high,
    rest,
    recv,
    wide,
    back,
    send,
    in_ss,
    in_rs,
    out_ss,
    out_rs,
    local,
    own,
    core_buf,
    step_buf,
    core_ss,
    core_rs,
    step_ss,
    step_rs,
    aug,
):
    me = lax.axis_index("seq")
    row = lax.axis_index("row")
    core = lax.rem(row, 2)
    narrow = h_spec.shape[1]
    count, freqs = wide.shape[0], high.shape[0]
    rows = g_ref.shape[0]
    unroll = UNROLL.get(freqs, 1)
    tables = [
        pltpu.make_async_copy(high_ref, high, local.at[0]),
        pltpu.make_async_copy(rest_ref, rest, local.at[1]),
    ]
    for c in tables:
        c.start()
    greet_all(rows_all, groups, me, row)
    inward = to_channels(groups, me, narrow, g_ref, recv, in_ss, in_rs, local.at[2])
    for c in inward:
        c.start()
    early = early_crew(groups, me, core, gout, gup, gdown, own)
    early.core_setup(core_buf, core_ss, core_rs, row + 1 - 2 * core)
    early.step_setup(step_buf, step_ss, step_rs, EARLY_STEPS)
    early.core_start()
    for n in range(groups):
        early.core_finish(n)
    for c in tables:
        c.wait()
    for c in inward:
        c.wait()
    spread(recv, wide, narrow)
    first_stage(
        lambda at: [wide[n, pl.ds(at, 8), :] for n in range(count)], back, rows * narrow // 8
    )

    def forward_step(k):
        back[k, : rows * narrow] = split_dot(back[k, : rows * narrow], high[k], rest[k], False)

    def inverse_step(k):
        h = h_spec[k]
        hr, hi = h[:, :LANES], h[:, LANES:]
        parts = []
        hsum = None
        for r in range(rows):
            w = w_spec[k, r * narrow : (r + 1) * narrow]
            wr, wi = w[:, :LANES], w[:, LANES:]
            g = back[k, r * narrow : (r + 1) * narrow]
            gr, gi = g[:, :LANES], g[:, LANES:]
            parts.append(jnp.concatenate([hr * gr + hi * gi, hr * gi - hi * gr], axis=1))
            pair = (wr * gr + wi * gi, wr * gi - wi * gr)
            hsum = pair if hsum is None else (hsum[0] + pair[0], hsum[1] + pair[1])
        parts.append(jnp.concatenate(hsum, axis=1))
        back[k] = split_dot(jnp.concatenate(parts, axis=0), high[k], rest[k], True)

    freq_loop(freqs, unroll, forward_step)
    freq_loop(freqs, unroll, inverse_step)

    def store(n, at, v):
        wide[n, pl.ds(at, 8), :] = v

    last_stage(back, store, (rows + 1) * narrow // 8, 1.0 / (2 * count * LANES))
    gather_back(wide, send, narrow)
    outward = to_positions(groups, me, narrow, send, gw_ref, out_ss, out_rs, local.at[3])
    for c in outward:
        c.start()
    net = FilterNet(me, narrow, (first, first_b, mid, mid_b, freq, last, skip, decay, feats), aug)
    for out in (first_o, mid_o, last_o):
        out[...] = jnp.zeros_like(out)

    def pull(i, carry):
        size = CHUNK * LANES
        grad = [wide[i * CHUNK + j, rows * narrow :, :] for j in range(CHUNK)]
        net.pull(
            pl.multiple_of(i * size, LANES),
            size,
            jnp.concatenate(grad, axis=1),
            first_o,
            mid_o,
            last_o,
        )
        return carry

    lax.fori_loop(0, count // CHUNK, pull, 0)
    for i in range(early.count(0)):
        early.finish(0, i, False)
        for p, h in enumerate(early.members):
            early_o[p][i] = own[p][h.slot(1) + i]
    early.wait_core_sends()
    early.wait_sends()
    for c in outward:
        c.wait()


def conv_scratch(groups, rows, narrow, tok, freqs, count, extra):
    low, f32 = jnp.bfloat16, jnp.float32
    dma = pltpu.SemaphoreType.DMA
    wide_rows = (rows + extra) * narrow
    out = [
        pltpu.VMEM((freqs, LANES, 2 * LANES), low),
        pltpu.VMEM((freqs, LANES, 2 * LANES), low),
        pltpu.VMEM((groups, rows, narrow, tok), low),
        pltpu.VMEM((count, wide_rows, LANES), f32),
    ]
    return out + [
        pltpu.VMEM((freqs, wide_rows, 2 * LANES), f32),
        pltpu.VMEM((groups, rows, narrow, tok), low),
        dma((groups - 1,)),
        dma((groups - 1,)),
        dma((groups - 1,)),
        dma((groups - 1,)),
        dma((4,)),
    ]


def conv_params(cid):
    return pltpu.CompilerParams(
        collective_id=cid, has_side_effects=True, vmem_limit_bytes=VMEM_LIMIT
    )


def conv_forward(block, lengths, gain, offset, weight, taps, params, tables):
    rows, tok, width = block.shape
    groups = lax.axis_size("seq")
    narrow, length = width // groups, tok * groups
    count = length // LANES
    freqs = count + 1
    low, f32 = jnp.bfloat16, jnp.float32
    vm = pl.BlockSpec(memory_space=pltpu.VMEM)
    sm = pl.BlockSpec(memory_space=pltpu.SMEM)
    hbm = pl.BlockSpec(memory_space=pl.ANY)
    return pl.pallas_call(
        functools.partial(conv_kernel, groups),
        out_shape=(
            jax.ShapeDtypeStruct((rows, width, tok), low),
            jax.ShapeDtypeStruct((freqs, rows * narrow, 2 * LANES), f32),
            jax.ShapeDtypeStruct((freqs, narrow, 2 * LANES), f32),
            jax.ShapeDtypeStruct((rows, 3 * width, tok), low),
            jax.ShapeDtypeStruct((rows, width, tok), f32),
            jax.ShapeDtypeStruct((8, 3 * width), f32),
        ),
        in_specs=[vm, sm] + [vm] * 13 + [hbm, hbm],
        out_specs=(vm,) * 6,
        scratch_shapes=conv_scratch(groups, rows, narrow, tok, freqs, count, 0)
        + [
            pltpu.VMEM((params[-1].shape[0], params[0].shape[1]), f32),
            pltpu.VMEM((count, narrow, LANES), f32),
            pltpu.VMEM((width, rows * tok), low),
            pltpu.VMEM((rows, width, tok), low),
            pltpu.VMEM((8, 3 * width), f32),
            pltpu.VMEM((3, 3 * width, LANES), f32),
            pltpu.VMEM((3 * width, LANES), f32),
            pltpu.VMEM((8, 3 * width), f32),
            pltpu.VMEM((8, 3 * width), f32),
            pltpu.SemaphoreType.DMA((2,)),
        ],
        compiler_params=conv_params(1),
        name="conv_forward",
    )(block, lengths, gain, offset, weight, taps, *params, *tables)


def conv_backward(grad, w_spec, h_spec, tables, gout, gup, gdown, params):
    rows, _, tok = grad.shape
    freqs, narrow, _ = h_spec.shape
    groups = lax.axis_size("seq")
    count = freqs - 1
    half = gout.shape[0] // 2
    vm = pl.BlockSpec(memory_space=pltpu.VMEM)
    hbm = pl.BlockSpec(memory_space=pl.ANY)
    low, f32 = jnp.bfloat16, jnp.float32
    dma = pltpu.SemaphoreType.DMA
    kept = groups >> len(EARLY_STEPS)
    feat_rows, hidden = params[-1].shape[0], params[0].shape[1]
    return pl.pallas_call(
        functools.partial(conv_back_kernel, lax.axis_size("row"), groups),
        out_shape=(
            jax.ShapeDtypeStruct(grad.shape, low),
            [jax.ShapeDtypeStruct((kept, n, narrow, half), low) for n in EARLY],
            jax.ShapeDtypeStruct((feat_rows, LANES), f32),
            jax.ShapeDtypeStruct((hidden, LANES), f32),
            jax.ShapeDtypeStruct((narrow, LANES), f32),
        ),
        in_specs=[vm, vm, vm, hbm, hbm] + [vm] * 12,
        out_specs=(vm, [vm] * 3, vm, vm, vm),
        scratch_shapes=conv_scratch(groups, rows, narrow, tok, freqs, count, 1)
        + [
            [pltpu.VMEM((groups, n, narrow, half), low) for n in EARLY],
            [
                pltpu.VMEM((groups, narrow, 4 * half), low),
                pltpu.VMEM((groups, 4 * narrow, half), low),
                pltpu.VMEM((groups, narrow, half), low),
            ],
            [
                [pltpu.VMEM((groups >> (k + 1), n, narrow, half), low) for k in EARLY_STEPS]
                for n in EARLY
            ],
            [dma((groups, 1)) for _ in EARLY],
            [dma((groups, 1)) for _ in EARLY],
            [[dma((groups >> (k + 1),)) for k in EARLY_STEPS] for _ in EARLY],
            [[dma((groups >> (k + 1),)) for k in EARLY_STEPS] for _ in EARLY],
            pltpu.VMEM((feat_rows, hidden), f32),
        ],
        compiler_params=conv_params(2),
        name="conv_backward",
    )(grad, w_spec, h_spec, *tables, gout, gup, gdown, *params)


def shards(
    block_in,
    lengths,
    mixer_gain,
    mixer_bias,
    in_weight,
    short_taps,
    filter_in,
    filter_in_bias,
    filter_mid,
    filter_mid_bias,
    filter_freq,
    filter_out,
    filter_skip,
    decay_rate,
    out_weight,
    feed_gain,
    feed_bias,
    up_weight,
    down_weight,
    cotangent,
):
    _, tok_count, model_width = block_in.shape
    length = tok_count * lax.axis_size("seq")
    block_float = block_in.astype(jnp.float32)
    tables = tuple(jnp.asarray(t) for t in spectrum_tables(length))
    params = (
        filter_in,
        filter_in_bias,
        filter_mid,
        filter_mid_bias,
        filter_freq,
        filter_out,
        filter_skip,
        decay_rate,
        jnp.asarray(feature_rows(length, filter_in.shape[0])),
    )
    back_home, w_spec, h_spec, projected, gate_out, edges = conv_forward(
        block_in, lengths, mixer_gain, mixer_bias, in_weight, short_taps, params, tables
    )
    conv_float = back_home.astype(jnp.float32)
    product_low = (gate_out * conv_float).astype(jnp.bfloat16)
    mixed = block_float + jnp.einsum(
        "rct,cd->rtd", product_low, out_weight, preferred_element_type=jnp.float32
    )
    normed_two, feed_pull = jax.vjp(layer_norm, mixed, feed_gain, feed_bias)
    normed_two_low = normed_two.astype(jnp.bfloat16)
    pre_act = jnp.einsum(
        "rtd,df->rtf", normed_two_low, up_weight, preferred_element_type=jnp.float32
    )
    activ, gelu_pull = jax.vjp(jax.nn.gelu, pre_act)
    activ_low = activ.astype(jnp.bfloat16)
    block_out = (
        mixed
        + jnp.einsum("rtf,fd->rtd", activ_low, down_weight, preferred_element_type=jnp.float32)
    ).astype(jnp.bfloat16)
    grad_float = cotangent.astype(jnp.float32)
    grad_down = jnp.einsum("rtf,rtd->fd", activ_low, cotangent, preferred_element_type=jnp.float32)
    grad_activ = jnp.einsum(
        "rtd,fd->rtf", cotangent, down_weight, preferred_element_type=jnp.float32
    )
    grad_pre = gelu_pull(grad_activ)[0].astype(jnp.bfloat16)
    grad_up = jnp.einsum(
        "rtd,rtf->df", normed_two_low, grad_pre, preferred_element_type=jnp.float32
    )
    grad_normed_two = jnp.einsum(
        "rtf,df->rtd", grad_pre, up_weight, preferred_element_type=jnp.float32
    )
    grad_mixed_part, grad_feed_gain, grad_feed_bias = feed_pull(grad_normed_two)
    grad_mixed = grad_float + grad_mixed_part
    grad_mixed_low = grad_mixed.astype(jnp.bfloat16)
    grad_outw = jnp.einsum(
        "rct,rtd->cd", product_low, grad_mixed_low, preferred_element_type=jnp.float32
    )
    grad_product = jnp.einsum(
        "rtd,cd->rct", grad_mixed_low, out_weight, preferred_element_type=jnp.float32
    )
    grad_gate_out = grad_product * conv_float
    grad_conv = (grad_product * gate_out).astype(jnp.bfloat16)
    low = jnp.bfloat16
    grad_carried, early, first_sum, mid_sum, last_sum = conv_backward(
        grad_conv,
        w_spec,
        h_spec,
        tables,
        grad_outw.astype(low),
        grad_up.astype(low),
        grad_down.astype(low),
        params,
    )
    grad_input, fin, small, last_all = finish(
        grad_carried,
        grad_gate_out,
        projected,
        edges,
        lengths,
        short_taps,
        in_weight,
        block_in,
        grad_mixed,
        (mixer_gain, mixer_bias, grad_feed_gain, grad_feed_bias),
        early,
        (mid_sum, first_sum, last_sum),
    )
    done = unpack(fin, small, last_all, filter_in.shape[0], filter_mid.shape[0], model_width)
    return (block_out, grad_input, *done)


def solution(mesh):
    placed = (
        P("row", "seq", None),
        P("row", None),
        P(),
        P(),
        P(),
        P(),
        P(),
        P(),
        P(),
        P(),
        P(),
        P(),
        P(),
        P(),
        P(),
        P(),
        P(),
        P(),
        P(),
        P("row", "seq", None),
    )
    return jax.shard_map(
        shards,
        mesh=mesh,
        in_specs=placed,
        out_specs=(
            P("row", "seq", None),
            P("row", "seq", None),
            P(),
            P(),
            P("seq", None),
            P(),
            P(),
            P(),
            P(),
            P(),
            P(),
            P(),
            P(),
            P("seq", None),
            P(),
            P(),
            P("seq", None),
            P("seq", None),
        ),
        check_vma=False,
    )
```

```python
import functools
import math

import jax
import jax.numpy as jnp
import numpy as np
from jax import lax
from jax.experimental import pallas as pl
from jax.experimental.pallas import tpu as pltpu
from jax.sharding import PartitionSpec as P

HIGHEST = lax.Precision.HIGHEST


def layer_norm(values, gain, offset):
    center = values - jnp.mean(values, axis=-1, keepdims=True)
    spread = jnp.mean(center * center, axis=-1, keepdims=True)
    return center * lax.rsqrt(spread + 1e-05) * gain + offset


MESH = pl.DeviceIdType.MESH
VMEM_LIMIT = 56 * 1024 * 1024
LANES = 128


def seq_weights(order, groups):
    weights = []
    w = 1
    while w < groups:
        weights.append(w)
        w *= 2
    first = weights[0] + order * (weights[1] - weights[0])
    second = weights[1] - order * (weights[1] - weights[0])
    return [first, second] + weights[2:]


class Halving:
    def __init__(self, groups, me, core, order, parts, own, first=0, base=0):
        self.groups, self.me, self.core, self.parts, self.own, self.first = (
            groups,
            me,
            core,
            parts,
            own,
            first,
        )
        self.order, self.other = (core, 1 - core) if order is None else (order, order)
        self.weights = seq_weights(self.order, groups)
        self.bits = [lax.rem(me // w, 2) for w in self.weights]
        self.steps = len(self.weights)
        self.half = own.shape[3]
        self.base = base * 2 * self.half
        self.source = None
        self.unit = own.shape[2]

    def shard_of(self, n, order):
        weights = seq_weights(order, self.groups)
        at = 0
        for j in range(self.steps):
            bit = lax.rem(self.me // weights[j], 2)
            keep = (n >> (self.steps - 1 - j)) & 1
            at = at + (bit if keep else 1 - bit) * weights[j]
        return at

    def core_setup(self, bufs, ss, rs, sib):
        self.bufs = bufs
        self.core_copies = []
        for n in range(self.groups):
            s = self.shard_of(n, self.other)
            row = []
            for p, (ref, high, cols, _) in enumerate(self.parts):
                src = (ref if self.source is None else self.source).at[
                    pl.ds(pl.multiple_of(s * high * self.unit, 8), high * self.unit),
                    pl.ds(
                        pl.multiple_of(self.base + (1 - self.core) * cols * self.half, LANES),
                        cols * self.half,
                    ),
                ]
                row.append(
                    pltpu.make_async_remote_copy(
                        src_ref=src,
                        dst_ref=bufs[p].at[n],
                        send_sem=ss.at[n, p],
                        recv_sem=rs.at[n, p],
                        device_id={"row": sib},
                        device_id_type=MESH,
                    )
                )
            self.core_copies.append(row)

    def core_start(self):
        for row in self.core_copies:
            for c in row:
                c.start()

    def core_finish(self, n):
        for c in self.core_copies[n]:
            c.wait_recv()
        s = self.shard_of(n, self.order)
        for p, (ref, high, cols, first) in enumerate(self.parts):
            for h in range(high):
                for c in range(cols):
                    mine = ref[
                        pl.ds(pl.multiple_of((s * high + h) * self.unit, 8), self.unit),
                        pl.ds(
                            pl.multiple_of(
                                self.base + (self.core * cols + c) * self.half, LANES
                            ),
                            self.half,
                        ),
                    ]
                    self.own[n, first + h * cols + c] = (
                        mine
                        + self.bufs[p][
                            n,
                            h * self.unit : (h + 1) * self.unit,
                            c * self.half : (c + 1) * self.half,
                        ]
                    )

    def step_setup(self, bufs, ss, rs, steps):
        self.step_bufs = dict(zip(steps, bufs))
        self.copies = {}
        for at, k in enumerate(steps):
            for i in range(self.groups >> (k + 1)):
                self.copies[k, i] = pltpu.make_async_remote_copy(
                    src_ref=self.own.at[self.slot(k) + i],
                    dst_ref=bufs[at].at[i],
                    send_sem=ss[at].at[i],
                    recv_sem=rs[at].at[i],
                    device_id={"seq": self.me + self.weights[k] * (1 - 2 * self.bits[k])},
                    device_id_type=MESH,
                )

    def slot(self, k):
        return self.groups - (self.groups >> k) - self.first

    def start(self, k, i):
        self.copies[k, i].start()

    def finish(self, k, i):
        self.copies[k, i].wait_recv()
        at = self.slot(k + 1) + i
        self.own[at] = self.own[at] + self.step_bufs[k][i]

    def count(self, k):
        return self.groups >> (k + 1)

    def wait_sends(self):
        for c in self.copies.values():
            c.wait_send()

    def wait_core_sends(self):
        for row in self.core_copies:
            for c in row:
                c.wait_send()


EARLY = (4, 4, 1)
LATE = (1, 1, 1)
ORDERS = (0, 1, None)
EARLY_STEPS = (0,)


class Crew:
    def __init__(self, members):
        self.members = members
        self.groups, self.steps = members[0].groups, members[0].steps

    def core_setup(self, bufs, ss, rs, sib):
        for p, h in enumerate(self.members):
            h.core_setup([bufs[p]], ss[p], rs[p], sib)

    def step_setup(self, bufs, ss, rs, steps):
        for p, h in enumerate(self.members):
            h.step_setup(bufs[p], ss[p], rs[p], steps)

    def core_start(self):
        for n in range(self.groups):
            for h in self.members:
                for c in h.core_copies[n]:
                    c.start()

    def count(self, k):
        return self.groups >> (k + 1)

    def core_finish(self, n):
        for h in self.members:
            h.core_finish(n)
            if n < self.count(0):
                h.start(0, n)

    def start(self, k, i):
        for h in self.members:
            h.start(k, i)

    def finish(self, k, i, onward):
        for h in self.members:
            h.finish(k, i)
            if onward and k + 1 < self.steps and i < self.count(k + 1):
                h.start(k + 1, i)

    def advance(self, k):
        for i in range(self.count(k)):
            self.finish(k, i, True)

    def wait_sends(self):
        for h in self.members:
            h.wait_sends()

    def wait_core_sends(self):
        for h in self.members:
            h.wait_core_sends()


def early_crew(groups, me, core, gout, gup, gdown, owns, down_src):
    parts = [[(gup, 1, 4, 0)], [(gdown, 4, 1, 0)], [(gout, 1, 1, 0)]]
    crew = Crew([Halving(groups, me, core, o, p, w) for o, p, w in zip(ORDERS, parts, owns)])
    crew.members[1].source = down_src
    return crew


def greet_all(rows, groups, me, row):
    barrier = pltpu.get_barrier_semaphore()
    for d in range(1, rows):
        pl.semaphore_signal(
            barrier, inc=1, device_id={"row": lax.rem(row + d, rows)}, device_id_type=MESH
        )
    for d in range(1, groups):
        pl.semaphore_signal(
            barrier, inc=1, device_id={"seq": lax.rem(me + d, groups)}, device_id_type=MESH
        )
    pl.semaphore_wait(barrier, rows + groups - 2)


def row_masks(lengths, row, start, tok):
    where = lax.broadcasted_iota(jnp.int32, (8, tok), 1) + start
    ends = []
    total = 0
    for k in range(lengths.shape[1]):
        total = total + lengths[row, k]
        ends.append(total)

    def doc(at):
        out = jnp.zeros(at.shape, jnp.int32)
        for e in ends:
            out = out + (at >= e).astype(jnp.int32)
        return out

    own = doc(where)
    masks = []
    for lag in (1, 2):
        same = (where >= lag) & (doc(where - lag) == own)
        masks.append(same.astype(jnp.float32)[:1])
    return masks + [(where < total).astype(jnp.float32)[:1]]


def edge_pick(r):
    line = lax.broadcasted_iota(jnp.int32, (8, LANES), 0)
    spot = lax.broadcasted_iota(jnp.int32, (8, LANES), 1)
    pick = (spot == line - 2 * r + LANES - 2) & (line >= 2 * r) & (line < 2 * r + 2)
    return pick.astype(jnp.bfloat16)


def pack_edges(tiles):
    out = None
    for r, tile in enumerate(tiles):
        piece = lax.dot_general(
            edge_pick(r), tile, (((1,), (1,)), ((), ())), preferred_element_type=jnp.float32
        )
        out = piece if out is None else out + piece
    return out


def unpack_edge(lines, r):
    return lax.dot_general(
        lines.astype(jnp.bfloat16),
        edge_pick(r),
        (((0,), (0,)), ((), ())),
        preferred_element_type=jnp.float32,
    )


def window_of(values, lane, edge):
    early, late = edge[:, LANES - 2 : LANES - 1], edge[:, LANES - 1 :]
    one = jnp.where(lane == 0, late, pltpu.roll(values, 1, 1))
    two = jnp.where(lane == 0, early, jnp.where(lane == 1, late, pltpu.roll(values, 2, 1)))
    return one, two


def spread_taps(taps, padded, wide):
    padded[...] = jnp.zeros_like(padded)
    padded[: taps.shape[0], :] = taps[...]
    turned = padded[...].T
    for j in range(taps.shape[0]):
        wide[j] = jnp.broadcast_to(turned[:, j : j + 1], wide.shape[1:])


def norm_parts(values):
    center = values - jnp.mean(values, axis=-1, keepdims=True)
    scale = lax.rsqrt(jnp.mean(center * center, axis=-1, keepdims=True) + 1e-05)
    return center * scale, scale


STRIP = 128


def finish_kernel(
    rows,
    groups,
    gw_ref,
    ggo_ref,
    u_hbm,
    edge_ref,
    lengths,
    taps,
    weight_hbm,
    block_hbm,
    gm_hbm,
    gain,
    offset,
    feed_gain,
    feed_bias,
    early,
    mid_s,
    first_s,
    last,
    gi_ref,
    fin_o,
    small_o,
    last_o,
    padded,
    wide_taps,
    edges,
    tap_sum,
    gu,
    gu_low,
    rim,
    rim_out,
    rim_in,
    normed,
    gin,
    small,
    own,
    own_early,
    core_buf,
    step_buf,
    early_buf,
    wide_buf,
    small_row,
    small_sum,
    small_part,
    small_done,
    last_row,
    last_sum,
    rim_sem,
    bring_sem,
    u_ref,
    weight,
    block,
    gm_ref,
    move_sem,
    core_ss,
    core_rs,
    step_ss,
    step_rs,
    early_ss,
    early_rs,
    wide_ss,
    wide_rs,
    fin_ss,
    fin_rs,
    srow_ss,
    srow_rs,
    spart_ss,
    spart_rs,
    sdone_ss,
    sdone_rs,
    lrow_ss,
    lrow_rs,
    last_ss,
    last_rs,
):
    me = lax.axis_index("seq")
    row = lax.axis_index("row")
    core = lax.rem(row, 2)
    sib = row + 1 - 2 * core
    chunk = small_part.shape[1]
    held, width, tok = gw_ref.shape
    low, f32 = jnp.bfloat16, jnp.float32

    late = Crew(
        [
            Halving(groups, me, core, o, [(gin, 1, 1, 0)], own[p], base=p)
            for p, o in enumerate(ORDERS)
        ]
    )
    late.core_setup(core_buf, core_ss, core_rs, sib)
    late.step_setup(step_buf, step_ss, step_rs, range(late.steps))
    later = range(EARLY_STEPS[-1] + 1, late.steps)
    rest = Crew(
        [
            Halving(groups, me, core, o, (), w, first=groups - e.shape[0])
            for o, w, e in zip(ORDERS, own_early, early)
        ]
    )
    rest.step_setup(early_buf, early_ss, early_rs, later)
    bring = [
        pltpu.make_async_copy(e, w, bring_sem.at[p])
        for p, (w, e) in enumerate(zip(own_early, early))
    ]
    moves = [
        pltpu.make_async_copy(src, dst, move_sem.at[p])
        for p, (src, dst) in enumerate(
            ((u_hbm, u_ref), (block_hbm, block), (weight_hbm, weight), (gm_hbm, gm_ref))
        )
    ]
    for c in bring + moves:
        c.start()
    greet_all(rows, groups, me, row)
    for c in bring:
        c.wait()
    for i in range(rest.count(later[0])):
        rest.start(later[0], i)
    lrow = [
        pltpu.make_async_remote_copy(
            src_ref=last,
            dst_ref=last_row.at[d - 1],
            send_sem=lrow_ss.at[d - 1],
            recv_sem=lrow_rs.at[d - 1],
            device_id={"row": lax.rem(row + d, rows)},
            device_id_type=MESH,
        )
        for d in range(1, rows)
    ]
    for c in lrow:
        c.start()

    spread_taps(taps, padded, wide_taps)
    tap_sum[...] = jnp.zeros_like(tap_sum)
    lane = lax.broadcasted_iota(jnp.int32, (STRIP, tok), 1)
    moves[0].wait()
    for r in range(held):
        same1, same2, live = row_masks(lengths, r, me * tok, tok)
        edges[...] = unpack_edge(edge_ref[...], r)

        def strip(i, carry, r=r, same1=same1, same2=same2, live=live):
            at = [pl.multiple_of(i * STRIP + g * width, STRIP) for g in range(3)]
            tap = [
                [
                    jnp.concatenate([wide_taps[j, pl.ds(a, STRIP), :]] * (tok // LANES), axis=1)
                    for j in range(3)
                ]
                for a in at
            ]
            u = [u_ref[r, pl.ds(a, STRIP), :].astype(f32) for a in at]
            shifts = [
                window_of(v, lane, edges[pl.ds(a, STRIP), :])
                for v, a in zip(u, at)
            ]
            gate_in, stream = [
                tap[g][0] * u[g] + tap[g][1] * shifts[g][0] * same1 + tap[g][2] * shifts[g][1] * same2
                for g in (1, 2)
            ]
            gw = gw_ref[r, pl.ds(at[0], STRIP), :].astype(f32) * live
            grads = [ggo_ref[r, pl.ds(at[0], STRIP), :] * live, gw * stream, gw * gate_in]
            for g in range(3):
                m1, m2 = grads[g] * same1, grads[g] * same2
                for j, p in enumerate((grads[g] * u[g], m1 * shifts[g][0], m2 * shifts[g][1])):
                    total = p[:, :LANES]
                    for h in range(1, tok // LANES):
                        total = total + p[:, h * LANES : (h + 1) * LANES]
                    tap_sum[j, pl.ds(at[g], STRIP), :] += total
                b1 = pltpu.roll(tap[g][1] * m1, tok - 1, 1)
                b2 = pltpu.roll(tap[g][2] * m2, tok - 2, 1)
                gu[r, pl.ds(at[g], STRIP), :] = (
                    tap[g][0] * grads[g]
                    + jnp.where(lane < tok - 1, b1, 0.0)
                    + jnp.where(lane < tok - 2, b2, 0.0)
                )
                over = jnp.where(lane < tok - 1, 0.0, b1) + jnp.where(lane < tok - 2, 0.0, b2)
                rim[r, pl.ds(at[g], STRIP), :] = over[:, tok - LANES :].astype(low)
            return carry

        lax.fori_loop(0, width // STRIP, strip, 0)

    rim_out[...] = pack_edges([rim[r] for r in range(held)])
    rim_copy = pltpu.make_async_remote_copy(
        src_ref=rim_out,
        dst_ref=rim_in,
        send_sem=rim_sem.at[0],
        recv_sem=rim_sem.at[1],
        device_id={"seq": lax.rem(me + groups - 1, groups)},
        device_id_type=MESH,
    )
    rim_copy.start()

    at = mid_s.shape[0] + first_s.shape[0]
    small[:at, :] = jnp.concatenate([mid_s[...], first_s[...]], axis=0)
    small[at:, :] = jnp.zeros((small.shape[0] - at, LANES), f32)
    per = width // LANES

    def put_small(first, line):
        for i in range(line.shape[1] // LANES):
            small[first + i : first + i + 1, :] = line[:, i * LANES : (i + 1) * LANES]

    ones = jnp.ones((8, LANES), low)

    def lane_sums(values):
        high = values.astype(low)
        rest = (values - high.astype(f32)).astype(low)
        dims = (((1,), (1,)), ((), ()))
        return lax.dot_general(ones, high, dims, preferred_element_type=f32) + lax.dot_general(
            ones, rest, dims, preferred_element_type=f32
        )

    for j in range(3):
        put_small(at + 2 * per + 3 * per * j, lane_sums(tap_sum[j])[:1])
    put_small(at + 11 * per, feed_gain[...][None, :])
    put_small(at + 12 * per, feed_bias[...][None, :])
    gain_row, offset_row = gain[...][None, :], offset[...][None, :]
    for c in moves[1:]:
        c.wait()
    for r in range(held):
        hat, _ = norm_parts(block[r].astype(f32))
        normed[:, r * tok : (r + 1) * tok] = (hat * gain_row + offset_row).T.astype(low)
    rest.advance(later[0])

    rim_copy.wait()
    for r in range(held):
        add = unpack_edge(rim_in[...], r)
        split = tok - LANES
        gu_low[:, r * tok : r * tok + split] = gu[r, :, :split].astype(low)
        gu_low[:, r * tok + split : (r + 1) * tok] = (gu[r, :, split:] + add).astype(low)

    piece = 256

    def weight_grad(i, carry):
        cols = pl.ds(pl.multiple_of(i * piece, piece), piece)
        gin[:, cols] = lax.dot_general(
            normed[...], gu_low[cols, :], (((1,), (1,)), ((), ())), preferred_element_type=f32
        ).astype(low)
        return carry

    lax.fori_loop(0, 3 * width // piece, weight_grad, 0)
    late.core_start()

    gains = [jnp.zeros((1, width), f32), jnp.zeros((1, width), f32)]
    for r in range(held):
        turned = lax.dot_general(
            weight[...],
            gu_low[:, r * tok : (r + 1) * tok],
            (((1,), (0,)), ((), ())),
            preferred_element_type=f32,
        )
        grad = turned.T
        hat, scale = norm_parts(block[r].astype(f32))
        gains[0] = gains[0] + jnp.sum(grad * hat, axis=0, keepdims=True)
        gains[1] = gains[1] + jnp.sum(grad, axis=0, keepdims=True)
        pulled = grad * gain_row
        pulled = pulled - jnp.mean(pulled, axis=-1, keepdims=True)
        pulled = pulled - hat * jnp.mean(pulled * hat, axis=-1, keepdims=True)
        gi_ref[r] = gm_ref[r] + scale * pulled
        if r == 0:
            for n in range(groups):
                late.core_finish(n)
    rest.advance(later[1])
    put_small(at, gains[0])
    put_small(at + per, gains[1])

    srow = [
        pltpu.make_async_remote_copy(
            src_ref=small,
            dst_ref=small_row.at[d - 1],
            send_sem=srow_ss.at[d - 1],
            recv_sem=srow_rs.at[d - 1],
            device_id={"row": lax.rem(row + d, rows)},
            device_id_type=MESH,
        )
        for d in range(1, rows)
    ]
    for c in srow:
        c.start()
    for c in srow + lrow:
        c.wait()
    total = small[...]
    tail = last[...]
    for d in range(rows - 1):
        total = total + small_row[d]
        tail = tail + last_row[d]
    small_sum[...] = total
    last_sum[...] = tail
    last_o[me] = tail
    spart = []
    lcp = []
    for d in range(1, groups):
        to = lax.rem(me + d, groups)
        spart.append(
            pltpu.make_async_remote_copy(
                src_ref=small_sum.at[pl.ds(to * chunk, chunk)],
                dst_ref=small_part.at[d - 1],
                send_sem=spart_ss.at[d - 1],
                recv_sem=spart_rs.at[d - 1],
                device_id={"seq": to},
                device_id_type=MESH,
            )
        )
        lcp.append(
            pltpu.make_async_remote_copy(
                src_ref=last_sum,
                dst_ref=last_o.at[me],
                send_sem=last_ss.at[d - 1],
                recv_sem=last_rs.at[d - 1],
                device_id={"seq": to},
                device_id_type=MESH,
            )
        )
    for c in spart + lcp:
        c.start()
    late.advance(0)
    for k in later[2:]:
        rest.advance(k)
    for c in spart:
        c.wait()
    total = small_sum[pl.ds(me * chunk, chunk)]
    for d in range(groups - 1):
        total = total + small_part[d]
    small_done[...] = total
    small_o[pl.ds(me * chunk, chunk)] = total
    sdone = [
        pltpu.make_async_remote_copy(
            src_ref=small_done,
            dst_ref=small_o.at[pl.ds(me * chunk, chunk)],
            send_sem=sdone_ss.at[d - 1],
            recv_sem=sdone_rs.at[d - 1],
            device_id={"seq": lax.rem(me + d, groups)},
            device_id_type=MESH,
        )
        for d in range(1, groups)
    ]
    for c in sdone:
        c.start()
    for k in range(1, late.steps):
        late.advance(k)

    halves = []
    place = 0
    for h, e, units in zip(rest.members, early, EARLY):
        halves.append((h, e.shape[0] - 1, place, units))
        place += units
    for h, units in zip(late.members, LATE):
        halves.append((h, groups - 1, place, units))
        place += units
    w = 2
    n = 0
    while w < rows:
        bit = lax.rem(row // w, 2)
        for p, (h, slot, _, _) in enumerate(halves):
            c = pltpu.make_async_remote_copy(
                src_ref=h.own.at[slot],
                dst_ref=wide_buf[p].at[n],
                send_sem=wide_ss.at[n, p],
                recv_sem=wide_rs.at[n, p],
                device_id={"row": row + w * (1 - 2 * bit)},
                device_id_type=MESH,
            )
            c.start()
            c.wait()
            h.own[slot] = h.own[slot] + wide_buf[p][n]
        w *= 2
        n += 1

    fin = []
    for p, (h, slot, first, units) in enumerate(halves):
        fin_o[core, first : first + units] = h.own[slot]
        c = pltpu.make_async_remote_copy(
            src_ref=h.own.at[slot],
            dst_ref=fin_o.at[core, pl.ds(first, units)],
            send_sem=fin_ss.at[p],
            recv_sem=fin_rs.at[p],
            device_id={"row": sib},
            device_id_type=MESH,
        )
        c.start()
        fin.append(c)
    late.wait_core_sends()
    late.wait_sends()
    rest.wait_sends()
    for c in sdone + lcp:
        c.wait()
    for c in fin:
        c.wait()


def finish(gw, ggo, u, edge, lengths, taps, weight, block, gm, vectors, early, sums):
    rows, groups = lax.axis_size("row"), lax.axis_size("seq")
    held, width, tok = gw.shape
    unit = width // groups
    half = width // 2
    wide = max(1, rows.bit_length() - 2)
    low, f32 = jnp.bfloat16, jnp.float32
    steps = groups.bit_length() - 1
    later = range(EARLY_STEPS[-1] + 1, steps)
    used = sums[0].shape[0] + sums[1].shape[0] + 13 * (width // LANES)
    lines = used + -used % (8 * groups)
    chunk = lines // groups
    last = sums[2]
    dma = pltpu.SemaphoreType.DMA
    vm = pl.BlockSpec(memory_space=pltpu.VMEM)
    sm = pl.BlockSpec(memory_space=pltpu.SMEM)
    hbm = pl.BlockSpec(memory_space=pl.ANY)
    return pl.pallas_call(
        functools.partial(finish_kernel, rows, groups),
        out_shape=(
            jax.ShapeDtypeStruct(gm.shape, f32),
            jax.ShapeDtypeStruct((2, sum(EARLY) + sum(LATE), unit, half), low),
            jax.ShapeDtypeStruct((lines, LANES), f32),
            jax.ShapeDtypeStruct((groups,) + last.shape, f32),
        ),
        in_specs=[vm, vm, hbm, vm, sm, vm, hbm, hbm, hbm] + [vm] * 4 + [[hbm] * 3] + [vm] * 3,
        out_specs=(vm,) * 4,
        scratch_shapes=[
            pltpu.VMEM((8, 3 * width), f32),
            pltpu.VMEM((3, 3 * width, LANES), f32),
            pltpu.VMEM((3 * width, LANES), f32),
            pltpu.VMEM((3, 3 * width, LANES), f32),
            pltpu.VMEM((held, 3 * width, tok), f32),
            pltpu.VMEM((3 * width, held * tok), low),
            pltpu.VMEM((held, 3 * width, LANES), low),
            pltpu.VMEM((8, 3 * width), f32),
            pltpu.VMEM((8, 3 * width), f32),
            pltpu.VMEM((width, held * tok), low),
            pltpu.VMEM((width, 3 * width), low),
            pltpu.VMEM((lines, LANES), f32),
            [pltpu.VMEM((groups, n, unit, half), low) for n in LATE],
            [pltpu.VMEM(e.shape, low) for e in early],
            [pltpu.VMEM((groups, unit, n * half), low) for n in LATE],
            [
                [pltpu.VMEM((groups >> (k + 1), n, unit, half), low) for k in range(steps)]
                for n in LATE
            ],
            [[pltpu.VMEM((groups >> (k + 1), n, unit, half), low) for k in later] for n in EARLY],
            [pltpu.VMEM((wide, n, unit, half), low) for n in EARLY + LATE],
            pltpu.VMEM((rows - 1, lines, LANES), f32),
            pltpu.VMEM((lines, LANES), f32),
            pltpu.VMEM((groups - 1, chunk, LANES), f32),
            pltpu.VMEM((chunk, LANES), f32),
            pltpu.VMEM((rows - 1,) + last.shape, f32),
            pltpu.VMEM(last.shape, f32),
            dma((2,)),
            dma((3,)),
            pltpu.VMEM(u.shape, low),
            pltpu.VMEM(weight.shape, low),
            pltpu.VMEM(block.shape, low),
            pltpu.VMEM(gm.shape, f32),
            dma((4,)),
            [dma((groups, 1)) for _ in LATE],
            [dma((groups, 1)) for _ in LATE],
            [[dma((groups >> (k + 1),)) for k in range(steps)] for _ in LATE],
            [[dma((groups >> (k + 1),)) for k in range(steps)] for _ in LATE],
            [[dma((groups >> (k + 1),)) for k in later] for _ in EARLY],
            [[dma((groups >> (k + 1),)) for k in later] for _ in EARLY],
            dma((wide, 6)),
            dma((wide, 6)),
            dma((6,)),
            dma((6,)),
            dma((rows - 1,)),
            dma((rows - 1,)),
            dma((groups - 1,)),
            dma((groups - 1,)),
            dma((groups - 1,)),
            dma((groups - 1,)),
            dma((rows - 1,)),
            dma((rows - 1,)),
            dma((groups - 1,)),
            dma((groups - 1,)),
        ],
        compiler_params=pltpu.CompilerParams(
            collective_id=0, has_side_effects=True, vmem_limit_bytes=VMEM_LIMIT
        ),
        name="finish",
    )(gw, ggo, u, edge, lengths, taps, weight, block, gm, *vectors, early, *sums)


def unpack_kernel(
    feat,
    fin,
    small,
    last,
    gi,
    gain_o,
    bias_o,
    in_o,
    taps_o,
    first_o,
    first_b_o,
    mid_o,
    mid_b_o,
    freq_o,
    last_o,
    skip_o,
    out_o,
    feed_gain_o,
    feed_bias_o,
    up_o,
    down_o,
    gi_o,
):
    f32 = jnp.float32
    gi_o[...] = gi[...]
    unit, half = fin.shape[2], fin.shape[3]
    hidden = mid_o.shape[0]
    width = gain_o.shape[0]
    per = width // LANES
    outs = [(up_o, 1, 4, 0, 0), (down_o, 4, 1, 4, 0), (out_o, 1, 1, 8, 0)]
    outs = outs + [(in_o, 1, 1, 9 + p, 2 * p) for p in range(3)]
    for core in range(2):
        for out, high, cols, first, base in outs:
            for h in range(high):
                for c in range(cols):
                    at = (base + core * cols + c) * half
                    out[h * unit : (h + 1) * unit, at : at + half] = fin[
                        core, first + h * cols + c
                    ].astype(f32)

    def line(first, count):
        pieces = [small[first + i : first + i + 1, :] for i in range(count)]
        return jnp.concatenate(pieces, axis=1)

    at = hidden + -(-(feat + 1) // 8) * 8
    gain_o[...] = line(at, per)[0]
    bias_o[...] = line(at + per, per)[0]
    for j in range(3):
        taps_o[j : j + 1, :] = line(at + 2 * per + 3 * per * j, 3 * per)
    feed_gain_o[...] = line(at + 11 * per, per)[0]
    feed_bias_o[...] = line(at + 12 * per, per)[0]
    first_o[...] = small[hidden : hidden + feat, :hidden]
    first_b_o[...] = small[hidden + feat : hidden + feat + 1, :hidden][0]
    mid_o[...] = small[:hidden, :hidden]
    shape = (hidden, hidden)
    same = lax.broadcasted_iota(jnp.int32, shape, 0) == lax.broadcasted_iota(jnp.int32, shape, 1)
    for out, col in ((mid_b_o, hidden), (freq_o, hidden + 1)):
        out[...] = jnp.sum(
            jnp.where(same, small[:hidden, col : col + 1], 0.0), axis=0, keepdims=True
        )[0]
    turned = last[...].T
    last_o[...] = turned[:hidden]
    skip_o[...] = turned[hidden : hidden + 1][0]


def unpack(fin, small, last, gi, feat, hidden, width):
    f32 = jnp.float32
    unit = fin.shape[2]
    vm = pl.BlockSpec(memory_space=pltpu.VMEM)
    shapes = [
        (width,),
        (width,),
        (unit, 3 * width),
        (3, 3 * width),
        (feat, hidden),
        (hidden,),
        (hidden, hidden),
        (hidden,),
        (hidden,),
        (hidden, width),
        (width,),
        (unit, width),
        (width,),
        (width,),
        (unit, 4 * width),
        (4 * unit, width),
        gi.shape,
    ]
    return pl.pallas_call(
        functools.partial(unpack_kernel, feat),
        out_shape=tuple(jax.ShapeDtypeStruct(x, f32) for x in shapes),
        in_specs=[vm] * 4,
        out_specs=(vm,) * len(shapes),
        compiler_params=pltpu.CompilerParams(vmem_limit_bytes=VMEM_LIMIT),
        name="unpack",
    )(fin, small, last.reshape(width, LANES), gi)


def spectrum_tables(length):
    period = 2 * length
    first = period // LANES
    k1 = np.arange(first // 2 + 1, dtype=np.int64)[:, None, None]
    n2 = np.arange(LANES, dtype=np.int64)[None, :, None]
    k2 = np.arange(LANES, dtype=np.int64)[None, None, :]
    angle = 2.0 * np.pi / period * (n2 * (k1 + first * k2) % period)
    full = np.concatenate([np.cos(angle), np.sin(angle)], axis=2).astype(np.float32)
    high = full.astype(jnp.bfloat16)
    rest = (full - high.astype(np.float32)).astype(jnp.bfloat16)
    return high, rest


def feature_rows(length, feat_count):
    bands = (feat_count - 1) // 2
    at = np.arange(length, dtype=np.int64)[None, :]
    angle = 2.0 * np.pi / length * (at * np.arange(1, bands + 1)[:, None] % length)
    rows = [at / length, np.cos(angle), -np.sin(angle), np.ones((1, length))]
    rows = np.concatenate(rows, axis=0)
    pad = -rows.shape[0] % 8
    return np.pad(rows, ((0, pad), (0, 0))).astype(np.float32)


def sin_cos(x):
    n = jnp.round(x * (2.0 / math.pi))
    r = x - n * 1.5703125
    r = r - n * 4.837512969970703125e-4
    r = r - n * 7.549789948768648e-8
    z = r * r
    s = r + r * z * (-1.6666654611e-1 + z * (8.3321608736e-3 - z * 1.9515295891e-4))
    c = (
        1.0
        - 0.5 * z
        + z * z * (4.166664568298827e-2 + z * (-1.388731625493765e-3 + z * 2.443315711809948e-5))
    )
    q = n.astype(jnp.int32) & 3
    odd = (q & 1) == 1
    sine = jnp.where(odd, c, s)
    cosine = jnp.where(odd, s, c)
    sine = jnp.where(q >= 2, -sine, sine)
    cosine = jnp.where((q == 1) | (q == 2), -cosine, cosine)
    return sine, cosine


def exact_dot(p, q, left, right):
    low = jnp.bfloat16

    def dot(x, y):
        return lax.dot_general(
            x, y, (((left,), (right,)), ((), ())), preferred_element_type=jnp.float32
        )

    ph, qh = p.astype(low), q.astype(low)
    pl_, ql = (p - ph.astype(jnp.float32)).astype(low), (q - qh.astype(jnp.float32)).astype(low)
    return dot(ph, qh) + (dot(pl_, qh) + dot(ph, ql))


def column_of(row):
    size = row.shape[1]
    shape = (size, size)
    same = lax.broadcasted_iota(jnp.int32, shape, 0) == lax.broadcasted_iota(jnp.int32, shape, 1)
    return jnp.sum(jnp.where(same, row, 0.0), axis=1, keepdims=True)


class FilterNet:
    def __init__(self, me, narrow, params, aug):
        first, first_b, mid, mid_b, freq, last, skip, decay, self.feats = params
        feat = first.shape[0]
        aug[...] = jnp.zeros_like(aug)
        aug[:feat, :] = first[...]
        aug[feat : feat + 1, :] = first_b[...][None, :]
        self.aug = aug
        self.mid = mid
        self.mid_b = column_of(mid_b[...][None, :])
        self.freq = column_of(freq[...][None, :])
        width = skip.shape[0]
        shape = (narrow, width)
        pick = (
            lax.broadcasted_iota(jnp.int32, shape, 1)
            == lax.broadcasted_iota(jnp.int32, shape, 0) + me * narrow
        )
        self.skip = jnp.sum(jnp.where(pick, skip[...][None, :], 0.0), axis=1, keepdims=True)
        self.decay = jnp.sum(jnp.where(pick, decay[...][None, :], 0.0), axis=1, keepdims=True)
        self.last = exact_dot(pick.astype(jnp.float32), last[...], 1, 1)
        self.narrow = narrow

    def layers(self, at, size):
        feats = self.feats[:, pl.ds(at, size)]
        pre1 = exact_dot(self.aug[...], feats, 0, 0)
        a1, c1 = sin_cos(self.freq * pre1)
        pre2 = exact_dot(self.mid[...], a1, 0, 0) + self.mid_b
        a2, c2 = sin_cos(self.freq * pre2)
        return feats, pre1, a1, c1, pre2, a2, c2

    def fade(self, at, size):
        where = lax.broadcasted_iota(jnp.int32, (self.narrow, size), 1) + at
        return jnp.exp(-self.decay * where.astype(jnp.float32)), where

    def build(self, at, size):
        a2 = self.layers(at, size)[5]
        fade, where = self.fade(at, size)
        return exact_dot(self.last, a2, 1, 0) * fade + jnp.where(where == 0, self.skip, 0.0)

    def pull(self, at, size, grad, first_o, mid_o, last_o):
        feats, pre1, a1, c1, pre2, a2, c2 = self.layers(at, size)
        fade, where = self.fade(at, size)
        hidden = a1.shape[0]
        raw = grad * fade
        last_o[:, :hidden] += exact_dot(raw, a2, 1, 1)
        last_o[:, hidden : hidden + 1] += jnp.sum(
            jnp.where(where == 0, grad, 0.0), axis=1, keepdims=True
        )
        turned2 = exact_dot(self.last, raw, 0, 0) * c2
        freq = jnp.sum(turned2 * pre2, axis=1, keepdims=True)
        down2 = turned2 * self.freq
        mid_o[:, :hidden] += exact_dot(a1, down2, 1, 1)
        mid_o[:, hidden : hidden + 1] += jnp.sum(down2, axis=1, keepdims=True)
        turned1 = exact_dot(self.mid[...], down2, 1, 0) * c1
        freq = freq + jnp.sum(turned1 * pre1, axis=1, keepdims=True)
        mid_o[:, hidden + 1 : hidden + 2] += freq
        down1 = turned1 * self.freq
        first_o[:, :hidden] += exact_dot(feats, down1, 1, 1)


CHUNK = 4


def half_dft(x):
    count = 2 * len(x)
    if count == 2:
        return [(x[0], None), (x[0], None)]
    even, odd = half_dft(x[0::2]), half_dft(x[1::2])
    out = [None] * (count // 2 + 1)
    for k in range(count // 4 + 1):
        er, ei = even[k]
        orr, oi = odd[k]
        if k == 0:
            out[0] = (er + orr, None)
            out[count // 2] = (er - orr, None)
        elif 4 * k == count:
            out[k] = (er, -orr)
        else:
            c, s = math.cos(2 * math.pi * k / count), math.sin(2 * math.pi * k / count)
            tr = orr * c + oi * s
            ti = oi * c - orr * s
            out[k] = (er + tr, ei + ti)
            out[count // 2 - k] = (er - tr, ti - ei)
    return out


def half_inverse(spec):
    count = 2 * (len(spec) - 1)
    if count == 2:
        return [spec[0][0] + spec[1][0]]
    even, odd = [], []
    for k in range(count // 4 + 1):
        ar, ai = spec[k]
        br, bi = spec[count // 2 - k]
        if k == 0:
            even.append((ar + br, None))
            odd.append((ar - br, None))
        elif 4 * k == count:
            even.append((ar + ar, None))
            odd.append((-(ai + ai), None))
        else:
            c, s = math.cos(2 * math.pi * k / count), math.sin(2 * math.pi * k / count)
            dr, di = ar - br, ai + bi
            even.append((ar + br, ai - bi))
            odd.append((dr * c - di * s, dr * s + di * c))
    out = [None] * (count // 2)
    out[0::2] = half_inverse(even)
    out[1::2] = half_inverse(odd)
    return out


def turn_of(table):
    cos, sin = table[:, :LANES], table[:, LANES:]
    return jnp.concatenate(
        [jnp.concatenate([cos, -sin], axis=1), jnp.concatenate([sin, cos], axis=1)], axis=0
    )


def split_dot(a, high, rest, back):
    a_high = a.astype(jnp.bfloat16)
    a_rest = (a - a_high.astype(jnp.float32)).astype(jnp.bfloat16)
    dims = (((1,), (1 if back else 0,)), ((), ()))
    high, rest = turn_of(high), turn_of(rest)

    def dot(p, q):
        return lax.dot_general(p, q, dims, preferred_element_type=jnp.float32)

    rows = a.shape[0]
    both = dot(jnp.concatenate([a_high, a_rest], axis=0), high)
    return both[:rows] + (both[rows:] + dot(a_high, rest))


def tile_loop(tiles, body):
    def step(i, carry):
        body(pl.multiple_of(i * 8, 8))
        return carry

    lax.fori_loop(0, tiles, step, 0, unroll=3 if tiles % 3 == 0 else 1)


def first_stage(load, spec, tiles):
    zero = jnp.zeros((8, LANES), jnp.float32)

    def body(at):
        for k, (re, im) in enumerate(half_dft(load(at))):
            spec[k, pl.ds(at, 8), :LANES] = re
            spec[k, pl.ds(at, 8), LANES:] = zero if im is None else im

    tile_loop(tiles, body)


def last_stage(spec, store, tiles, scale, start):
    def body(at):
        at = pl.multiple_of(at + start, 8)
        freqs = spec.shape[0]
        values = []
        for k in range(freqs):
            re = spec[k, pl.ds(at, 8), :LANES]
            im = None if k in (0, freqs - 1) else spec[k, pl.ds(at, 8), LANES:]
            values.append((re, im))
        for n, v in enumerate(half_inverse(values)):
            store(n, at, v * scale)

    tile_loop(tiles, body)


def greet(groups, me):
    barrier = pltpu.get_barrier_semaphore()
    for d in range(1, groups):
        pl.semaphore_signal(
            barrier, inc=1, device_id={"seq": lax.rem(me + d, groups)}, device_id_type=MESH
        )


def met(groups):
    pl.semaphore_wait(pltpu.get_barrier_semaphore(), groups - 1)


def to_channels(groups, me, narrow, r, src, recv, ss, rs, ls):
    local = pltpu.make_async_copy(
        src.at[r, pl.ds(pl.multiple_of(me * narrow, 8), narrow), :], recv.at[me, r], ls
    )
    out = [local]
    for d in range(1, groups):
        to = lax.rem(me + d, groups)
        out.append(
            pltpu.make_async_remote_copy(
                src_ref=src.at[r, pl.ds(pl.multiple_of(to * narrow, 8), narrow), :],
                dst_ref=recv.at[me, r],
                send_sem=ss.at[d - 1, r],
                recv_sem=rs.at[d - 1, r],
                device_id={"seq": to},
                device_id_type=MESH,
            )
        )
    return out


def to_positions(groups, me, narrow, r, send, dst, ss, rs, ls):
    mine = dst.at[r, pl.ds(pl.multiple_of(me * narrow, 8), narrow), :]
    out = [pltpu.make_async_copy(send.at[me, r], mine, ls)]
    for d in range(1, groups):
        to = lax.rem(me + d, groups)
        out.append(
            pltpu.make_async_remote_copy(
                src_ref=send.at[to, r],
                dst_ref=mine,
                send_sem=ss.at[d - 1, r],
                recv_sem=rs.at[d - 1, r],
                device_id={"seq": to},
                device_id_type=MESH,
            )
        )
    return out


def spread(recv, wide, narrow):
    per = recv.shape[3] // LANES

    def step(s, carry):
        for r in range(recv.shape[1]):
            for h in range(per):
                wide[s * per + h, r * narrow : (r + 1) * narrow, :] = recv[
                    s, r, :, h * LANES : (h + 1) * LANES
                ].astype(jnp.float32)
        return carry

    lax.fori_loop(0, recv.shape[0], step, 0, unroll=4)


def gather_back(wide, send, narrow, r):
    per = send.shape[3] // LANES

    def step(s, carry):
        for h in range(per):
            send[s, r, :, h * LANES : (h + 1) * LANES] = wide[
                s * per + h, r * narrow : (r + 1) * narrow, :
            ].astype(jnp.bfloat16)
        return carry

    lax.fori_loop(0, send.shape[0], step, 0, unroll=4)


def freq_loop(freqs, unroll, body):
    def step(i, carry):
        for j in range(unroll):
            body(i * unroll + j)
        return carry

    lax.fori_loop(0, freqs // unroll, step, 0)


UNROLL = {33: 11, 65: 13}


def conv_kernel(
    groups,
    block,
    lengths,
    gain,
    offset,
    weight_hbm,
    taps,
    first,
    first_b,
    mid,
    mid_b,
    freq,
    last,
    skip,
    decay,
    feats,
    high_ref,
    rest_ref,
    z_ref,
    w_spec_o,
    h_spec_o,
    u_o,
    gate_o,
    edge_o,
    high,
    rest,
    recv,
    wide,
    back,
    send,
    in_ss,
    in_rs,
    out_ss,
    out_rs,
    local,
    aug,
    filt,
    normed,
    w_ref,
    padded,
    wide_taps,
    edges,
    rim_out,
    rim_in,
    rim_sem,
    w_spec,
    h_spec,
    u_ref,
    gate_ref,
    weight,
    move_sem,
):
    me = lax.axis_index("seq")
    narrow = h_spec.shape[1]
    count, freqs = wide.shape[0], high.shape[0]
    rows, width, tok = w_ref.shape
    low, f32 = jnp.bfloat16, jnp.float32
    unroll = UNROLL.get(freqs, 1)
    tables = [
        pltpu.make_async_copy(high_ref, high, local.at[0]),
        pltpu.make_async_copy(rest_ref, rest, local.at[1]),
    ]
    bring = pltpu.make_async_copy(weight_hbm, weight, move_sem.at[0])
    keep_u, keep_gate, keep_h, keep_w = [
        pltpu.make_async_copy(src, dst, move_sem.at[1 + n])
        for n, (src, dst) in enumerate(
            ((u_ref, u_o), (gate_ref, gate_o), (h_spec, h_spec_o), (w_spec, w_spec_o))
        )
    ]
    bring.start()
    for c in tables:
        c.start()
    greet(groups, me)

    gain_row, offset_row = gain[...][None, :], offset[...][None, :]
    for r in range(rows):
        hat, _ = norm_parts(block[r].astype(f32))
        normed[:, r * tok : (r + 1) * tok] = (hat * gain_row + offset_row).T.astype(low)
    piece = 256

    def project(i, carry):
        cols = pl.ds(pl.multiple_of(i * piece, piece), piece)
        part = lax.dot_general(
            weight[:, cols], normed[...], (((0,), (0,)), ((), ())), preferred_element_type=f32
        ).astype(low)
        for r in range(rows):
            u_ref[r, cols, :] = part[:, r * tok : (r + 1) * tok]
        return carry

    bring.wait()
    lax.fori_loop(0, 3 * width // piece, project, 0)
    keep_u.start()
    rim_out[...] = pack_edges([u_ref[r, :, tok - LANES :] for r in range(rows)])
    met(groups)
    rim_copy = pltpu.make_async_remote_copy(
        src_ref=rim_out,
        dst_ref=rim_in,
        send_sem=rim_sem.at[0],
        recv_sem=rim_sem.at[1],
        device_id={"seq": lax.rem(me + 1, groups)},
        device_id_type=MESH,
    )
    rim_copy.start()
    spread_taps(taps, padded, wide_taps)
    lane = lax.broadcasted_iota(jnp.int32, (STRIP, tok), 1)
    masks = [row_masks(lengths, r, me * tok, tok) for r in range(rows)]
    rim_copy.wait()
    edge_o[...] = rim_in[...]
    inward = []
    for r in range(rows):
        same1, same2, live = masks[r]
        edges[...] = unpack_edge(rim_in[...], r)

        def strip(i, carry, r=r, same1=same1, same2=same2, live=live):
            mixes = []
            for g in range(3):
                at = pl.ds(pl.multiple_of(i * STRIP + g * width, STRIP), STRIP)
                tap = [
                    jnp.concatenate([wide_taps[j, at, :]] * (tok // LANES), axis=1)
                    for j in range(3)
                ]
                u = u_ref[r, at, :].astype(f32)
                one, two = window_of(u, lane, edges[at, :])
                mixes.append(tap[0] * u + tap[1] * one * same1 + tap[2] * two * same2)
            at = pl.ds(pl.multiple_of(i * STRIP, STRIP), STRIP)
            gate_ref[r, at, :] = mixes[0] * live
            w_ref[r, at, :] = (mixes[1] * mixes[2] * live).astype(low)
            return carry

        lax.fori_loop(0, width // STRIP, strip, 0)
        ready = to_channels(
            groups, me, narrow, r, w_ref, recv, in_ss, in_rs, local.at[3 + rows + r]
        )
        for c in ready:
            c.start()
        inward = inward + ready

    keep_gate.start()
    net = FilterNet(me, narrow, (first, first_b, mid, mid_b, freq, last, skip, decay, feats), aug)

    def build(i, carry):
        size = CHUNK * LANES
        values = net.build(pl.multiple_of(i * size, LANES), size)
        for j in range(CHUNK):
            filt[i * CHUNK + j] = values[:, j * LANES : (j + 1) * LANES]
        return carry

    lax.fori_loop(0, count // CHUNK, build, 0)
    first_stage(
        lambda at: [filt[n, pl.ds(at, 8), :] for n in range(count)], h_spec, narrow // 8
    )
    for c in tables:
        c.wait()

    def filter_freq_step(k):
        h_spec[k] = split_dot(h_spec[k], high[k], rest[k], False)

    freq_loop(freqs, unroll, filter_freq_step)
    keep_h.start()
    for c in inward:
        c.wait()
    spread(recv, wide, narrow)
    first_stage(
        lambda at: [wide[n, pl.ds(at, 8), :] for n in range(count)], w_spec, rows * narrow // 8
    )

    def forward_step(k):
        w_spec[k] = split_dot(w_spec[k], high[k], rest[k], False)

    def inverse_step(k):
        h = h_spec[k]
        hr, hi = h[:, :LANES], h[:, LANES:]
        parts = []
        for r in range(rows):
            w = w_spec[k, r * narrow : (r + 1) * narrow]
            wr, wi = w[:, :LANES], w[:, LANES:]
            parts.append(jnp.concatenate([wr * hr - wi * hi, wr * hi + wi * hr], axis=1))
        back[k] = split_dot(jnp.concatenate(parts, axis=0), high[k], rest[k], True)

    freq_loop(freqs, unroll, forward_step)
    keep_w.start()
    freq_loop(freqs, unroll, inverse_step)

    def store(n, at, v):
        wide[n, pl.ds(at, 8), :] = v

    outward = []
    for r in range(rows):
        last_stage(back, store, narrow // 8, 1.0 / (2 * count * LANES), r * narrow)
        gather_back(wide, send, narrow, r)
        ready = to_positions(groups, me, narrow, r, send, z_ref, out_ss, out_rs, local.at[3 + r])
        for c in ready:
            c.start()
        outward = outward + ready
    for c in outward + [keep_u, keep_gate, keep_h, keep_w]:
        c.wait()


def conv_back_kernel(
    rows_all,
    groups,
    g_ref,
    w_hbm,
    h_hbm,
    high_ref,
    rest_ref,
    down_hbm,
    ga_hbm,
    y2,
    q_ref,
    gm_ref,
    first,
    first_b,
    mid,
    mid_b,
    freq,
    last,
    skip,
    decay,
    feats,
    gw_ref,
    early_o,
    first_o,
    mid_o,
    last_o,
    high,
    rest,
    recv,
    wide,
    back,
    send,
    in_ss,
    in_rs,
    out_ss,
    out_rs,
    local,
    own,
    core_buf,
    step_buf,
    core_ss,
    core_rs,
    step_ss,
    step_rs,
    aug,
    w_spec,
    h_spec,
    gout,
    gup,
    gdown,
    ga_buf,
    y2_turned,
    ga_sem,
    spec_sem,
    keep_sem,
):
    me = lax.axis_index("seq")
    row = lax.axis_index("row")
    core = lax.rem(row, 2)
    narrow = h_spec.shape[1]
    count, freqs = wide.shape[0], high.shape[0]
    rows = g_ref.shape[0]
    unroll = UNROLL.get(freqs, 1)
    tables = [
        pltpu.make_async_copy(high_ref, high, local.at[0]),
        pltpu.make_async_copy(rest_ref, rest, local.at[1]),
    ]
    piece = ga_buf.shape[2]
    pieces = ga_hbm.shape[1] // piece
    low, f32 = jnp.bfloat16, jnp.float32

    def part_copy(src, buf, sem, i, slot):
        cols = pl.ds(pl.multiple_of(i * piece, piece), piece)
        return pltpu.make_async_copy(src.at[:, cols], buf.at[slot], sem.at[slot])

    def stream(src, buf, sem, body):
        def step(i, carry):
            slot = lax.rem(i, 2)

            @pl.when(i + 1 < pieces)
            def _():
                part_copy(src, buf, sem, i + 1, 1 - slot).start()

            part_copy(src, buf, sem, i, slot).wait()
            body(pl.ds(pl.multiple_of(i * piece, piece), piece), buf[slot])
            return carry

        lax.fori_loop(0, pieces, step, 0)

    bring = pltpu.make_async_copy(down_hbm, gdown, spec_sem.at[2])
    bring.start()
    part_copy(ga_hbm, ga_buf, ga_sem, 0, 0).start()
    spectra = [
        pltpu.make_async_copy(w_hbm, w_spec, spec_sem.at[0]),
        pltpu.make_async_copy(h_hbm, h_spec, spec_sem.at[1]),
    ]
    for c in tables + spectra:
        c.start()
    greet_all(rows_all, groups, me, row)
    inward = []
    for r in range(rows):
        inward = inward + to_channels(
            groups, me, narrow, r, g_ref, recv, in_ss, in_rs, local.at[3 + rows + r]
        )
    for c in inward:
        c.start()
    early = early_crew(groups, me, core, gout, gup, gdown, own, down_hbm)
    early.core_setup(core_buf, core_ss, core_rs, row + 1 - 2 * core)
    early.step_setup(step_buf, step_ss, step_rs, EARLY_STEPS)

    def up_part(cols, part):
        gup[:, cols] = jnp.dot(y2_turned[...], part, preferred_element_type=f32).astype(low)

    up_sum, down_sum, out_sum = early.members
    down_sum.core_start()

    def begin(h):
        for n in range(groups):
            h.core_finish(n)
            if n < h.count(0):
                h.start(0, n)

    y2_turned[...] = y2[...].T
    stream(ga_hbm, ga_buf, ga_sem, up_part)
    up_sum.core_start()
    bring.wait()
    begin(down_sum)
    total = None
    for r in range(rows):
        tok = q_ref.shape[2]
        part = jnp.dot(
            q_ref[r], gm_ref[r * tok : (r + 1) * tok, :], preferred_element_type=f32
        )
        total = part if total is None else total + part
    gout[...] = total.astype(low)
    out_sum.core_start()
    begin(up_sum)
    begin(out_sum)
    for c in tables + spectra:
        c.wait()
    for c in inward:
        c.wait()
    spread(recv, wide, narrow)
    first_stage(
        lambda at: [wide[n, pl.ds(at, 8), :] for n in range(count)], back, rows * narrow // 8
    )

    def forward_step(k):
        back[k, : rows * narrow] = split_dot(back[k, : rows * narrow], high[k], rest[k], False)

    def inverse_step(k):
        h = h_spec[k]
        hr, hi = h[:, :LANES], h[:, LANES:]
        parts = []
        hsum = None
        for r in range(rows):
            w = w_spec[k, r * narrow : (r + 1) * narrow]
            wr, wi = w[:, :LANES], w[:, LANES:]
            g = back[k, r * narrow : (r + 1) * narrow]
            gr, gi = g[:, :LANES], g[:, LANES:]
            parts.append(jnp.concatenate([hr * gr + hi * gi, hr * gi - hi * gr], axis=1))
            pair = (wr * gr + wi * gi, wr * gi - wi * gr)
            hsum = pair if hsum is None else (hsum[0] + pair[0], hsum[1] + pair[1])
        parts.append(jnp.concatenate(hsum, axis=1))
        back[k] = split_dot(jnp.concatenate(parts, axis=0), high[k], rest[k], True)

    freq_loop(freqs, unroll, forward_step)
    freq_loop(freqs, unroll, inverse_step)

    def store(n, at, v):
        wide[n, pl.ds(at, 8), :] = v

    outward = []
    for r in range(rows):
        last_stage(back, store, narrow // 8, 1.0 / (2 * count * LANES), r * narrow)
        gather_back(wide, send, narrow, r)
        ready = to_positions(groups, me, narrow, r, send, gw_ref, out_ss, out_rs, local.at[3 + r])
        for c in ready:
            c.start()
        outward = outward + ready
    last_stage(back, store, narrow // 8, 1.0 / (2 * count * LANES), rows * narrow)
    net = FilterNet(me, narrow, (first, first_b, mid, mid_b, freq, last, skip, decay, feats), aug)
    for out in (first_o, mid_o, last_o):
        out[...] = jnp.zeros_like(out)

    def pull(i, carry):
        size = CHUNK * LANES
        grad = [wide[i * CHUNK + j, rows * narrow :, :] for j in range(CHUNK)]
        net.pull(
            pl.multiple_of(i * size, LANES),
            size,
            jnp.concatenate(grad, axis=1),
            first_o,
            mid_o,
            last_o,
        )
        return carry

    lax.fori_loop(0, count // CHUNK, pull, 0)
    kept = []
    for i in range(early.count(0)):
        early.finish(0, i, False)
        for p, h in enumerate(early.members):
            kept.append(
                pltpu.make_async_copy(
                    own[p].at[h.slot(1) + i], early_o[p].at[i], keep_sem.at[p, i]
                )
            )
            kept[-1].start()
    for c in kept:
        c.wait()
    early.wait_core_sends()
    early.wait_sends()
    for c in outward:
        c.wait()


def conv_scratch(groups, rows, narrow, tok, freqs, count, extra):
    low, f32 = jnp.bfloat16, jnp.float32
    dma = pltpu.SemaphoreType.DMA
    wide_rows = (rows + extra) * narrow
    out = [
        pltpu.VMEM((freqs, LANES, 2 * LANES), low),
        pltpu.VMEM((freqs, LANES, 2 * LANES), low),
        pltpu.VMEM((groups, rows, narrow, tok), low),
        pltpu.VMEM((count, wide_rows, LANES), f32),
    ]
    return out + [
        pltpu.VMEM((freqs, wide_rows, 2 * LANES), f32),
        pltpu.VMEM((groups, rows, narrow, tok), low),
        dma((groups - 1, rows)),
        dma((groups - 1, rows)),
        dma((groups - 1, rows)),
        dma((groups - 1, rows)),
        dma((3 + 2 * rows,)),
    ]


def conv_params(cid):
    return pltpu.CompilerParams(
        collective_id=cid, has_side_effects=True, vmem_limit_bytes=VMEM_LIMIT
    )


def conv_forward(block, lengths, gain, offset, weight, taps, params, tables):
    rows, tok, width = block.shape
    groups = lax.axis_size("seq")
    narrow, length = width // groups, tok * groups
    count = length // LANES
    freqs = count + 1
    low, f32 = jnp.bfloat16, jnp.float32
    vm = pl.BlockSpec(memory_space=pltpu.VMEM)
    sm = pl.BlockSpec(memory_space=pltpu.SMEM)
    hbm = pl.BlockSpec(memory_space=pl.ANY)
    return pl.pallas_call(
        functools.partial(conv_kernel, groups),
        out_shape=(
            jax.ShapeDtypeStruct((rows, width, tok), low),
            jax.ShapeDtypeStruct((freqs, rows * narrow, 2 * LANES), f32),
            jax.ShapeDtypeStruct((freqs, narrow, 2 * LANES), f32),
            jax.ShapeDtypeStruct((rows, 3 * width, tok), low),
            jax.ShapeDtypeStruct((rows, width, tok), f32),
            jax.ShapeDtypeStruct((8, 3 * width), f32),
        ),
        in_specs=[vm, sm, vm, vm, hbm] + [vm] * 10 + [hbm, hbm],
        out_specs=(vm, hbm, hbm, hbm, hbm, vm),
        scratch_shapes=conv_scratch(groups, rows, narrow, tok, freqs, count, 0)
        + [
            pltpu.VMEM((params[-1].shape[0], params[0].shape[1]), f32),
            pltpu.VMEM((count, narrow, LANES), f32),
            pltpu.VMEM((width, rows * tok), low),
            pltpu.VMEM((rows, width, tok), low),
            pltpu.VMEM((8, 3 * width), f32),
            pltpu.VMEM((3, 3 * width, LANES), f32),
            pltpu.VMEM((3 * width, LANES), f32),
            pltpu.VMEM((8, 3 * width), f32),
            pltpu.VMEM((8, 3 * width), f32),
            pltpu.SemaphoreType.DMA((2,)),
            pltpu.VMEM((freqs, rows * narrow, 2 * LANES), f32),
            pltpu.VMEM((freqs, narrow, 2 * LANES), f32),
            pltpu.VMEM((rows, 3 * width, tok), low),
            pltpu.VMEM((rows, width, tok), f32),
            pltpu.VMEM(weight.shape, low),
            pltpu.SemaphoreType.DMA((5,)),
        ],
        compiler_params=conv_params(1),
        name="conv_forward",
    )(block, lengths, gain, offset, weight, taps, *params, *tables)


def conv_backward(grad, w_spec, h_spec, tables, grad_down, grad_pre, y2, q, gm, params):
    rows, _, tok = grad.shape
    freqs, narrow, _ = h_spec.shape
    groups = lax.axis_size("seq")
    count = freqs - 1
    width, ffn = q.shape[1], grad_pre.shape[1]
    half = width // 2
    piece = width
    vm = pl.BlockSpec(memory_space=pltpu.VMEM)
    hbm = pl.BlockSpec(memory_space=pl.ANY)
    low, f32 = jnp.bfloat16, jnp.float32
    dma = pltpu.SemaphoreType.DMA
    kept = groups >> len(EARLY_STEPS)
    feat_rows, hidden = params[-1].shape[0], params[0].shape[1]
    return pl.pallas_call(
        functools.partial(conv_back_kernel, lax.axis_size("row"), groups),
        out_shape=(
            jax.ShapeDtypeStruct(grad.shape, low),
            [jax.ShapeDtypeStruct((kept, n, narrow, half), low) for n in EARLY],
            jax.ShapeDtypeStruct((feat_rows, LANES), f32),
            jax.ShapeDtypeStruct((hidden, LANES), f32),
            jax.ShapeDtypeStruct((narrow, LANES), f32),
        ),
        in_specs=[vm] + [hbm] * 6 + [vm] * 12,
        out_specs=(vm, [hbm] * 3, vm, vm, vm),
        scratch_shapes=conv_scratch(groups, rows, narrow, tok, freqs, count, 1)
        + [
            [pltpu.VMEM((groups, n, narrow, half), low) for n in EARLY],
            [
                pltpu.VMEM((groups, narrow, 4 * half), low),
                pltpu.VMEM((groups, 4 * narrow, half), low),
                pltpu.VMEM((groups, narrow, half), low),
            ],
            [
                [pltpu.VMEM((groups >> (k + 1), n, narrow, half), low) for k in EARLY_STEPS]
                for n in EARLY
            ],
            [dma((groups, 1)) for _ in EARLY],
            [dma((groups, 1)) for _ in EARLY],
            [[dma((groups >> (k + 1),)) for k in EARLY_STEPS] for _ in EARLY],
            [[dma((groups >> (k + 1),)) for k in EARLY_STEPS] for _ in EARLY],
            pltpu.VMEM((feat_rows, hidden), f32),
            pltpu.VMEM(w_spec.shape, f32),
            pltpu.VMEM(h_spec.shape, f32),
            pltpu.VMEM((width, width), low),
            pltpu.VMEM((width, ffn), low),
            pltpu.VMEM((ffn, width), low),
            pltpu.VMEM((2, y2.shape[0], piece), low),
            pltpu.VMEM((width, y2.shape[0]), low),
            dma((2,)),
            dma((3,)),
            dma((len(EARLY), kept)),
        ],
        compiler_params=conv_params(2),
        name="conv_backward",
    )(grad, w_spec, h_spec, *tables, grad_down, grad_pre, y2, q, gm, *params)


def shards(
    block_in,
    lengths,
    mixer_gain,
    mixer_bias,
    in_weight,
    short_taps,
    filter_in,
    filter_in_bias,
    filter_mid,
    filter_mid_bias,
    filter_freq,
    filter_out,
    filter_skip,
    decay_rate,
    out_weight,
    feed_gain,
    feed_bias,
    up_weight,
    down_weight,
    cotangent,
):
    _, tok_count, model_width = block_in.shape
    length = tok_count * lax.axis_size("seq")
    block_float = block_in.astype(jnp.float32)
    tables = tuple(jnp.asarray(t) for t in spectrum_tables(length))
    params = (
        filter_in,
        filter_in_bias,
        filter_mid,
        filter_mid_bias,
        filter_freq,
        filter_out,
        filter_skip,
        decay_rate,
        jnp.asarray(feature_rows(length, filter_in.shape[0])),
    )
    back_home, w_spec, h_spec, projected, gate_out, edges = conv_forward(
        block_in, lengths, mixer_gain, mixer_bias, in_weight, short_taps, params, tables
    )
    conv_float = back_home.astype(jnp.float32)
    product_low = (gate_out * conv_float).astype(jnp.bfloat16)
    mixed = block_float + jnp.einsum(
        "rct,cd->rtd", product_low, out_weight, preferred_element_type=jnp.float32
    )
    normed_two, feed_pull = jax.vjp(layer_norm, mixed, feed_gain, feed_bias)
    normed_two_low = normed_two.astype(jnp.bfloat16)
    pre_act = jnp.einsum(
        "rtd,df->rtf", normed_two_low, up_weight, preferred_element_type=jnp.float32
    )
    activ, gelu_pull = jax.vjp(jax.nn.gelu, pre_act)
    activ_low = activ.astype(jnp.bfloat16)
    block_out = (
        mixed
        + jnp.einsum("rtf,fd->rtd", activ_low, down_weight, preferred_element_type=jnp.float32)
    ).astype(jnp.bfloat16)
    grad_float = cotangent.astype(jnp.float32)
    grad_down = jnp.einsum("rtf,rtd->fd", activ_low, cotangent, preferred_element_type=jnp.float32)
    grad_activ = jnp.einsum(
        "rtd,fd->rtf", cotangent, down_weight, preferred_element_type=jnp.float32
    )
    grad_pre = gelu_pull(grad_activ)[0].astype(jnp.bfloat16)
    grad_normed_two = jnp.einsum(
        "rtf,df->rtd", grad_pre, up_weight, preferred_element_type=jnp.float32
    )
    grad_mixed_part, grad_feed_gain, grad_feed_bias = feed_pull(grad_normed_two)
    grad_mixed = grad_float + grad_mixed_part
    grad_mixed_low = grad_mixed.astype(jnp.bfloat16)
    grad_product = jnp.einsum(
        "rtd,cd->rct", grad_mixed_low, out_weight, preferred_element_type=jnp.float32
    )
    grad_gate_out = grad_product * conv_float
    grad_conv = (grad_product * gate_out).astype(jnp.bfloat16)

    def flat_rows(v):
        return v.reshape(-1, v.shape[-1])

    grad_carried, early, first_sum, mid_sum, last_sum = conv_backward(
        grad_conv,
        w_spec,
        h_spec,
        tables,
        grad_down.astype(jnp.bfloat16),
        flat_rows(grad_pre),
        flat_rows(normed_two_low),
        product_low,
        flat_rows(grad_mixed_low),
        params,
    )
    grad_input, fin, small, last_all = finish(
        grad_carried,
        grad_gate_out,
        projected,
        edges,
        lengths,
        short_taps,
        in_weight,
        block_in,
        grad_mixed,
        (mixer_gain, mixer_bias, grad_feed_gain, grad_feed_bias),
        early,
        (mid_sum, first_sum, last_sum),
    )
    *done, grad_input = unpack(
        fin, small, last_all, grad_input, filter_in.shape[0], filter_mid.shape[0], model_width
    )
    return (block_out, grad_input, *done)


def solution(mesh):
    placed = (
        P("row", "seq", None),
        P("row", None),
        P(),
        P(),
        P(),
        P(),
        P(),
        P(),
        P(),
        P(),
        P(),
        P(),
        P(),
        P(),
        P(),
        P(),
        P(),
        P(),
        P(),
        P("row", "seq", None),
    )
    return jax.shard_map(
        shards,
        mesh=mesh,
        in_specs=placed,
        out_specs=(
            P("row", "seq", None),
            P("row", "seq", None),
            P(),
            P(),
            P("seq", None),
            P(),
            P(),
            P(),
            P(),
            P(),
            P(),
            P(),
            P(),
            P("seq", None),
            P(),
            P(),
            P("seq", None),
            P("seq", None),
        ),
        check_vma=False,
    )
```

```python
import functools
import math

import jax
import jax.numpy as jnp
import numpy as np
from jax import lax
from jax.experimental import pallas as pl
from jax.experimental.pallas import tpu as pltpu
from jax.sharding import PartitionSpec as P

HIGHEST = lax.Precision.HIGHEST


def layer_norm(values, gain, offset):
    center = values - jnp.mean(values, axis=-1, keepdims=True)
    spread = jnp.mean(center * center, axis=-1, keepdims=True)
    return center * lax.rsqrt(spread + 1e-05) * gain + offset


MESH = pl.DeviceIdType.MESH
VMEM_LIMIT = 56 * 1024 * 1024
LANES = 128


def seq_weights(order, groups):
    weights = []
    w = 1
    while w < groups:
        weights.append(w)
        w *= 2
    first = weights[0] + order * (weights[1] - weights[0])
    second = weights[1] - order * (weights[1] - weights[0])
    return [first, second] + weights[2:]


class Halving:
    def __init__(self, groups, me, core, order, parts, own, first=0, base=0):
        self.groups, self.me, self.core, self.parts, self.own, self.first = (
            groups,
            me,
            core,
            parts,
            own,
            first,
        )
        self.order, self.other = (core, 1 - core) if order is None else (order, order)
        self.weights = seq_weights(self.order, groups)
        self.bits = [lax.rem(me // w, 2) for w in self.weights]
        self.steps = len(self.weights)
        self.half = own.shape[3]
        self.base = base * 2 * self.half
        self.source = None
        self.unit = own.shape[2]

    def shard_of(self, n, order):
        weights = seq_weights(order, self.groups)
        at = 0
        for j in range(self.steps):
            bit = lax.rem(self.me // weights[j], 2)
            keep = (n >> (self.steps - 1 - j)) & 1
            at = at + (bit if keep else 1 - bit) * weights[j]
        return at

    def core_setup(self, buf, ss, rs, sib):
        self.buf = buf
        (ref, _, cols, _) = self.parts[0]
        src = (ref if self.source is None else self.source).at[
            :,
            pl.ds(
                pl.multiple_of(self.base + (1 - self.core) * cols * self.half, LANES),
                cols * self.half,
            ),
        ]
        self.core_copy = pltpu.make_async_remote_copy(
            src_ref=src,
            dst_ref=buf,
            send_sem=ss,
            recv_sem=rs,
            device_id={"row": sib},
            device_id_type=MESH,
        )

    def core_start(self):
        self.core_copy.start()

    def core_finish(self):
        self.core_copy.wait_recv()
        (ref, high, cols, _) = self.parts[0]
        first = self.count(0)
        for n in range(self.groups):
            s = self.shard_of(n, self.order)
            for h in range(high):
                lines = pl.ds(pl.multiple_of((s * high + h) * self.unit, 8), self.unit)
                for c in range(cols):
                    mine = ref[
                        lines,
                        pl.ds(
                            pl.multiple_of(
                                self.base + (self.core * cols + c) * self.half, LANES
                            ),
                            self.half,
                        ),
                    ]
                    self.own[n, h * cols + c] = (
                        mine + self.buf[lines, c * self.half : (c + 1) * self.half]
                    )
            if n + 1 == first // 2:
                self.start(0, 0)
            if n + 1 == first:
                self.start(0, 1)

    def pieces(self, k):
        count = self.count(k)
        return [(0, count // 2), (count // 2, count // 2)] if count > 1 else [(0, 1)]

    def step_setup(self, bufs, ss, rs, steps):
        self.step_bufs = dict(zip(steps, bufs))
        self.copies = {}
        for at, k in enumerate(steps):
            for j, (i, size) in enumerate(self.pieces(k)):
                self.copies[k, j] = pltpu.make_async_remote_copy(
                    src_ref=self.own.at[pl.ds(self.slot(k) + i, size)],
                    dst_ref=bufs[at].at[pl.ds(i, size)],
                    send_sem=ss[at].at[j],
                    recv_sem=rs[at].at[j],
                    device_id={"seq": self.me + self.weights[k] * (1 - 2 * self.bits[k])},
                    device_id_type=MESH,
                )

    def slot(self, k):
        return self.groups - (self.groups >> k) - self.first

    def start(self, k, j):
        self.copies[k, j].start()

    def start_step(self, k):
        for j in range(len(self.pieces(k))):
            self.start(k, j)

    def finish(self, k, j):
        self.copies[k, j].wait_recv()
        first, size = self.pieces(k)[j]
        for i in range(first, first + size):
            at = self.slot(k + 1) + i
            self.own[at] = self.own[at] + self.step_bufs[k][i]

    def count(self, k):
        return self.groups >> (k + 1)

    def wait_sends(self):
        for c in self.copies.values():
            c.wait_send()

    def wait_core_sends(self):
        self.core_copy.wait_send()


EARLY = (4, 4, 1)
LATE = (1, 1, 1)
ORDERS = (0, 1, None)
EARLY_STEPS = (1, 1, 1)


class Crew:
    def __init__(self, members):
        self.members = members
        self.steps = members[0].steps

    def core_setup(self, bufs, ss, rs, sib):
        for p, h in enumerate(self.members):
            h.core_setup(bufs[p], ss.at[p], rs.at[p], sib)

    def step_setup(self, bufs, ss, rs, steps):
        for p, h in enumerate(self.members):
            h.step_setup(bufs[p], ss[p], rs[p], steps[p])

    def core_start(self):
        for h in self.members:
            h.core_start()

    def core_finish(self):
        for h in self.members:
            h.core_finish()

    def part(self, k, j):
        for h in self.members:
            if (k, j) in h.copies:
                h.finish(k, j)
                if j == 0 and k + 1 < self.steps:
                    h.start_step(k + 1)

    def advance(self, k):
        self.part(k, 0)
        self.part(k, 1)

    def wait_sends(self):
        for h in self.members:
            h.wait_sends()

    def wait_core_sends(self):
        for h in self.members:
            h.wait_core_sends()


def early_crew(groups, me, core, gout, gup, gdown, owns, down_src):
    parts = [[(gup, 1, 4, 0)], [(gdown, 4, 1, 0)], [(gout, 1, 1, 0)]]
    crew = Crew([Halving(groups, me, core, o, p, w) for o, p, w in zip(ORDERS, parts, owns)])
    crew.members[1].source = down_src
    return crew


def greet_all(rows, groups, me, row):
    barrier = pltpu.get_barrier_semaphore()
    for d in range(1, rows):
        pl.semaphore_signal(
            barrier, inc=1, device_id={"row": lax.rem(row + d, rows)}, device_id_type=MESH
        )
    for d in range(1, groups):
        pl.semaphore_signal(
            barrier, inc=1, device_id={"seq": lax.rem(me + d, groups)}, device_id_type=MESH
        )
    pl.semaphore_wait(barrier, rows + groups - 2)


def row_masks(lengths, row, start, tok):
    where = lax.broadcasted_iota(jnp.int32, (8, tok), 1) + start
    ends = []
    total = 0
    for k in range(lengths.shape[1]):
        total = total + lengths[row, k]
        ends.append(total)

    def doc(at):
        out = jnp.zeros(at.shape, jnp.int32)
        for e in ends:
            out = out + (at >= e).astype(jnp.int32)
        return out

    own = doc(where)
    masks = []
    for lag in (1, 2):
        same = (where >= lag) & (doc(where - lag) == own)
        masks.append(same.astype(jnp.float32)[:1])
    return masks + [(where < total).astype(jnp.float32)[:1]]


def edge_pick(r):
    line = lax.broadcasted_iota(jnp.int32, (8, LANES), 0)
    spot = lax.broadcasted_iota(jnp.int32, (8, LANES), 1)
    pick = (spot == line - 2 * r + LANES - 2) & (line >= 2 * r) & (line < 2 * r + 2)
    return pick.astype(jnp.bfloat16)


def pack_edges(tiles):
    out = None
    for r, tile in enumerate(tiles):
        piece = lax.dot_general(
            edge_pick(r), tile, (((1,), (1,)), ((), ())), preferred_element_type=jnp.float32
        )
        out = piece if out is None else out + piece
    return out


def unpack_edge(lines, r):
    return lax.dot_general(
        lines.astype(jnp.bfloat16),
        edge_pick(r),
        (((0,), (0,)), ((), ())),
        preferred_element_type=jnp.float32,
    )


def window_of(values, lane, edge):
    early, late = edge[:, LANES - 2 : LANES - 1], edge[:, LANES - 1 :]
    one = jnp.where(lane == 0, late, pltpu.roll(values, 1, 1))
    two = jnp.where(lane == 0, early, jnp.where(lane == 1, late, pltpu.roll(values, 2, 1)))
    return one, two


def spread_taps(taps, padded, wide):
    padded[...] = jnp.zeros_like(padded)
    padded[: taps.shape[0], :] = taps[...]
    turned = padded[...].T
    for j in range(taps.shape[0]):
        wide[j] = jnp.broadcast_to(turned[:, j : j + 1], wide.shape[1:])


def norm_parts(values):
    center = values - jnp.mean(values, axis=-1, keepdims=True)
    scale = lax.rsqrt(jnp.mean(center * center, axis=-1, keepdims=True) + 1e-05)
    return center * scale, scale


STRIP = 128


def finish_kernel(
    rows,
    groups,
    gw_ref,
    ggo_ref,
    u_hbm,
    edge_ref,
    lengths,
    taps,
    weight_hbm,
    block_hbm,
    gm_hbm,
    gain,
    offset,
    feed_gain,
    feed_bias,
    early,
    mid_s,
    first_s,
    last,
    gi_ref,
    fin_o,
    small_o,
    gains_o,
    padded,
    wide_taps,
    edges,
    tap_sum,
    gu,
    gu_low,
    rim,
    rim_out,
    rim_in,
    normed,
    gin,
    small,
    own,
    own_early,
    core_buf,
    step_buf,
    early_buf,
    wide_buf,
    small_row,
    small_sum,
    small_part,
    small_done,
    last_row,
    last_sum,
    rim_sem,
    bring_sem,
    u_ref,
    weight,
    block,
    gm_ref,
    move_sem,
    core_ss,
    core_rs,
    step_ss,
    step_rs,
    early_ss,
    early_rs,
    wide_ss,
    wide_rs,
    fin_ss,
    fin_rs,
    srow_ss,
    srow_rs,
    spart_ss,
    spart_rs,
    sdone_ss,
    sdone_rs,
    lrow_ss,
    lrow_rs,
    gain_own,
    gain_row_buf,
    gain_sum,
    grow_ss,
    grow_rs,
    gcast_ss,
    gcast_rs,
):
    me = lax.axis_index("seq")
    row = lax.axis_index("row")
    core = lax.rem(row, 2)
    sib = row + 1 - 2 * core
    chunk = small_part.shape[1]
    held, width, tok = gw_ref.shape
    low, f32 = jnp.bfloat16, jnp.float32

    late = Crew(
        [
            Halving(groups, me, core, o, [(gin, 1, 1, 0)], own[p], base=p)
            for p, o in enumerate(ORDERS)
        ]
    )
    late.core_setup(core_buf, core_ss, core_rs, sib)
    late.step_setup(step_buf, step_ss, step_rs, [range(late.steps)] * len(LATE))
    later = [range(n, late.steps) for n in EARLY_STEPS]
    rest = Crew(
        [
            Halving(groups, me, core, o, (), w, first=groups - e.shape[0])
            for o, w, e in zip(ORDERS, own_early, early)
        ]
    )
    rest.step_setup(early_buf, early_ss, early_rs, later)
    bring = [
        pltpu.make_async_copy(e, w, bring_sem.at[p])
        for p, (w, e) in enumerate(zip(own_early, early))
    ]
    moves = [
        pltpu.make_async_copy(src, dst, move_sem.at[p])
        for p, (src, dst) in enumerate(
            ((u_hbm, u_ref), (block_hbm, block), (weight_hbm, weight), (gm_hbm, gm_ref))
        )
    ]
    for c in bring + moves:
        c.start()
    greet_all(rows, groups, me, row)
    for c in bring:
        c.wait()
    for h, ks in zip(rest.members, later):
        h.start_step(ks[0])
    lrow = [
        pltpu.make_async_remote_copy(
            src_ref=last,
            dst_ref=last_row.at[d - 1],
            send_sem=lrow_ss.at[d - 1],
            recv_sem=lrow_rs.at[d - 1],
            device_id={"row": lax.rem(row + d, rows)},
            device_id_type=MESH,
        )
        for d in range(1, rows)
    ]
    for c in lrow:
        c.start()

    spread_taps(taps, padded, wide_taps)
    tap_sum[...] = jnp.zeros_like(tap_sum)
    lane = lax.broadcasted_iota(jnp.int32, (STRIP, tok), 1)
    moves[0].wait()
    for r in range(held):
        same1, same2, live = row_masks(lengths, r, me * tok, tok)
        edges[...] = unpack_edge(edge_ref[...], r)

        def strip(i, carry, r=r, same1=same1, same2=same2, live=live):
            at = [pl.multiple_of(i * STRIP + g * width, STRIP) for g in range(3)]
            tap = [
                [
                    jnp.concatenate([wide_taps[j, pl.ds(a, STRIP), :]] * (tok // LANES), axis=1)
                    for j in range(3)
                ]
                for a in at
            ]
            u = [u_ref[r, pl.ds(a, STRIP), :].astype(f32) for a in at]
            shifts = [
                window_of(v, lane, edges[pl.ds(a, STRIP), :])
                for v, a in zip(u, at)
            ]
            gate_in, stream = [
                tap[g][0] * u[g] + tap[g][1] * shifts[g][0] * same1 + tap[g][2] * shifts[g][1] * same2
                for g in (1, 2)
            ]
            gw = gw_ref[r, pl.ds(at[0], STRIP), :].astype(f32) * live
            grads = [ggo_ref[r, pl.ds(at[0], STRIP), :] * live, gw * stream, gw * gate_in]
            for g in range(3):
                m1, m2 = grads[g] * same1, grads[g] * same2
                for j, p in enumerate((grads[g] * u[g], m1 * shifts[g][0], m2 * shifts[g][1])):
                    total = p[:, :LANES]
                    for h in range(1, tok // LANES):
                        total = total + p[:, h * LANES : (h + 1) * LANES]
                    tap_sum[j, pl.ds(at[g], STRIP), :] += total
                b1 = pltpu.roll(tap[g][1] * m1, tok - 1, 1)
                b2 = pltpu.roll(tap[g][2] * m2, tok - 2, 1)
                gu[r, pl.ds(at[g], STRIP), :] = (
                    tap[g][0] * grads[g]
                    + jnp.where(lane < tok - 1, b1, 0.0)
                    + jnp.where(lane < tok - 2, b2, 0.0)
                )
                over = jnp.where(lane < tok - 1, 0.0, b1) + jnp.where(lane < tok - 2, 0.0, b2)
                rim[r, pl.ds(at[g], STRIP), :] = over[:, tok - LANES :].astype(low)
            return carry

        lax.fori_loop(0, width // STRIP, strip, 0)
        if r == 0:
            rest.part(1, 0)

    rim_out[...] = pack_edges([rim[r] for r in range(held)])
    rim_copy = pltpu.make_async_remote_copy(
        src_ref=rim_out,
        dst_ref=rim_in,
        send_sem=rim_sem.at[0],
        recv_sem=rim_sem.at[1],
        device_id={"seq": lax.rem(me + groups - 1, groups)},
        device_id_type=MESH,
    )
    rim_copy.start()

    at = mid_s.shape[0] + first_s.shape[0]
    small[:at, :] = jnp.concatenate([mid_s[...], first_s[...]], axis=0)
    small[at:, :] = jnp.zeros((small.shape[0] - at, LANES), f32)
    per = width // LANES

    def put_small(first, line):
        for i in range(line.shape[1] // LANES):
            small[first + i : first + i + 1, :] = line[:, i * LANES : (i + 1) * LANES]

    ones = jnp.ones((8, LANES), low)

    def lane_sums(values):
        high = values.astype(low)
        rest = (values - high.astype(f32)).astype(low)
        dims = (((1,), (1,)), ((), ()))
        return lax.dot_general(ones, high, dims, preferred_element_type=f32) + lax.dot_general(
            ones, rest, dims, preferred_element_type=f32
        )

    for j in range(3):
        put_small(at + 2 * per + 3 * per * j, lane_sums(tap_sum[j])[:1])
    put_small(at + 11 * per, feed_gain[...][None, :])
    put_small(at + 12 * per, feed_bias[...][None, :])
    srow = [
        pltpu.make_async_remote_copy(
            src_ref=small,
            dst_ref=small_row.at[d - 1],
            send_sem=srow_ss.at[d - 1],
            recv_sem=srow_rs.at[d - 1],
            device_id={"row": lax.rem(row + d, rows)},
            device_id_type=MESH,
        )
        for d in range(1, rows)
    ]
    for c in srow:
        c.start()
    gain_row, offset_row = gain[...][None, :], offset[...][None, :]
    for c in moves[1:]:
        c.wait()
    for r in range(held):
        hat, _ = norm_parts(block[r].astype(f32))
        normed[:, r * tok : (r + 1) * tok] = (hat * gain_row + offset_row).T.astype(low)
    rest.part(1, 1)
    for c in srow + lrow:
        c.wait()
    total = small[...]
    tail = last[...]
    for d in range(rows - 1):
        total = total + small_row[d]
        tail = tail + last_row[d]
    small_sum[...] = total
    last_sum[...] = tail
    spart = []
    for d in range(1, groups):
        to = lax.rem(me + d, groups)
        spart.append(
            pltpu.make_async_remote_copy(
                src_ref=small_sum.at[pl.ds(to * chunk, chunk)],
                dst_ref=small_part.at[d - 1],
                send_sem=spart_ss.at[d - 1],
                recv_sem=spart_rs.at[d - 1],
                device_id={"seq": to},
                device_id_type=MESH,
            )
        )
    for c in spart:
        c.start()

    rim_copy.wait()
    for r in range(held):
        add = unpack_edge(rim_in[...], r)
        split = tok - LANES
        gu_low[:, r * tok : r * tok + split] = gu[r, :, :split].astype(low)
        gu_low[:, r * tok + split : (r + 1) * tok] = (gu[r, :, split:] + add).astype(low)

    rest.part(2, 0)
    piece = 256

    def weight_grad(i, carry):
        cols = pl.ds(pl.multiple_of(i * piece, piece), piece)
        gin[:, cols] = lax.dot_general(
            normed[...], gu_low[cols, :], (((1,), (1,)), ((), ())), preferred_element_type=f32
        ).astype(low)
        return carry

    lax.fori_loop(0, 3 * width // piece, weight_grad, 0)
    late.core_start()
    rest.part(2, 1)

    fin = []

    def close(crew, arrays, units, base):
        place = sum((EARLY + LATE)[:base])
        for p, (h, array, count) in enumerate(zip(crew.members, arrays, units)):
            q, slot = base + p, array.shape[0] - 1
            w, n = 2, 0
            while w < rows:
                bit = lax.rem(row // w, 2)
                c = pltpu.make_async_remote_copy(
                    src_ref=h.own.at[slot],
                    dst_ref=wide_buf[q].at[n],
                    send_sem=wide_ss.at[n, q],
                    recv_sem=wide_rs.at[n, q],
                    device_id={"row": row + w * (1 - 2 * bit)},
                    device_id_type=MESH,
                )
                c.start()
                c.wait()
                h.own[slot] = h.own[slot] + wide_buf[q][n]
                w, n = 2 * w, n + 1
            fin_o[core, place : place + count] = h.own[slot]
            c = pltpu.make_async_remote_copy(
                src_ref=h.own.at[slot],
                dst_ref=fin_o.at[core, pl.ds(place, count)],
                send_sem=fin_ss.at[q],
                recv_sem=fin_rs.at[q],
                device_id={"row": sib},
                device_id_type=MESH,
            )
            c.start()
            fin.append(c)
            place += count

    gains = [jnp.zeros((1, width), f32), jnp.zeros((1, width), f32)]
    for r in range(held):
        turned = lax.dot_general(
            weight[...],
            gu_low[:, r * tok : (r + 1) * tok],
            (((1,), (0,)), ((), ())),
            preferred_element_type=f32,
        )
        grad = turned.T
        hat, scale = norm_parts(block[r].astype(f32))
        gains[0] = gains[0] + jnp.sum(grad * hat, axis=0, keepdims=True)
        gains[1] = gains[1] + jnp.sum(grad, axis=0, keepdims=True)
        pulled = grad * gain_row
        pulled = pulled - jnp.mean(pulled, axis=-1, keepdims=True)
        pulled = pulled - hat * jnp.mean(pulled * hat, axis=-1, keepdims=True)
        gi_ref[r] = gm_ref[r] + scale * pulled
        if r == 0:
            late.core_finish()
            for c in spart:
                c.wait()
            total = small_sum[pl.ds(me * chunk, chunk)]
            for d in range(groups - 1):
                total = total + small_part[d]
            small_done[:chunk] = total
            small_done[chunk:] = last_sum[...]
            small_o[me] = small_done[...]
            sdone = [
                pltpu.make_async_remote_copy(
                    src_ref=small_done,
                    dst_ref=small_o.at[me],
                    send_sem=sdone_ss.at[d - 1],
                    recv_sem=sdone_rs.at[d - 1],
                    device_id={"seq": lax.rem(me + d, groups)},
                    device_id_type=MESH,
                )
                for d in range(1, groups)
            ]
            for c in sdone:
                c.start()
    gain_own[...] = jnp.zeros_like(gain_own)
    for g in range(2):
        for n in range(per):
            line = g * per + n
            gain_own[line : line + 1, :] = gains[g][:, n * LANES : (n + 1) * LANES]
    grow = [
        pltpu.make_async_remote_copy(
            src_ref=gain_own,
            dst_ref=gain_row_buf.at[d - 1],
            send_sem=grow_ss.at[d - 1],
            recv_sem=grow_rs.at[d - 1],
            device_id={"row": lax.rem(row + d, rows)},
            device_id_type=MESH,
        )
        for d in range(1, rows)
    ]
    for c in grow:
        c.start()

    late.advance(0)
    for c in grow:
        c.wait()
    total = gain_own[...]
    for d in range(rows - 1):
        total = total + gain_row_buf[d]
    gain_sum[...] = total
    gains_o[me] = total
    gcast = [
        pltpu.make_async_remote_copy(
            src_ref=gain_sum,
            dst_ref=gains_o.at[me],
            send_sem=gcast_ss.at[d - 1],
            recv_sem=gcast_rs.at[d - 1],
            device_id={"seq": lax.rem(me + d, groups)},
            device_id_type=MESH,
        )
        for d in range(1, groups)
    ]
    for c in gcast:
        c.start()
    for k in range(3, rest.steps):
        rest.advance(k)
    close(rest, early, EARLY, 0)
    late.advance(1)
    for k in range(2, late.steps):
        late.advance(k)

    close(late, own, LATE, len(EARLY))
    late.wait_core_sends()
    late.wait_sends()
    rest.wait_sends()
    for c in sdone + gcast:
        c.wait()
    for c in fin:
        c.wait()


def finish(gw, ggo, u, edge, lengths, taps, weight, block, gm, vectors, early, sums):
    rows, groups = lax.axis_size("row"), lax.axis_size("seq")
    held, width, tok = gw.shape
    unit = width // groups
    half = width // 2
    wide = max(1, rows.bit_length() - 2)
    low, f32 = jnp.bfloat16, jnp.float32
    steps = groups.bit_length() - 1
    later = [range(n, steps) for n in EARLY_STEPS]
    used = sums[0].shape[0] + sums[1].shape[0] + 13 * (width // LANES)
    lines = used + -used % (8 * groups)
    chunk = lines // groups
    lead = -(-2 * (width // LANES) // 8) * 8
    last = sums[2]
    dma = pltpu.SemaphoreType.DMA
    vm = pl.BlockSpec(memory_space=pltpu.VMEM)
    sm = pl.BlockSpec(memory_space=pltpu.SMEM)
    hbm = pl.BlockSpec(memory_space=pl.ANY)
    return pl.pallas_call(
        functools.partial(finish_kernel, rows, groups),
        out_shape=(
            jax.ShapeDtypeStruct(gm.shape, f32),
            jax.ShapeDtypeStruct((2, sum(EARLY) + sum(LATE), unit, half), low),
            jax.ShapeDtypeStruct((groups, chunk + last.shape[0], LANES), f32),
            jax.ShapeDtypeStruct((groups, lead, LANES), f32),
        ),
        in_specs=[vm, vm, hbm, vm, sm, vm, hbm, hbm, hbm] + [vm] * 4 + [[hbm] * 3] + [vm] * 3,
        out_specs=(vm,) * 4,
        scratch_shapes=[
            pltpu.VMEM((8, 3 * width), f32),
            pltpu.VMEM((3, 3 * width, LANES), f32),
            pltpu.VMEM((3 * width, LANES), f32),
            pltpu.VMEM((3, 3 * width, LANES), f32),
            pltpu.VMEM((held, 3 * width, tok), f32),
            pltpu.VMEM((3 * width, held * tok), low),
            pltpu.VMEM((held, 3 * width, LANES), low),
            pltpu.VMEM((8, 3 * width), f32),
            pltpu.VMEM((8, 3 * width), f32),
            pltpu.VMEM((width, held * tok), low),
            pltpu.VMEM((width, 3 * width), low),
            pltpu.VMEM((lines, LANES), f32),
            [pltpu.VMEM((groups, n, unit, half), low) for n in LATE],
            [pltpu.VMEM(e.shape, low) for e in early],
            [pltpu.VMEM((width, n * half), low) for n in LATE],
            [
                [pltpu.VMEM((groups >> (k + 1), n, unit, half), low) for k in range(steps)]
                for n in LATE
            ],
            [
                [pltpu.VMEM((groups >> (k + 1), n, unit, half), low) for k in ks]
                for ks, n in zip(later, EARLY)
            ],
            [pltpu.VMEM((wide, n, unit, half), low) for n in EARLY + LATE],
            pltpu.VMEM((rows - 1, lines, LANES), f32),
            pltpu.VMEM((lines, LANES), f32),
            pltpu.VMEM((groups - 1, chunk, LANES), f32),
            pltpu.VMEM((chunk + last.shape[0], LANES), f32),
            pltpu.VMEM((rows - 1,) + last.shape, f32),
            pltpu.VMEM(last.shape, f32),
            dma((2,)),
            dma((3,)),
            pltpu.VMEM(u.shape, low),
            pltpu.VMEM(weight.shape, low),
            pltpu.VMEM(block.shape, low),
            pltpu.VMEM(gm.shape, f32),
            dma((4,)),
            dma((len(LATE),)),
            dma((len(LATE),)),
            [[dma((2,)) for k in range(steps)] for _ in LATE],
            [[dma((2,)) for k in range(steps)] for _ in LATE],
            [[dma((2,)) for k in ks] for ks in later],
            [[dma((2,)) for k in ks] for ks in later],
            dma((wide, 6)),
            dma((wide, 6)),
            dma((6,)),
            dma((6,)),
            dma((rows - 1,)),
            dma((rows - 1,)),
            dma((groups - 1,)),
            dma((groups - 1,)),
            dma((groups - 1,)),
            dma((groups - 1,)),
            dma((rows - 1,)),
            dma((rows - 1,)),
            pltpu.VMEM((lead, LANES), f32),
            pltpu.VMEM((rows - 1, lead, LANES), f32),
            pltpu.VMEM((lead, LANES), f32),
            dma((rows - 1,)),
            dma((rows - 1,)),
            dma((groups - 1,)),
            dma((groups - 1,)),
        ],
        compiler_params=pltpu.CompilerParams(
            collective_id=0, has_side_effects=True, vmem_limit_bytes=VMEM_LIMIT
        ),
        name="finish",
    )(gw, ggo, u, edge, lengths, taps, weight, block, gm, *vectors, early, *sums)


def unpack_kernel(
    feat,
    fin,
    packed,
    leads,
    gi,
    gain_o,
    bias_o,
    in_o,
    taps_o,
    first_o,
    first_b_o,
    mid_o,
    mid_b_o,
    freq_o,
    last_o,
    skip_o,
    out_o,
    feed_gain_o,
    feed_bias_o,
    up_o,
    down_o,
    gi_o,
    small,
    last,
):
    f32 = jnp.float32
    chunk, narrow = small.shape[0] // packed.shape[0], last.shape[0] // packed.shape[0]
    for g in range(packed.shape[0]):
        small[g * chunk : (g + 1) * chunk] = packed[g, :chunk]
        last[g * narrow : (g + 1) * narrow] = packed[g, chunk:]
    gi_o[...] = gi[...]
    unit, half = fin.shape[2], fin.shape[3]
    hidden = mid_o.shape[0]
    width = gain_o.shape[0]
    per = width // LANES
    outs = [(up_o, 1, 4, 0, 0), (down_o, 4, 1, 4, 0), (out_o, 1, 1, 8, 0)]
    outs = outs + [(in_o, 1, 1, 9 + p, 2 * p) for p in range(3)]
    for core in range(2):
        for out, high, cols, first, base in outs:
            for h in range(high):
                for c in range(cols):
                    at = (base + core * cols + c) * half
                    out[h * unit : (h + 1) * unit, at : at + half] = fin[
                        core, first + h * cols + c
                    ].astype(f32)

    def line(first, count):
        pieces = [small[first + i : first + i + 1, :] for i in range(count)]
        return jnp.concatenate(pieces, axis=1)

    at = hidden + -(-(feat + 1) // 8) * 8
    total = leads[0]
    for g in range(1, leads.shape[0]):
        total = total + leads[g]
    for out, first in ((gain_o, 0), (bias_o, per)):
        out[...] = jnp.concatenate([total[first + i : first + i + 1] for i in range(per)], axis=1)[0]
    for j in range(3):
        taps_o[j : j + 1, :] = line(at + 2 * per + 3 * per * j, 3 * per)
    feed_gain_o[...] = line(at + 11 * per, per)[0]
    feed_bias_o[...] = line(at + 12 * per, per)[0]
    first_o[...] = small[hidden : hidden + feat, :hidden]
    first_b_o[...] = small[hidden + feat : hidden + feat + 1, :hidden][0]
    mid_o[...] = small[:hidden, :hidden]
    shape = (hidden, hidden)
    same = lax.broadcasted_iota(jnp.int32, shape, 0) == lax.broadcasted_iota(jnp.int32, shape, 1)
    for out, col in ((mid_b_o, hidden), (freq_o, hidden + 1)):
        out[...] = jnp.sum(
            jnp.where(same, small[:hidden, col : col + 1], 0.0), axis=0, keepdims=True
        )[0]
    turned = last[...].T
    last_o[...] = turned[:hidden]
    skip_o[...] = turned[hidden : hidden + 1][0]


def unpack(fin, packed, leads, gi, feat, hidden, width):
    f32 = jnp.float32
    unit = fin.shape[2]
    vm = pl.BlockSpec(memory_space=pltpu.VMEM)
    shapes = [
        (width,),
        (width,),
        (unit, 3 * width),
        (3, 3 * width),
        (feat, hidden),
        (hidden,),
        (hidden, hidden),
        (hidden,),
        (hidden,),
        (hidden, width),
        (width,),
        (unit, width),
        (width,),
        (width,),
        (unit, 4 * width),
        (4 * unit, width),
        gi.shape,
    ]
    return pl.pallas_call(
        functools.partial(unpack_kernel, feat),
        out_shape=tuple(jax.ShapeDtypeStruct(x, f32) for x in shapes),
        in_specs=[vm] * 4,
        out_specs=(vm,) * len(shapes),
        scratch_shapes=[
            pltpu.VMEM((packed.shape[0] * packed.shape[1] - width, LANES), f32),
            pltpu.VMEM((width, LANES), f32),
        ],
        compiler_params=pltpu.CompilerParams(vmem_limit_bytes=VMEM_LIMIT),
        name="unpack",
    )(fin, packed, leads, gi)


def spectrum_tables(length):
    period = 2 * length
    first = period // LANES
    k1 = np.arange(first // 2 + 1, dtype=np.int64)[:, None, None]
    n2 = np.arange(LANES, dtype=np.int64)[None, :, None]
    k2 = np.arange(LANES, dtype=np.int64)[None, None, :]
    angle = 2.0 * np.pi / period * (n2 * (k1 + first * k2) % period)
    full = np.concatenate([np.cos(angle), np.sin(angle)], axis=2).astype(np.float32)
    high = full.astype(jnp.bfloat16)
    rest = (full - high.astype(np.float32)).astype(jnp.bfloat16)
    return high, rest


def feature_rows(length, feat_count):
    bands = (feat_count - 1) // 2
    at = np.arange(length, dtype=np.int64)[None, :]
    angle = 2.0 * np.pi / length * (at * np.arange(1, bands + 1)[:, None] % length)
    rows = [at / length, np.cos(angle), -np.sin(angle), np.ones((1, length))]
    rows = np.concatenate(rows, axis=0)
    pad = -rows.shape[0] % 8
    return np.pad(rows, ((0, pad), (0, 0))).astype(np.float32)


def sin_cos(x):
    n = jnp.round(x * (2.0 / math.pi))
    r = x - n * 1.5703125
    r = r - n * 4.837512969970703125e-4
    r = r - n * 7.549789948768648e-8
    z = r * r
    s = r + r * z * (-1.6666654611e-1 + z * (8.3321608736e-3 - z * 1.9515295891e-4))
    c = (
        1.0
        - 0.5 * z
        + z * z * (4.166664568298827e-2 + z * (-1.388731625493765e-3 + z * 2.443315711809948e-5))
    )
    q = n.astype(jnp.int32) & 3
    odd = (q & 1) == 1
    sine = jnp.where(odd, c, s)
    cosine = jnp.where(odd, s, c)
    sine = jnp.where(q >= 2, -sine, sine)
    cosine = jnp.where((q == 1) | (q == 2), -cosine, cosine)
    return sine, cosine


def exact_dot(p, q, left, right):
    low = jnp.bfloat16

    def dot(x, y):
        return lax.dot_general(
            x, y, (((left,), (right,)), ((), ())), preferred_element_type=jnp.float32
        )

    ph, qh = p.astype(low), q.astype(low)
    pl_, ql = (p - ph.astype(jnp.float32)).astype(low), (q - qh.astype(jnp.float32)).astype(low)
    return dot(ph, qh) + (dot(pl_, qh) + dot(ph, ql))


def column_of(row):
    size = row.shape[1]
    shape = (size, size)
    same = lax.broadcasted_iota(jnp.int32, shape, 0) == lax.broadcasted_iota(jnp.int32, shape, 1)
    return jnp.sum(jnp.where(same, row, 0.0), axis=1, keepdims=True)


class FilterNet:
    def __init__(self, me, narrow, params, aug):
        first, first_b, mid, mid_b, freq, last, skip, decay, self.feats = params
        feat = first.shape[0]
        aug[...] = jnp.zeros_like(aug)
        aug[:feat, :] = first[...]
        aug[feat : feat + 1, :] = first_b[...][None, :]
        self.aug = aug
        self.mid = mid
        self.mid_b = column_of(mid_b[...][None, :])
        self.freq = column_of(freq[...][None, :])
        width = skip.shape[0]
        shape = (narrow, width)
        pick = (
            lax.broadcasted_iota(jnp.int32, shape, 1)
            == lax.broadcasted_iota(jnp.int32, shape, 0) + me * narrow
        )
        self.skip = jnp.sum(jnp.where(pick, skip[...][None, :], 0.0), axis=1, keepdims=True)
        self.decay = jnp.sum(jnp.where(pick, decay[...][None, :], 0.0), axis=1, keepdims=True)
        self.last = exact_dot(pick.astype(jnp.float32), last[...], 1, 1)
        self.narrow = narrow

    def layers(self, at, size):
        feats = self.feats[:, pl.ds(at, size)]
        pre1 = exact_dot(self.aug[...], feats, 0, 0)
        a1, c1 = sin_cos(self.freq * pre1)
        pre2 = exact_dot(self.mid[...], a1, 0, 0) + self.mid_b
        a2, c2 = sin_cos(self.freq * pre2)
        return feats, pre1, a1, c1, pre2, a2, c2

    def fade(self, at, size):
        where = lax.broadcasted_iota(jnp.int32, (self.narrow, size), 1) + at
        return jnp.exp(-self.decay * where.astype(jnp.float32)), where

    def build(self, at, size):
        a2 = self.layers(at, size)[5]
        fade, where = self.fade(at, size)
        return exact_dot(self.last, a2, 1, 0) * fade + jnp.where(where == 0, self.skip, 0.0)

    def pull(self, at, size, grad, first_o, mid_o, last_o):
        feats, pre1, a1, c1, pre2, a2, c2 = self.layers(at, size)
        fade, where = self.fade(at, size)
        hidden = a1.shape[0]
        raw = grad * fade
        last_o[:, :hidden] += exact_dot(raw, a2, 1, 1)
        last_o[:, hidden : hidden + 1] += jnp.sum(
            jnp.where(where == 0, grad, 0.0), axis=1, keepdims=True
        )
        turned2 = exact_dot(self.last, raw, 0, 0) * c2
        freq = jnp.sum(turned2 * pre2, axis=1, keepdims=True)
        down2 = turned2 * self.freq
        mid_o[:, :hidden] += exact_dot(a1, down2, 1, 1)
        mid_o[:, hidden : hidden + 1] += jnp.sum(down2, axis=1, keepdims=True)
        turned1 = exact_dot(self.mid[...], down2, 1, 0) * c1
        freq = freq + jnp.sum(turned1 * pre1, axis=1, keepdims=True)
        mid_o[:, hidden + 1 : hidden + 2] += freq
        down1 = turned1 * self.freq
        first_o[:, :hidden] += exact_dot(feats, down1, 1, 1)


CHUNK = 4


def half_dft(x):
    count = 2 * len(x)
    if count == 2:
        return [(x[0], None), (x[0], None)]
    even, odd = half_dft(x[0::2]), half_dft(x[1::2])
    out = [None] * (count // 2 + 1)
    for k in range(count // 4 + 1):
        er, ei = even[k]
        orr, oi = odd[k]
        if k == 0:
            out[0] = (er + orr, None)
            out[count // 2] = (er - orr, None)
        elif 4 * k == count:
            out[k] = (er, -orr)
        else:
            c, s = math.cos(2 * math.pi * k / count), math.sin(2 * math.pi * k / count)
            tr = orr * c + oi * s
            ti = oi * c - orr * s
            out[k] = (er + tr, ei + ti)
            out[count // 2 - k] = (er - tr, ti - ei)
    return out


def half_inverse(spec):
    count = 2 * (len(spec) - 1)
    if count == 2:
        return [spec[0][0] + spec[1][0]]
    even, odd = [], []
    for k in range(count // 4 + 1):
        ar, ai = spec[k]
        br, bi = spec[count // 2 - k]
        if k == 0:
            even.append((ar + br, None))
            odd.append((ar - br, None))
        elif 4 * k == count:
            even.append((ar + ar, None))
            odd.append((-(ai + ai), None))
        else:
            c, s = math.cos(2 * math.pi * k / count), math.sin(2 * math.pi * k / count)
            dr, di = ar - br, ai + bi
            even.append((ar + br, ai - bi))
            odd.append((dr * c - di * s, dr * s + di * c))
    out = [None] * (count // 2)
    out[0::2] = half_inverse(even)
    out[1::2] = half_inverse(odd)
    return out


def turn_of(table):
    cos, sin = table[:, :LANES], table[:, LANES:]
    return jnp.concatenate(
        [jnp.concatenate([cos, -sin], axis=1), jnp.concatenate([sin, cos], axis=1)], axis=0
    )


def split_dot(a, high, rest, back):
    a_high = a.astype(jnp.bfloat16)
    a_rest = (a - a_high.astype(jnp.float32)).astype(jnp.bfloat16)
    dims = (((1,), (1 if back else 0,)), ((), ()))
    high, rest = turn_of(high), turn_of(rest)

    def dot(p, q):
        return lax.dot_general(p, q, dims, preferred_element_type=jnp.float32)

    rows = a.shape[0]
    both = dot(jnp.concatenate([a_high, a_rest], axis=0), high)
    return both[:rows] + (both[rows:] + dot(a_high, rest))


def tile_loop(tiles, body):
    def step(i, carry):
        body(pl.multiple_of(i * 8, 8))
        return carry

    lax.fori_loop(0, tiles, step, 0, unroll=3 if tiles % 3 == 0 else 1)


def first_stage(load, spec, tiles):
    zero = jnp.zeros((8, LANES), jnp.float32)

    def body(at):
        for k, (re, im) in enumerate(half_dft(load(at))):
            spec[k, pl.ds(at, 8), :LANES] = re
            spec[k, pl.ds(at, 8), LANES:] = zero if im is None else im

    tile_loop(tiles, body)


def last_stage(spec, store, tiles, scale, start):
    def body(at):
        at = pl.multiple_of(at + start, 8)
        freqs = spec.shape[0]
        values = []
        for k in range(freqs):
            re = spec[k, pl.ds(at, 8), :LANES]
            im = None if k in (0, freqs - 1) else spec[k, pl.ds(at, 8), LANES:]
            values.append((re, im))
        for n, v in enumerate(half_inverse(values)):
            store(n, at, v * scale)

    tile_loop(tiles, body)


def greet(groups, me):
    barrier = pltpu.get_barrier_semaphore()
    for d in range(1, groups):
        pl.semaphore_signal(
            barrier, inc=1, device_id={"seq": lax.rem(me + d, groups)}, device_id_type=MESH
        )


def met(groups):
    pl.semaphore_wait(pltpu.get_barrier_semaphore(), groups - 1)


def to_channels(groups, me, narrow, r, src, recv, ss, rs, ls):
    local = pltpu.make_async_copy(
        src.at[r, pl.ds(pl.multiple_of(me * narrow, 8), narrow), :], recv.at[me, r], ls
    )
    out = [local]
    for d in range(1, groups):
        to = lax.rem(me + d, groups)
        out.append(
            pltpu.make_async_remote_copy(
                src_ref=src.at[r, pl.ds(pl.multiple_of(to * narrow, 8), narrow), :],
                dst_ref=recv.at[me, r],
                send_sem=ss.at[d - 1, r],
                recv_sem=rs.at[d - 1, r],
                device_id={"seq": to},
                device_id_type=MESH,
            )
        )
    return out


def to_positions(groups, me, narrow, r, send, dst, ss, rs, ls):
    mine = dst.at[r, pl.ds(pl.multiple_of(me * narrow, 8), narrow), :]
    out = [pltpu.make_async_copy(send.at[me, r], mine, ls)]
    for d in range(1, groups):
        to = lax.rem(me + d, groups)
        out.append(
            pltpu.make_async_remote_copy(
                src_ref=send.at[to, r],
                dst_ref=mine,
                send_sem=ss.at[d - 1, r],
                recv_sem=rs.at[d - 1, r],
                device_id={"seq": to},
                device_id_type=MESH,
            )
        )
    return out


def spread(recv, wide, narrow):
    per = recv.shape[3] // LANES

    def step(s, carry):
        for r in range(recv.shape[1]):
            for h in range(per):
                wide[s * per + h, r * narrow : (r + 1) * narrow, :] = recv[
                    s, r, :, h * LANES : (h + 1) * LANES
                ].astype(jnp.float32)
        return carry

    lax.fori_loop(0, recv.shape[0], step, 0, unroll=4)


def gather_back(wide, send, narrow, r):
    per = send.shape[3] // LANES

    def step(s, carry):
        for h in range(per):
            send[s, r, :, h * LANES : (h + 1) * LANES] = wide[
                s * per + h, r * narrow : (r + 1) * narrow, :
            ].astype(jnp.bfloat16)
        return carry

    lax.fori_loop(0, send.shape[0], step, 0, unroll=4)


def freq_loop(freqs, unroll, body):
    def step(i, carry):
        for j in range(unroll):
            body(i * unroll + j)
        return carry

    lax.fori_loop(0, freqs // unroll, step, 0)


UNROLL = {33: 11, 65: 13}


def conv_kernel(
    groups,
    block,
    lengths,
    gain,
    offset,
    weight_hbm,
    taps,
    first,
    first_b,
    mid,
    mid_b,
    freq,
    last,
    skip,
    decay,
    feats,
    high_ref,
    rest_ref,
    z_ref,
    w_spec_o,
    h_spec_o,
    u_o,
    gate_o,
    edge_o,
    high,
    rest,
    recv,
    wide,
    back,
    send,
    in_ss,
    in_rs,
    out_ss,
    out_rs,
    local,
    aug,
    filt,
    normed,
    w_ref,
    padded,
    wide_taps,
    edges,
    rim_out,
    rim_in,
    rim_sem,
    w_spec,
    h_spec,
    u_ref,
    gate_ref,
    weight,
    move_sem,
):
    me = lax.axis_index("seq")
    narrow = h_spec.shape[1]
    count, freqs = wide.shape[0], high.shape[0]
    rows, width, tok = w_ref.shape
    low, f32 = jnp.bfloat16, jnp.float32
    unroll = UNROLL.get(freqs, 1)
    tables = [
        pltpu.make_async_copy(high_ref, high, local.at[0]),
        pltpu.make_async_copy(rest_ref, rest, local.at[1]),
    ]
    bring = pltpu.make_async_copy(weight_hbm, weight, move_sem.at[0])
    keep_u, keep_gate, keep_h, keep_w = [
        pltpu.make_async_copy(src, dst, move_sem.at[1 + n])
        for n, (src, dst) in enumerate(
            ((u_ref, u_o), (gate_ref, gate_o), (h_spec, h_spec_o), (w_spec, w_spec_o))
        )
    ]
    bring.start()
    for c in tables:
        c.start()
    greet(groups, me)

    gain_row, offset_row = gain[...][None, :], offset[...][None, :]
    for r in range(rows):
        hat, _ = norm_parts(block[r].astype(f32))
        normed[:, r * tok : (r + 1) * tok] = (hat * gain_row + offset_row).T.astype(low)
    piece = 256

    def project(i, carry):
        cols = pl.ds(pl.multiple_of(i * piece, piece), piece)
        part = lax.dot_general(
            weight[:, cols], normed[...], (((0,), (0,)), ((), ())), preferred_element_type=f32
        ).astype(low)
        for r in range(rows):
            u_ref[r, cols, :] = part[:, r * tok : (r + 1) * tok]
        return carry

    bring.wait()
    lax.fori_loop(0, 3 * width // piece, project, 0)
    keep_u.start()
    rim_out[...] = pack_edges([u_ref[r, :, tok - LANES :] for r in range(rows)])
    met(groups)
    rim_copy = pltpu.make_async_remote_copy(
        src_ref=rim_out,
        dst_ref=rim_in,
        send_sem=rim_sem.at[0],
        recv_sem=rim_sem.at[1],
        device_id={"seq": lax.rem(me + 1, groups)},
        device_id_type=MESH,
    )
    rim_copy.start()
    spread_taps(taps, padded, wide_taps)
    lane = lax.broadcasted_iota(jnp.int32, (STRIP, tok), 1)
    masks = [row_masks(lengths, r, me * tok, tok) for r in range(rows)]
    rim_copy.wait()
    edge_o[...] = rim_in[...]
    inward = []
    for r in range(rows):
        same1, same2, live = masks[r]
        edges[...] = unpack_edge(rim_in[...], r)

        def strip(i, carry, r=r, same1=same1, same2=same2, live=live):
            mixes = []
            for g in range(3):
                at = pl.ds(pl.multiple_of(i * STRIP + g * width, STRIP), STRIP)
                tap = [
                    jnp.concatenate([wide_taps[j, at, :]] * (tok // LANES), axis=1)
                    for j in range(3)
                ]
                u = u_ref[r, at, :].astype(f32)
                one, two = window_of(u, lane, edges[at, :])
                mixes.append(tap[0] * u + tap[1] * one * same1 + tap[2] * two * same2)
            at = pl.ds(pl.multiple_of(i * STRIP, STRIP), STRIP)
            gate_ref[r, at, :] = mixes[0] * live
            w_ref[r, at, :] = (mixes[1] * mixes[2] * live).astype(low)
            return carry

        lax.fori_loop(0, width // STRIP, strip, 0)
        ready = to_channels(
            groups, me, narrow, r, w_ref, recv, in_ss, in_rs, local.at[3 + rows + r]
        )
        for c in ready:
            c.start()
        inward = inward + ready

    keep_gate.start()
    net = FilterNet(me, narrow, (first, first_b, mid, mid_b, freq, last, skip, decay, feats), aug)

    def build(i, carry):
        size = CHUNK * LANES
        values = net.build(pl.multiple_of(i * size, LANES), size)
        for j in range(CHUNK):
            filt[i * CHUNK + j] = values[:, j * LANES : (j + 1) * LANES]
        return carry

    lax.fori_loop(0, count // CHUNK, build, 0)
    first_stage(
        lambda at: [filt[n, pl.ds(at, 8), :] for n in range(count)], h_spec, narrow // 8
    )
    for c in tables:
        c.wait()

    def filter_freq_step(k):
        h_spec[k] = split_dot(h_spec[k], high[k], rest[k], False)

    freq_loop(freqs, unroll, filter_freq_step)
    keep_h.start()
    for c in inward:
        c.wait()
    spread(recv, wide, narrow)
    first_stage(
        lambda at: [wide[n, pl.ds(at, 8), :] for n in range(count)], w_spec, rows * narrow // 8
    )

    def forward_step(k):
        w_spec[k] = split_dot(w_spec[k], high[k], rest[k], False)

    def inverse_step(k):
        h = h_spec[k]
        hr, hi = h[:, :LANES], h[:, LANES:]
        parts = []
        for r in range(rows):
            w = w_spec[k, r * narrow : (r + 1) * narrow]
            wr, wi = w[:, :LANES], w[:, LANES:]
            parts.append(jnp.concatenate([wr * hr - wi * hi, wr * hi + wi * hr], axis=1))
        back[k] = split_dot(jnp.concatenate(parts, axis=0), high[k], rest[k], True)

    freq_loop(freqs, unroll, forward_step)
    keep_w.start()
    freq_loop(freqs, unroll, inverse_step)

    def store(n, at, v):
        wide[n, pl.ds(at, 8), :] = v

    outward = []
    for r in range(rows):
        last_stage(back, store, narrow // 8, 1.0 / (2 * count * LANES), r * narrow)
        gather_back(wide, send, narrow, r)
        ready = to_positions(groups, me, narrow, r, send, z_ref, out_ss, out_rs, local.at[3 + r])
        for c in ready:
            c.start()
        outward = outward + ready
    for c in outward + [keep_u, keep_gate, keep_h, keep_w]:
        c.wait()


def conv_back_kernel(
    rows_all,
    groups,
    g_ref,
    w_hbm,
    h_hbm,
    high_ref,
    rest_ref,
    down_hbm,
    ga_hbm,
    y2,
    q_ref,
    gm_ref,
    first,
    first_b,
    mid,
    mid_b,
    freq,
    last,
    skip,
    decay,
    feats,
    gw_ref,
    early_o,
    first_o,
    mid_o,
    last_o,
    high,
    rest,
    recv,
    wide,
    back,
    send,
    in_ss,
    in_rs,
    out_ss,
    out_rs,
    local,
    own,
    core_buf,
    step_buf,
    core_ss,
    core_rs,
    step_ss,
    step_rs,
    aug,
    w_spec,
    h_spec,
    gout,
    gup,
    gdown,
    ga_buf,
    y2_turned,
    ga_sem,
    spec_sem,
    keep_sem,
):
    me = lax.axis_index("seq")
    row = lax.axis_index("row")
    core = lax.rem(row, 2)
    narrow = h_spec.shape[1]
    count, freqs = wide.shape[0], high.shape[0]
    rows = g_ref.shape[0]
    unroll = UNROLL.get(freqs, 1)
    tables = [
        pltpu.make_async_copy(high_ref, high, local.at[0]),
        pltpu.make_async_copy(rest_ref, rest, local.at[1]),
    ]
    piece = ga_buf.shape[2]
    pieces = ga_hbm.shape[1] // piece
    low, f32 = jnp.bfloat16, jnp.float32

    def part_copy(src, buf, sem, i, slot):
        cols = pl.ds(pl.multiple_of(i * piece, piece), piece)
        return pltpu.make_async_copy(src.at[:, cols], buf.at[slot], sem.at[slot])

    def stream(src, buf, sem, body):
        def step(i, carry):
            slot = lax.rem(i, 2)

            @pl.when(i + 1 < pieces)
            def _():
                part_copy(src, buf, sem, i + 1, 1 - slot).start()

            part_copy(src, buf, sem, i, slot).wait()
            body(pl.ds(pl.multiple_of(i * piece, piece), piece), buf[slot])
            return carry

        lax.fori_loop(0, pieces, step, 0)

    bring = pltpu.make_async_copy(down_hbm, gdown, spec_sem.at[2])
    bring.start()
    part_copy(ga_hbm, ga_buf, ga_sem, 0, 0).start()
    spectra = [
        pltpu.make_async_copy(w_hbm, w_spec, spec_sem.at[0]),
        pltpu.make_async_copy(h_hbm, h_spec, spec_sem.at[1]),
    ]
    for c in tables + spectra:
        c.start()
    greet_all(rows_all, groups, me, row)
    inward = []
    for r in range(rows):
        inward = inward + to_channels(
            groups, me, narrow, r, g_ref, recv, in_ss, in_rs, local.at[3 + rows + r]
        )
    for c in inward:
        c.start()
    early = early_crew(groups, me, core, gout, gup, gdown, own, down_hbm)
    early.core_setup(core_buf, core_ss, core_rs, row + 1 - 2 * core)
    early.step_setup(step_buf, step_ss, step_rs, [range(n) for n in EARLY_STEPS])

    def up_part(cols, part):
        gup[:, cols] = jnp.dot(y2_turned[...], part, preferred_element_type=f32).astype(low)

    up_sum, down_sum, out_sum = early.members
    down_sum.core_start()

    y2_turned[...] = y2[...].T
    stream(ga_hbm, ga_buf, ga_sem, up_part)
    up_sum.core_start()
    bring.wait()
    down_sum.core_finish()
    total = None
    for r in range(rows):
        tok = q_ref.shape[2]
        part = jnp.dot(
            q_ref[r], gm_ref[r * tok : (r + 1) * tok, :], preferred_element_type=f32
        )
        total = part if total is None else total + part
    gout[...] = total.astype(low)
    out_sum.core_start()
    up_sum.core_finish()
    out_sum.core_finish()
    for c in tables + spectra:
        c.wait()
    for c in inward:
        c.wait()
    spread(recv, wide, narrow)
    first_stage(
        lambda at: [wide[n, pl.ds(at, 8), :] for n in range(count)], back, rows * narrow // 8
    )

    def forward_step(k):
        back[k, : rows * narrow] = split_dot(back[k, : rows * narrow], high[k], rest[k], False)

    def inverse_step(k):
        h = h_spec[k]
        hr, hi = h[:, :LANES], h[:, LANES:]
        parts = []
        hsum = None
        for r in range(rows):
            w = w_spec[k, r * narrow : (r + 1) * narrow]
            wr, wi = w[:, :LANES], w[:, LANES:]
            g = back[k, r * narrow : (r + 1) * narrow]
            gr, gi = g[:, :LANES], g[:, LANES:]
            parts.append(jnp.concatenate([hr * gr + hi * gi, hr * gi - hi * gr], axis=1))
            pair = (wr * gr + wi * gi, wr * gi - wi * gr)
            hsum = pair if hsum is None else (hsum[0] + pair[0], hsum[1] + pair[1])
        parts.append(jnp.concatenate(hsum, axis=1))
        back[k] = split_dot(jnp.concatenate(parts, axis=0), high[k], rest[k], True)

    freq_loop(freqs, unroll, forward_step)
    freq_loop(freqs, unroll, inverse_step)

    def store(n, at, v):
        wide[n, pl.ds(at, 8), :] = v

    outward = []
    for r in range(rows):
        last_stage(back, store, narrow // 8, 1.0 / (2 * count * LANES), r * narrow)
        gather_back(wide, send, narrow, r)
        ready = to_positions(groups, me, narrow, r, send, gw_ref, out_ss, out_rs, local.at[3 + r])
        for c in ready:
            c.start()
        outward = outward + ready
    last_stage(back, store, narrow // 8, 1.0 / (2 * count * LANES), rows * narrow)
    net = FilterNet(me, narrow, (first, first_b, mid, mid_b, freq, last, skip, decay, feats), aug)
    for out in (first_o, mid_o, last_o):
        out[...] = jnp.zeros_like(out)

    def pull(i, carry):
        size = CHUNK * LANES
        grad = [wide[i * CHUNK + j, rows * narrow :, :] for j in range(CHUNK)]
        net.pull(
            pl.multiple_of(i * size, LANES),
            size,
            jnp.concatenate(grad, axis=1),
            first_o,
            mid_o,
            last_o,
        )
        return carry

    lax.fori_loop(0, count // CHUNK, pull, 0)
    kept = []
    for p, h in enumerate(early.members):
        k = EARLY_STEPS[p] - 1
        for j in range(2):
            h.finish(k, j)
            i, size = h.pieces(k)[j]
            kept.append(
                pltpu.make_async_copy(
                    own[p].at[pl.ds(h.slot(k + 1) + i, size)],
                    early_o[p].at[pl.ds(i, size)],
                    keep_sem.at[p, j],
                )
            )
            kept[-1].start()
    for c in kept:
        c.wait()
    early.wait_core_sends()
    early.wait_sends()
    for c in outward:
        c.wait()


def conv_scratch(groups, rows, narrow, tok, freqs, count, extra):
    low, f32 = jnp.bfloat16, jnp.float32
    dma = pltpu.SemaphoreType.DMA
    wide_rows = (rows + extra) * narrow
    out = [
        pltpu.VMEM((freqs, LANES, 2 * LANES), low),
        pltpu.VMEM((freqs, LANES, 2 * LANES), low),
        pltpu.VMEM((groups, rows, narrow, tok), low),
        pltpu.VMEM((count, wide_rows, LANES), f32),
    ]
    return out + [
        pltpu.VMEM((freqs, wide_rows, 2 * LANES), f32),
        pltpu.VMEM((groups, rows, narrow, tok), low),
        dma((groups - 1, rows)),
        dma((groups - 1, rows)),
        dma((groups - 1, rows)),
        dma((groups - 1, rows)),
        dma((3 + 2 * rows,)),
    ]


def conv_params(cid):
    return pltpu.CompilerParams(
        collective_id=cid, has_side_effects=True, vmem_limit_bytes=VMEM_LIMIT
    )


def conv_forward(block, lengths, gain, offset, weight, taps, params, tables):
    rows, tok, width = block.shape
    groups = lax.axis_size("seq")
    narrow, length = width // groups, tok * groups
    count = length // LANES
    freqs = count + 1
    low, f32 = jnp.bfloat16, jnp.float32
    vm = pl.BlockSpec(memory_space=pltpu.VMEM)
    sm = pl.BlockSpec(memory_space=pltpu.SMEM)
    hbm = pl.BlockSpec(memory_space=pl.ANY)
    return pl.pallas_call(
        functools.partial(conv_kernel, groups),
        out_shape=(
            jax.ShapeDtypeStruct((rows, width, tok), low),
            jax.ShapeDtypeStruct((freqs, rows * narrow, 2 * LANES), f32),
            jax.ShapeDtypeStruct((freqs, narrow, 2 * LANES), f32),
            jax.ShapeDtypeStruct((rows, 3 * width, tok), low),
            jax.ShapeDtypeStruct((rows, width, tok), f32),
            jax.ShapeDtypeStruct((8, 3 * width), f32),
        ),
        in_specs=[vm, sm, vm, vm, hbm] + [vm] * 10 + [hbm, hbm],
        out_specs=(vm, hbm, hbm, hbm, hbm, vm),
        scratch_shapes=conv_scratch(groups, rows, narrow, tok, freqs, count, 0)
        + [
            pltpu.VMEM((params[-1].shape[0], params[0].shape[1]), f32),
            pltpu.VMEM((count, narrow, LANES), f32),
            pltpu.VMEM((width, rows * tok), low),
            pltpu.VMEM((rows, width, tok), low),
            pltpu.VMEM((8, 3 * width), f32),
            pltpu.VMEM((3, 3 * width, LANES), f32),
            pltpu.VMEM((3 * width, LANES), f32),
            pltpu.VMEM((8, 3 * width), f32),
            pltpu.VMEM((8, 3 * width), f32),
            pltpu.SemaphoreType.DMA((2,)),
            pltpu.VMEM((freqs, rows * narrow, 2 * LANES), f32),
            pltpu.VMEM((freqs, narrow, 2 * LANES), f32),
            pltpu.VMEM((rows, 3 * width, tok), low),
            pltpu.VMEM((rows, width, tok), f32),
            pltpu.VMEM(weight.shape, low),
            pltpu.SemaphoreType.DMA((5,)),
        ],
        compiler_params=conv_params(1),
        name="conv_forward",
    )(block, lengths, gain, offset, weight, taps, *params, *tables)


def conv_backward(grad, w_spec, h_spec, tables, grad_down, grad_pre, y2, q, gm, params):
    rows, _, tok = grad.shape
    freqs, narrow, _ = h_spec.shape
    groups = lax.axis_size("seq")
    count = freqs - 1
    width, ffn = q.shape[1], grad_pre.shape[1]
    half = width // 2
    piece = width
    vm = pl.BlockSpec(memory_space=pltpu.VMEM)
    hbm = pl.BlockSpec(memory_space=pl.ANY)
    low, f32 = jnp.bfloat16, jnp.float32
    dma = pltpu.SemaphoreType.DMA
    kept = [groups >> n for n in EARLY_STEPS]
    feat_rows, hidden = params[-1].shape[0], params[0].shape[1]
    return pl.pallas_call(
        functools.partial(conv_back_kernel, lax.axis_size("row"), groups),
        out_shape=(
            jax.ShapeDtypeStruct(grad.shape, low),
            [jax.ShapeDtypeStruct((c, n, narrow, half), low) for c, n in zip(kept, EARLY)],
            jax.ShapeDtypeStruct((feat_rows, LANES), f32),
            jax.ShapeDtypeStruct((hidden, LANES), f32),
            jax.ShapeDtypeStruct((narrow, LANES), f32),
        ),
        in_specs=[vm] + [hbm] * 6 + [vm] * 12,
        out_specs=(vm, [hbm] * 3, vm, vm, vm),
        scratch_shapes=conv_scratch(groups, rows, narrow, tok, freqs, count, 1)
        + [
            [pltpu.VMEM((groups, n, narrow, half), low) for n in EARLY],
            [
                pltpu.VMEM((width, 4 * half), low),
                pltpu.VMEM((ffn, half), low),
                pltpu.VMEM((width, half), low),
            ],
            [
                [pltpu.VMEM((groups >> (k + 1), n, narrow, half), low) for k in range(c)]
                for c, n in zip(EARLY_STEPS, EARLY)
            ],
            dma((len(EARLY),)),
            dma((len(EARLY),)),
            [[dma((2,)) for k in range(c)] for c in EARLY_STEPS],
            [[dma((2,)) for k in range(c)] for c in EARLY_STEPS],
            pltpu.VMEM((feat_rows, hidden), f32),
            pltpu.VMEM(w_spec.shape, f32),
            pltpu.VMEM(h_spec.shape, f32),
            pltpu.VMEM((width, width), low),
            pltpu.VMEM((width, ffn), low),
            pltpu.VMEM((ffn, width), low),
            pltpu.VMEM((2, y2.shape[0], piece), low),
            pltpu.VMEM((width, y2.shape[0]), low),
            dma((2,)),
            dma((3,)),
            dma((len(EARLY), 2)),
        ],
        compiler_params=conv_params(2),
        name="conv_backward",
    )(grad, w_spec, h_spec, *tables, grad_down, grad_pre, y2, q, gm, *params)


def shards(
    block_in,
    lengths,
    mixer_gain,
    mixer_bias,
    in_weight,
    short_taps,
    filter_in,
    filter_in_bias,
    filter_mid,
    filter_mid_bias,
    filter_freq,
    filter_out,
    filter_skip,
    decay_rate,
    out_weight,
    feed_gain,
    feed_bias,
    up_weight,
    down_weight,
    cotangent,
):
    _, tok_count, model_width = block_in.shape
    length = tok_count * lax.axis_size("seq")
    block_float = block_in.astype(jnp.float32)
    tables = tuple(jnp.asarray(t) for t in spectrum_tables(length))
    params = (
        filter_in,
        filter_in_bias,
        filter_mid,
        filter_mid_bias,
        filter_freq,
        filter_out,
        filter_skip,
        decay_rate,
        jnp.asarray(feature_rows(length, filter_in.shape[0])),
    )
    back_home, w_spec, h_spec, projected, gate_out, edges = conv_forward(
        block_in, lengths, mixer_gain, mixer_bias, in_weight, short_taps, params, tables
    )
    conv_float = back_home.astype(jnp.float32)
    product_low = (gate_out * conv_float).astype(jnp.bfloat16)
    mixed = block_float + jnp.einsum(
        "rct,cd->rtd", product_low, out_weight, preferred_element_type=jnp.float32
    )
    normed_two, feed_pull = jax.vjp(layer_norm, mixed, feed_gain, feed_bias)
    normed_two_low = normed_two.astype(jnp.bfloat16)
    pre_act = jnp.einsum(
        "rtd,df->rtf", normed_two_low, up_weight, preferred_element_type=jnp.float32
    )
    activ, gelu_pull = jax.vjp(jax.nn.gelu, pre_act)
    activ_low = activ.astype(jnp.bfloat16)
    block_out = (
        mixed
        + jnp.einsum("rtf,fd->rtd", activ_low, down_weight, preferred_element_type=jnp.float32)
    ).astype(jnp.bfloat16)
    grad_float = cotangent.astype(jnp.float32)
    grad_down = jnp.einsum("rtf,rtd->fd", activ_low, cotangent, preferred_element_type=jnp.float32)
    grad_activ = jnp.einsum(
        "rtd,fd->rtf", cotangent, down_weight, preferred_element_type=jnp.float32
    )
    grad_pre = gelu_pull(grad_activ)[0].astype(jnp.bfloat16)
    grad_normed_two = jnp.einsum(
        "rtf,df->rtd", grad_pre, up_weight, preferred_element_type=jnp.float32
    )
    grad_mixed_part, grad_feed_gain, grad_feed_bias = feed_pull(grad_normed_two)
    grad_mixed = grad_float + grad_mixed_part
    grad_mixed_low = grad_mixed.astype(jnp.bfloat16)
    grad_product = jnp.einsum(
        "rtd,cd->rct", grad_mixed_low, out_weight, preferred_element_type=jnp.float32
    )
    grad_gate_out = grad_product * conv_float
    grad_conv = (grad_product * gate_out).astype(jnp.bfloat16)

    def flat_rows(v):
        return v.reshape(-1, v.shape[-1])

    grad_carried, early, first_sum, mid_sum, last_sum = conv_backward(
        grad_conv,
        w_spec,
        h_spec,
        tables,
        grad_down.astype(jnp.bfloat16),
        flat_rows(grad_pre),
        flat_rows(normed_two_low),
        product_low,
        flat_rows(grad_mixed_low),
        params,
    )
    grad_input, fin, small, leads = finish(
        grad_carried,
        grad_gate_out,
        projected,
        edges,
        lengths,
        short_taps,
        in_weight,
        block_in,
        grad_mixed,
        (mixer_gain, mixer_bias, grad_feed_gain, grad_feed_bias),
        early,
        (mid_sum, first_sum, last_sum),
    )
    *done, grad_input = unpack(
        fin, small, leads, grad_input, filter_in.shape[0], filter_mid.shape[0], model_width
    )
    return (block_out, grad_input, *done)


def solution(mesh):
    placed = (
        P("row", "seq", None),
        P("row", None),
        P(),
        P(),
        P(),
        P(),
        P(),
        P(),
        P(),
        P(),
        P(),
        P(),
        P(),
        P(),
        P(),
        P(),
        P(),
        P(),
        P(),
        P("row", "seq", None),
    )
    return jax.shard_map(
        shards,
        mesh=mesh,
        in_specs=placed,
        out_specs=(
            P("row", "seq", None),
            P("row", "seq", None),
            P(),
            P(),
            P("seq", None),
            P(),
            P(),
            P(),
            P(),
            P(),
            P(),
            P(),
            P(),
            P("seq", None),
            P(),
            P(),
            P("seq", None),
            P("seq", None),
        ),
        check_vma=False,
    )
```

```python
import functools
import math

import jax
import jax.numpy as jnp
import numpy as np
from jax import lax
from jax.experimental import pallas as pl
from jax.experimental.pallas import tpu as pltpu
from jax.sharding import PartitionSpec as P

HIGHEST = lax.Precision.HIGHEST


def layer_norm(values, gain, offset):
    center = values - jnp.mean(values, axis=-1, keepdims=True)
    spread = jnp.mean(center * center, axis=-1, keepdims=True)
    return center * lax.rsqrt(spread + 1e-05) * gain + offset


MESH = pl.DeviceIdType.MESH
VMEM_LIMIT = 56 * 1024 * 1024
LANES = 128


def seq_weights(order, groups):
    weights = []
    w = 1
    while w < groups:
        weights.append(w)
        w *= 2
    first = weights[0] + order * (weights[1] - weights[0])
    second = weights[1] - order * (weights[1] - weights[0])
    return [first, second] + weights[2:]


class Halving:
    def __init__(self, groups, me, core, order, parts, own, first=0, base=0):
        self.groups, self.me, self.core, self.parts, self.own, self.first = (
            groups,
            me,
            core,
            parts,
            own,
            first,
        )
        self.order, self.other = (core, 1 - core) if order is None else (order, order)
        self.weights = seq_weights(self.order, groups)
        self.bits = [lax.rem(me // w, 2) for w in self.weights]
        self.steps = len(self.weights)
        self.half = own.shape[3]
        self.base = base * 2 * self.half
        self.source = None
        self.unit = own.shape[2]

    def shard_of(self, n, order):
        weights = seq_weights(order, self.groups)
        at = 0
        for j in range(self.steps):
            bit = lax.rem(self.me // weights[j], 2)
            keep = (n >> (self.steps - 1 - j)) & 1
            at = at + (bit if keep else 1 - bit) * weights[j]
        return at

    def core_setup(self, buf, ss, rs, sib):
        self.buf = buf
        (ref, _, cols, _) = self.parts[0]
        src = (ref if self.source is None else self.source).at[
            :,
            pl.ds(
                pl.multiple_of(self.base + (1 - self.core) * cols * self.half, LANES),
                cols * self.half,
            ),
        ]
        self.core_copy = pltpu.make_async_remote_copy(
            src_ref=src,
            dst_ref=buf,
            send_sem=ss,
            recv_sem=rs,
            device_id={"row": sib},
            device_id_type=MESH,
        )

    def core_start(self):
        self.core_copy.start()

    def core_finish(self):
        self.core_copy.wait_recv()
        (ref, high, cols, _) = self.parts[0]
        first = self.count(0)
        for n in range(self.groups):
            s = self.shard_of(n, self.order)
            for h in range(high):
                lines = pl.ds(pl.multiple_of((s * high + h) * self.unit, 8), self.unit)
                for c in range(cols):
                    mine = ref[
                        lines,
                        pl.ds(
                            pl.multiple_of(
                                self.base + (self.core * cols + c) * self.half, LANES
                            ),
                            self.half,
                        ),
                    ]
                    self.own[n, h * cols + c] = (
                        mine + self.buf[lines, c * self.half : (c + 1) * self.half]
                    )
            if n + 1 == first // 2:
                self.start(0, 0)
            if n + 1 == first:
                self.start(0, 1)

    def pieces(self, k):
        count = self.count(k)
        return [(0, count // 2), (count // 2, count // 2)] if count > 1 else [(0, 1)]

    def step_setup(self, bufs, ss, rs, steps):
        self.step_bufs = dict(zip(steps, bufs))
        self.copies = {}
        for at, k in enumerate(steps):
            for j, (i, size) in enumerate(self.pieces(k)):
                self.copies[k, j] = pltpu.make_async_remote_copy(
                    src_ref=self.own.at[pl.ds(self.slot(k) + i, size)],
                    dst_ref=bufs[at].at[pl.ds(i, size)],
                    send_sem=ss[at].at[j],
                    recv_sem=rs[at].at[j],
                    device_id={"seq": self.me + self.weights[k] * (1 - 2 * self.bits[k])},
                    device_id_type=MESH,
                )

    def slot(self, k):
        return self.groups - (self.groups >> k) - self.first

    def start(self, k, j):
        self.copies[k, j].start()

    def start_step(self, k):
        for j in range(len(self.pieces(k))):
            self.start(k, j)

    def finish(self, k, j):
        self.copies[k, j].wait_recv()
        first, size = self.pieces(k)[j]
        for i in range(first, first + size):
            at = self.slot(k + 1) + i
            self.own[at] = self.own[at] + self.step_bufs[k][i]

    def count(self, k):
        return self.groups >> (k + 1)

    def wait_sends(self):
        for c in self.copies.values():
            c.wait_send()

    def wait_core_sends(self):
        self.core_copy.wait_send()


EARLY = (4, 4, 1)
LATE = (1, 1, 1)
ORDERS = (0, 1, None)
EARLY_STEPS = (1, 1, 1)


class Crew:
    def __init__(self, members):
        self.members = members
        self.steps = members[0].steps

    def core_setup(self, bufs, ss, rs, sib):
        for p, h in enumerate(self.members):
            h.core_setup(bufs[p], ss.at[p], rs.at[p], sib)

    def step_setup(self, bufs, ss, rs, steps):
        for p, h in enumerate(self.members):
            h.step_setup(bufs[p], ss[p], rs[p], steps[p])

    def core_start(self):
        for h in self.members:
            h.core_start()

    def core_finish(self):
        for h in self.members:
            h.core_finish()

    def part(self, k, j):
        for h in self.members:
            if (k, j) in h.copies:
                h.finish(k, j)
                if j == 0 and k + 1 < self.steps:
                    h.start_step(k + 1)

    def advance(self, k):
        self.part(k, 0)
        self.part(k, 1)

    def wait_sends(self):
        for h in self.members:
            h.wait_sends()

    def wait_core_sends(self):
        for h in self.members:
            h.wait_core_sends()


def early_crew(groups, me, core, gout, gup, gdown, owns, down_src):
    parts = [[(gup, 1, 4, 0)], [(gdown, 4, 1, 0)], [(gout, 1, 1, 0)]]
    crew = Crew([Halving(groups, me, core, o, p, w) for o, p, w in zip(ORDERS, parts, owns)])
    crew.members[1].source = down_src
    return crew


def greet_all(rows, groups, me, row):
    barrier = pltpu.get_barrier_semaphore()
    for d in range(1, rows):
        pl.semaphore_signal(
            barrier, inc=1, device_id={"row": lax.rem(row + d, rows)}, device_id_type=MESH
        )
    for d in range(1, groups):
        pl.semaphore_signal(
            barrier, inc=1, device_id={"seq": lax.rem(me + d, groups)}, device_id_type=MESH
        )
    pl.semaphore_wait(barrier, rows + groups - 2)


def row_masks(lengths, row, start, tok):
    where = lax.broadcasted_iota(jnp.int32, (8, tok), 1) + start
    ends = []
    total = 0
    for k in range(lengths.shape[1]):
        total = total + lengths[row, k]
        ends.append(total)

    def doc(at):
        out = jnp.zeros(at.shape, jnp.int32)
        for e in ends:
            out = out + (at >= e).astype(jnp.int32)
        return out

    own = doc(where)
    masks = []
    for lag in (1, 2):
        same = (where >= lag) & (doc(where - lag) == own)
        masks.append(same.astype(jnp.float32)[:1])
    return masks + [(where < total).astype(jnp.float32)[:1]]


def edge_pick(r):
    line = lax.broadcasted_iota(jnp.int32, (8, LANES), 0)
    spot = lax.broadcasted_iota(jnp.int32, (8, LANES), 1)
    pick = (spot == line - 2 * r + LANES - 2) & (line >= 2 * r) & (line < 2 * r + 2)
    return pick.astype(jnp.bfloat16)


def pack_edges(tiles):
    out = None
    for r, tile in enumerate(tiles):
        piece = lax.dot_general(
            edge_pick(r), tile, (((1,), (1,)), ((), ())), preferred_element_type=jnp.float32
        )
        out = piece if out is None else out + piece
    return out


def unpack_edge(lines, r):
    return lax.dot_general(
        lines.astype(jnp.bfloat16),
        edge_pick(r),
        (((0,), (0,)), ((), ())),
        preferred_element_type=jnp.float32,
    )


def window_of(values, lane, edge):
    early, late = edge[:, LANES - 2 : LANES - 1], edge[:, LANES - 1 :]
    one = jnp.where(lane == 0, late, pltpu.roll(values, 1, 1))
    two = jnp.where(lane == 0, early, jnp.where(lane == 1, late, pltpu.roll(values, 2, 1)))
    return one, two


def spread_taps(taps, padded, wide):
    padded[...] = jnp.zeros_like(padded)
    padded[: taps.shape[0], :] = taps[...]
    turned = padded[...].T
    for j in range(taps.shape[0]):
        wide[j] = jnp.broadcast_to(turned[:, j : j + 1], wide.shape[1:])


def norm_parts(values):
    center = values - jnp.mean(values, axis=-1, keepdims=True)
    scale = lax.rsqrt(jnp.mean(center * center, axis=-1, keepdims=True) + 1e-05)
    return center * scale, scale


STRIP = 128


def finish_kernel(
    rows,
    groups,
    gw_ref,
    ggo_ref,
    u_hbm,
    edge_ref,
    lengths,
    taps,
    weight_hbm,
    block_hbm,
    gm_hbm,
    gain,
    offset,
    feed_gain,
    feed_bias,
    early,
    mid_s,
    first_s,
    last,
    gi_ref,
    fin_o,
    small_o,
    gains_o,
    padded,
    wide_taps,
    edges,
    tap_sum,
    gu,
    gu_low,
    rim,
    rim_out,
    rim_in,
    normed,
    gin,
    small,
    own,
    own_early,
    core_buf,
    step_buf,
    early_buf,
    wide_buf,
    small_row,
    small_sum,
    small_part,
    small_done,
    last_row,
    last_sum,
    rim_sem,
    bring_sem,
    u_ref,
    weight,
    block,
    gm_ref,
    move_sem,
    core_ss,
    core_rs,
    step_ss,
    step_rs,
    early_ss,
    early_rs,
    wide_ss,
    wide_rs,
    fin_ss,
    fin_rs,
    srow_ss,
    srow_rs,
    spart_ss,
    spart_rs,
    sdone_ss,
    sdone_rs,
    lrow_ss,
    lrow_rs,
    gain_own,
    gain_row_buf,
    gain_sum,
    grow_ss,
    grow_rs,
    gcast_ss,
    gcast_rs,
):
    me = lax.axis_index("seq")
    row = lax.axis_index("row")
    core = lax.rem(row, 2)
    sib = row + 1 - 2 * core
    chunk = small_part.shape[1]
    held, width, tok = gw_ref.shape
    low, f32 = jnp.bfloat16, jnp.float32

    late = Crew(
        [
            Halving(groups, me, core, o, [(gin, 1, 1, 0)], own[p], base=p)
            for p, o in enumerate(ORDERS)
        ]
    )
    late.core_setup(core_buf, core_ss, core_rs, sib)
    late.step_setup(step_buf, step_ss, step_rs, [range(late.steps)] * len(LATE))
    later = [range(n, late.steps) for n in EARLY_STEPS]
    rest = Crew(
        [
            Halving(groups, me, core, o, (), w, first=groups - e.shape[0])
            for o, w, e in zip(ORDERS, own_early, early)
        ]
    )
    rest.step_setup(early_buf, early_ss, early_rs, later)
    bring = [
        pltpu.make_async_copy(e, w, bring_sem.at[p])
        for p, (w, e) in enumerate(zip(own_early, early))
    ]
    moves = [
        pltpu.make_async_copy(src, dst, move_sem.at[p])
        for p, (src, dst) in enumerate(
            ((u_hbm, u_ref), (block_hbm, block), (weight_hbm, weight), (gm_hbm, gm_ref))
        )
    ]
    for c in bring + moves:
        c.start()
    greet_all(rows, groups, me, row)
    for c in bring:
        c.wait()
    for h, ks in zip(rest.members, later):
        h.start_step(ks[0])
    lrow = [
        pltpu.make_async_remote_copy(
            src_ref=last,
            dst_ref=last_row.at[d - 1],
            send_sem=lrow_ss.at[d - 1],
            recv_sem=lrow_rs.at[d - 1],
            device_id={"row": lax.rem(row + d, rows)},
            device_id_type=MESH,
        )
        for d in range(1, rows)
    ]
    for c in lrow:
        c.start()

    spread_taps(taps, padded, wide_taps)
    tap_sum[...] = jnp.zeros_like(tap_sum)
    lane = lax.broadcasted_iota(jnp.int32, (STRIP, tok), 1)
    moves[0].wait()
    for r in range(held):
        same1, same2, live = row_masks(lengths, r, me * tok, tok)
        edges[...] = unpack_edge(edge_ref[...], r)

        def strip(i, carry, r=r, same1=same1, same2=same2, live=live):
            at = [pl.multiple_of(i * STRIP + g * width, STRIP) for g in range(3)]
            tap = [
                [
                    jnp.concatenate([wide_taps[j, pl.ds(a, STRIP), :]] * (tok // LANES), axis=1)
                    for j in range(3)
                ]
                for a in at
            ]
            u = [u_ref[r, pl.ds(a, STRIP), :].astype(f32) for a in at]
            shifts = [
                window_of(v, lane, edges[pl.ds(a, STRIP), :])
                for v, a in zip(u, at)
            ]
            gate_in, stream = [
                tap[g][0] * u[g] + tap[g][1] * shifts[g][0] * same1 + tap[g][2] * shifts[g][1] * same2
                for g in (1, 2)
            ]
            gw = gw_ref[r, pl.ds(at[0], STRIP), :].astype(f32) * live
            grads = [ggo_ref[r, pl.ds(at[0], STRIP), :] * live, gw * stream, gw * gate_in]
            for g in range(3):
                m1, m2 = grads[g] * same1, grads[g] * same2
                for j, p in enumerate((grads[g] * u[g], m1 * shifts[g][0], m2 * shifts[g][1])):
                    total = p[:, :LANES]
                    for h in range(1, tok // LANES):
                        total = total + p[:, h * LANES : (h + 1) * LANES]
                    tap_sum[j, pl.ds(at[g], STRIP), :] += total
                b1 = pltpu.roll(tap[g][1] * m1, tok - 1, 1)
                b2 = pltpu.roll(tap[g][2] * m2, tok - 2, 1)
                gu[r, pl.ds(at[g], STRIP), :] = (
                    tap[g][0] * grads[g]
                    + jnp.where(lane < tok - 1, b1, 0.0)
                    + jnp.where(lane < tok - 2, b2, 0.0)
                )
                over = jnp.where(lane < tok - 1, 0.0, b1) + jnp.where(lane < tok - 2, 0.0, b2)
                rim[r, pl.ds(at[g], STRIP), :] = over[:, tok - LANES :].astype(low)
            return carry

        lax.fori_loop(0, width // STRIP, strip, 0)
        if r == 0:
            rest.part(1, 0)

    rim_out[...] = pack_edges([rim[r] for r in range(held)])
    rim_copy = pltpu.make_async_remote_copy(
        src_ref=rim_out,
        dst_ref=rim_in,
        send_sem=rim_sem.at[0],
        recv_sem=rim_sem.at[1],
        device_id={"seq": lax.rem(me + groups - 1, groups)},
        device_id_type=MESH,
    )
    rim_copy.start()

    at = mid_s.shape[0] + first_s.shape[0]
    small[:at, :] = jnp.concatenate([mid_s[...], first_s[...]], axis=0)
    small[at:, :] = jnp.zeros((small.shape[0] - at, LANES), f32)
    per = width // LANES

    def put_small(first, line):
        for i in range(line.shape[1] // LANES):
            small[first + i : first + i + 1, :] = line[:, i * LANES : (i + 1) * LANES]

    ones = jnp.ones((8, LANES), low)

    def lane_sums(values):
        high = values.astype(low)
        rest = (values - high.astype(f32)).astype(low)
        dims = (((1,), (1,)), ((), ()))
        return lax.dot_general(ones, high, dims, preferred_element_type=f32) + lax.dot_general(
            ones, rest, dims, preferred_element_type=f32
        )

    for j in range(3):
        put_small(at + 2 * per + 3 * per * j, lane_sums(tap_sum[j])[:1])
    put_small(at + 11 * per, feed_gain[...][None, :])
    put_small(at + 12 * per, feed_bias[...][None, :])
    srow = [
        pltpu.make_async_remote_copy(
            src_ref=small,
            dst_ref=small_row.at[d - 1],
            send_sem=srow_ss.at[d - 1],
            recv_sem=srow_rs.at[d - 1],
            device_id={"row": lax.rem(row + d, rows)},
            device_id_type=MESH,
        )
        for d in range(1, rows)
    ]
    for c in srow:
        c.start()
    gain_row, offset_row = gain[...][None, :], offset[...][None, :]
    for c in moves[1:]:
        c.wait()
    for r in range(held):
        hat, _ = norm_parts(block[r].astype(f32))
        normed[:, r * tok : (r + 1) * tok] = (hat * gain_row + offset_row).T.astype(low)
    rest.part(1, 1)
    for c in srow + lrow:
        c.wait()
    total = small[...]
    tail = last[...]
    for d in range(rows - 1):
        total = total + small_row[d]
        tail = tail + last_row[d]
    small_sum[...] = total
    last_sum[...] = tail
    spart = []
    for d in range(1, groups):
        to = lax.rem(me + d, groups)
        spart.append(
            pltpu.make_async_remote_copy(
                src_ref=small_sum.at[pl.ds(to * chunk, chunk)],
                dst_ref=small_part.at[d - 1],
                send_sem=spart_ss.at[d - 1],
                recv_sem=spart_rs.at[d - 1],
                device_id={"seq": to},
                device_id_type=MESH,
            )
        )
    for c in spart:
        c.start()

    rim_copy.wait()
    for r in range(held):
        add = unpack_edge(rim_in[...], r)
        split = tok - LANES
        gu_low[:, r * tok : r * tok + split] = gu[r, :, :split].astype(low)
        gu_low[:, r * tok + split : (r + 1) * tok] = (gu[r, :, split:] + add).astype(low)

    rest.part(2, 0)
    piece = 256

    def weight_grad(i, carry):
        cols = pl.ds(pl.multiple_of(i * piece, piece), piece)
        gin[:, cols] = lax.dot_general(
            normed[...], gu_low[cols, :], (((1,), (1,)), ((), ())), preferred_element_type=f32
        ).astype(low)
        return carry

    per_unit = width // piece
    first_unit, second_unit, third_unit = late.members
    lax.fori_loop(0, per_unit, weight_grad, 0)
    first_unit.core_start()
    lax.fori_loop(per_unit, 2 * per_unit, weight_grad, 0)
    second_unit.core_start()
    first_unit.core_finish()
    lax.fori_loop(2 * per_unit, 3 * per_unit, weight_grad, 0)
    third_unit.core_start()
    second_unit.core_finish()
    rest.part(2, 1)

    fin = []

    def close(crew, arrays, units, base):
        place = sum((EARLY + LATE)[:base])
        for p, (h, array, count) in enumerate(zip(crew.members, arrays, units)):
            q, slot = base + p, array.shape[0] - 1
            w, n = 2, 0
            while w < rows:
                bit = lax.rem(row // w, 2)
                c = pltpu.make_async_remote_copy(
                    src_ref=h.own.at[slot],
                    dst_ref=wide_buf[q].at[n],
                    send_sem=wide_ss.at[n, q],
                    recv_sem=wide_rs.at[n, q],
                    device_id={"row": row + w * (1 - 2 * bit)},
                    device_id_type=MESH,
                )
                c.start()
                c.wait()
                h.own[slot] = h.own[slot] + wide_buf[q][n]
                w, n = 2 * w, n + 1
            fin_o[core, place : place + count] = h.own[slot]
            c = pltpu.make_async_remote_copy(
                src_ref=h.own.at[slot],
                dst_ref=fin_o.at[core, pl.ds(place, count)],
                send_sem=fin_ss.at[q],
                recv_sem=fin_rs.at[q],
                device_id={"row": sib},
                device_id_type=MESH,
            )
            c.start()
            fin.append(c)
            place += count

    gains = [jnp.zeros((1, width), f32), jnp.zeros((1, width), f32)]
    for r in range(held):
        turned = lax.dot_general(
            weight[...],
            gu_low[:, r * tok : (r + 1) * tok],
            (((1,), (0,)), ((), ())),
            preferred_element_type=f32,
        )
        grad = turned.T
        hat, scale = norm_parts(block[r].astype(f32))
        gains[0] = gains[0] + jnp.sum(grad * hat, axis=0, keepdims=True)
        gains[1] = gains[1] + jnp.sum(grad, axis=0, keepdims=True)
        pulled = grad * gain_row
        pulled = pulled - jnp.mean(pulled, axis=-1, keepdims=True)
        pulled = pulled - hat * jnp.mean(pulled * hat, axis=-1, keepdims=True)
        gi_ref[r] = gm_ref[r] + scale * pulled
        if r == 0:
            third_unit.core_finish()
            for c in spart:
                c.wait()
            total = small_sum[pl.ds(me * chunk, chunk)]
            for d in range(groups - 1):
                total = total + small_part[d]
            small_done[:chunk] = total
            small_done[chunk:] = last_sum[...]
            small_o[me] = small_done[...]
            sdone = [
                pltpu.make_async_remote_copy(
                    src_ref=small_done,
                    dst_ref=small_o.at[me],
                    send_sem=sdone_ss.at[d - 1],
                    recv_sem=sdone_rs.at[d - 1],
                    device_id={"seq": lax.rem(me + d, groups)},
                    device_id_type=MESH,
                )
                for d in range(1, groups)
            ]
            for c in sdone:
                c.start()
    gain_own[...] = jnp.zeros_like(gain_own)
    for g in range(2):
        for n in range(per):
            line = g * per + n
            gain_own[line : line + 1, :] = gains[g][:, n * LANES : (n + 1) * LANES]
    grow = [
        pltpu.make_async_remote_copy(
            src_ref=gain_own,
            dst_ref=gain_row_buf.at[d - 1],
            send_sem=grow_ss.at[d - 1],
            recv_sem=grow_rs.at[d - 1],
            device_id={"row": lax.rem(row + d, rows)},
            device_id_type=MESH,
        )
        for d in range(1, rows)
    ]
    for c in grow:
        c.start()

    late.advance(0)
    for c in grow:
        c.wait()
    total = gain_own[...]
    for d in range(rows - 1):
        total = total + gain_row_buf[d]
    gain_sum[...] = total
    gains_o[me] = total
    gcast = [
        pltpu.make_async_remote_copy(
            src_ref=gain_sum,
            dst_ref=gains_o.at[me],
            send_sem=gcast_ss.at[d - 1],
            recv_sem=gcast_rs.at[d - 1],
            device_id={"seq": lax.rem(me + d, groups)},
            device_id_type=MESH,
        )
        for d in range(1, groups)
    ]
    for c in gcast:
        c.start()
    for k in range(3, rest.steps):
        rest.advance(k)
    close(rest, early, EARLY, 0)
    late.advance(1)
    for k in range(2, late.steps):
        late.advance(k)

    close(late, own, LATE, len(EARLY))
    late.wait_core_sends()
    late.wait_sends()
    rest.wait_sends()
    for c in sdone + gcast:
        c.wait()
    for c in fin:
        c.wait()


def finish(gw, ggo, u, edge, lengths, taps, weight, block, gm, vectors, early, sums):
    rows, groups = lax.axis_size("row"), lax.axis_size("seq")
    held, width, tok = gw.shape
    unit = width // groups
    half = width // 2
    wide = max(1, rows.bit_length() - 2)
    low, f32 = jnp.bfloat16, jnp.float32
    steps = groups.bit_length() - 1
    later = [range(n, steps) for n in EARLY_STEPS]
    used = sums[0].shape[0] + sums[1].shape[0] + 13 * (width // LANES)
    lines = used + -used % (8 * groups)
    chunk = lines // groups
    lead = -(-2 * (width // LANES) // 8) * 8
    last = sums[2]
    dma = pltpu.SemaphoreType.DMA
    vm = pl.BlockSpec(memory_space=pltpu.VMEM)
    sm = pl.BlockSpec(memory_space=pltpu.SMEM)
    hbm = pl.BlockSpec(memory_space=pl.ANY)
    return pl.pallas_call(
        functools.partial(finish_kernel, rows, groups),
        out_shape=(
            jax.ShapeDtypeStruct(gm.shape, f32),
            jax.ShapeDtypeStruct((2, sum(EARLY) + sum(LATE), unit, half), low),
            jax.ShapeDtypeStruct((groups, chunk + last.shape[0], LANES), f32),
            jax.ShapeDtypeStruct((groups, lead, LANES), f32),
        ),
        in_specs=[vm, vm, hbm, vm, sm, vm, hbm, hbm, hbm] + [vm] * 4 + [[hbm] * 3] + [vm] * 3,
        out_specs=(vm,) * 4,
        scratch_shapes=[
            pltpu.VMEM((8, 3 * width), f32),
            pltpu.VMEM((3, 3 * width, LANES), f32),
            pltpu.VMEM((3 * width, LANES), f32),
            pltpu.VMEM((3, 3 * width, LANES), f32),
            pltpu.VMEM((held, 3 * width, tok), f32),
            pltpu.VMEM((3 * width, held * tok), low),
            pltpu.VMEM((held, 3 * width, LANES), low),
            pltpu.VMEM((8, 3 * width), f32),
            pltpu.VMEM((8, 3 * width), f32),
            pltpu.VMEM((width, held * tok), low),
            pltpu.VMEM((width, 3 * width), low),
            pltpu.VMEM((lines, LANES), f32),
            [pltpu.VMEM((groups, n, unit, half), low) for n in LATE],
            [pltpu.VMEM(e.shape, low) for e in early],
            [pltpu.VMEM((width, n * half), low) for n in LATE],
            [
                [pltpu.VMEM((groups >> (k + 1), n, unit, half), low) for k in range(steps)]
                for n in LATE
            ],
            [
                [pltpu.VMEM((groups >> (k + 1), n, unit, half), low) for k in ks]
                for ks, n in zip(later, EARLY)
            ],
            [pltpu.VMEM((wide, n, unit, half), low) for n in EARLY + LATE],
            pltpu.VMEM((rows - 1, lines, LANES), f32),
            pltpu.VMEM((lines, LANES), f32),
            pltpu.VMEM((groups - 1, chunk, LANES), f32),
            pltpu.VMEM((chunk + last.shape[0], LANES), f32),
            pltpu.VMEM((rows - 1,) + last.shape, f32),
            pltpu.VMEM(last.shape, f32),
            dma((2,)),
            dma((3,)),
            pltpu.VMEM(u.shape, low),
            pltpu.VMEM(weight.shape, low),
            pltpu.VMEM(block.shape, low),
            pltpu.VMEM(gm.shape, f32),
            dma((4,)),
            dma((len(LATE),)),
            dma((len(LATE),)),
            [[dma((2,)) for k in range(steps)] for _ in LATE],
            [[dma((2,)) for k in range(steps)] for _ in LATE],
            [[dma((2,)) for k in ks] for ks in later],
            [[dma((2,)) for k in ks] for ks in later],
            dma((wide, 6)),
            dma((wide, 6)),
            dma((6,)),
            dma((6,)),
            dma((rows - 1,)),
            dma((rows - 1,)),
            dma((groups - 1,)),
            dma((groups - 1,)),
            dma((groups - 1,)),
            dma((groups - 1,)),
            dma((rows - 1,)),
            dma((rows - 1,)),
            pltpu.VMEM((lead, LANES), f32),
            pltpu.VMEM((rows - 1, lead, LANES), f32),
            pltpu.VMEM((lead, LANES), f32),
            dma((rows - 1,)),
            dma((rows - 1,)),
            dma((groups - 1,)),
            dma((groups - 1,)),
        ],
        compiler_params=pltpu.CompilerParams(
            collective_id=0, has_side_effects=True, vmem_limit_bytes=VMEM_LIMIT
        ),
        name="finish",
    )(gw, ggo, u, edge, lengths, taps, weight, block, gm, *vectors, early, *sums)


def unpack_kernel(
    feat,
    fin,
    packed,
    leads,
    gi,
    gain_o,
    bias_o,
    in_o,
    taps_o,
    first_o,
    first_b_o,
    mid_o,
    mid_b_o,
    freq_o,
    last_o,
    skip_o,
    out_o,
    feed_gain_o,
    feed_bias_o,
    up_o,
    down_o,
    gi_o,
    small,
    last,
):
    f32 = jnp.float32
    chunk, narrow = small.shape[0] // packed.shape[0], last.shape[0] // packed.shape[0]
    for g in range(packed.shape[0]):
        small[g * chunk : (g + 1) * chunk] = packed[g, :chunk]
        last[g * narrow : (g + 1) * narrow] = packed[g, chunk:]
    gi_o[...] = gi[...]
    unit, half = fin.shape[2], fin.shape[3]
    hidden = mid_o.shape[0]
    width = gain_o.shape[0]
    per = width // LANES
    outs = [(up_o, 1, 4, 0, 0), (down_o, 4, 1, 4, 0), (out_o, 1, 1, 8, 0)]
    outs = outs + [(in_o, 1, 1, 9 + p, 2 * p) for p in range(3)]
    for core in range(2):
        for out, high, cols, first, base in outs:
            for h in range(high):
                for c in range(cols):
                    at = (base + core * cols + c) * half
                    out[h * unit : (h + 1) * unit, at : at + half] = fin[
                        core, first + h * cols + c
                    ].astype(f32)

    def line(first, count):
        pieces = [small[first + i : first + i + 1, :] for i in range(count)]
        return jnp.concatenate(pieces, axis=1)

    at = hidden + -(-(feat + 1) // 8) * 8
    total = leads[0]
    for g in range(1, leads.shape[0]):
        total = total + leads[g]
    for out, first in ((gain_o, 0), (bias_o, per)):
        out[...] = jnp.concatenate([total[first + i : first + i + 1] for i in range(per)], axis=1)[0]
    for j in range(3):
        taps_o[j : j + 1, :] = line(at + 2 * per + 3 * per * j, 3 * per)
    feed_gain_o[...] = line(at + 11 * per, per)[0]
    feed_bias_o[...] = line(at + 12 * per, per)[0]
    first_o[...] = small[hidden : hidden + feat, :hidden]
    first_b_o[...] = small[hidden + feat : hidden + feat + 1, :hidden][0]
    mid_o[...] = small[:hidden, :hidden]
    shape = (hidden, hidden)
    same = lax.broadcasted_iota(jnp.int32, shape, 0) == lax.broadcasted_iota(jnp.int32, shape, 1)
    for out, col in ((mid_b_o, hidden), (freq_o, hidden + 1)):
        out[...] = jnp.sum(
            jnp.where(same, small[:hidden, col : col + 1], 0.0), axis=0, keepdims=True
        )[0]
    turned = last[...].T
    last_o[...] = turned[:hidden]
    skip_o[...] = turned[hidden : hidden + 1][0]


def unpack(fin, packed, leads, gi, feat, hidden, width):
    f32 = jnp.float32
    unit = fin.shape[2]
    vm = pl.BlockSpec(memory_space=pltpu.VMEM)
    shapes = [
        (width,),
        (width,),
        (unit, 3 * width),
        (3, 3 * width),
        (feat, hidden),
        (hidden,),
        (hidden, hidden),
        (hidden,),
        (hidden,),
        (hidden, width),
        (width,),
        (unit, width),
        (width,),
        (width,),
        (unit, 4 * width),
        (4 * unit, width),
        gi.shape,
    ]
    return pl.pallas_call(
        functools.partial(unpack_kernel, feat),
        out_shape=tuple(jax.ShapeDtypeStruct(x, f32) for x in shapes),
        in_specs=[vm] * 4,
        out_specs=(vm,) * len(shapes),
        scratch_shapes=[
            pltpu.VMEM((packed.shape[0] * packed.shape[1] - width, LANES), f32),
            pltpu.VMEM((width, LANES), f32),
        ],
        compiler_params=pltpu.CompilerParams(vmem_limit_bytes=VMEM_LIMIT),
        name="unpack",
    )(fin, packed, leads, gi)


def spectrum_tables(length):
    period = 2 * length
    first = period // LANES
    k1 = np.arange(first // 2 + 1, dtype=np.int64)[:, None, None]
    n2 = np.arange(LANES, dtype=np.int64)[None, :, None]
    k2 = np.arange(LANES, dtype=np.int64)[None, None, :]
    angle = 2.0 * np.pi / period * (n2 * (k1 + first * k2) % period)
    full = np.concatenate([np.cos(angle), np.sin(angle)], axis=2).astype(np.float32)
    high = full.astype(jnp.bfloat16)
    rest = (full - high.astype(np.float32)).astype(jnp.bfloat16)
    return high, rest


def feature_rows(length, feat_count):
    bands = (feat_count - 1) // 2
    at = np.arange(length, dtype=np.int64)[None, :]
    angle = 2.0 * np.pi / length * (at * np.arange(1, bands + 1)[:, None] % length)
    rows = [at / length, np.cos(angle), -np.sin(angle), np.ones((1, length))]
    rows = np.concatenate(rows, axis=0)
    pad = -rows.shape[0] % 8
    return np.pad(rows, ((0, pad), (0, 0))).astype(np.float32)


def sin_cos(x):
    n = jnp.round(x * (2.0 / math.pi))
    r = x - n * 1.5703125
    r = r - n * 4.837512969970703125e-4
    r = r - n * 7.549789948768648e-8
    z = r * r
    s = r + r * z * (-1.6666654611e-1 + z * (8.3321608736e-3 - z * 1.9515295891e-4))
    c = (
        1.0
        - 0.5 * z
        + z * z * (4.166664568298827e-2 + z * (-1.388731625493765e-3 + z * 2.443315711809948e-5))
    )
    q = n.astype(jnp.int32) & 3
    odd = (q & 1) == 1
    sine = jnp.where(odd, c, s)
    cosine = jnp.where(odd, s, c)
    sine = jnp.where(q >= 2, -sine, sine)
    cosine = jnp.where((q == 1) | (q == 2), -cosine, cosine)
    return sine, cosine


def exact_dot(p, q, left, right):
    low = jnp.bfloat16

    def dot(x, y):
        return lax.dot_general(
            x, y, (((left,), (right,)), ((), ())), preferred_element_type=jnp.float32
        )

    ph, qh = p.astype(low), q.astype(low)
    pl_, ql = (p - ph.astype(jnp.float32)).astype(low), (q - qh.astype(jnp.float32)).astype(low)
    return dot(ph, qh) + (dot(pl_, qh) + dot(ph, ql))


def column_of(row):
    size = row.shape[1]
    shape = (size, size)
    same = lax.broadcasted_iota(jnp.int32, shape, 0) == lax.broadcasted_iota(jnp.int32, shape, 1)
    return jnp.sum(jnp.where(same, row, 0.0), axis=1, keepdims=True)


class FilterNet:
    def __init__(self, me, narrow, params, aug):
        first, first_b, mid, mid_b, freq, last, skip, decay, self.feats = params
        feat = first.shape[0]
        aug[...] = jnp.zeros_like(aug)
        aug[:feat, :] = first[...]
        aug[feat : feat + 1, :] = first_b[...][None, :]
        self.aug = aug
        self.mid = mid
        self.mid_b = column_of(mid_b[...][None, :])
        self.freq = column_of(freq[...][None, :])
        width = skip.shape[0]
        shape = (narrow, width)
        pick = (
            lax.broadcasted_iota(jnp.int32, shape, 1)
            == lax.broadcasted_iota(jnp.int32, shape, 0) + me * narrow
        )
        self.skip = jnp.sum(jnp.where(pick, skip[...][None, :], 0.0), axis=1, keepdims=True)
        self.decay = jnp.sum(jnp.where(pick, decay[...][None, :], 0.0), axis=1, keepdims=True)
        self.last = exact_dot(pick.astype(jnp.float32), last[...], 1, 1)
        self.narrow = narrow

    def layers(self, at, size):
        feats = self.feats[:, pl.ds(at, size)]
        pre1 = exact_dot(self.aug[...], feats, 0, 0)
        a1, c1 = sin_cos(self.freq * pre1)
        pre2 = exact_dot(self.mid[...], a1, 0, 0) + self.mid_b
        a2, c2 = sin_cos(self.freq * pre2)
        return feats, pre1, a1, c1, pre2, a2, c2

    def fade(self, at, size):
        where = lax.broadcasted_iota(jnp.int32, (self.narrow, size), 1) + at
        return jnp.exp(-self.decay * where.astype(jnp.float32)), where

    def build(self, at, size):
        a2 = self.layers(at, size)[5]
        fade, where = self.fade(at, size)
        return exact_dot(self.last, a2, 1, 0) * fade + jnp.where(where == 0, self.skip, 0.0)

    def pull(self, at, size, grad, first_o, mid_o, last_o):
        feats, pre1, a1, c1, pre2, a2, c2 = self.layers(at, size)
        fade, where = self.fade(at, size)
        hidden = a1.shape[0]
        raw = grad * fade
        last_o[:, :hidden] += exact_dot(raw, a2, 1, 1)
        last_o[:, hidden : hidden + 1] += jnp.sum(
            jnp.where(where == 0, grad, 0.0), axis=1, keepdims=True
        )
        turned2 = exact_dot(self.last, raw, 0, 0) * c2
        freq = jnp.sum(turned2 * pre2, axis=1, keepdims=True)
        down2 = turned2 * self.freq
        mid_o[:, :hidden] += exact_dot(a1, down2, 1, 1)
        mid_o[:, hidden : hidden + 1] += jnp.sum(down2, axis=1, keepdims=True)
        turned1 = exact_dot(self.mid[...], down2, 1, 0) * c1
        freq = freq + jnp.sum(turned1 * pre1, axis=1, keepdims=True)
        mid_o[:, hidden + 1 : hidden + 2] += freq
        down1 = turned1 * self.freq
        first_o[:, :hidden] += exact_dot(feats, down1, 1, 1)


CHUNK = 4


def half_dft(x):
    count = 2 * len(x)
    if count == 2:
        return [(x[0], None), (x[0], None)]
    even, odd = half_dft(x[0::2]), half_dft(x[1::2])
    out = [None] * (count // 2 + 1)
    for k in range(count // 4 + 1):
        er, ei = even[k]
        orr, oi = odd[k]
        if k == 0:
            out[0] = (er + orr, None)
            out[count // 2] = (er - orr, None)
        elif 4 * k == count:
            out[k] = (er, -orr)
        else:
            c, s = math.cos(2 * math.pi * k / count), math.sin(2 * math.pi * k / count)
            tr = orr * c + oi * s
            ti = oi * c - orr * s
            out[k] = (er + tr, ei + ti)
            out[count // 2 - k] = (er - tr, ti - ei)
    return out


def half_inverse(spec):
    count = 2 * (len(spec) - 1)
    if count == 2:
        return [spec[0][0] + spec[1][0]]
    even, odd = [], []
    for k in range(count // 4 + 1):
        ar, ai = spec[k]
        br, bi = spec[count // 2 - k]
        if k == 0:
            even.append((ar + br, None))
            odd.append((ar - br, None))
        elif 4 * k == count:
            even.append((ar + ar, None))
            odd.append((-(ai + ai), None))
        else:
            c, s = math.cos(2 * math.pi * k / count), math.sin(2 * math.pi * k / count)
            dr, di = ar - br, ai + bi
            even.append((ar + br, ai - bi))
            odd.append((dr * c - di * s, dr * s + di * c))
    out = [None] * (count // 2)
    out[0::2] = half_inverse(even)
    out[1::2] = half_inverse(odd)
    return out


def turn_of(table):
    cos, sin = table[:, :LANES], table[:, LANES:]
    return jnp.concatenate(
        [jnp.concatenate([cos, -sin], axis=1), jnp.concatenate([sin, cos], axis=1)], axis=0
    )


def split_dot(a, high, rest, back):
    a_high = a.astype(jnp.bfloat16)
    a_rest = (a - a_high.astype(jnp.float32)).astype(jnp.bfloat16)
    dims = (((1,), (1 if back else 0,)), ((), ()))
    high, rest = turn_of(high), turn_of(rest)

    def dot(p, q):
        return lax.dot_general(p, q, dims, preferred_element_type=jnp.float32)

    rows = a.shape[0]
    both = dot(jnp.concatenate([a_high, a_rest], axis=0), high)
    return both[:rows] + (both[rows:] + dot(a_high, rest))


def tile_loop(tiles, body):
    def step(i, carry):
        body(pl.multiple_of(i * 8, 8))
        return carry

    lax.fori_loop(0, tiles, step, 0, unroll=3 if tiles % 3 == 0 else 1)


def first_stage(load, spec, tiles):
    zero = jnp.zeros((8, LANES), jnp.float32)

    def body(at):
        for k, (re, im) in enumerate(half_dft(load(at))):
            spec[k, pl.ds(at, 8), :LANES] = re
            spec[k, pl.ds(at, 8), LANES:] = zero if im is None else im

    tile_loop(tiles, body)


def last_stage(spec, store, tiles, scale, start):
    def body(at):
        at = pl.multiple_of(at + start, 8)
        freqs = spec.shape[0]
        values = []
        for k in range(freqs):
            re = spec[k, pl.ds(at, 8), :LANES]
            im = None if k in (0, freqs - 1) else spec[k, pl.ds(at, 8), LANES:]
            values.append((re, im))
        for n, v in enumerate(half_inverse(values)):
            store(n, at, v * scale)

    tile_loop(tiles, body)


def greet(groups, me):
    barrier = pltpu.get_barrier_semaphore()
    for d in range(1, groups):
        pl.semaphore_signal(
            barrier, inc=1, device_id={"seq": lax.rem(me + d, groups)}, device_id_type=MESH
        )


def met(groups):
    pl.semaphore_wait(pltpu.get_barrier_semaphore(), groups - 1)


def to_channels(groups, me, narrow, r, src, recv, ss, rs, ls):
    local = pltpu.make_async_copy(
        src.at[r, pl.ds(pl.multiple_of(me * narrow, 8), narrow), :], recv.at[me, r], ls
    )
    out = [local]
    for d in range(1, groups):
        to = lax.rem(me + d, groups)
        out.append(
            pltpu.make_async_remote_copy(
                src_ref=src.at[r, pl.ds(pl.multiple_of(to * narrow, 8), narrow), :],
                dst_ref=recv.at[me, r],
                send_sem=ss.at[d - 1, r],
                recv_sem=rs.at[d - 1, r],
                device_id={"seq": to},
                device_id_type=MESH,
            )
        )
    return out


def to_positions(groups, me, narrow, r, send, dst, ss, rs, ls):
    mine = dst.at[r, pl.ds(pl.multiple_of(me * narrow, 8), narrow), :]
    out = [pltpu.make_async_copy(send.at[me, r], mine, ls)]
    for d in range(1, groups):
        to = lax.rem(me + d, groups)
        out.append(
            pltpu.make_async_remote_copy(
                src_ref=send.at[to, r],
                dst_ref=mine,
                send_sem=ss.at[d - 1, r],
                recv_sem=rs.at[d - 1, r],
                device_id={"seq": to},
                device_id_type=MESH,
            )
        )
    return out


def spread(recv, wide, narrow):
    per = recv.shape[3] // LANES

    def step(s, carry):
        for r in range(recv.shape[1]):
            for h in range(per):
                wide[s * per + h, r * narrow : (r + 1) * narrow, :] = recv[
                    s, r, :, h * LANES : (h + 1) * LANES
                ].astype(jnp.float32)
        return carry

    lax.fori_loop(0, recv.shape[0], step, 0, unroll=4)


def gather_back(wide, send, narrow, r):
    per = send.shape[3] // LANES

    def step(s, carry):
        for h in range(per):
            send[s, r, :, h * LANES : (h + 1) * LANES] = wide[
                s * per + h, r * narrow : (r + 1) * narrow, :
            ].astype(jnp.bfloat16)
        return carry

    lax.fori_loop(0, send.shape[0], step, 0, unroll=4)


def freq_loop(freqs, unroll, body):
    def step(i, carry):
        for j in range(unroll):
            body(i * unroll + j)
        return carry

    lax.fori_loop(0, freqs // unroll, step, 0)


UNROLL = {33: 11, 65: 13}


def conv_kernel(
    groups,
    block,
    lengths,
    gain,
    offset,
    weight_hbm,
    taps,
    first,
    first_b,
    mid,
    mid_b,
    freq,
    last,
    skip,
    decay,
    feats,
    high_ref,
    rest_ref,
    z_ref,
    w_spec_o,
    h_spec_o,
    u_o,
    gate_o,
    edge_o,
    high,
    rest,
    recv,
    wide,
    back,
    send,
    in_ss,
    in_rs,
    out_ss,
    out_rs,
    local,
    aug,
    filt,
    normed,
    w_ref,
    padded,
    wide_taps,
    edges,
    rim_out,
    rim_in,
    rim_sem,
    w_spec,
    h_spec,
    u_ref,
    gate_ref,
    weight,
    move_sem,
):
    me = lax.axis_index("seq")
    narrow = h_spec.shape[1]
    count, freqs = wide.shape[0], high.shape[0]
    rows, width, tok = w_ref.shape
    low, f32 = jnp.bfloat16, jnp.float32
    unroll = UNROLL.get(freqs, 1)
    tables = [
        pltpu.make_async_copy(high_ref, high, local.at[0]),
        pltpu.make_async_copy(rest_ref, rest, local.at[1]),
    ]
    bring = pltpu.make_async_copy(weight_hbm, weight, move_sem.at[0])
    keep_u, keep_gate, keep_h, keep_w = [
        pltpu.make_async_copy(src, dst, move_sem.at[1 + n])
        for n, (src, dst) in enumerate(
            ((u_ref, u_o), (gate_ref, gate_o), (h_spec, h_spec_o), (w_spec, w_spec_o))
        )
    ]
    bring.start()
    for c in tables:
        c.start()
    greet(groups, me)

    gain_row, offset_row = gain[...][None, :], offset[...][None, :]
    for r in range(rows):
        hat, _ = norm_parts(block[r].astype(f32))
        normed[:, r * tok : (r + 1) * tok] = (hat * gain_row + offset_row).T.astype(low)
    piece = 256

    def project(i, carry):
        cols = pl.ds(pl.multiple_of(i * piece, piece), piece)
        part = lax.dot_general(
            weight[:, cols], normed[...], (((0,), (0,)), ((), ())), preferred_element_type=f32
        ).astype(low)
        for r in range(rows):
            u_ref[r, cols, :] = part[:, r * tok : (r + 1) * tok]
        return carry

    bring.wait()
    lax.fori_loop(0, 3 * width // piece, project, 0)
    keep_u.start()
    rim_out[...] = pack_edges([u_ref[r, :, tok - LANES :] for r in range(rows)])
    met(groups)
    rim_copy = pltpu.make_async_remote_copy(
        src_ref=rim_out,
        dst_ref=rim_in,
        send_sem=rim_sem.at[0],
        recv_sem=rim_sem.at[1],
        device_id={"seq": lax.rem(me + 1, groups)},
        device_id_type=MESH,
    )
    rim_copy.start()
    spread_taps(taps, padded, wide_taps)
    lane = lax.broadcasted_iota(jnp.int32, (STRIP, tok), 1)
    masks = [row_masks(lengths, r, me * tok, tok) for r in range(rows)]
    rim_copy.wait()
    edge_o[...] = rim_in[...]
    inward = []
    def mix(i, r, g):
        at = pl.ds(pl.multiple_of(i * STRIP + g * width, STRIP), STRIP)
        tap = [jnp.concatenate([wide_taps[j, at, :]] * (tok // LANES), axis=1) for j in range(3)]
        u = u_ref[r, at, :].astype(f32)
        one, two = window_of(u, lane, edges[at, :])
        return tap[0] * u + tap[1] * one * masks[r][0] + tap[2] * two * masks[r][1]

    for r in range(rows):
        edges[...] = unpack_edge(rim_in[...], r)

        def strip(i, carry, r=r):
            at = pl.ds(pl.multiple_of(i * STRIP, STRIP), STRIP)
            w_ref[r, at, :] = (mix(i, r, 1) * mix(i, r, 2) * masks[r][2]).astype(low)
            return carry

        lax.fori_loop(0, width // STRIP, strip, 0)
        ready = to_channels(
            groups, me, narrow, r, w_ref, recv, in_ss, in_rs, local.at[3 + rows + r]
        )
        for c in ready:
            c.start()
        inward = inward + ready

    for r in range(rows):
        edges[:width, :] = unpack_edge(rim_in[:, :width], r)

        def gate(i, carry, r=r):
            at = pl.ds(pl.multiple_of(i * STRIP, STRIP), STRIP)
            gate_ref[r, at, :] = mix(i, r, 0) * masks[r][2]
            return carry

        lax.fori_loop(0, width // STRIP, gate, 0)
    keep_gate.start()
    net = FilterNet(me, narrow, (first, first_b, mid, mid_b, freq, last, skip, decay, feats), aug)

    def build(i, carry):
        size = CHUNK * LANES
        values = net.build(pl.multiple_of(i * size, LANES), size)
        for j in range(CHUNK):
            filt[i * CHUNK + j] = values[:, j * LANES : (j + 1) * LANES]
        return carry

    lax.fori_loop(0, count // CHUNK, build, 0)
    first_stage(
        lambda at: [filt[n, pl.ds(at, 8), :] for n in range(count)], h_spec, narrow // 8
    )
    for c in tables:
        c.wait()

    def filter_freq_step(k):
        h_spec[k] = split_dot(h_spec[k], high[k], rest[k], False)

    freq_loop(freqs, unroll, filter_freq_step)
    keep_h.start()
    for c in inward:
        c.wait()
    spread(recv, wide, narrow)
    first_stage(
        lambda at: [wide[n, pl.ds(at, 8), :] for n in range(count)], w_spec, rows * narrow // 8
    )

    def forward_step(k):
        w_spec[k] = split_dot(w_spec[k], high[k], rest[k], False)

    def inverse_step(k):
        h = h_spec[k]
        hr, hi = h[:, :LANES], h[:, LANES:]
        parts = []
        for r in range(rows):
            w = w_spec[k, r * narrow : (r + 1) * narrow]
            wr, wi = w[:, :LANES], w[:, LANES:]
            parts.append(jnp.concatenate([wr * hr - wi * hi, wr * hi + wi * hr], axis=1))
        back[k] = split_dot(jnp.concatenate(parts, axis=0), high[k], rest[k], True)

    freq_loop(freqs, unroll, forward_step)
    keep_w.start()
    freq_loop(freqs, unroll, inverse_step)

    def store(n, at, v):
        wide[n, pl.ds(at, 8), :] = v

    outward = []
    for r in range(rows):
        last_stage(back, store, narrow // 8, 1.0 / (2 * count * LANES), r * narrow)
        gather_back(wide, send, narrow, r)
        ready = to_positions(groups, me, narrow, r, send, z_ref, out_ss, out_rs, local.at[3 + r])
        for c in ready:
            c.start()
        outward = outward + ready
    for c in outward + [keep_u, keep_gate, keep_h, keep_w]:
        c.wait()


def conv_back_kernel(
    rows_all,
    groups,
    g_ref,
    w_hbm,
    h_hbm,
    high_ref,
    rest_ref,
    down_hbm,
    ga_hbm,
    y2,
    q_ref,
    gm_ref,
    first,
    first_b,
    mid,
    mid_b,
    freq,
    last,
    skip,
    decay,
    feats,
    gw_ref,
    early_o,
    first_o,
    mid_o,
    last_o,
    high,
    rest,
    recv,
    wide,
    back,
    send,
    in_ss,
    in_rs,
    out_ss,
    out_rs,
    local,
    own,
    core_buf,
    step_buf,
    core_ss,
    core_rs,
    step_ss,
    step_rs,
    aug,
    w_spec,
    h_spec,
    gout,
    gup,
    gdown,
    ga_buf,
    y2_turned,
    ga_sem,
    spec_sem,
    keep_sem,
):
    me = lax.axis_index("seq")
    row = lax.axis_index("row")
    core = lax.rem(row, 2)
    narrow = h_spec.shape[1]
    count, freqs = wide.shape[0], high.shape[0]
    rows = g_ref.shape[0]
    unroll = UNROLL.get(freqs, 1)
    tables = [
        pltpu.make_async_copy(high_ref, high, local.at[0]),
        pltpu.make_async_copy(rest_ref, rest, local.at[1]),
    ]
    piece = ga_buf.shape[2]
    pieces = ga_hbm.shape[1] // piece
    low, f32 = jnp.bfloat16, jnp.float32

    def part_copy(src, buf, sem, i, slot):
        cols = pl.ds(pl.multiple_of(i * piece, piece), piece)
        return pltpu.make_async_copy(src.at[:, cols], buf.at[slot], sem.at[slot])

    def stream(src, buf, sem, body):
        def step(i, carry):
            slot = lax.rem(i, 2)

            @pl.when(i + 1 < pieces)
            def _():
                part_copy(src, buf, sem, i + 1, 1 - slot).start()

            part_copy(src, buf, sem, i, slot).wait()
            body(pl.ds(pl.multiple_of(i * piece, piece), piece), buf[slot])
            return carry

        lax.fori_loop(0, pieces, step, 0)

    bring = pltpu.make_async_copy(down_hbm, gdown, spec_sem.at[2])
    bring.start()
    part_copy(ga_hbm, ga_buf, ga_sem, 0, 0).start()
    spectra = [
        pltpu.make_async_copy(w_hbm, w_spec, spec_sem.at[0]),
        pltpu.make_async_copy(h_hbm, h_spec, spec_sem.at[1]),
    ]
    for c in tables + spectra:
        c.start()
    greet_all(rows_all, groups, me, row)
    inward = []
    for r in range(rows):
        inward = inward + to_channels(
            groups, me, narrow, r, g_ref, recv, in_ss, in_rs, local.at[3 + rows + r]
        )
    for c in inward:
        c.start()
    early = early_crew(groups, me, core, gout, gup, gdown, own, down_hbm)
    early.core_setup(core_buf, core_ss, core_rs, row + 1 - 2 * core)
    early.step_setup(step_buf, step_ss, step_rs, [range(n) for n in EARLY_STEPS])

    def up_part(cols, part):
        gup[:, cols] = jnp.dot(y2_turned[...], part, preferred_element_type=f32).astype(low)

    up_sum, down_sum, out_sum = early.members
    down_sum.core_start()

    y2_turned[...] = y2[...].T
    stream(ga_hbm, ga_buf, ga_sem, up_part)
    up_sum.core_start()
    bring.wait()
    down_sum.core_finish()
    total = None
    for r in range(rows):
        tok = q_ref.shape[2]
        part = jnp.dot(
            q_ref[r], gm_ref[r * tok : (r + 1) * tok, :], preferred_element_type=f32
        )
        total = part if total is None else total + part
    gout[...] = total.astype(low)
    out_sum.core_start()
    up_sum.core_finish()
    out_sum.core_finish()
    for c in tables + spectra:
        c.wait()
    for c in inward:
        c.wait()
    spread(recv, wide, narrow)
    first_stage(
        lambda at: [wide[n, pl.ds(at, 8), :] for n in range(count)], back, rows * narrow // 8
    )

    def forward_step(k):
        back[k, : rows * narrow] = split_dot(back[k, : rows * narrow], high[k], rest[k], False)

    def inverse_step(k):
        h = h_spec[k]
        hr, hi = h[:, :LANES], h[:, LANES:]
        parts = []
        hsum = None
        for r in range(rows):
            w = w_spec[k, r * narrow : (r + 1) * narrow]
            wr, wi = w[:, :LANES], w[:, LANES:]
            g = back[k, r * narrow : (r + 1) * narrow]
            gr, gi = g[:, :LANES], g[:, LANES:]
            parts.append(jnp.concatenate([hr * gr + hi * gi, hr * gi - hi * gr], axis=1))
            pair = (wr * gr + wi * gi, wr * gi - wi * gr)
            hsum = pair if hsum is None else (hsum[0] + pair[0], hsum[1] + pair[1])
        parts.append(jnp.concatenate(hsum, axis=1))
        back[k] = split_dot(jnp.concatenate(parts, axis=0), high[k], rest[k], True)

    freq_loop(freqs, unroll, forward_step)
    freq_loop(freqs, unroll, inverse_step)

    def store(n, at, v):
        wide[n, pl.ds(at, 8), :] = v

    outward = []
    for r in range(rows):
        last_stage(back, store, narrow // 8, 1.0 / (2 * count * LANES), r * narrow)
        gather_back(wide, send, narrow, r)
        ready = to_positions(groups, me, narrow, r, send, gw_ref, out_ss, out_rs, local.at[3 + r])
        for c in ready:
            c.start()
        outward = outward + ready
    last_stage(back, store, narrow // 8, 1.0 / (2 * count * LANES), rows * narrow)
    net = FilterNet(me, narrow, (first, first_b, mid, mid_b, freq, last, skip, decay, feats), aug)
    for out in (first_o, mid_o, last_o):
        out[...] = jnp.zeros_like(out)

    def pull(i, carry):
        size = CHUNK * LANES
        grad = [wide[i * CHUNK + j, rows * narrow :, :] for j in range(CHUNK)]
        net.pull(
            pl.multiple_of(i * size, LANES),
            size,
            jnp.concatenate(grad, axis=1),
            first_o,
            mid_o,
            last_o,
        )
        return carry

    lax.fori_loop(0, count // CHUNK, pull, 0)
    kept = []
    for p, h in enumerate(early.members):
        k = EARLY_STEPS[p] - 1
        for j in range(2):
            h.finish(k, j)
            i, size = h.pieces(k)[j]
            kept.append(
                pltpu.make_async_copy(
                    own[p].at[pl.ds(h.slot(k + 1) + i, size)],
                    early_o[p].at[pl.ds(i, size)],
                    keep_sem.at[p, j],
                )
            )
            kept[-1].start()
    for c in kept:
        c.wait()
    early.wait_core_sends()
    early.wait_sends()
    for c in outward:
        c.wait()


def conv_scratch(groups, rows, narrow, tok, freqs, count, extra):
    low, f32 = jnp.bfloat16, jnp.float32
    dma = pltpu.SemaphoreType.DMA
    wide_rows = (rows + extra) * narrow
    out = [
        pltpu.VMEM((freqs, LANES, 2 * LANES), low),
        pltpu.VMEM((freqs, LANES, 2 * LANES), low),
        pltpu.VMEM((groups, rows, narrow, tok), low),
        pltpu.VMEM((count, wide_rows, LANES), f32),
    ]
    return out + [
        pltpu.VMEM((freqs, wide_rows, 2 * LANES), f32),
        pltpu.VMEM((groups, rows, narrow, tok), low),
        dma((groups - 1, rows)),
        dma((groups - 1, rows)),
        dma((groups - 1, rows)),
        dma((groups - 1, rows)),
        dma((3 + 2 * rows,)),
    ]


def conv_params(cid):
    return pltpu.CompilerParams(
        collective_id=cid, has_side_effects=True, vmem_limit_bytes=VMEM_LIMIT
    )


def conv_forward(block, lengths, gain, offset, weight, taps, params, tables):
    rows, tok, width = block.shape
    groups = lax.axis_size("seq")
    narrow, length = width // groups, tok * groups
    count = length // LANES
    freqs = count + 1
    low, f32 = jnp.bfloat16, jnp.float32
    vm = pl.BlockSpec(memory_space=pltpu.VMEM)
    sm = pl.BlockSpec(memory_space=pltpu.SMEM)
    hbm = pl.BlockSpec(memory_space=pl.ANY)
    return pl.pallas_call(
        functools.partial(conv_kernel, groups),
        out_shape=(
            jax.ShapeDtypeStruct((rows, width, tok), low),
            jax.ShapeDtypeStruct((freqs, rows * narrow, 2 * LANES), f32),
            jax.ShapeDtypeStruct((freqs, narrow, 2 * LANES), f32),
            jax.ShapeDtypeStruct((rows, 3 * width, tok), low),
            jax.ShapeDtypeStruct((rows, width, tok), f32),
            jax.ShapeDtypeStruct((8, 3 * width), f32),
        ),
        in_specs=[vm, sm, vm, vm, hbm] + [vm] * 10 + [hbm, hbm],
        out_specs=(vm, hbm, hbm, hbm, hbm, vm),
        scratch_shapes=conv_scratch(groups, rows, narrow, tok, freqs, count, 0)
        + [
            pltpu.VMEM((params[-1].shape[0], params[0].shape[1]), f32),
            pltpu.VMEM((count, narrow, LANES), f32),
            pltpu.VMEM((width, rows * tok), low),
            pltpu.VMEM((rows, width, tok), low),
            pltpu.VMEM((8, 3 * width), f32),
            pltpu.VMEM((3, 3 * width, LANES), f32),
            pltpu.VMEM((3 * width, LANES), f32),
            pltpu.VMEM((8, 3 * width), f32),
            pltpu.VMEM((8, 3 * width), f32),
            pltpu.SemaphoreType.DMA((2,)),
            pltpu.VMEM((freqs, rows * narrow, 2 * LANES), f32),
            pltpu.VMEM((freqs, narrow, 2 * LANES), f32),
            pltpu.VMEM((rows, 3 * width, tok), low),
            pltpu.VMEM((rows, width, tok), f32),
            pltpu.VMEM(weight.shape, low),
            pltpu.SemaphoreType.DMA((5,)),
        ],
        compiler_params=conv_params(1),
        name="conv_forward",
    )(block, lengths, gain, offset, weight, taps, *params, *tables)


def conv_backward(grad, w_spec, h_spec, tables, grad_down, grad_pre, y2, q, gm, params):
    rows, _, tok = grad.shape
    freqs, narrow, _ = h_spec.shape
    groups = lax.axis_size("seq")
    count = freqs - 1
    width, ffn = q.shape[1], grad_pre.shape[1]
    half = width // 2
    piece = width
    vm = pl.BlockSpec(memory_space=pltpu.VMEM)
    hbm = pl.BlockSpec(memory_space=pl.ANY)
    low, f32 = jnp.bfloat16, jnp.float32
    dma = pltpu.SemaphoreType.DMA
    kept = [groups >> n for n in EARLY_STEPS]
    feat_rows, hidden = params[-1].shape[0], params[0].shape[1]
    return pl.pallas_call(
        functools.partial(conv_back_kernel, lax.axis_size("row"), groups),
        out_shape=(
            jax.ShapeDtypeStruct(grad.shape, low),
            [jax.ShapeDtypeStruct((c, n, narrow, half), low) for c, n in zip(kept, EARLY)],
            jax.ShapeDtypeStruct((feat_rows, LANES), f32),
            jax.ShapeDtypeStruct((hidden, LANES), f32),
            jax.ShapeDtypeStruct((narrow, LANES), f32),
        ),
        in_specs=[vm] + [hbm] * 6 + [vm] * 12,
        out_specs=(vm, [hbm] * 3, vm, vm, vm),
        scratch_shapes=conv_scratch(groups, rows, narrow, tok, freqs, count, 1)
        + [
            [pltpu.VMEM((groups, n, narrow, half), low) for n in EARLY],
            [
                pltpu.VMEM((width, 4 * half), low),
                pltpu.VMEM((ffn, half), low),
                pltpu.VMEM((width, half), low),
            ],
            [
                [pltpu.VMEM((groups >> (k + 1), n, narrow, half), low) for k in range(c)]
                for c, n in zip(EARLY_STEPS, EARLY)
            ],
            dma((len(EARLY),)),
            dma((len(EARLY),)),
            [[dma((2,)) for k in range(c)] for c in EARLY_STEPS],
            [[dma((2,)) for k in range(c)] for c in EARLY_STEPS],
            pltpu.VMEM((feat_rows, hidden), f32),
            pltpu.VMEM(w_spec.shape, f32),
            pltpu.VMEM(h_spec.shape, f32),
            pltpu.VMEM((width, width), low),
            pltpu.VMEM((width, ffn), low),
            pltpu.VMEM((ffn, width), low),
            pltpu.VMEM((2, y2.shape[0], piece), low),
            pltpu.VMEM((width, y2.shape[0]), low),
            dma((2,)),
            dma((3,)),
            dma((len(EARLY), 2)),
        ],
        compiler_params=conv_params(2),
        name="conv_backward",
    )(grad, w_spec, h_spec, *tables, grad_down, grad_pre, y2, q, gm, *params)


def shards(
    block_in,
    lengths,
    mixer_gain,
    mixer_bias,
    in_weight,
    short_taps,
    filter_in,
    filter_in_bias,
    filter_mid,
    filter_mid_bias,
    filter_freq,
    filter_out,
    filter_skip,
    decay_rate,
    out_weight,
    feed_gain,
    feed_bias,
    up_weight,
    down_weight,
    cotangent,
):
    _, tok_count, model_width = block_in.shape
    length = tok_count * lax.axis_size("seq")
    block_float = block_in.astype(jnp.float32)
    tables = tuple(jnp.asarray(t) for t in spectrum_tables(length))
    params = (
        filter_in,
        filter_in_bias,
        filter_mid,
        filter_mid_bias,
        filter_freq,
        filter_out,
        filter_skip,
        decay_rate,
        jnp.asarray(feature_rows(length, filter_in.shape[0])),
    )
    back_home, w_spec, h_spec, projected, gate_out, edges = conv_forward(
        block_in, lengths, mixer_gain, mixer_bias, in_weight, short_taps, params, tables
    )
    conv_float = back_home.astype(jnp.float32)
    product_low = (gate_out * conv_float).astype(jnp.bfloat16)
    mixed = block_float + jnp.einsum(
        "rct,cd->rtd", product_low, out_weight, preferred_element_type=jnp.float32
    )
    normed_two, feed_pull = jax.vjp(layer_norm, mixed, feed_gain, feed_bias)
    normed_two_low = normed_two.astype(jnp.bfloat16)
    pre_act = jnp.einsum(
        "rtd,df->rtf", normed_two_low, up_weight, preferred_element_type=jnp.float32
    )
    activ, gelu_pull = jax.vjp(jax.nn.gelu, pre_act)
    activ_low = activ.astype(jnp.bfloat16)
    block_out = (
        mixed
        + jnp.einsum("rtf,fd->rtd", activ_low, down_weight, preferred_element_type=jnp.float32)
    ).astype(jnp.bfloat16)
    grad_float = cotangent.astype(jnp.float32)
    grad_down = jnp.einsum("rtf,rtd->fd", activ_low, cotangent, preferred_element_type=jnp.float32)
    grad_activ = jnp.einsum(
        "rtd,fd->rtf", cotangent, down_weight, preferred_element_type=jnp.float32
    )
    grad_pre = gelu_pull(grad_activ)[0].astype(jnp.bfloat16)
    grad_normed_two = jnp.einsum(
        "rtf,df->rtd", grad_pre, up_weight, preferred_element_type=jnp.float32
    )
    grad_mixed_part, grad_feed_gain, grad_feed_bias = feed_pull(grad_normed_two)
    grad_mixed = grad_float + grad_mixed_part
    grad_mixed_low = grad_mixed.astype(jnp.bfloat16)
    grad_product = jnp.einsum(
        "rtd,cd->rct", grad_mixed_low, out_weight, preferred_element_type=jnp.float32
    )
    grad_gate_out = grad_product * conv_float
    grad_conv = (grad_product * gate_out).astype(jnp.bfloat16)

    def flat_rows(v):
        return v.reshape(-1, v.shape[-1])

    grad_carried, early, first_sum, mid_sum, last_sum = conv_backward(
        grad_conv,
        w_spec,
        h_spec,
        tables,
        grad_down.astype(jnp.bfloat16),
        flat_rows(grad_pre),
        flat_rows(normed_two_low),
        product_low,
        flat_rows(grad_mixed_low),
        params,
    )
    grad_input, fin, small, leads = finish(
        grad_carried,
        grad_gate_out,
        projected,
        edges,
        lengths,
        short_taps,
        in_weight,
        block_in,
        grad_mixed,
        (mixer_gain, mixer_bias, grad_feed_gain, grad_feed_bias),
        early,
        (mid_sum, first_sum, last_sum),
    )
    *done, grad_input = unpack(
        fin, small, leads, grad_input, filter_in.shape[0], filter_mid.shape[0], model_width
    )
    return (block_out, grad_input, *done)


def solution(mesh):
    placed = (
        P("row", "seq", None),
        P("row", None),
        P(),
        P(),
        P(),
        P(),
        P(),
        P(),
        P(),
        P(),
        P(),
        P(),
        P(),
        P(),
        P(),
        P(),
        P(),
        P(),
        P(),
        P("row", "seq", None),
    )
    return jax.shard_map(
        shards,
        mesh=mesh,
        in_specs=placed,
        out_specs=(
            P("row", "seq", None),
            P("row", "seq", None),
            P(),
            P(),
            P("seq", None),
            P(),
            P(),
            P(),
            P(),
            P(),
            P(),
            P(),
            P(),
            P("seq", None),
            P(),
            P(),
            P("seq", None),
            P("seq", None),
        ),
        check_vma=False,
    )
```

```python
import functools
import math

import jax
import jax.numpy as jnp
import numpy as np
from jax import lax
from jax.experimental import pallas as pl
from jax.experimental.pallas import tpu as pltpu
from jax.sharding import PartitionSpec as P

HIGHEST = lax.Precision.HIGHEST


def layer_norm(values, gain, offset):
    center = values - jnp.mean(values, axis=-1, keepdims=True)
    spread = jnp.mean(center * center, axis=-1, keepdims=True)
    return center * lax.rsqrt(spread + 1e-05) * gain + offset


MESH = pl.DeviceIdType.MESH
VMEM_LIMIT = 56 * 1024 * 1024
LANES = 128


def seq_weights(order, groups):
    weights = []
    w = 1
    while w < groups:
        weights.append(w)
        w *= 2
    first = weights[0] + order * (weights[1] - weights[0])
    second = weights[1] - order * (weights[1] - weights[0])
    return [first, second] + weights[2:]


class Halving:
    def __init__(self, groups, me, core, order, parts, own, first=0, base=0):
        self.groups, self.me, self.core, self.parts, self.own, self.first = (
            groups,
            me,
            core,
            parts,
            own,
            first,
        )
        self.order, self.other = (core, 1 - core) if order is None else (order, order)
        self.weights = seq_weights(self.order, groups)
        self.bits = [lax.rem(me // w, 2) for w in self.weights]
        self.steps = len(self.weights)
        self.half = own.shape[3]
        self.base = base * 2 * self.half
        self.source = None
        self.unit = own.shape[2]

    def shard_of(self, n, order):
        weights = seq_weights(order, self.groups)
        at = 0
        for j in range(self.steps):
            bit = lax.rem(self.me // weights[j], 2)
            keep = (n >> (self.steps - 1 - j)) & 1
            at = at + (bit if keep else 1 - bit) * weights[j]
        return at

    def core_setup(self, buf, ss, rs, sib):
        self.buf = buf
        (ref, _, cols, _) = self.parts[0]
        src = (ref if self.source is None else self.source).at[
            :,
            pl.ds(
                pl.multiple_of(self.base + (1 - self.core) * cols * self.half, LANES),
                cols * self.half,
            ),
        ]
        self.core_copy = pltpu.make_async_remote_copy(
            src_ref=src,
            dst_ref=buf,
            send_sem=ss,
            recv_sem=rs,
            device_id={"row": sib},
            device_id_type=MESH,
        )

    def core_start(self):
        self.core_copy.start()

    def core_finish(self):
        self.core_copy.wait_recv()
        (ref, high, cols, _) = self.parts[0]
        first = self.count(0)
        for n in range(self.groups):
            s = self.shard_of(n, self.order)
            for h in range(high):
                lines = pl.ds(pl.multiple_of((s * high + h) * self.unit, 8), self.unit)
                for c in range(cols):
                    mine = ref[
                        lines,
                        pl.ds(
                            pl.multiple_of(
                                self.base + (self.core * cols + c) * self.half, LANES
                            ),
                            self.half,
                        ),
                    ]
                    self.own[n, h * cols + c] = (
                        mine + self.buf[lines, c * self.half : (c + 1) * self.half]
                    )
            if n + 1 == first // 2:
                self.start(0, 0)
            if n + 1 == first:
                self.start(0, 1)

    def pieces(self, k):
        count = self.count(k)
        return [(0, count // 2), (count // 2, count // 2)] if count > 1 else [(0, 1)]

    def step_setup(self, bufs, ss, rs, steps):
        self.step_bufs = dict(zip(steps, bufs))
        self.copies = {}
        for at, k in enumerate(steps):
            for j, (i, size) in enumerate(self.pieces(k)):
                self.copies[k, j] = pltpu.make_async_remote_copy(
                    src_ref=self.own.at[pl.ds(self.slot(k) + i, size)],
                    dst_ref=bufs[at].at[pl.ds(i, size)],
                    send_sem=ss[at].at[j],
                    recv_sem=rs[at].at[j],
                    device_id={"seq": self.me + self.weights[k] * (1 - 2 * self.bits[k])},
                    device_id_type=MESH,
                )

    def slot(self, k):
        return self.groups - (self.groups >> k) - self.first

    def start(self, k, j):
        self.copies[k, j].start()

    def start_step(self, k):
        for j in range(len(self.pieces(k))):
            self.start(k, j)

    def finish(self, k, j):
        self.copies[k, j].wait_recv()
        first, size = self.pieces(k)[j]
        for i in range(first, first + size):
            at = self.slot(k + 1) + i
            self.own[at] = self.own[at] + self.step_bufs[k][i]

    def count(self, k):
        return self.groups >> (k + 1)

    def wait_sends(self):
        for c in self.copies.values():
            c.wait_send()

    def wait_core_sends(self):
        self.core_copy.wait_send()


EARLY = (4, 4, 1)
LATE = (1, 1, 1)
ORDERS = (0, 1, None)
EARLY_STEPS = (1, 1, 1)


class Crew:
    def __init__(self, members):
        self.members = members
        self.steps = members[0].steps

    def core_setup(self, bufs, ss, rs, sib):
        for p, h in enumerate(self.members):
            h.core_setup(bufs[p], ss.at[p], rs.at[p], sib)

    def step_setup(self, bufs, ss, rs, steps):
        for p, h in enumerate(self.members):
            h.step_setup(bufs[p], ss[p], rs[p], steps[p])

    def core_start(self):
        for h in self.members:
            h.core_start()

    def core_finish(self):
        for h in self.members:
            h.core_finish()

    def part(self, k, j):
        for h in self.members:
            if (k, j) in h.copies:
                h.finish(k, j)
                if j == 0 and k + 1 < self.steps:
                    h.start_step(k + 1)

    def advance(self, k):
        self.part(k, 0)
        self.part(k, 1)

    def wait_sends(self):
        for h in self.members:
            h.wait_sends()

    def wait_core_sends(self):
        for h in self.members:
            h.wait_core_sends()


def early_crew(groups, me, core, gout, gup, gdown, owns, down_src):
    parts = [[(gup, 1, 4, 0)], [(gdown, 4, 1, 0)], [(gout, 1, 1, 0)]]
    crew = Crew([Halving(groups, me, core, o, p, w) for o, p, w in zip(ORDERS, parts, owns)])
    crew.members[1].source = down_src
    return crew


def greet_all(rows, groups, me, row):
    barrier = pltpu.get_barrier_semaphore()
    for d in range(1, rows):
        pl.semaphore_signal(
            barrier, inc=1, device_id={"row": lax.rem(row + d, rows)}, device_id_type=MESH
        )
    for d in range(1, groups):
        pl.semaphore_signal(
            barrier, inc=1, device_id={"seq": lax.rem(me + d, groups)}, device_id_type=MESH
        )
    pl.semaphore_wait(barrier, rows + groups - 2)


def row_masks(lengths, row, start, tok):
    where = lax.broadcasted_iota(jnp.int32, (8, tok), 1) + start
    ends = []
    total = 0
    for k in range(lengths.shape[1]):
        total = total + lengths[row, k]
        ends.append(total)

    def doc(at):
        out = jnp.zeros(at.shape, jnp.int32)
        for e in ends:
            out = out + (at >= e).astype(jnp.int32)
        return out

    own = doc(where)
    masks = []
    for lag in (1, 2):
        same = (where >= lag) & (doc(where - lag) == own)
        masks.append(same.astype(jnp.float32)[:1])
    return masks + [(where < total).astype(jnp.float32)[:1]]


def edge_pick(r):
    line = lax.broadcasted_iota(jnp.int32, (8, LANES), 0)
    spot = lax.broadcasted_iota(jnp.int32, (8, LANES), 1)
    pick = (spot == line - 2 * r + LANES - 2) & (line >= 2 * r) & (line < 2 * r + 2)
    return pick.astype(jnp.bfloat16)


def pack_edges(tiles):
    out = None
    for r, tile in enumerate(tiles):
        piece = lax.dot_general(
            edge_pick(r), tile, (((1,), (1,)), ((), ())), preferred_element_type=jnp.float32
        )
        out = piece if out is None else out + piece
    return out


def unpack_edge(lines, r):
    return lax.dot_general(
        lines.astype(jnp.bfloat16),
        edge_pick(r),
        (((0,), (0,)), ((), ())),
        preferred_element_type=jnp.float32,
    )


def window_of(values, lane, edge):
    early, late = edge[:, LANES - 2 : LANES - 1], edge[:, LANES - 1 :]
    one = jnp.where(lane == 0, late, pltpu.roll(values, 1, 1))
    two = jnp.where(lane == 0, early, jnp.where(lane == 1, late, pltpu.roll(values, 2, 1)))
    return one, two


def spread_taps(taps, padded, wide):
    padded[...] = jnp.zeros_like(padded)
    padded[: taps.shape[0], :] = taps[...]
    turned = padded[...].T
    for j in range(taps.shape[0]):
        wide[j] = jnp.broadcast_to(turned[:, j : j + 1], wide.shape[1:])


def norm_parts(values):
    center = values - jnp.mean(values, axis=-1, keepdims=True)
    scale = lax.rsqrt(jnp.mean(center * center, axis=-1, keepdims=True) + 1e-05)
    return center * scale, scale


STRIP = 128


def finish_kernel(
    rows,
    groups,
    gw_ref,
    ggo_ref,
    u_hbm,
    edge_ref,
    lengths,
    taps,
    weight_hbm,
    block_hbm,
    gm_hbm,
    gain,
    offset,
    feed_gain,
    feed_bias,
    early,
    mid_s,
    first_s,
    last,
    gi_ref,
    fin_o,
    small_o,
    gains_o,
    padded,
    wide_taps,
    edges,
    tap_sum,
    gu,
    gu_low,
    rim,
    rim_out,
    rim_in,
    normed,
    gin,
    small,
    own,
    own_early,
    core_buf,
    step_buf,
    early_buf,
    wide_buf,
    small_row,
    small_sum,
    small_part,
    small_done,
    last_row,
    last_sum,
    rim_sem,
    bring_sem,
    u_ref,
    weight,
    block,
    gm_ref,
    move_sem,
    core_ss,
    core_rs,
    step_ss,
    step_rs,
    early_ss,
    early_rs,
    wide_ss,
    wide_rs,
    fin_ss,
    fin_rs,
    srow_ss,
    srow_rs,
    spart_ss,
    spart_rs,
    sdone_ss,
    sdone_rs,
    lrow_ss,
    lrow_rs,
    gain_own,
    gain_row_buf,
    gain_sum,
    grow_ss,
    grow_rs,
    gcast_ss,
    gcast_rs,
):
    me = lax.axis_index("seq")
    row = lax.axis_index("row")
    core = lax.rem(row, 2)
    sib = row + 1 - 2 * core
    chunk = small_part.shape[1]
    held, width, tok = gw_ref.shape
    low, f32 = jnp.bfloat16, jnp.float32

    late = Crew(
        [
            Halving(groups, me, core, o, [(gin, 1, 1, 0)], own[p], base=p)
            for p, o in enumerate(ORDERS)
        ]
    )
    late.core_setup(core_buf, core_ss, core_rs, sib)
    late.step_setup(step_buf, step_ss, step_rs, [range(late.steps)] * len(LATE))
    later = [range(n, late.steps) for n in EARLY_STEPS]
    rest = Crew(
        [
            Halving(groups, me, core, o, (), w, first=groups - e.shape[0])
            for o, w, e in zip(ORDERS, own_early, early)
        ]
    )
    rest.step_setup(early_buf, early_ss, early_rs, later)
    bring = [
        pltpu.make_async_copy(e, w, bring_sem.at[p])
        for p, (w, e) in enumerate(zip(own_early, early))
    ]
    moves = [
        pltpu.make_async_copy(src, dst, move_sem.at[p])
        for p, (src, dst) in enumerate(
            ((u_hbm, u_ref), (block_hbm, block), (weight_hbm, weight), (gm_hbm, gm_ref))
        )
    ]
    for c in bring + moves:
        c.start()
    greet_all(rows, groups, me, row)
    for c in bring:
        c.wait()
    for h, ks in zip(rest.members, later):
        h.start_step(ks[0])
    lrow = [
        pltpu.make_async_remote_copy(
            src_ref=last,
            dst_ref=last_row.at[d - 1],
            send_sem=lrow_ss.at[d - 1],
            recv_sem=lrow_rs.at[d - 1],
            device_id={"row": lax.rem(row + d, rows)},
            device_id_type=MESH,
        )
        for d in range(1, rows)
    ]
    for c in lrow:
        c.start()

    spread_taps(taps, padded, wide_taps)
    tap_sum[...] = jnp.zeros_like(tap_sum)
    lane = lax.broadcasted_iota(jnp.int32, (STRIP, tok), 1)
    moves[0].wait()
    for r in range(held):
        same1, same2, live = row_masks(lengths, r, me * tok, tok)
        edges[...] = unpack_edge(edge_ref[...], r)

        def strip(i, carry, r=r, same1=same1, same2=same2, live=live):
            at = [pl.multiple_of(i * STRIP + g * width, STRIP) for g in range(3)]
            tap = [
                [
                    jnp.concatenate([wide_taps[j, pl.ds(a, STRIP), :]] * (tok // LANES), axis=1)
                    for j in range(3)
                ]
                for a in at
            ]
            u = [u_ref[r, pl.ds(a, STRIP), :].astype(f32) for a in at]
            shifts = [
                window_of(v, lane, edges[pl.ds(a, STRIP), :])
                for v, a in zip(u, at)
            ]
            gate_in, stream = [
                tap[g][0] * u[g] + tap[g][1] * shifts[g][0] * same1 + tap[g][2] * shifts[g][1] * same2
                for g in (1, 2)
            ]
            gw = gw_ref[r, pl.ds(at[0], STRIP), :].astype(f32) * live
            grads = [ggo_ref[r, pl.ds(at[0], STRIP), :] * live, gw * stream, gw * gate_in]
            for g in range(3):
                m1, m2 = grads[g] * same1, grads[g] * same2
                for j, p in enumerate((grads[g] * u[g], m1 * shifts[g][0], m2 * shifts[g][1])):
                    total = p[:, :LANES]
                    for h in range(1, tok // LANES):
                        total = total + p[:, h * LANES : (h + 1) * LANES]
                    tap_sum[j, pl.ds(at[g], STRIP), :] += total
                b1 = pltpu.roll(tap[g][1] * m1, tok - 1, 1)
                b2 = pltpu.roll(tap[g][2] * m2, tok - 2, 1)
                gu[r, pl.ds(at[g], STRIP), :] = (
                    tap[g][0] * grads[g]
                    + jnp.where(lane < tok - 1, b1, 0.0)
                    + jnp.where(lane < tok - 2, b2, 0.0)
                )
                over = jnp.where(lane < tok - 1, 0.0, b1) + jnp.where(lane < tok - 2, 0.0, b2)
                rim[r, pl.ds(at[g], STRIP), :] = over[:, tok - LANES :].astype(low)
            return carry

        lax.fori_loop(0, width // STRIP, strip, 0)
        if r == 0:
            rest.part(1, 0)

    rim_out[...] = pack_edges([rim[r] for r in range(held)])
    rim_copy = pltpu.make_async_remote_copy(
        src_ref=rim_out,
        dst_ref=rim_in,
        send_sem=rim_sem.at[0],
        recv_sem=rim_sem.at[1],
        device_id={"seq": lax.rem(me + groups - 1, groups)},
        device_id_type=MESH,
    )
    rim_copy.start()

    at = mid_s.shape[0] + first_s.shape[0]
    small[:at, :] = jnp.concatenate([mid_s[...], first_s[...]], axis=0)
    small[at:, :] = jnp.zeros((small.shape[0] - at, LANES), f32)
    per = width // LANES

    def put_small(first, line):
        for i in range(line.shape[1] // LANES):
            small[first + i : first + i + 1, :] = line[:, i * LANES : (i + 1) * LANES]

    ones = jnp.ones((8, LANES), low)

    def lane_sums(values):
        high = values.astype(low)
        rest = (values - high.astype(f32)).astype(low)
        dims = (((1,), (1,)), ((), ()))
        return lax.dot_general(ones, high, dims, preferred_element_type=f32) + lax.dot_general(
            ones, rest, dims, preferred_element_type=f32
        )

    for j in range(3):
        put_small(at + 2 * per + 3 * per * j, lane_sums(tap_sum[j])[:1])
    put_small(at + 11 * per, feed_gain[...][None, :])
    put_small(at + 12 * per, feed_bias[...][None, :])
    srow = [
        pltpu.make_async_remote_copy(
            src_ref=small,
            dst_ref=small_row.at[d - 1],
            send_sem=srow_ss.at[d - 1],
            recv_sem=srow_rs.at[d - 1],
            device_id={"row": lax.rem(row + d, rows)},
            device_id_type=MESH,
        )
        for d in range(1, rows)
    ]
    for c in srow:
        c.start()
    gain_row, offset_row = gain[...][None, :], offset[...][None, :]
    for c in moves[1:]:
        c.wait()
    for r in range(held):
        hat, _ = norm_parts(block[r].astype(f32))
        normed[:, r * tok : (r + 1) * tok] = (hat * gain_row + offset_row).T.astype(low)
    rest.part(1, 1)
    for c in srow + lrow:
        c.wait()
    total = small[...]
    tail = last[...]
    for d in range(rows - 1):
        total = total + small_row[d]
        tail = tail + last_row[d]
    small_sum[...] = total
    last_sum[...] = tail
    spart = []
    for d in range(1, groups):
        to = lax.rem(me + d, groups)
        spart.append(
            pltpu.make_async_remote_copy(
                src_ref=small_sum.at[pl.ds(to * chunk, chunk)],
                dst_ref=small_part.at[d - 1],
                send_sem=spart_ss.at[d - 1],
                recv_sem=spart_rs.at[d - 1],
                device_id={"seq": to},
                device_id_type=MESH,
            )
        )
    for c in spart:
        c.start()

    rim_copy.wait()
    for r in range(held):
        add = unpack_edge(rim_in[...], r)
        split = tok - LANES
        gu_low[:, r * tok : r * tok + split] = gu[r, :, :split].astype(low)
        gu_low[:, r * tok + split : (r + 1) * tok] = (gu[r, :, split:] + add).astype(low)

    rest.part(2, 0)
    piece = 256

    def weight_grad(i, carry):
        cols = pl.ds(pl.multiple_of(i * piece, piece), piece)
        gin[:, cols] = lax.dot_general(
            normed[...], gu_low[cols, :], (((1,), (1,)), ((), ())), preferred_element_type=f32
        ).astype(low)
        return carry

    per_unit = width // piece
    first_unit, second_unit, third_unit = late.members
    lax.fori_loop(0, per_unit, weight_grad, 0)
    first_unit.core_start()
    lax.fori_loop(per_unit, 2 * per_unit, weight_grad, 0)
    second_unit.core_start()
    first_unit.core_finish()
    lax.fori_loop(2 * per_unit, 3 * per_unit, weight_grad, 0)
    third_unit.core_start()
    second_unit.core_finish()
    rest.part(2, 1)

    fin = []

    def close(crew, arrays, units, base):
        place = sum((EARLY + LATE)[:base])
        for p, (h, array, count) in enumerate(zip(crew.members, arrays, units)):
            q, slot = base + p, array.shape[0] - 1
            w, n = 2, 0
            while w < rows:
                bit = lax.rem(row // w, 2)
                c = pltpu.make_async_remote_copy(
                    src_ref=h.own.at[slot],
                    dst_ref=wide_buf[q].at[n],
                    send_sem=wide_ss.at[n, q],
                    recv_sem=wide_rs.at[n, q],
                    device_id={"row": row + w * (1 - 2 * bit)},
                    device_id_type=MESH,
                )
                c.start()
                c.wait()
                h.own[slot] = h.own[slot] + wide_buf[q][n]
                w, n = 2 * w, n + 1
            fin_o[core, place : place + count] = h.own[slot]
            c = pltpu.make_async_remote_copy(
                src_ref=h.own.at[slot],
                dst_ref=fin_o.at[core, pl.ds(place, count)],
                send_sem=fin_ss.at[q],
                recv_sem=fin_rs.at[q],
                device_id={"row": sib},
                device_id_type=MESH,
            )
            c.start()
            fin.append(c)
            place += count

    gains = [jnp.zeros((1, width), f32), jnp.zeros((1, width), f32)]
    for r in range(held):
        turned = lax.dot_general(
            weight[...],
            gu_low[:, r * tok : (r + 1) * tok],
            (((1,), (0,)), ((), ())),
            preferred_element_type=f32,
        )
        grad = turned.T
        hat, scale = norm_parts(block[r].astype(f32))
        gains[0] = gains[0] + jnp.sum(grad * hat, axis=0, keepdims=True)
        gains[1] = gains[1] + jnp.sum(grad, axis=0, keepdims=True)
        pulled = grad * gain_row
        pulled = pulled - jnp.mean(pulled, axis=-1, keepdims=True)
        pulled = pulled - hat * jnp.mean(pulled * hat, axis=-1, keepdims=True)
        gi_ref[r] = gm_ref[r] + scale * pulled
        if r == 0:
            third_unit.core_finish()
            for c in spart:
                c.wait()
            total = small_sum[pl.ds(me * chunk, chunk)]
            for d in range(groups - 1):
                total = total + small_part[d]
            small_done[:chunk] = total
            small_done[chunk:] = last_sum[...]
            small_o[me] = small_done[...]
            sdone = [
                pltpu.make_async_remote_copy(
                    src_ref=small_done,
                    dst_ref=small_o.at[me],
                    send_sem=sdone_ss.at[d - 1],
                    recv_sem=sdone_rs.at[d - 1],
                    device_id={"seq": lax.rem(me + d, groups)},
                    device_id_type=MESH,
                )
                for d in range(1, groups)
            ]
            for c in sdone:
                c.start()
    gain_own[...] = jnp.zeros_like(gain_own)
    for g in range(2):
        for n in range(per):
            line = g * per + n
            gain_own[line : line + 1, :] = gains[g][:, n * LANES : (n + 1) * LANES]
    grow = [
        pltpu.make_async_remote_copy(
            src_ref=gain_own,
            dst_ref=gain_row_buf.at[d - 1],
            send_sem=grow_ss.at[d - 1],
            recv_sem=grow_rs.at[d - 1],
            device_id={"row": lax.rem(row + d, rows)},
            device_id_type=MESH,
        )
        for d in range(1, rows)
    ]
    for c in grow:
        c.start()

    late.advance(0)
    for c in grow:
        c.wait()
    total = gain_own[...]
    for d in range(rows - 1):
        total = total + gain_row_buf[d]
    gain_sum[...] = total
    gains_o[me] = total
    gcast = [
        pltpu.make_async_remote_copy(
            src_ref=gain_sum,
            dst_ref=gains_o.at[me],
            send_sem=gcast_ss.at[d - 1],
            recv_sem=gcast_rs.at[d - 1],
            device_id={"seq": lax.rem(me + d, groups)},
            device_id_type=MESH,
        )
        for d in range(1, groups)
    ]
    for c in gcast:
        c.start()
    for k in range(3, rest.steps):
        rest.advance(k)
    close(rest, early, EARLY, 0)
    late.advance(1)
    for k in range(2, late.steps):
        late.advance(k)

    close(late, own, LATE, len(EARLY))
    late.wait_core_sends()
    late.wait_sends()
    rest.wait_sends()
    for c in sdone + gcast:
        c.wait()
    for c in fin:
        c.wait()


def finish(gw, ggo, u, edge, lengths, taps, weight, block, gm, vectors, early, sums):
    rows, groups = lax.axis_size("row"), lax.axis_size("seq")
    held, width, tok = gw.shape
    unit = width // groups
    half = width // 2
    wide = max(1, rows.bit_length() - 2)
    low, f32 = jnp.bfloat16, jnp.float32
    steps = groups.bit_length() - 1
    later = [range(n, steps) for n in EARLY_STEPS]
    used = sums[0].shape[0] + sums[1].shape[0] + 13 * (width // LANES)
    lines = used + -used % (8 * groups)
    chunk = lines // groups
    lead = -(-2 * (width // LANES) // 8) * 8
    last = sums[2]
    dma = pltpu.SemaphoreType.DMA
    vm = pl.BlockSpec(memory_space=pltpu.VMEM)
    sm = pl.BlockSpec(memory_space=pltpu.SMEM)
    hbm = pl.BlockSpec(memory_space=pl.ANY)
    return pl.pallas_call(
        functools.partial(finish_kernel, rows, groups),
        out_shape=(
            jax.ShapeDtypeStruct(gm.shape, f32),
            jax.ShapeDtypeStruct((2, sum(EARLY) + sum(LATE), unit, half), low),
            jax.ShapeDtypeStruct((groups, chunk + last.shape[0], LANES), f32),
            jax.ShapeDtypeStruct((groups, lead, LANES), f32),
        ),
        in_specs=[vm, vm, hbm, vm, sm, vm, hbm, hbm, hbm] + [vm] * 4 + [[hbm] * 3] + [vm] * 3,
        out_specs=(vm,) * 4,
        scratch_shapes=[
            pltpu.VMEM((8, 3 * width), f32),
            pltpu.VMEM((3, 3 * width, LANES), f32),
            pltpu.VMEM((3 * width, LANES), f32),
            pltpu.VMEM((3, 3 * width, LANES), f32),
            pltpu.VMEM((held, 3 * width, tok), f32),
            pltpu.VMEM((3 * width, held * tok), low),
            pltpu.VMEM((held, 3 * width, LANES), low),
            pltpu.VMEM((8, 3 * width), f32),
            pltpu.VMEM((8, 3 * width), f32),
            pltpu.VMEM((width, held * tok), low),
            pltpu.VMEM((width, 3 * width), low),
            pltpu.VMEM((lines, LANES), f32),
            [pltpu.VMEM((groups, n, unit, half), low) for n in LATE],
            [pltpu.VMEM(e.shape, low) for e in early],
            [pltpu.VMEM((width, n * half), low) for n in LATE],
            [
                [pltpu.VMEM((groups >> (k + 1), n, unit, half), low) for k in range(steps)]
                for n in LATE
            ],
            [
                [pltpu.VMEM((groups >> (k + 1), n, unit, half), low) for k in ks]
                for ks, n in zip(later, EARLY)
            ],
            [pltpu.VMEM((wide, n, unit, half), low) for n in EARLY + LATE],
            pltpu.VMEM((rows - 1, lines, LANES), f32),
            pltpu.VMEM((lines, LANES), f32),
            pltpu.VMEM((groups - 1, chunk, LANES), f32),
            pltpu.VMEM((chunk + last.shape[0], LANES), f32),
            pltpu.VMEM((rows - 1,) + last.shape, f32),
            pltpu.VMEM(last.shape, f32),
            dma((2,)),
            dma((3,)),
            pltpu.VMEM(u.shape, low),
            pltpu.VMEM(weight.shape, low),
            pltpu.VMEM(block.shape, low),
            pltpu.VMEM(gm.shape, f32),
            dma((4,)),
            dma((len(LATE),)),
            dma((len(LATE),)),
            [[dma((2,)) for k in range(steps)] for _ in LATE],
            [[dma((2,)) for k in range(steps)] for _ in LATE],
            [[dma((2,)) for k in ks] for ks in later],
            [[dma((2,)) for k in ks] for ks in later],
            dma((wide, 6)),
            dma((wide, 6)),
            dma((6,)),
            dma((6,)),
            dma((rows - 1,)),
            dma((rows - 1,)),
            dma((groups - 1,)),
            dma((groups - 1,)),
            dma((groups - 1,)),
            dma((groups - 1,)),
            dma((rows - 1,)),
            dma((rows - 1,)),
            pltpu.VMEM((lead, LANES), f32),
            pltpu.VMEM((rows - 1, lead, LANES), f32),
            pltpu.VMEM((lead, LANES), f32),
            dma((rows - 1,)),
            dma((rows - 1,)),
            dma((groups - 1,)),
            dma((groups - 1,)),
        ],
        compiler_params=pltpu.CompilerParams(
            collective_id=0, has_side_effects=True, vmem_limit_bytes=VMEM_LIMIT
        ),
        name="finish",
    )(gw, ggo, u, edge, lengths, taps, weight, block, gm, *vectors, early, *sums)


def unpack_kernel(
    feat,
    fin,
    packed,
    leads,
    gi,
    gain_o,
    bias_o,
    in_o,
    taps_o,
    first_o,
    first_b_o,
    mid_o,
    mid_b_o,
    freq_o,
    last_o,
    skip_o,
    out_o,
    feed_gain_o,
    feed_bias_o,
    up_o,
    down_o,
    gi_o,
    small,
    last,
):
    f32 = jnp.float32
    chunk, narrow = small.shape[0] // packed.shape[0], last.shape[0] // packed.shape[0]
    for g in range(packed.shape[0]):
        small[g * chunk : (g + 1) * chunk] = packed[g, :chunk]
        last[g * narrow : (g + 1) * narrow] = packed[g, chunk:]
    gi_o[...] = gi[...]
    unit, half = fin.shape[2], fin.shape[3]
    hidden = mid_o.shape[0]
    width = gain_o.shape[0]
    per = width // LANES
    outs = [(up_o, 1, 4, 0, 0), (down_o, 4, 1, 4, 0), (out_o, 1, 1, 8, 0)]
    outs = outs + [(in_o, 1, 1, 9 + p, 2 * p) for p in range(3)]
    for core in range(2):
        for out, high, cols, first, base in outs:
            for h in range(high):
                for c in range(cols):
                    at = (base + core * cols + c) * half
                    out[h * unit : (h + 1) * unit, at : at + half] = fin[
                        core, first + h * cols + c
                    ].astype(f32)

    def line(first, count):
        pieces = [small[first + i : first + i + 1, :] for i in range(count)]
        return jnp.concatenate(pieces, axis=1)

    at = hidden + -(-(feat + 1) // 8) * 8
    total = leads[0]
    for g in range(1, leads.shape[0]):
        total = total + leads[g]
    for out, first in ((gain_o, 0), (bias_o, per)):
        out[...] = jnp.concatenate([total[first + i : first + i + 1] for i in range(per)], axis=1)[0]
    for j in range(3):
        taps_o[j : j + 1, :] = line(at + 2 * per + 3 * per * j, 3 * per)
    feed_gain_o[...] = line(at + 11 * per, per)[0]
    feed_bias_o[...] = line(at + 12 * per, per)[0]
    first_o[...] = small[hidden : hidden + feat, :hidden]
    first_b_o[...] = small[hidden + feat : hidden + feat + 1, :hidden][0]
    mid_o[...] = small[:hidden, :hidden]
    shape = (hidden, hidden)
    same = lax.broadcasted_iota(jnp.int32, shape, 0) == lax.broadcasted_iota(jnp.int32, shape, 1)
    for out, col in ((mid_b_o, hidden), (freq_o, hidden + 1)):
        out[...] = jnp.sum(
            jnp.where(same, small[:hidden, col : col + 1], 0.0), axis=0, keepdims=True
        )[0]
    turned = last[...].T
    last_o[...] = turned[:hidden]
    skip_o[...] = turned[hidden : hidden + 1][0]


def unpack(fin, packed, leads, gi, feat, hidden, width):
    f32 = jnp.float32
    unit = fin.shape[2]
    vm = pl.BlockSpec(memory_space=pltpu.VMEM)
    shapes = [
        (width,),
        (width,),
        (unit, 3 * width),
        (3, 3 * width),
        (feat, hidden),
        (hidden,),
        (hidden, hidden),
        (hidden,),
        (hidden,),
        (hidden, width),
        (width,),
        (unit, width),
        (width,),
        (width,),
        (unit, 4 * width),
        (4 * unit, width),
        gi.shape,
    ]
    return pl.pallas_call(
        functools.partial(unpack_kernel, feat),
        out_shape=tuple(jax.ShapeDtypeStruct(x, f32) for x in shapes),
        in_specs=[vm] * 4,
        out_specs=(vm,) * len(shapes),
        scratch_shapes=[
            pltpu.VMEM((packed.shape[0] * packed.shape[1] - width, LANES), f32),
            pltpu.VMEM((width, LANES), f32),
        ],
        compiler_params=pltpu.CompilerParams(vmem_limit_bytes=VMEM_LIMIT),
        name="unpack",
    )(fin, packed, leads, gi)


def spectrum_tables(length):
    period = 2 * length
    first = period // LANES
    k1 = np.arange(first // 2 + 1, dtype=np.int64)[:, None, None]
    n2 = np.arange(LANES, dtype=np.int64)[None, :, None]
    k2 = np.arange(LANES, dtype=np.int64)[None, None, :]
    angle = 2.0 * np.pi / period * (n2 * (k1 + first * k2) % period)
    full = np.concatenate([np.cos(angle), np.sin(angle)], axis=2).astype(np.float32)
    high = full.astype(jnp.bfloat16)
    rest = (full - high.astype(np.float32)).astype(jnp.bfloat16)
    return high, rest


def feature_rows(length, feat_count):
    bands = (feat_count - 1) // 2
    at = np.arange(length, dtype=np.int64)[None, :]
    angle = 2.0 * np.pi / length * (at * np.arange(1, bands + 1)[:, None] % length)
    rows = [at / length, np.cos(angle), -np.sin(angle), np.ones((1, length))]
    rows = np.concatenate(rows, axis=0)
    pad = -rows.shape[0] % 8
    return np.pad(rows, ((0, pad), (0, 0))).astype(np.float32)


def sin_cos(x):
    n = jnp.round(x * (2.0 / math.pi))
    r = x - n * 1.5703125
    r = r - n * 4.837512969970703125e-4
    r = r - n * 7.549789948768648e-8
    z = r * r
    s = r + r * z * (-1.6666654611e-1 + z * (8.3321608736e-3 - z * 1.9515295891e-4))
    c = (
        1.0
        - 0.5 * z
        + z * z * (4.166664568298827e-2 + z * (-1.388731625493765e-3 + z * 2.443315711809948e-5))
    )
    q = n.astype(jnp.int32) & 3
    odd = (q & 1) == 1
    sine = jnp.where(odd, c, s)
    cosine = jnp.where(odd, s, c)
    sine = jnp.where(q >= 2, -sine, sine)
    cosine = jnp.where((q == 1) | (q == 2), -cosine, cosine)
    return sine, cosine


def exact_dot(p, q, left, right):
    low = jnp.bfloat16

    def dot(x, y):
        return lax.dot_general(
            x, y, (((left,), (right,)), ((), ())), preferred_element_type=jnp.float32
        )

    ph, qh = p.astype(low), q.astype(low)
    pl_, ql = (p - ph.astype(jnp.float32)).astype(low), (q - qh.astype(jnp.float32)).astype(low)
    return dot(ph, qh) + (dot(pl_, qh) + dot(ph, ql))


def column_of(row):
    size = row.shape[1]
    shape = (size, size)
    same = lax.broadcasted_iota(jnp.int32, shape, 0) == lax.broadcasted_iota(jnp.int32, shape, 1)
    return jnp.sum(jnp.where(same, row, 0.0), axis=1, keepdims=True)


class FilterNet:
    def __init__(self, me, narrow, params, aug):
        first, first_b, mid, mid_b, freq, last, skip, decay, self.feats = params
        feat = first.shape[0]
        aug[...] = jnp.zeros_like(aug)
        aug[:feat, :] = first[...]
        aug[feat : feat + 1, :] = first_b[...][None, :]
        self.aug = aug
        self.mid = mid
        self.mid_b = column_of(mid_b[...][None, :])
        self.freq = column_of(freq[...][None, :])
        width = skip.shape[0]
        shape = (narrow, width)
        pick = (
            lax.broadcasted_iota(jnp.int32, shape, 1)
            == lax.broadcasted_iota(jnp.int32, shape, 0) + me * narrow
        )
        self.skip = jnp.sum(jnp.where(pick, skip[...][None, :], 0.0), axis=1, keepdims=True)
        self.decay = jnp.sum(jnp.where(pick, decay[...][None, :], 0.0), axis=1, keepdims=True)
        self.last = exact_dot(pick.astype(jnp.float32), last[...], 1, 1)
        self.narrow = narrow

    def layers(self, at, size):
        feats = self.feats[:, pl.ds(at, size)]
        pre1 = exact_dot(self.aug[...], feats, 0, 0)
        a1, c1 = sin_cos(self.freq * pre1)
        pre2 = exact_dot(self.mid[...], a1, 0, 0) + self.mid_b
        a2, c2 = sin_cos(self.freq * pre2)
        return feats, pre1, a1, c1, pre2, a2, c2

    def fade(self, at, size):
        where = lax.broadcasted_iota(jnp.int32, (self.narrow, size), 1) + at
        return jnp.exp(-self.decay * where.astype(jnp.float32)), where

    def build(self, at, size):
        a2 = self.layers(at, size)[5]
        fade, where = self.fade(at, size)
        return exact_dot(self.last, a2, 1, 0) * fade + jnp.where(where == 0, self.skip, 0.0)

    def pull(self, at, size, grad, first_o, mid_o, last_o):
        feats, pre1, a1, c1, pre2, a2, c2 = self.layers(at, size)
        fade, where = self.fade(at, size)
        hidden = a1.shape[0]
        raw = grad * fade
        last_o[:, :hidden] += exact_dot(raw, a2, 1, 1)
        last_o[:, hidden : hidden + 1] += jnp.sum(
            jnp.where(where == 0, grad, 0.0), axis=1, keepdims=True
        )
        turned2 = exact_dot(self.last, raw, 0, 0) * c2
        freq = jnp.sum(turned2 * pre2, axis=1, keepdims=True)
        down2 = turned2 * self.freq
        mid_o[:, :hidden] += exact_dot(a1, down2, 1, 1)
        mid_o[:, hidden : hidden + 1] += jnp.sum(down2, axis=1, keepdims=True)
        turned1 = exact_dot(self.mid[...], down2, 1, 0) * c1
        freq = freq + jnp.sum(turned1 * pre1, axis=1, keepdims=True)
        mid_o[:, hidden + 1 : hidden + 2] += freq
        down1 = turned1 * self.freq
        first_o[:, :hidden] += exact_dot(feats, down1, 1, 1)


CHUNK = 4


def half_dft(x):
    count = 2 * len(x)
    if count == 2:
        return [(x[0], None), (x[0], None)]
    even, odd = half_dft(x[0::2]), half_dft(x[1::2])
    out = [None] * (count // 2 + 1)
    for k in range(count // 4 + 1):
        er, ei = even[k]
        orr, oi = odd[k]
        if k == 0:
            out[0] = (er + orr, None)
            out[count // 2] = (er - orr, None)
        elif 4 * k == count:
            out[k] = (er, -orr)
        else:
            c, s = math.cos(2 * math.pi * k / count), math.sin(2 * math.pi * k / count)
            tr = orr * c + oi * s
            ti = oi * c - orr * s
            out[k] = (er + tr, ei + ti)
            out[count // 2 - k] = (er - tr, ti - ei)
    return out


def half_inverse(spec):
    count = 2 * (len(spec) - 1)
    if count == 2:
        return [spec[0][0] + spec[1][0]]
    even, odd = [], []
    for k in range(count // 4 + 1):
        ar, ai = spec[k]
        br, bi = spec[count // 2 - k]
        if k == 0:
            even.append((ar + br, None))
            odd.append((ar - br, None))
        elif 4 * k == count:
            even.append((ar + ar, None))
            odd.append((-(ai + ai), None))
        else:
            c, s = math.cos(2 * math.pi * k / count), math.sin(2 * math.pi * k / count)
            dr, di = ar - br, ai + bi
            even.append((ar + br, ai - bi))
            odd.append((dr * c - di * s, dr * s + di * c))
    out = [None] * (count // 2)
    out[0::2] = half_inverse(even)
    out[1::2] = half_inverse(odd)
    return out


def turn_of(table):
    cos, sin = table[:, :LANES], table[:, LANES:]
    return jnp.concatenate(
        [jnp.concatenate([cos, -sin], axis=1), jnp.concatenate([sin, cos], axis=1)], axis=0
    )


def split_dot(a, high, rest, back):
    a_high = a.astype(jnp.bfloat16)
    a_rest = (a - a_high.astype(jnp.float32)).astype(jnp.bfloat16)
    dims = (((1,), (1 if back else 0,)), ((), ()))
    high, rest = turn_of(high), turn_of(rest)

    def dot(p, q):
        return lax.dot_general(p, q, dims, preferred_element_type=jnp.float32)

    rows = a.shape[0]
    both = dot(jnp.concatenate([a_high, a_rest], axis=0), high)
    return both[:rows] + (both[rows:] + dot(a_high, rest))


def tile_loop(tiles, body):
    def step(i, carry):
        body(pl.multiple_of(i * 8, 8))
        return carry

    lax.fori_loop(0, tiles, step, 0, unroll=3 if tiles % 3 == 0 else 1)


def first_stage(load, spec, tiles):
    zero = jnp.zeros((8, LANES), jnp.float32)

    def body(at):
        for k, (re, im) in enumerate(half_dft(load(at))):
            spec[k, pl.ds(at, 8), :LANES] = re
            spec[k, pl.ds(at, 8), LANES:] = zero if im is None else im

    tile_loop(tiles, body)


def last_stage(spec, store, tiles, scale, start):
    def body(at):
        at = pl.multiple_of(at + start, 8)
        freqs = spec.shape[0]
        values = []
        for k in range(freqs):
            re = spec[k, pl.ds(at, 8), :LANES]
            im = None if k in (0, freqs - 1) else spec[k, pl.ds(at, 8), LANES:]
            values.append((re, im))
        for n, v in enumerate(half_inverse(values)):
            store(n, at, v * scale)

    tile_loop(tiles, body)


def greet(groups, me):
    barrier = pltpu.get_barrier_semaphore()
    for d in range(1, groups):
        pl.semaphore_signal(
            barrier, inc=1, device_id={"seq": lax.rem(me + d, groups)}, device_id_type=MESH
        )


def met(groups):
    pl.semaphore_wait(pltpu.get_barrier_semaphore(), groups - 1)


def far_first(groups):
    return sorted(range(1, groups), key=lambda d: abs(d - groups // 2))


def to_channels(groups, me, narrow, r, src, recv, ss, rs, ls):
    local = pltpu.make_async_copy(
        src.at[r, pl.ds(pl.multiple_of(me * narrow, 8), narrow), :], recv.at[me, r], ls
    )
    out = [local]
    for d in far_first(groups):
        to = lax.rem(me + d, groups)
        out.append(
            pltpu.make_async_remote_copy(
                src_ref=src.at[r, pl.ds(pl.multiple_of(to * narrow, 8), narrow), :],
                dst_ref=recv.at[me, r],
                send_sem=ss.at[d - 1, r],
                recv_sem=rs.at[d - 1, r],
                device_id={"seq": to},
                device_id_type=MESH,
            )
        )
    return out


def to_positions(groups, me, narrow, r, send, dst, ss, rs, ls):
    mine = dst.at[r, pl.ds(pl.multiple_of(me * narrow, 8), narrow), :]
    out = [pltpu.make_async_copy(send.at[me, r], mine, ls)]
    for d in far_first(groups):
        to = lax.rem(me + d, groups)
        out.append(
            pltpu.make_async_remote_copy(
                src_ref=send.at[to, r],
                dst_ref=mine,
                send_sem=ss.at[d - 1, r],
                recv_sem=rs.at[d - 1, r],
                device_id={"seq": to},
                device_id_type=MESH,
            )
        )
    return out


def spread(recv, wide, narrow):
    per = recv.shape[3] // LANES

    def step(s, carry):
        for r in range(recv.shape[1]):
            for h in range(per):
                wide[s * per + h, r * narrow : (r + 1) * narrow, :] = recv[
                    s, r, :, h * LANES : (h + 1) * LANES
                ].astype(jnp.float32)
        return carry

    lax.fori_loop(0, recv.shape[0], step, 0, unroll=4)


def gather_back(wide, send, narrow, r):
    per = send.shape[3] // LANES

    def step(s, carry):
        for h in range(per):
            send[s, r, :, h * LANES : (h + 1) * LANES] = wide[
                s * per + h, r * narrow : (r + 1) * narrow, :
            ].astype(jnp.bfloat16)
        return carry

    lax.fori_loop(0, send.shape[0], step, 0, unroll=4)


def freq_loop(freqs, unroll, body):
    def step(i, carry):
        for j in range(unroll):
            body(i * unroll + j)
        return carry

    lax.fori_loop(0, freqs // unroll, step, 0)


UNROLL = {33: 11, 65: 13}


def conv_kernel(
    groups,
    block,
    lengths,
    gain,
    offset,
    weight_hbm,
    taps,
    first,
    first_b,
    mid,
    mid_b,
    freq,
    last,
    skip,
    decay,
    feats,
    high_ref,
    rest_ref,
    z_ref,
    w_spec_o,
    h_spec_o,
    u_o,
    gate_o,
    edge_o,
    high,
    rest,
    recv,
    wide,
    back,
    send,
    in_ss,
    in_rs,
    out_ss,
    out_rs,
    local,
    aug,
    filt,
    normed,
    w_ref,
    padded,
    wide_taps,
    edges,
    rim_out,
    rim_in,
    rim_sem,
    w_spec,
    h_spec,
    u_ref,
    gate_ref,
    weight,
    move_sem,
):
    me = lax.axis_index("seq")
    narrow = h_spec.shape[1]
    count, freqs = wide.shape[0], high.shape[0]
    rows, width, tok = w_ref.shape
    low, f32 = jnp.bfloat16, jnp.float32
    unroll = UNROLL.get(freqs, 1)
    tables = [
        pltpu.make_async_copy(high_ref, high, local.at[0]),
        pltpu.make_async_copy(rest_ref, rest, local.at[1]),
    ]
    bring = pltpu.make_async_copy(weight_hbm, weight, move_sem.at[0])
    keep_u, keep_gate, keep_h, keep_w = [
        pltpu.make_async_copy(src, dst, move_sem.at[1 + n])
        for n, (src, dst) in enumerate(
            ((u_ref, u_o), (gate_ref, gate_o), (h_spec, h_spec_o), (w_spec, w_spec_o))
        )
    ]
    bring.start()
    for c in tables:
        c.start()
    greet(groups, me)

    gain_row, offset_row = gain[...][None, :], offset[...][None, :]
    for r in range(rows):
        hat, _ = norm_parts(block[r].astype(f32))
        normed[:, r * tok : (r + 1) * tok] = (hat * gain_row + offset_row).T.astype(low)
    piece = 256

    def project(i, carry):
        cols = pl.ds(pl.multiple_of(i * piece, piece), piece)
        part = lax.dot_general(
            weight[:, cols], normed[...], (((0,), (0,)), ((), ())), preferred_element_type=f32
        ).astype(low)
        for r in range(rows):
            u_ref[r, cols, :] = part[:, r * tok : (r + 1) * tok]
        return carry

    bring.wait()
    lax.fori_loop(0, 3 * width // piece, project, 0)
    keep_u.start()
    rim_out[...] = pack_edges([u_ref[r, :, tok - LANES :] for r in range(rows)])
    met(groups)
    rim_copy = pltpu.make_async_remote_copy(
        src_ref=rim_out,
        dst_ref=rim_in,
        send_sem=rim_sem.at[0],
        recv_sem=rim_sem.at[1],
        device_id={"seq": lax.rem(me + 1, groups)},
        device_id_type=MESH,
    )
    rim_copy.start()
    spread_taps(taps, padded, wide_taps)
    lane = lax.broadcasted_iota(jnp.int32, (STRIP, tok), 1)
    masks = [row_masks(lengths, r, me * tok, tok) for r in range(rows)]
    rim_copy.wait()
    edge_o[...] = rim_in[...]
    inward = []
    def mix(i, r, g):
        at = pl.ds(pl.multiple_of(i * STRIP + g * width, STRIP), STRIP)
        tap = [jnp.concatenate([wide_taps[j, at, :]] * (tok // LANES), axis=1) for j in range(3)]
        u = u_ref[r, at, :].astype(f32)
        one, two = window_of(u, lane, edges[at, :])
        return tap[0] * u + tap[1] * one * masks[r][0] + tap[2] * two * masks[r][1]

    for r in range(rows):
        edges[...] = unpack_edge(rim_in[...], r)

        def strip(i, carry, r=r):
            at = pl.ds(pl.multiple_of(i * STRIP, STRIP), STRIP)
            w_ref[r, at, :] = (mix(i, r, 1) * mix(i, r, 2) * masks[r][2]).astype(low)
            return carry

        lax.fori_loop(0, width // STRIP, strip, 0)
        ready = to_channels(
            groups, me, narrow, r, w_ref, recv, in_ss, in_rs, local.at[3 + rows + r]
        )
        for c in ready:
            c.start()
        inward = inward + ready

    for r in range(rows):
        edges[:width, :] = unpack_edge(rim_in[:, :width], r)

        def gate(i, carry, r=r):
            at = pl.ds(pl.multiple_of(i * STRIP, STRIP), STRIP)
            gate_ref[r, at, :] = mix(i, r, 0) * masks[r][2]
            return carry

        lax.fori_loop(0, width // STRIP, gate, 0)
    keep_gate.start()
    net = FilterNet(me, narrow, (first, first_b, mid, mid_b, freq, last, skip, decay, feats), aug)

    def build(i, carry):
        size = CHUNK * LANES
        values = net.build(pl.multiple_of(i * size, LANES), size)
        for j in range(CHUNK):
            filt[i * CHUNK + j] = values[:, j * LANES : (j + 1) * LANES]
        return carry

    lax.fori_loop(0, count // CHUNK, build, 0)
    first_stage(
        lambda at: [filt[n, pl.ds(at, 8), :] for n in range(count)], h_spec, narrow // 8
    )
    for c in tables:
        c.wait()

    def filter_freq_step(k):
        h_spec[k] = split_dot(h_spec[k], high[k], rest[k], False)

    freq_loop(freqs, unroll, filter_freq_step)
    keep_h.start()
    for c in inward:
        c.wait()
    spread(recv, wide, narrow)
    first_stage(
        lambda at: [wide[n, pl.ds(at, 8), :] for n in range(count)], w_spec, rows * narrow // 8
    )

    def forward_step(k):
        w_spec[k] = split_dot(w_spec[k], high[k], rest[k], False)

    def inverse_step(k):
        h = h_spec[k]
        hr, hi = h[:, :LANES], h[:, LANES:]
        parts = []
        for r in range(rows):
            w = w_spec[k, r * narrow : (r + 1) * narrow]
            wr, wi = w[:, :LANES], w[:, LANES:]
            parts.append(jnp.concatenate([wr * hr - wi * hi, wr * hi + wi * hr], axis=1))
        back[k] = split_dot(jnp.concatenate(parts, axis=0), high[k], rest[k], True)

    freq_loop(freqs, unroll, forward_step)
    keep_w.start()
    freq_loop(freqs, unroll, inverse_step)

    def store(n, at, v):
        wide[n, pl.ds(at, 8), :] = v

    outward = []
    for r in range(rows):
        last_stage(back, store, narrow // 8, 1.0 / (2 * count * LANES), r * narrow)
        gather_back(wide, send, narrow, r)
        ready = to_positions(groups, me, narrow, r, send, z_ref, out_ss, out_rs, local.at[3 + r])
        for c in ready:
            c.start()
        outward = outward + ready
    for c in outward + [keep_u, keep_gate, keep_h, keep_w]:
        c.wait()


def conv_back_kernel(
    rows_all,
    groups,
    g_ref,
    w_hbm,
    h_hbm,
    high_ref,
    rest_ref,
    down_hbm,
    ga_hbm,
    y2,
    q_ref,
    gm_ref,
    first,
    first_b,
    mid,
    mid_b,
    freq,
    last,
    skip,
    decay,
    feats,
    gw_ref,
    early_o,
    first_o,
    mid_o,
    last_o,
    high,
    rest,
    recv,
    wide,
    back,
    send,
    in_ss,
    in_rs,
    out_ss,
    out_rs,
    local,
    own,
    core_buf,
    step_buf,
    core_ss,
    core_rs,
    step_ss,
    step_rs,
    aug,
    w_spec,
    h_spec,
    gout,
    gup,
    gdown,
    ga_buf,
    y2_turned,
    ga_sem,
    spec_sem,
    keep_sem,
):
    me = lax.axis_index("seq")
    row = lax.axis_index("row")
    core = lax.rem(row, 2)
    narrow = h_spec.shape[1]
    count, freqs = wide.shape[0], high.shape[0]
    rows = g_ref.shape[0]
    unroll = UNROLL.get(freqs, 1)
    tables = [
        pltpu.make_async_copy(high_ref, high, local.at[0]),
        pltpu.make_async_copy(rest_ref, rest, local.at[1]),
    ]
    piece = ga_buf.shape[2]
    pieces = ga_hbm.shape[1] // piece
    low, f32 = jnp.bfloat16, jnp.float32

    def part_copy(src, buf, sem, i, slot):
        cols = pl.ds(pl.multiple_of(i * piece, piece), piece)
        return pltpu.make_async_copy(src.at[:, cols], buf.at[slot], sem.at[slot])

    def stream(src, buf, sem, body):
        def step(i, carry):
            slot = lax.rem(i, 2)

            @pl.when(i + 1 < pieces)
            def _():
                part_copy(src, buf, sem, i + 1, 1 - slot).start()

            part_copy(src, buf, sem, i, slot).wait()
            body(pl.ds(pl.multiple_of(i * piece, piece), piece), buf[slot])
            return carry

        lax.fori_loop(0, pieces, step, 0)

    bring = pltpu.make_async_copy(down_hbm, gdown, spec_sem.at[2])
    bring.start()
    part_copy(ga_hbm, ga_buf, ga_sem, 0, 0).start()
    spectra = [
        pltpu.make_async_copy(w_hbm, w_spec, spec_sem.at[0]),
        pltpu.make_async_copy(h_hbm, h_spec, spec_sem.at[1]),
    ]
    for c in tables + spectra:
        c.start()
    greet_all(rows_all, groups, me, row)
    inward = []
    for r in range(rows):
        inward = inward + to_channels(
            groups, me, narrow, r, g_ref, recv, in_ss, in_rs, local.at[3 + rows + r]
        )
    for c in inward:
        c.start()
    early = early_crew(groups, me, core, gout, gup, gdown, own, down_hbm)
    early.core_setup(core_buf, core_ss, core_rs, row + 1 - 2 * core)
    early.step_setup(step_buf, step_ss, step_rs, [range(n) for n in EARLY_STEPS])

    def up_part(cols, part):
        gup[:, cols] = jnp.dot(y2_turned[...], part, preferred_element_type=f32).astype(low)

    up_sum, down_sum, out_sum = early.members
    down_sum.core_start()

    y2_turned[...] = y2[...].T
    stream(ga_hbm, ga_buf, ga_sem, up_part)
    up_sum.core_start()
    bring.wait()
    down_sum.core_finish()
    total = None
    for r in range(rows):
        tok = q_ref.shape[2]
        part = jnp.dot(
            q_ref[r], gm_ref[r * tok : (r + 1) * tok, :], preferred_element_type=f32
        )
        total = part if total is None else total + part
    gout[...] = total.astype(low)
    out_sum.core_start()
    up_sum.core_finish()
    out_sum.core_finish()
    for c in tables + spectra:
        c.wait()
    for c in inward:
        c.wait()
    spread(recv, wide, narrow)
    first_stage(
        lambda at: [wide[n, pl.ds(at, 8), :] for n in range(count)], back, rows * narrow // 8
    )

    def forward_step(k):
        back[k, : rows * narrow] = split_dot(back[k, : rows * narrow], high[k], rest[k], False)

    def inverse_step(k):
        h = h_spec[k]
        hr, hi = h[:, :LANES], h[:, LANES:]
        parts = []
        hsum = None
        for r in range(rows):
            w = w_spec[k, r * narrow : (r + 1) * narrow]
            wr, wi = w[:, :LANES], w[:, LANES:]
            g = back[k, r * narrow : (r + 1) * narrow]
            gr, gi = g[:, :LANES], g[:, LANES:]
            parts.append(jnp.concatenate([hr * gr + hi * gi, hr * gi - hi * gr], axis=1))
            pair = (wr * gr + wi * gi, wr * gi - wi * gr)
            hsum = pair if hsum is None else (hsum[0] + pair[0], hsum[1] + pair[1])
        parts.append(jnp.concatenate(hsum, axis=1))
        back[k] = split_dot(jnp.concatenate(parts, axis=0), high[k], rest[k], True)

    freq_loop(freqs, unroll, forward_step)
    freq_loop(freqs, unroll, inverse_step)

    def store(n, at, v):
        wide[n, pl.ds(at, 8), :] = v

    outward = []
    for r in range(rows):
        last_stage(back, store, narrow // 8, 1.0 / (2 * count * LANES), r * narrow)
        gather_back(wide, send, narrow, r)
        ready = to_positions(groups, me, narrow, r, send, gw_ref, out_ss, out_rs, local.at[3 + r])
        for c in ready:
            c.start()
        outward = outward + ready
    last_stage(back, store, narrow // 8, 1.0 / (2 * count * LANES), rows * narrow)
    net = FilterNet(me, narrow, (first, first_b, mid, mid_b, freq, last, skip, decay, feats), aug)
    for out in (first_o, mid_o, last_o):
        out[...] = jnp.zeros_like(out)

    def pull(i, carry):
        size = CHUNK * LANES
        grad = [wide[i * CHUNK + j, rows * narrow :, :] for j in range(CHUNK)]
        net.pull(
            pl.multiple_of(i * size, LANES),
            size,
            jnp.concatenate(grad, axis=1),
            first_o,
            mid_o,
            last_o,
        )
        return carry

    lax.fori_loop(0, count // CHUNK, pull, 0)
    kept = []
    for p, h in enumerate(early.members):
        k = EARLY_STEPS[p] - 1
        for j in range(2):
            h.finish(k, j)
            i, size = h.pieces(k)[j]
            kept.append(
                pltpu.make_async_copy(
                    own[p].at[pl.ds(h.slot(k + 1) + i, size)],
                    early_o[p].at[pl.ds(i, size)],
                    keep_sem.at[p, j],
                )
            )
            kept[-1].start()
    for c in kept:
        c.wait()
    early.wait_core_sends()
    early.wait_sends()
    for c in outward:
        c.wait()


def conv_scratch(groups, rows, narrow, tok, freqs, count, extra):
    low, f32 = jnp.bfloat16, jnp.float32
    dma = pltpu.SemaphoreType.DMA
    wide_rows = (rows + extra) * narrow
    out = [
        pltpu.VMEM((freqs, LANES, 2 * LANES), low),
        pltpu.VMEM((freqs, LANES, 2 * LANES), low),
        pltpu.VMEM((groups, rows, narrow, tok), low),
        pltpu.VMEM((count, wide_rows, LANES), f32),
    ]
    return out + [
        pltpu.VMEM((freqs, wide_rows, 2 * LANES), f32),
        pltpu.VMEM((groups, rows, narrow, tok), low),
        dma((groups - 1, rows)),
        dma((groups - 1, rows)),
        dma((groups - 1, rows)),
        dma((groups - 1, rows)),
        dma((3 + 2 * rows,)),
    ]


def conv_params(cid):
    return pltpu.CompilerParams(
        collective_id=cid, has_side_effects=True, vmem_limit_bytes=VMEM_LIMIT
    )


def conv_forward(block, lengths, gain, offset, weight, taps, params, tables):
    rows, tok, width = block.shape
    groups = lax.axis_size("seq")
    narrow, length = width // groups, tok * groups
    count = length // LANES
    freqs = count + 1
    low, f32 = jnp.bfloat16, jnp.float32
    vm = pl.BlockSpec(memory_space=pltpu.VMEM)
    sm = pl.BlockSpec(memory_space=pltpu.SMEM)
    hbm = pl.BlockSpec(memory_space=pl.ANY)
    return pl.pallas_call(
        functools.partial(conv_kernel, groups),
        out_shape=(
            jax.ShapeDtypeStruct((rows, width, tok), low),
            jax.ShapeDtypeStruct((freqs, rows * narrow, 2 * LANES), f32),
            jax.ShapeDtypeStruct((freqs, narrow, 2 * LANES), f32),
            jax.ShapeDtypeStruct((rows, 3 * width, tok), low),
            jax.ShapeDtypeStruct((rows, width, tok), f32),
            jax.ShapeDtypeStruct((8, 3 * width), f32),
        ),
        in_specs=[vm, sm, vm, vm, hbm] + [vm] * 10 + [hbm, hbm],
        out_specs=(vm, hbm, hbm, hbm, hbm, vm),
        scratch_shapes=conv_scratch(groups, rows, narrow, tok, freqs, count, 0)
        + [
            pltpu.VMEM((params[-1].shape[0], params[0].shape[1]), f32),
            pltpu.VMEM((count, narrow, LANES), f32),
            pltpu.VMEM((width, rows * tok), low),
            pltpu.VMEM((rows, width, tok), low),
            pltpu.VMEM((8, 3 * width), f32),
            pltpu.VMEM((3, 3 * width, LANES), f32),
            pltpu.VMEM((3 * width, LANES), f32),
            pltpu.VMEM((8, 3 * width), f32),
            pltpu.VMEM((8, 3 * width), f32),
            pltpu.SemaphoreType.DMA((2,)),
            pltpu.VMEM((freqs, rows * narrow, 2 * LANES), f32),
            pltpu.VMEM((freqs, narrow, 2 * LANES), f32),
            pltpu.VMEM((rows, 3 * width, tok), low),
            pltpu.VMEM((rows, width, tok), f32),
            pltpu.VMEM(weight.shape, low),
            pltpu.SemaphoreType.DMA((5,)),
        ],
        compiler_params=conv_params(1),
        name="conv_forward",
    )(block, lengths, gain, offset, weight, taps, *params, *tables)


def conv_backward(grad, w_spec, h_spec, tables, grad_down, grad_pre, y2, q, gm, params):
    rows, _, tok = grad.shape
    freqs, narrow, _ = h_spec.shape
    groups = lax.axis_size("seq")
    count = freqs - 1
    width, ffn = q.shape[1], grad_pre.shape[1]
    half = width // 2
    piece = width
    vm = pl.BlockSpec(memory_space=pltpu.VMEM)
    hbm = pl.BlockSpec(memory_space=pl.ANY)
    low, f32 = jnp.bfloat16, jnp.float32
    dma = pltpu.SemaphoreType.DMA
    kept = [groups >> n for n in EARLY_STEPS]
    feat_rows, hidden = params[-1].shape[0], params[0].shape[1]
    return pl.pallas_call(
        functools.partial(conv_back_kernel, lax.axis_size("row"), groups),
        out_shape=(
            jax.ShapeDtypeStruct(grad.shape, low),
            [jax.ShapeDtypeStruct((c, n, narrow, half), low) for c, n in zip(kept, EARLY)],
            jax.ShapeDtypeStruct((feat_rows, LANES), f32),
            jax.ShapeDtypeStruct((hidden, LANES), f32),
            jax.ShapeDtypeStruct((narrow, LANES), f32),
        ),
        in_specs=[vm] + [hbm] * 6 + [vm] * 12,
        out_specs=(vm, [hbm] * 3, vm, vm, vm),
        scratch_shapes=conv_scratch(groups, rows, narrow, tok, freqs, count, 1)
        + [
            [pltpu.VMEM((groups, n, narrow, half), low) for n in EARLY],
            [
                pltpu.VMEM((width, 4 * half), low),
                pltpu.VMEM((ffn, half), low),
                pltpu.VMEM((width, half), low),
            ],
            [
                [pltpu.VMEM((groups >> (k + 1), n, narrow, half), low) for k in range(c)]
                for c, n in zip(EARLY_STEPS, EARLY)
            ],
            dma((len(EARLY),)),
            dma((len(EARLY),)),
            [[dma((2,)) for k in range(c)] for c in EARLY_STEPS],
            [[dma((2,)) for k in range(c)] for c in EARLY_STEPS],
            pltpu.VMEM((feat_rows, hidden), f32),
            pltpu.VMEM(w_spec.shape, f32),
            pltpu.VMEM(h_spec.shape, f32),
            pltpu.VMEM((width, width), low),
            pltpu.VMEM((width, ffn), low),
            pltpu.VMEM((ffn, width), low),
            pltpu.VMEM((2, y2.shape[0], piece), low),
            pltpu.VMEM((width, y2.shape[0]), low),
            dma((2,)),
            dma((3,)),
            dma((len(EARLY), 2)),
        ],
        compiler_params=conv_params(2),
        name="conv_backward",
    )(grad, w_spec, h_spec, *tables, grad_down, grad_pre, y2, q, gm, *params)


def shards(
    block_in,
    lengths,
    mixer_gain,
    mixer_bias,
    in_weight,
    short_taps,
    filter_in,
    filter_in_bias,
    filter_mid,
    filter_mid_bias,
    filter_freq,
    filter_out,
    filter_skip,
    decay_rate,
    out_weight,
    feed_gain,
    feed_bias,
    up_weight,
    down_weight,
    cotangent,
):
    _, tok_count, model_width = block_in.shape
    length = tok_count * lax.axis_size("seq")
    block_float = block_in.astype(jnp.float32)
    tables = tuple(jnp.asarray(t) for t in spectrum_tables(length))
    params = (
        filter_in,
        filter_in_bias,
        filter_mid,
        filter_mid_bias,
        filter_freq,
        filter_out,
        filter_skip,
        decay_rate,
        jnp.asarray(feature_rows(length, filter_in.shape[0])),
    )
    back_home, w_spec, h_spec, projected, gate_out, edges = conv_forward(
        block_in, lengths, mixer_gain, mixer_bias, in_weight, short_taps, params, tables
    )
    conv_float = back_home.astype(jnp.float32)
    product_low = (gate_out * conv_float).astype(jnp.bfloat16)
    mixed = block_float + jnp.einsum(
        "rct,cd->rtd", product_low, out_weight, preferred_element_type=jnp.float32
    )
    normed_two, feed_pull = jax.vjp(layer_norm, mixed, feed_gain, feed_bias)
    normed_two_low = normed_two.astype(jnp.bfloat16)
    pre_act = jnp.einsum(
        "rtd,df->rtf", normed_two_low, up_weight, preferred_element_type=jnp.float32
    )
    activ, gelu_pull = jax.vjp(jax.nn.gelu, pre_act)
    activ_low = activ.astype(jnp.bfloat16)
    block_out = (
        mixed
        + jnp.einsum("rtf,fd->rtd", activ_low, down_weight, preferred_element_type=jnp.float32)
    ).astype(jnp.bfloat16)
    grad_float = cotangent.astype(jnp.float32)
    grad_down = jnp.einsum("rtf,rtd->fd", activ_low, cotangent, preferred_element_type=jnp.float32)
    grad_activ = jnp.einsum(
        "rtd,fd->rtf", cotangent, down_weight, preferred_element_type=jnp.float32
    )
    grad_pre = gelu_pull(grad_activ)[0].astype(jnp.bfloat16)
    grad_normed_two = jnp.einsum(
        "rtf,df->rtd", grad_pre, up_weight, preferred_element_type=jnp.float32
    )
    grad_mixed_part, grad_feed_gain, grad_feed_bias = feed_pull(grad_normed_two)
    grad_mixed = grad_float + grad_mixed_part
    grad_mixed_low = grad_mixed.astype(jnp.bfloat16)
    grad_product = jnp.einsum(
        "rtd,cd->rct", grad_mixed_low, out_weight, preferred_element_type=jnp.float32
    )
    grad_gate_out = grad_product * conv_float
    grad_conv = (grad_product * gate_out).astype(jnp.bfloat16)

    def flat_rows(v):
        return v.reshape(-1, v.shape[-1])

    grad_carried, early, first_sum, mid_sum, last_sum = conv_backward(
        grad_conv,
        w_spec,
        h_spec,
        tables,
        grad_down.astype(jnp.bfloat16),
        flat_rows(grad_pre),
        flat_rows(normed_two_low),
        product_low,
        flat_rows(grad_mixed_low),
        params,
    )
    grad_input, fin, small, leads = finish(
        grad_carried,
        grad_gate_out,
        projected,
        edges,
        lengths,
        short_taps,
        in_weight,
        block_in,
        grad_mixed,
        (mixer_gain, mixer_bias, grad_feed_gain, grad_feed_bias),
        early,
        (mid_sum, first_sum, last_sum),
    )
    *done, grad_input = unpack(
        fin, small, leads, grad_input, filter_in.shape[0], filter_mid.shape[0], model_width
    )
    return (block_out, grad_input, *done)


def solution(mesh):
    placed = (
        P("row", "seq", None),
        P("row", None),
        P(),
        P(),
        P(),
        P(),
        P(),
        P(),
        P(),
        P(),
        P(),
        P(),
        P(),
        P(),
        P(),
        P(),
        P(),
        P(),
        P(),
        P("row", "seq", None),
    )
    return jax.shard_map(
        shards,
        mesh=mesh,
        in_specs=placed,
        out_specs=(
            P("row", "seq", None),
            P("row", "seq", None),
            P(),
            P(),
            P("seq", None),
            P(),
            P(),
            P(),
            P(),
            P(),
            P(),
            P(),
            P(),
            P("seq", None),
            P(),
            P(),
            P("seq", None),
            P("seq", None),
        ),
        check_vma=False,
    )
```
